128 devices in a mesh: ch: 32 (over y, z_hi, x), img: 4 (over z_lo, core).
Axes of the slice: x: 4, y: 4, z: 4 (z_hi: 2, z_lo: 2; z = z_hi * 2 + z_lo), core: 2. Of those that a mesh axis runs over, the one named last changes fastest.
Arguments:
- inputs: bfloat16 [256, 128, 256], P('ch', 'img'), may hold values from -6 to 6
- timesteps: int32 [128], P('img'), may hold values from 0 to 999
- keep_mask: int32 [256, 128, 256], P('ch', 'img'), may hold values 0 or 1
- norm_gain: float32 [3, 256], P(None, 'ch'), may hold values from 0.1 to 1.9
- norm_bias: float32 [3, 256], P(None, 'ch'), may hold values from -4 to 4
- conv_weight: bfloat16 [2, 9, 256, 256], P(None, None, 'ch'), may hold values from -0.125 to 0.125
- conv_bias: float32 [2, 256], P(None, 'ch'), may hold values from -4 to 4
- temb_weight: bfloat16 [512, 256], P(None, 'ch'), may hold values from -0.25 to 0.25
- temb_bias: float32 [256], P('ch'), may hold values from -4 to 4
- qkv_weight: bfloat16 [3, 256, 256], P(None, 'ch'), may hold values from -0.375 to 0.375
- qv_bias: float32 [2, 256], P(None, 'ch'), may hold values from -4 to 4
- out_weight: bfloat16 [256, 256], P('ch'), may hold values from -3 to 3
- out_bias: float32 [256], P('ch'), may hold values from -4 to 4
- cotangent: bfloat16 [256, 128, 256], P('ch', 'img'), may hold values from -6 to 6
Outputs:
- outputs: bfloat16 [256, 128, 256], P('ch', 'img')
- input_grad: bfloat16 [256, 128, 256], P('ch', 'img')
- norm_gain_grad: float32 [3, 256], P(None, 'ch')
- norm_bias_grad: float32 [3, 256], P(None, 'ch')
- conv_weight_grad: float32 [2, 9, 256, 256], P(None, None, 'ch')
- conv_bias_grad: float32 [2, 256], P(None, 'ch')
- temb_weight_grad: float32 [512, 256], P(None, 'ch')
- temb_bias_grad: float32 [256], P('ch')
- qkv_weight_grad: float32 [3, 256, 256], P(None, 'ch')
- qv_bias_grad: float32 [2, 256], P(None, 'ch')
- out_weight_grad: float32 [256, 256], P('ch')
- out_bias_grad: float32 [256], P('ch')
The draws below stay inside these ranges and needn't reach their ends.
All inputs are finite; a program needn't handle non-finite values. No bound on the sum of `keep_mask` on one device may be relied on, other than what follows from the above.
Results may differ from the reference program's by a relative error of at most 0.04.
Values may be sent and summed in bfloat16 or wider, within the bound.
No kernel may reach another device: no remote copies, remote signals or barrier semaphores. Data moves between devices by JAX's collectives and lax.ppermute only.
A program may use at most 256 MiB of HBM per device.

```python
import math
import jax
import jax.numpy as jnp
from jax import lax

C = 256
TEMB = 512
GROUPS = 32
SIDE = 16
P_SIZE = 256
IMAGES = 128


def place_ends(values, own_key, low, top_value):
    longest = values.shape.index(max(values.shape))
    spots = []
    for shift in (0, 1):
        where = [jax.random.randint(jax.random.fold_in(own_key, axis), (), 0, length) for axis, length in enumerate(values.shape)]
        where[longest] = (where[longest] + shift) % values.shape[longest]
        spots.append(tuple(where))
    return values.at[spots[0]].set(low).at[spots[1]].set(top_value)


def steps_of(own_key, dims, cuts, smallest, top_value):
    factor_of = 1.0
    for axis_at, blocks in cuts:
        steps = jax.random.uniform(jax.random.fold_in(jax.random.fold_in(own_key, 6), axis_at), (blocks,), jnp.float32, smallest / len(cuts), top_value / len(cuts))
        factor_of = factor_of * jnp.repeat(jnp.exp(steps), dims[axis_at] // blocks).reshape((-1,) + (1,) * (len(dims) - 1 - axis_at))
    return factor_of


def scatter_about(own_key, extent, scale, bound, split=(), held_as=jnp.bfloat16):
    factor_of = steps_of(own_key, extent, split, -0.22, 0.18) if split else 1.0
    result = jax.random.normal(own_key, extent, jnp.float32) * scale * factor_of
    return jnp.minimum(jnp.maximum(result, -bound), bound).astype(held_as)


def setup_inputs(seed: int = 0) -> dict:
    streams_of = jax.random.split(jax.random.key(seed), 15)
    inputs = scatter_about(streams_of[0], (C, IMAGES, P_SIZE), 1.0, 6.0, ((0, 32), (1, 4)))
    timesteps = place_ends(jax.random.randint(streams_of[1], (IMAGES,), 0, 1000), jax.random.fold_in(streams_of[1], 1), 0, 999).astype(jnp.int32)
    keep_mask = place_ends((jax.random.randint(streams_of[2], (C, IMAGES, P_SIZE), 0, 10) < 9).astype(jnp.int32), jax.random.fold_in(streams_of[2], 1), 0, 1)
    norm_gain = jnp.clip(1.0 + 0.18 * jax.random.normal(streams_of[3], (3, C), jnp.float32), 0.1, 1.9)
    norm_bias = scatter_about(streams_of[4], (3, C), 0.3, 4.0, ((1, 32),), jnp.float32)
    conv_weight = scatter_about(streams_of[5], (2, 9, C, C), (9 * C) ** -0.5, 0.125, ((2, 32),))
    conv_bias = scatter_about(streams_of[6], (2, C), 0.3, 4.0, ((1, 32),), jnp.float32)
    temb_weight = scatter_about(streams_of[7], (TEMB, C), TEMB ** -0.5, 0.25, ((1, 32),))
    temb_bias = scatter_about(streams_of[8], (C,), 0.3, 4.0, ((0, 32),), jnp.float32)
    qkv_weight = scatter_about(streams_of[9], (3, C, C), C ** -0.5, 0.375, ((1, 32),))
    qv_bias = scatter_about(streams_of[10], (2, C), 0.3, 4.0, ((1, 32),), jnp.float32)
    out_weight = scatter_about(streams_of[11], (C, C), (C // 64) ** -0.5, 3.0, ((0, 32),))
    out_bias = scatter_about(streams_of[12], (C,), 0.3, 4.0, ((0, 32),), jnp.float32)
    cotangent = scatter_about(streams_of[13], (C, IMAGES, P_SIZE), 1.0, 6.0, ((0, 32), (1, 4)))
    return dict(inputs=inputs, timesteps=timesteps, keep_mask=keep_mask, norm_gain=norm_gain, norm_bias=norm_bias, conv_weight=conv_weight, conv_bias=conv_bias, temb_weight=temb_weight, temb_bias=temb_bias, qkv_weight=qkv_weight, qv_bias=qv_bias, out_weight=out_weight, out_bias=out_bias, cotangent=cotangent)


@jax.custom_vjp
def low(v):
    return lax.optimization_barrier(v.astype(jnp.bfloat16)).astype(jnp.float32)

@jax.custom_vjp
def low_back(v):
    return v

def low_keep(v):
    return (low(v), None)

def low_pass(kept, grad):
    return (grad,)

def back_keep(v):
    return (v, None)

def back_low(kept, grad):
    return (low(grad),)
low.defvjp(low_keep, low_pass)
low_back.defvjp(back_keep, back_low)
norm_eps = 1e-06
group_images = 16

def swish(values):
    return values * jax.nn.sigmoid(values)

def group_norm(values, gain_row, bias_row):
    channels, images, positions = values.shape
    grouped = values.reshape(GROUPS, channels // GROUPS, images, positions)
    average = lax.optimization_barrier(jnp.mean(grouped, axis=(1, 3), keepdims=True))
    centered = grouped - average
    spread = lax.optimization_barrier(jnp.mean(centered * centered, axis=(1, 3), keepdims=True))
    normalized = (centered * lax.rsqrt(spread + norm_eps)).reshape(channels, images, positions)
    return normalized * gain_row[:, None, None] + bias_row[:, None, None]

def shift_cells(values, row_step, col_step):
    margin = SIDE + 1
    positions = values.shape[2]
    padded = jnp.pad(values, ((0, 0), (0, 0), (margin, margin)))
    offset = margin + row_step * SIDE + col_step
    moved = lax.slice_in_dim(padded, offset, offset + positions, axis=2)
    column = jnp.arange(positions, dtype=jnp.int32) % SIDE + col_step
    valid = ((column >= 0) & (column < SIDE)).astype(values.dtype)
    return moved * valid

def convolve(kernel, values):
    summed = jnp.zeros((kernel.shape[1],) + values.shape[1:], jnp.float32)
    for tap_index in range(9):
        moved = shift_cells(values, tap_index // 3 - 1, tap_index % 3 - 1)
        summed = summed + jnp.einsum('oi,ibp->obp', kernel[tap_index], moved, precision=lax.Precision.HIGHEST)
    return summed

def time_features(timesteps):
    half_dim = TEMB // 2
    rates = jnp.exp(-math.log(10000.0) * jnp.arange(half_dim, dtype=jnp.float32) / (half_dim - 1))
    angles = timesteps.astype(jnp.float32)[:, None] * rates[None, :]
    return jnp.concatenate([jnp.sin(angles), jnp.cos(angles)], axis=1)

def softmax_rows(scores):
    row_max = lax.optimization_barrier(jnp.max(scores, axis=-1, keepdims=True))
    shifted_exp = jnp.exp(scores - row_max)
    return shifted_exp / lax.optimization_barrier(jnp.sum(shifted_exp, axis=-1, keepdims=True))

def forward(values, features, keep_scale, weights):
    norm_gain, norm_bias, conv_weight, conv_bias, temb_weight, temb_bias, qkv_weight, qv_bias, out_weight, out_bias = weights
    highest = lax.Precision.HIGHEST
    first_act = low(swish(group_norm(values, norm_gain[0], norm_bias[0])))
    offsets = jnp.dot(swish(features), temb_weight, precision=highest) + temb_bias[None, :]
    middle = low_back(convolve(conv_weight[0], first_act)) + conv_bias[0][:, None, None] + offsets.T[:, :, None]
    second_act = low(swish(group_norm(middle, norm_gain[1], norm_bias[1])) * keep_scale)
    residual = values + low_back(convolve(conv_weight[1], second_act)) + conv_bias[1][:, None, None]
    normed = low(group_norm(residual, norm_gain[2], norm_bias[2]))
    projected = jnp.einsum('goi,ibp->gobp', qkv_weight, normed, precision=highest)
    queries = low_back(low(projected[0] + qv_bias[0][:, None, None]))
    keys_proj = low_back(low(projected[1]))
    vals = low_back(low(projected[2] + qv_bias[1][:, None, None]))
    scores = low_back(jnp.einsum('cbp,cbj->bpj', queries, keys_proj, precision=highest) * C ** (-0.5))
    probs_low = low(softmax_rows(scores))
    attended = low_back(low(jnp.einsum('cbj,bpj->cbp', vals, probs_low, precision=highest)))
    return residual + jnp.einsum('oi,ibp->obp', out_weight, attended, precision=highest) + out_bias[:, None, None]

def reference(inputs, timesteps, keep_mask, norm_gain, norm_bias, conv_weight, conv_bias, temb_weight, temb_bias, qkv_weight, qv_bias, out_weight, out_bias, cotangent):
    params = (norm_gain, norm_bias, conv_weight.astype(jnp.float32), conv_bias, temb_weight.astype(jnp.float32), temb_bias, qkv_weight.astype(jnp.float32), qv_bias, out_weight.astype(jnp.float32), out_bias)
    group_count = IMAGES // group_images

    def split_images(array):
        return jnp.moveaxis(array.reshape(array.shape[0], group_count, group_images, P_SIZE), 1, 0)
    stacked_inputs = split_images(inputs.astype(jnp.float32))
    stacked_mask = split_images(keep_mask.astype(jnp.float32) * (1.0 / 0.9))
    stacked_cot = split_images(cotangent.astype(jnp.float32))
    stacked_steps = timesteps.reshape(group_count, group_images)

    def one_group(summed, pieces):
        group_inputs, group_steps, group_mask, group_cot = pieces
        features = time_features(group_steps)

        def local_forward(values, weights):
            return forward(values, features, group_mask, weights)
        results, pullback = jax.vjp(local_forward, group_inputs, params)
        group_grad, weight_grads = pullback(group_cot)
        summed = jax.tree.map(lambda a, b: a + b, summed, weight_grads)
        return (summed, (results, group_grad))
    zeros_tree = jax.tree.map(jnp.zeros_like, params)
    totals, (results, group_grads) = lax.scan(one_group, zeros_tree, (stacked_inputs, stacked_steps, stacked_mask, stacked_cot))

    def join_images(array):
        return jnp.moveaxis(array, 0, 1).reshape(array.shape[1], IMAGES, P_SIZE).astype(jnp.bfloat16)
    return (join_images(results), join_images(group_grads), totals[0], totals[1], totals[2], totals[3], totals[4], totals[5], totals[6], totals[7], totals[8], totals[9])
```

```python
import functools
import math

import jax
import jax.numpy as jnp
from jax import lax
from jax.experimental import pallas as pl
from jax.experimental.pallas import tpu as pltpu
from jax.sharding import PartitionSpec as P

C = 256
TEMB = 512
SIDE = 16
POS = 256
SHARDS = 32
ROWS = C // SHARDS
HALF = 128
WBLOCKS = 22
WROWS = WBLOCKS * ROWS
NORM_EPS = 1e-06
GROUP_SIZE = ROWS * POS
F32 = jnp.float32
BF16 = jnp.bfloat16

OFFSETS, GAINS, BIASES, CONV_BIAS, QV_BIAS, OUT_BIAS = 0, 1, 4, 7, 9, 11
D_GAINS, D_BIASES, D_CONV_BIAS, D_QV_BIAS, D_OUT_BIAS = 0, 3, 6, 8, 10
PART = 16


def dot_nn(a, b):
    return lax.dot_general(a, b, (((1,), (0,)), ((), ())), preferred_element_type=F32)


def dot_nt(a, b):
    return lax.dot_general(a, b, (((1,), (1,)), ((), ())), preferred_element_type=F32)


def dot_tn(a, b):
    return lax.dot_general(a, b, (((0,), (0,)), ((), ())), preferred_element_type=F32)


def group_sum(values):
    column = jnp.sum(values, axis=1, keepdims=True)
    return group_column(column)


def group_column(column):
    grouped = column.reshape(SHARDS, ROWS, 1)
    total = jnp.sum(grouped, axis=1, keepdims=True)
    return jnp.broadcast_to(total, grouped.shape).reshape(C, 1)


def norm_hat(values):
    average = group_sum(values) * (1.0 / GROUP_SIZE)
    centered = values - average
    spread = group_sum(centered * centered) * (1.0 / GROUP_SIZE)
    inverse = lax.rsqrt(spread + NORM_EPS)
    return centered * inverse, inverse


def norm_back(hat, inverse, grad_out, gain):
    gain_grad = jnp.sum(grad_out * hat, axis=1, keepdims=True)
    bias_grad = jnp.sum(grad_out, axis=1, keepdims=True)
    first_mean = group_column(bias_grad * gain) * (1.0 / GROUP_SIZE)
    second_mean = group_column(gain_grad * gain) * (1.0 / GROUP_SIZE)
    grad_in = inverse * (grad_out * gain - first_mean - hat * second_mean)
    return grad_in, gain_grad, bias_grad


def sigmoid(values):
    return 1.0 / (1.0 + jnp.exp(-values))


def tap_steps(tap):
    return tap // 3 - 1, tap % 3 - 1


def shifted(values, row_step, col_step, axis):
    if row_step == 0 and col_step == 0:
        return values
    moved = pltpu.roll(values, (-(row_step * SIDE + col_step)) % POS, axis)
    shape = (1, POS) if axis == 1 else (POS, POS)
    cell = lax.broadcasted_iota(jnp.int32, shape, axis)
    valid = None
    if col_step:
        column = (cell & (SIDE - 1)) + col_step
        valid = (column >= 0) & (column < SIDE)
    if row_step:
        row = cell + row_step * SIDE
        inside = (row >= 0) & (row < POS)
        valid = inside if valid is None else valid & inside
    return moved * valid.astype(F32)


def block_kernel(
    core_ref, recv_ref, other_ref, send_ref, swap_ref, weights, taps_one, taps_two, back
):
    first_core = core_ref[0] == 0

    for pair in range(WBLOCKS // 2):
        mine = recv_ref[:, 16 * pair : 16 * pair + 16, :].astype(F32)
        theirs = other_ref[:, 16 * pair : 16 * pair + 16, :].astype(F32)
        for part in range(2):
            rows = slice(ROWS * part, ROWS * part + ROWS)
            a = mine[:, rows, :].reshape(C, HALF)
            b = theirs[:, rows, :].reshape(C, HALF)
            weights[2 * pair + part, :, 0:HALF] = jnp.where(first_core, a, b).astype(BF16)
            weights[2 * pair + part, :, HALF:C] = jnp.where(first_core, b, a).astype(BF16)

    def image(at):
        block = recv_ref[:, at : at + 16, :].astype(F32)
        left = block[:, 0:ROWS, :].reshape(C, HALF)
        right = block[:, ROWS : 2 * ROWS, :].reshape(C, HALF)
        return jnp.concatenate([left, right], axis=1)

    source = image(WROWS)
    keep = image(WROWS + 16) * (1.0 / 0.9)
    cotangent = image(WROWS + 32)
    columns = recv_ref[:, WROWS + 48 : WROWS + 56, :].astype(F32).reshape(C, HALF)

    def param(lane):
        high = columns[:, lane : lane + 1]
        middle_part = columns[:, PART + lane : PART + lane + 1]
        low = columns[:, 2 * PART + lane : 2 * PART + lane + 1]
        return high + middle_part + low

    gains = [param(GAINS + j) for j in range(3)]
    biases = [param(BIASES + j) for j in range(3)]

    def store_taps(target, values):
        for tap in range(9):
            row_step, col_step = tap_steps(tap)
            target[tap, :, :] = shifted(values, row_step, col_step, 1).astype(BF16)

    def convolve(first_block, taps):
        total = None
        for tap in range(9):
            product = dot_nn(weights[first_block + tap], taps[tap])
            total = product if total is None else total + product
        return total

    hat_one, inverse_one = norm_hat(source)
    pre_one = hat_one * gains[0] + biases[0]
    first_act = (pre_one * sigmoid(pre_one)).astype(BF16).astype(F32)
    store_taps(taps_one, first_act)
    middle = convolve(0, taps_one) + (param(CONV_BIAS) + param(OFFSETS))
    hat_two, inverse_two = norm_hat(middle)
    pre_two = hat_two * gains[1] + biases[1]
    second_act = (pre_two * sigmoid(pre_two) * keep).astype(BF16).astype(F32)
    store_taps(taps_two, second_act)
    residual = source + convolve(9, taps_two) + param(CONV_BIAS + 1)
    hat_three, inverse_three = norm_hat(residual)
    normed = (hat_three * gains[2] + biases[2]).astype(BF16)
    queries = (dot_nn(weights[18], normed) + param(QV_BIAS)).astype(BF16)
    keys = dot_nn(weights[19], normed).astype(BF16)
    vals = (dot_nn(weights[20], normed) + param(QV_BIAS + 1)).astype(BF16)
    scale = C ** (-0.5)
    scores = dot_tn(queries, keys) * scale
    exps = jnp.exp(scores - jnp.max(scores, axis=1, keepdims=True))
    probs = exps / jnp.sum(exps, axis=1, keepdims=True)
    probs_low = probs.astype(BF16)
    attended = dot_nt(vals, probs_low).astype(BF16)
    outputs = residual + dot_nn(weights[21], attended) + param(OUT_BIAS)

    def put_image(at, values):
        left = values[:, 0:HALF].reshape(SHARDS, ROWS, HALF)
        right = values[:, HALF:C].reshape(SHARDS, ROWS, HALF)
        send_ref[:, at : at + 16, :] = jnp.concatenate([left, right], axis=1).astype(BF16)

    put_image(WROWS, outputs)

    pending = {}

    def put_weight_grad(block, values):
        pending[block] = values
        pair = block // 2
        if 2 * pair in pending and 2 * pair + 1 in pending:
            a, b = pending.pop(2 * pair), pending.pop(2 * pair + 1)
            low = [v[:, 0:HALF].reshape(SHARDS, ROWS, HALF) for v in (a, b)]
            high = [v[:, HALF:C].reshape(SHARDS, ROWS, HALF) for v in (a, b)]
            low, high = jnp.concatenate(low, axis=1), jnp.concatenate(high, axis=1)
            rows = slice(16 * pair, 16 * pair + 16)
            send_ref[:, rows, :] = jnp.where(first_core, low, high).astype(BF16)
            swap_ref[:, rows, :] = jnp.where(first_core, high, low).astype(BF16)

    cot_low = cotangent.astype(BF16)
    out_bias_grad = jnp.sum(cotangent, axis=1, keepdims=True)
    put_weight_grad(21, dot_nt(cot_low, attended))
    attended_grad = dot_tn(weights[21], cot_low).astype(BF16)
    dprobs = dot_tn(attended_grad, vals)
    row_dot = jnp.sum(probs * dprobs, axis=1, keepdims=True)
    dscores = (probs * (dprobs - row_dot)).astype(BF16)
    query_grad = (dot_nt(keys, dscores) * scale).astype(BF16)
    key_grad = (dot_nn(queries, dscores) * scale).astype(BF16)
    value_grad = dot_nn(attended_grad, probs_low).astype(BF16)
    query_bias_grad = jnp.sum(query_grad.astype(F32), axis=1, keepdims=True)
    value_bias_grad = jnp.sum(value_grad.astype(F32), axis=1, keepdims=True)
    normed_grad = None
    for k, gradient in enumerate((query_grad, key_grad, value_grad)):
        put_weight_grad(18 + k, dot_nt(gradient, normed))
        product = dot_tn(weights[18 + k], gradient)
        normed_grad = product if normed_grad is None else normed_grad + product
    branch_three, gain_three, bias_three = norm_back(
        hat_three, inverse_three, normed_grad, gains[2]
    )
    residual_grad = cotangent + branch_three
    conv_two_bias = jnp.sum(residual_grad, axis=1, keepdims=True)

    def conv_back(first_block, gradient, taps):
        low = gradient.astype(BF16)
        for tap in range(9):
            put_weight_grad(first_block + tap, dot_nt(low, taps[tap]))
        turned = low.astype(F32).T
        total = None
        for tap in range(9):
            row_step, col_step = tap_steps(tap)
            moved = shifted(turned, -row_step, -col_step, 0).astype(BF16)
            product = dot_nn(moved, weights[first_block + tap])
            total = product if total is None else total + product
        return total.T

    def slope(values):
        sigma = sigmoid(values)
        return sigma * (1.0 + values * (1.0 - sigma))

    second_grad = conv_back(9, residual_grad, taps_two)
    pre_two_grad = second_grad * keep * slope(pre_two)
    middle_grad, gain_two, bias_two = norm_back(hat_two, inverse_two, pre_two_grad, gains[1])
    conv_one_bias = jnp.sum(middle_grad, axis=1, keepdims=True)
    first_grad = conv_back(0, middle_grad, taps_one)
    pre_one_grad = first_grad * slope(pre_one)
    branch_one, gain_one, bias_one = norm_back(hat_one, inverse_one, pre_one_grad, gains[0])
    put_image(WROWS + 16, residual_grad + branch_one)

    lane = lax.broadcasted_iota(jnp.int32, (C, HALF), 1)
    table = jnp.zeros((C, HALF), F32)
    listed = (
        gain_one, gain_two, gain_three, bias_one, bias_two, bias_three,
        conv_one_bias, conv_two_bias, query_bias_grad, value_bias_grad, out_bias_grad,
    )
    for k, column in enumerate(listed):
        table = jnp.where((lane & (PART - 1)) == k, column, table)
    high = table.astype(BF16).astype(F32)
    table = jnp.where(lane < PART, high, jnp.where(lane < 2 * PART, table - high, 0.0))
    send_ref[:, WROWS + 32 : WROWS + 40, :] = table.reshape(SHARDS, ROWS, HALF).astype(BF16)


IN_ROWS = WROWS + 56
OUT_ROWS = WROWS + 40


def run_block(core, received, other):
    return pl.pallas_call(
        block_kernel,
        out_shape=(
            jax.ShapeDtypeStruct((SHARDS, OUT_ROWS, HALF), BF16),
            jax.ShapeDtypeStruct((SHARDS, WROWS, HALF), BF16),
        ),
        in_specs=[
            pl.BlockSpec(memory_space=pltpu.SMEM),
            pl.BlockSpec(memory_space=pltpu.VMEM),
            pl.BlockSpec(memory_space=pltpu.VMEM),
        ],
        out_specs=(
            pl.BlockSpec(memory_space=pltpu.VMEM),
            pl.BlockSpec(memory_space=pltpu.VMEM),
        ),
        scratch_shapes=[
            pltpu.VMEM((WBLOCKS, C, C), BF16),
            pltpu.VMEM((9, C, POS), BF16),
            pltpu.VMEM((9, C, POS), BF16),
            pltpu.VMEM((9, POS, C), BF16),
        ],
        compiler_params=pltpu.CompilerParams(vmem_limit_bytes=48 * 1024 * 1024),
    )(core, received, other)


def time_features(timesteps):
    half_dim = TEMB // 2
    rates = jnp.exp(-math.log(10000.0) * jnp.arange(half_dim, dtype=F32) / (half_dim - 1))
    angles = timesteps.astype(F32)[:, None] * rates[None, :]
    return jnp.concatenate([jnp.sin(angles), jnp.cos(angles)], axis=1)


def halves(values):
    rows, images, positions = values.shape
    cut = values.reshape(rows, images, 2, HALF).transpose(1, 2, 0, 3)
    return cut.reshape(images, 2 * rows, HALF)


def whole(blocks):
    images = blocks.shape[0]
    cut = blocks.reshape(images, 2, ROWS, HALF).transpose(2, 0, 1, 3)
    return cut.reshape(ROWS, images, POS)


def bf16_part(values):
    return lax.reduce_precision(values, exponent_bits=8, mantissa_bits=7)


def on_device(
    inputs,
    timesteps,
    keep_mask,
    norm_gain,
    norm_bias,
    conv_weight,
    conv_bias,
    temb_weight,
    temb_bias,
    qkv_weight,
    qv_bias,
    out_weight,
    out_bias,
    cotangent,
):
    member = lax.axis_index("img")
    core = member % 2
    core_pairs = [(m, m ^ 1) for m in range(4)]
    plane_pairs = [(m, m ^ 2) for m in range(4)]
    highest = lax.Precision.HIGHEST

    features = time_features(timesteps)
    swished = features * jax.nn.sigmoid(features)
    offsets = jnp.dot(swished, temb_weight.astype(F32), precision=highest) + temb_bias[None, :]

    shard = jnp.concatenate(
        [
            conv_weight.reshape(18 * ROWS, C),
            qkv_weight.reshape(3 * ROWS, C),
            out_weight.reshape(ROWS, C),
        ],
        axis=0,
    )
    shard = lax.dynamic_slice_in_dim(shard, core * HALF, HALF, 1)
    fixed = jnp.stack(
        [*norm_gain, *norm_bias, *conv_bias, *qv_bias, out_bias], axis=-1
    )
    params = jnp.concatenate(
        [offsets[:, :, None], jnp.broadcast_to(fixed[None], (SHARDS,) + fixed.shape)], axis=2
    )
    params = jnp.pad(params, ((0, 0), (0, 0), (0, PART - params.shape[2])))
    high = bf16_part(params)
    mid = bf16_part(params - high)
    low = params - high - mid
    params = jnp.pad(
        jnp.concatenate([high, mid, low], axis=2), ((0, 0), (0, 0), (0, HALF - 3 * PART))
    ).astype(BF16)
    sent = jnp.concatenate(
        [
            jnp.broadcast_to(shard[None], (SHARDS,) + shard.shape),
            halves(inputs),
            halves(keep_mask.astype(BF16)),
            halves(cotangent),
            params,
        ],
        axis=1,
    )
    received = lax.all_to_all(sent, "ch", split_axis=0, concat_axis=0, tiled=True)
    other = lax.ppermute(received, "img", core_pairs)

    send, swap = run_block(core.reshape(1), received, other)

    swapped = lax.ppermute(swap, "img", core_pairs)
    send = send + jnp.pad(swapped, ((0, 0), (0, OUT_ROWS - WROWS), (0, 0)))
    back = lax.all_to_all(send, "ch", split_axis=0, concat_axis=0, tiled=True)

    outputs = whole(back[:, WROWS : WROWS + 16])
    input_grad = whole(back[:, WROWS + 16 : WROWS + 32])
    weight_sums = jnp.sum(back[:, :WROWS].astype(F32), axis=0)
    small = back[:, WROWS + 32 :].astype(F32)
    small = small[:, :, :PART] + small[:, :, PART : 2 * PART]
    offsets_grad = small[:, :, D_CONV_BIAS]
    temb_grad = lax.dot_general(
        offsets_grad, swished, (((0,), (0,)), ((), ())), precision=highest,
        preferred_element_type=F32,
    )
    small_sums = jnp.pad(jnp.sum(small, axis=0), ((0, 0), (0, HALF - PART)))
    sums = jnp.concatenate(
        [weight_sums, small_sums, temb_grad.reshape(TEMB * ROWS // HALF, HALF)], axis=0
    )
    sums = sums + lax.ppermute(sums, "img", plane_pairs)
    theirs = lax.ppermute(sums, "img", core_pairs)

    mine_w, their_w = sums[:WROWS], theirs[:WROWS]
    weight_grads = jnp.where(
        core == 0,
        jnp.concatenate([mine_w, their_w], axis=1),
        jnp.concatenate([their_w, mine_w], axis=1),
    )
    shared = sums[WROWS:] + theirs[WROWS:]
    table = shared[:ROWS].T
    temb_weight_grad = shared[ROWS:].reshape(ROWS, TEMB).T
    return (
        outputs,
        input_grad,
        table[D_GAINS : D_GAINS + 3],
        table[D_BIASES : D_BIASES + 3],
        weight_grads[: 18 * ROWS].reshape(2, 9, ROWS, C),
        table[D_CONV_BIAS : D_CONV_BIAS + 2],
        temb_weight_grad,
        table[D_CONV_BIAS],
        weight_grads[18 * ROWS : 21 * ROWS].reshape(3, ROWS, C),
        table[D_QV_BIAS : D_QV_BIAS + 2],
        weight_grads[21 * ROWS :],
        table[D_OUT_BIAS],
    )


def solution(mesh):
    placed = (
        P("ch", "img", None),
        P("img"),
        P("ch", "img", None),
        P(None, "ch"),
        P(None, "ch"),
        P(None, None, "ch", None),
        P(None, "ch"),
        P(None, "ch"),
        P("ch"),
        P(None, "ch", None),
        P(None, "ch"),
        P("ch", None),
        P("ch"),
        P("ch", "img", None),
    )
    return jax.shard_map(
        on_device,
        mesh=mesh,
        in_specs=placed,
        out_specs=(
            P("ch", "img", None),
            P("ch", "img", None),
            P(None, "ch"),
            P(None, "ch"),
            P(None, None, "ch", None),
            P(None, "ch"),
            P(None, "ch"),
            P("ch"),
            P(None, "ch", None),
            P(None, "ch"),
            P("ch", None),
            P("ch"),
        ),
        check_vma=False,
    )
```

```python
import functools
import math

import jax
import jax.numpy as jnp
from jax import lax
from jax.experimental import pallas as pl
from jax.experimental.pallas import tpu as pltpu
from jax.sharding import PartitionSpec as P

C = 256
TEMB = 512
SIDE = 16
POS = 256
SHARDS = 32
ROWS = C // SHARDS
HALF = 128
WBLOCKS = 22
WROWS = WBLOCKS * ROWS
NORM_EPS = 1e-06
GROUP_SIZE = ROWS * POS
F32 = jnp.float32
BF16 = jnp.bfloat16

OFFSETS, GAINS, BIASES, CONV_BIAS, QV_BIAS, OUT_BIAS, TEMB_BIAS = 0, 1, 4, 7, 9, 11, 12
D_GAINS, D_BIASES, D_CONV_BIAS, D_QV_BIAS, D_OUT_BIAS = 0, 3, 6, 8, 10
PART = 16


def dot_nn(a, b):
    return lax.dot_general(a, b, (((1,), (0,)), ((), ())), preferred_element_type=F32)


def dot_nt(a, b):
    return lax.dot_general(a, b, (((1,), (1,)), ((), ())), preferred_element_type=F32)


def dot_tn(a, b):
    return lax.dot_general(a, b, (((0,), (0,)), ((), ())), preferred_element_type=F32)


def group_sum(values):
    column = jnp.sum(values, axis=1, keepdims=True)
    return group_column(column)


def group_column(column):
    grouped = column.reshape(SHARDS, ROWS, 1)
    total = jnp.sum(grouped, axis=1, keepdims=True)
    return jnp.broadcast_to(total, grouped.shape).reshape(C, 1)


def norm_hat(values):
    average = group_sum(values) * (1.0 / GROUP_SIZE)
    centered = values - average
    spread = group_sum(centered * centered) * (1.0 / GROUP_SIZE)
    inverse = lax.rsqrt(spread + NORM_EPS)
    return centered * inverse, inverse


def norm_back(hat, inverse, grad_out, gain):
    gain_grad = jnp.sum(grad_out * hat, axis=1, keepdims=True)
    bias_grad = jnp.sum(grad_out, axis=1, keepdims=True)
    first_mean = group_column(bias_grad * gain) * (1.0 / GROUP_SIZE)
    second_mean = group_column(gain_grad * gain) * (1.0 / GROUP_SIZE)
    grad_in = inverse * (grad_out * gain - first_mean - hat * second_mean)
    return grad_in, gain_grad, bias_grad


def sigmoid(values):
    return 1.0 / (1.0 + jnp.exp(-values))


def tap_steps(tap):
    return tap // 3 - 1, tap % 3 - 1


def shifted(values, row_step, col_step, axis):
    if row_step == 0 and col_step == 0:
        return values
    moved = pltpu.roll(values, (-(row_step * SIDE + col_step)) % POS, axis)
    shape = (1, POS) if axis == 1 else (POS, POS)
    cell = lax.broadcasted_iota(jnp.int32, shape, axis)
    valid = None
    if col_step:
        column = (cell & (SIDE - 1)) + col_step
        valid = (column >= 0) & (column < SIDE)
    if row_step:
        row = cell + row_step * SIDE
        inside = (row >= 0) & (row < POS)
        valid = inside if valid is None else valid & inside
    return moved * valid.astype(F32)


def block_kernel(
    core_ref, recv_ref, other_ref, send_ref, swap_ref, weights, taps_one, taps_two, back
):
    first_core = core_ref[0] == 0

    for pair in range(WBLOCKS // 2):
        mine = recv_ref[:, 16 * pair : 16 * pair + 16, :].astype(F32)
        theirs = other_ref[:, 16 * pair : 16 * pair + 16, :].astype(F32)
        for part in range(2):
            rows = slice(ROWS * part, ROWS * part + ROWS)
            a = mine[:, rows, :].reshape(C, HALF)
            b = theirs[:, rows, :].reshape(C, HALF)
            weights[2 * pair + part, :, 0:HALF] = jnp.where(first_core, a, b).astype(BF16)
            weights[2 * pair + part, :, HALF:C] = jnp.where(first_core, b, a).astype(BF16)

    def image(at):
        block = recv_ref[:, at : at + 16, :].astype(F32)
        left = block[:, 0:ROWS, :].reshape(C, HALF)
        right = block[:, ROWS : 2 * ROWS, :].reshape(C, HALF)
        return jnp.concatenate([left, right], axis=1)

    source = image(WROWS)
    keep = image(WROWS + 16) * (1.0 / 0.9)
    cotangent = image(WROWS + 32)
    columns = recv_ref[:, WROWS + 48 : WROWS + 56, :].astype(F32).reshape(C, HALF)

    def param(lane):
        high = columns[:, lane : lane + 1]
        middle_part = columns[:, PART + lane : PART + lane + 1]
        low = columns[:, 2 * PART + lane : 2 * PART + lane + 1]
        return high + middle_part + low

    gains = [param(GAINS + j) for j in range(3)]
    biases = [param(BIASES + j) for j in range(3)]

    def store_taps(target, values):
        for tap in range(9):
            row_step, col_step = tap_steps(tap)
            target[tap, :, :] = shifted(values, row_step, col_step, 1).astype(BF16)

    def convolve(first_block, taps):
        total = None
        for tap in range(9):
            product = dot_nn(weights[first_block + tap], taps[tap])
            total = product if total is None else total + product
        return total

    hat_one, inverse_one = norm_hat(source)
    pre_one = hat_one * gains[0] + biases[0]
    first_act = (pre_one * sigmoid(pre_one)).astype(BF16).astype(F32)
    store_taps(taps_one, first_act)
    middle = convolve(0, taps_one) + (param(CONV_BIAS) + param(OFFSETS))
    hat_two, inverse_two = norm_hat(middle)
    pre_two = hat_two * gains[1] + biases[1]
    second_act = (pre_two * sigmoid(pre_two) * keep).astype(BF16).astype(F32)
    store_taps(taps_two, second_act)
    residual = source + convolve(9, taps_two) + param(CONV_BIAS + 1)
    hat_three, inverse_three = norm_hat(residual)
    normed = (hat_three * gains[2] + biases[2]).astype(BF16)
    queries = (dot_nn(weights[18], normed) + param(QV_BIAS)).astype(BF16)
    keys = dot_nn(weights[19], normed).astype(BF16)
    vals = (dot_nn(weights[20], normed) + param(QV_BIAS + 1)).astype(BF16)
    scale = C ** (-0.5)
    scores = dot_tn(queries, keys) * scale
    exps = jnp.exp(scores - jnp.max(scores, axis=1, keepdims=True))
    probs = exps / jnp.sum(exps, axis=1, keepdims=True)
    probs_low = probs.astype(BF16)
    attended = dot_nt(vals, probs_low).astype(BF16)
    outputs = residual + dot_nn(weights[21], attended) + param(OUT_BIAS)

    def put_image(at, values):
        left = values[:, 0:HALF].reshape(SHARDS, ROWS, HALF)
        right = values[:, HALF:C].reshape(SHARDS, ROWS, HALF)
        send_ref[:, at : at + 16, :] = jnp.concatenate([left, right], axis=1).astype(BF16)

    put_image(WROWS, outputs)

    pending = {}

    def put_weight_grad(block, values):
        pending[block] = values
        pair = block // 2
        if 2 * pair in pending and 2 * pair + 1 in pending:
            a, b = pending.pop(2 * pair), pending.pop(2 * pair + 1)
            low = [v[:, 0:HALF].reshape(SHARDS, ROWS, HALF) for v in (a, b)]
            high = [v[:, HALF:C].reshape(SHARDS, ROWS, HALF) for v in (a, b)]
            low, high = jnp.concatenate(low, axis=1), jnp.concatenate(high, axis=1)
            rows = slice(16 * pair, 16 * pair + 16)
            send_ref[:, rows, :] = jnp.where(first_core, low, high).astype(BF16)
            swap_ref[:, rows, :] = jnp.where(first_core, high, low).astype(BF16)

    cot_low = cotangent.astype(BF16)
    out_bias_grad = jnp.sum(cotangent, axis=1, keepdims=True)
    put_weight_grad(21, dot_nt(cot_low, attended))
    attended_grad = dot_tn(weights[21], cot_low).astype(BF16)
    dprobs = dot_tn(attended_grad, vals)
    row_dot = jnp.sum(probs * dprobs, axis=1, keepdims=True)
    dscores = (probs * (dprobs - row_dot)).astype(BF16)
    query_grad = (dot_nt(keys, dscores) * scale).astype(BF16)
    key_grad = (dot_nn(queries, dscores) * scale).astype(BF16)
    value_grad = dot_nn(attended_grad, probs_low).astype(BF16)
    query_bias_grad = jnp.sum(query_grad.astype(F32), axis=1, keepdims=True)
    value_bias_grad = jnp.sum(value_grad.astype(F32), axis=1, keepdims=True)
    normed_grad = None
    for k, gradient in enumerate((query_grad, key_grad, value_grad)):
        put_weight_grad(18 + k, dot_nt(gradient, normed))
        product = dot_tn(weights[18 + k], gradient)
        normed_grad = product if normed_grad is None else normed_grad + product
    branch_three, gain_three, bias_three = norm_back(
        hat_three, inverse_three, normed_grad, gains[2]
    )
    residual_grad = cotangent + branch_three
    conv_two_bias = jnp.sum(residual_grad, axis=1, keepdims=True)

    def conv_back(first_block, gradient, taps):
        low = gradient.astype(BF16)
        for tap in range(9):
            put_weight_grad(first_block + tap, dot_nt(low, taps[tap]))
        turned = low.astype(F32).T
        total = None
        for tap in range(9):
            row_step, col_step = tap_steps(tap)
            moved = shifted(turned, -row_step, -col_step, 0).astype(BF16)
            product = dot_nn(moved, weights[first_block + tap])
            total = product if total is None else total + product
        return total.T

    def slope(values):
        sigma = sigmoid(values)
        return sigma * (1.0 + values * (1.0 - sigma))

    second_grad = conv_back(9, residual_grad, taps_two)
    pre_two_grad = second_grad * keep * slope(pre_two)
    middle_grad, gain_two, bias_two = norm_back(hat_two, inverse_two, pre_two_grad, gains[1])
    conv_one_bias = jnp.sum(middle_grad, axis=1, keepdims=True)
    first_grad = conv_back(0, middle_grad, taps_one)
    pre_one_grad = first_grad * slope(pre_one)
    branch_one, gain_one, bias_one = norm_back(hat_one, inverse_one, pre_one_grad, gains[0])
    put_image(WROWS + 16, residual_grad + branch_one)

    lane = lax.broadcasted_iota(jnp.int32, (C, HALF), 1)
    table = jnp.zeros((C, HALF), F32)
    listed = (
        gain_one, gain_two, gain_three, bias_one, bias_two, bias_three,
        conv_one_bias, conv_two_bias, query_bias_grad, value_bias_grad, out_bias_grad,
    )
    for k, column in enumerate(listed):
        table = jnp.where((lane & (PART - 1)) == k, column, table)
    high = table.astype(BF16).astype(F32)
    table = jnp.where(lane < PART, high, jnp.where(lane < 2 * PART, table - high, 0.0))
    send_ref[:, WROWS + 32 : WROWS + 40, :] = table.reshape(SHARDS, ROWS, HALF).astype(BF16)


IN_ROWS = WROWS + 56
OUT_ROWS = WROWS + 40


def run_block(core, received, other):
    return pl.pallas_call(
        block_kernel,
        out_shape=(
            jax.ShapeDtypeStruct((SHARDS, OUT_ROWS, HALF), BF16),
            jax.ShapeDtypeStruct((SHARDS, WROWS, HALF), BF16),
        ),
        in_specs=[
            pl.BlockSpec(memory_space=pltpu.SMEM),
            pl.BlockSpec(memory_space=pltpu.VMEM),
            pl.BlockSpec(memory_space=pltpu.VMEM),
        ],
        out_specs=(
            pl.BlockSpec(memory_space=pltpu.VMEM),
            pl.BlockSpec(memory_space=pltpu.VMEM),
        ),
        scratch_shapes=[
            pltpu.VMEM((WBLOCKS, C, C), BF16),
            pltpu.VMEM((9, C, POS), BF16),
            pltpu.VMEM((9, C, POS), BF16),
            pltpu.VMEM((9, POS, C), BF16),
        ],
        compiler_params=pltpu.CompilerParams(vmem_limit_bytes=24 * 1024 * 1024),
    )(core, received, other)


def finish_kernel(core_ref, mine_ref, theirs_ref, *refs):
    results, scratch, sems = refs[:10], refs[10:20], refs[20]
    first_core = core_ref[0] == 0
    (gain, bias, conv_w, conv_b, temb_w, temb_b, qkv_w, qv_b, out_w, out_b) = scratch

    def weight_grad(block):
        rows = slice(ROWS * block, ROWS * block + ROWS)
        mine, theirs = mine_ref[rows, :], theirs_ref[rows, :]
        return jnp.concatenate(
            [jnp.where(first_core, mine, theirs), jnp.where(first_core, theirs, mine)], axis=1
        )

    copies = [pltpu.make_async_copy(scratch[k], results[k], sems.at[k]) for k in range(10)]
    for block in range(18):
        conv_w[block // 9, block % 9, :, :] = weight_grad(block)
    copies[2].start()
    for k in range(3):
        qkv_w[k, :, :] = weight_grad(18 + k)
    copies[6].start()
    out_w[...] = weight_grad(21)
    copies[8].start()
    shared = mine_ref[WROWS:, :] + theirs_ref[WROWS:, :]
    for part in range(TEMB // HALF):
        rows = slice(ROWS + ROWS * part, 2 * ROWS + ROWS * part)
        temb_w[:, HALF * part : HALF * part + HALF] = shared[rows, :]
    copies[4].start()
    padded = jnp.concatenate([shared[:ROWS, :], jnp.zeros((HALF - ROWS, HALF), F32)], axis=0)
    table = padded.T[:PART, :ROWS]
    gain[...] = table[D_GAINS : D_GAINS + 3]
    bias[...] = table[D_BIASES : D_BIASES + 3]
    conv_b[...] = table[D_CONV_BIAS : D_CONV_BIAS + 2]
    temb_b[...] = table[D_CONV_BIAS : D_CONV_BIAS + 1]
    qv_b[...] = table[D_QV_BIAS : D_QV_BIAS + 2]
    out_b[...] = table[D_OUT_BIAS : D_OUT_BIAS + 1]
    for k in (0, 1, 3, 5, 7, 9):
        copies[k].start()
    for copy in copies:
        copy.wait()


def finish(core, mine, theirs):
    shapes = [
        (3, ROWS), (3, ROWS), (2, 9, ROWS, C), (2, ROWS), (ROWS, TEMB), (1, ROWS),
        (3, ROWS, C), (2, ROWS), (ROWS, C), (1, ROWS),
    ]
    return pl.pallas_call(
        finish_kernel,
        out_shape=[jax.ShapeDtypeStruct(shape, F32) for shape in shapes],
        in_specs=[
            pl.BlockSpec(memory_space=pltpu.SMEM),
            pl.BlockSpec(memory_space=pltpu.VMEM),
            pl.BlockSpec(memory_space=pltpu.VMEM),
        ],
        out_specs=[pl.BlockSpec(memory_space=pltpu.HBM) for _ in shapes],
        scratch_shapes=[pltpu.VMEM(shape, F32) for shape in shapes]
        + [pltpu.SemaphoreType.DMA((10,))],
        compiler_params=pltpu.CompilerParams(vmem_limit_bytes=8 * 1024 * 1024),
    )(core, mine, theirs)


def prepare_kernel(core_ref, *refs):
    count = PREPARE_ARRAYS
    arrays, (send_ref, swished_ref) = refs[:count], refs[count : count + 2]
    held, (angles, sems) = refs[count + 2 : 2 * count + 2], refs[2 * count + 2 :]
    (
        steps_ref, gain_ref, bias_ref, conv_bias_ref, qv_ref, out_bias_ref, temb_bias_ref,
        temb_ref, conv_ref, qkv_ref, out_ref, inputs_ref, mask_ref, cotangent_ref,
    ) = held
    copies = [pltpu.make_async_copy(arrays[k], held[k], sems.at[k]) for k in range(count)]
    for copy in copies:
        copy.start()
    first_core = core_ref[0] == 0
    for copy in copies[:8]:
        copy.wait()

    half_dim = TEMB // 2
    index = lax.broadcasted_iota(jnp.int32, (1, half_dim), 1).astype(F32)
    rates = jnp.exp(-math.log(10000.0) * index / (half_dim - 1))
    for image in range(SHARDS):
        angles[image : image + 1, :] = rates * steps_ref[image].astype(F32)
    features = jnp.concatenate([jnp.sin(angles[...]), jnp.cos(angles[...])], axis=1)
    swished = features * sigmoid(features)
    swished_ref[...] = swished
    offsets = None
    rest = swished
    for _ in range(3):
        part = rest.astype(BF16)
        rest = rest - part.astype(F32)
        product = dot_nt(temb_ref[...], part)
        offsets = product if offsets is None else offsets + product

    rows = jnp.concatenate(
        [
            jnp.zeros((1, ROWS), F32), gain_ref[...], bias_ref[...], conv_bias_ref[...],
            qv_ref[...], out_bias_ref[...], temb_bias_ref[...], jnp.zeros((3, ROWS), F32),
        ],
        axis=0,
    )
    square = jnp.concatenate([rows] * (HALF // PART), axis=0)
    square = jnp.concatenate([square, jnp.zeros((HALF, HALF - ROWS), F32)], axis=1)
    columns = square.T[:ROWS, :]
    lane = lax.broadcasted_iota(jnp.int32, (ROWS, HALF), 1)
    offset_lane = (lane & (PART - 1)) == OFFSETS
    offsets = offsets + columns[:, TEMB_BIAS : TEMB_BIAS + 1]
    for image in range(SHARDS):
        values = jnp.where(offset_lane, offsets[:, image : image + 1], columns)
        high = values.astype(BF16).astype(F32)
        mid = (values - high).astype(BF16).astype(F32)
        low = values - high - mid
        parts = jnp.where(
            lane < PART,
            high,
            jnp.where(lane < 2 * PART, mid, jnp.where(lane < 3 * PART, low, 0.0)),
        )
        send_ref[image, WROWS + 48 : WROWS + 56, :] = parts.astype(BF16)

    for copy in copies[8:]:
        copy.wait()

    def half(values):
        values = values.astype(F32)
        return jnp.where(first_core, values[:, :HALF], values[:, HALF:])

    shard = jnp.concatenate(
        [
            half(conv_ref[...].reshape(18 * ROWS, C)),
            half(qkv_ref[...].reshape(3 * ROWS, C)),
            half(out_ref[...]),
        ],
        axis=0,
    ).astype(BF16)
    send_ref[:, :WROWS, :] = jnp.broadcast_to(shard[None], (SHARDS, WROWS, HALF))

    def put(at, values):
        turned = jnp.swapaxes(values.astype(F32), 0, 1)
        cut = jnp.concatenate([turned[:, :, :HALF], turned[:, :, HALF:]], axis=1)
        send_ref[:, at : at + 16, :] = cut.astype(BF16)

    put(WROWS, inputs_ref[...])
    put(WROWS + 16, mask_ref[...])
    put(WROWS + 32, cotangent_ref[...])


PREPARE_ARRAYS = 14


def prepare(core, timesteps, *arrays):
    held = [pltpu.SMEM((SHARDS,), jnp.int32)]
    held += [pltpu.VMEM(array.shape, array.dtype) for array in arrays]
    return pl.pallas_call(
        prepare_kernel,
        out_shape=(
            jax.ShapeDtypeStruct((SHARDS, IN_ROWS, HALF), BF16),
            jax.ShapeDtypeStruct((SHARDS, TEMB), F32),
        ),
        in_specs=[pl.BlockSpec(memory_space=pltpu.SMEM)]
        + [pl.BlockSpec(memory_space=pltpu.HBM)] * PREPARE_ARRAYS,
        out_specs=(pl.BlockSpec(memory_space=pltpu.VMEM), pl.BlockSpec(memory_space=pltpu.VMEM)),
        scratch_shapes=held
        + [pltpu.VMEM((SHARDS, TEMB // 2), F32), pltpu.SemaphoreType.DMA((PREPARE_ARRAYS,))],
        compiler_params=pltpu.CompilerParams(vmem_limit_bytes=16 * 1024 * 1024),
    )(core, *[pltpu.with_memory_space_constraint(a, pltpu.HBM) for a in (timesteps, *arrays)])


def whole(blocks):
    turned = blocks.transpose(1, 0, 2)
    return jnp.concatenate([turned[:ROWS], turned[ROWS:]], axis=2)


def on_device(
    inputs,
    timesteps,
    keep_mask,
    norm_gain,
    norm_bias,
    conv_weight,
    conv_bias,
    temb_weight,
    temb_bias,
    qkv_weight,
    qv_bias,
    out_weight,
    out_bias,
    cotangent,
):
    member = lax.axis_index("img")
    core = member % 2
    core_pairs = [(m, m ^ 1) for m in range(4)]
    plane_pairs = [(m, m ^ 2) for m in range(4)]
    highest = lax.Precision.HIGHEST

    sent, swished = prepare(
        core.reshape(1),
        timesteps,
        norm_gain,
        norm_bias,
        conv_bias,
        qv_bias,
        out_bias.reshape(1, ROWS),
        temb_bias.reshape(1, ROWS),
        temb_weight.T,
        conv_weight,
        qkv_weight,
        out_weight,
        inputs,
        keep_mask,
        cotangent,
    )
    received = lax.all_to_all(sent, "ch", split_axis=0, concat_axis=0, tiled=True)
    other = lax.ppermute(received, "img", core_pairs)

    send, swap = run_block(core.reshape(1), received, other)

    swapped = lax.ppermute(swap, "img", core_pairs)
    send = send + jnp.pad(swapped, ((0, 0), (0, OUT_ROWS - WROWS), (0, 0)))
    back = lax.all_to_all(send, "ch", split_axis=0, concat_axis=0, tiled=True)

    outputs = whole(back[:, WROWS : WROWS + 16])
    input_grad = whole(back[:, WROWS + 16 : WROWS + 32])
    weight_sums = jnp.sum(back[:, :WROWS].astype(F32), axis=0)
    small = back[:, WROWS + 32 :].astype(F32)
    small = small[:, :, :PART] + small[:, :, PART : 2 * PART]
    offsets_grad = small[:, :, D_CONV_BIAS]
    temb_grad = lax.dot_general(
        offsets_grad, swished, (((0,), (0,)), ((), ())), precision=highest,
        preferred_element_type=F32,
    )
    small_sums = jnp.pad(jnp.sum(small, axis=0), ((0, 0), (0, HALF - PART)))
    temb_rows = [temb_grad[:, HALF * k : HALF * k + HALF] for k in range(TEMB // HALF)]
    sums = jnp.concatenate([weight_sums, small_sums, *temb_rows], axis=0)
    plane = lax.ppermute(sums, "img", plane_pairs)
    plane, outputs, input_grad = lax.optimization_barrier((plane, outputs, input_grad))
    sums = sums + plane
    theirs = lax.ppermute(sums, "img", core_pairs)
    (gain, bias, conv_w, conv_b, temb_w, temb_b, qkv_w, qv_b, out_w, out_b) = finish(
        core.reshape(1), sums, theirs
    )
    return (
        outputs,
        input_grad,
        gain,
        bias,
        conv_w,
        conv_b,
        temb_w.T,
        temb_b[0],
        qkv_w,
        qv_b,
        out_w,
        out_b[0],
    )


def solution(mesh):
    placed = (
        P("ch", "img", None),
        P("img"),
        P("ch", "img", None),
        P(None, "ch"),
        P(None, "ch"),
        P(None, None, "ch", None),
        P(None, "ch"),
        P(None, "ch"),
        P("ch"),
        P(None, "ch", None),
        P(None, "ch"),
        P("ch", None),
        P("ch"),
        P("ch", "img", None),
    )
    return jax.shard_map(
        on_device,
        mesh=mesh,
        in_specs=placed,
        out_specs=(
            P("ch", "img", None),
            P("ch", "img", None),
            P(None, "ch"),
            P(None, "ch"),
            P(None, None, "ch", None),
            P(None, "ch"),
            P(None, "ch"),
            P("ch"),
            P(None, "ch", None),
            P(None, "ch"),
            P("ch", None),
            P("ch"),
        ),
        check_vma=False,
    )
```

```python
import functools
import math

import jax
import jax.numpy as jnp
from jax import lax
from jax.experimental import pallas as pl
from jax.experimental.pallas import tpu as pltpu
from jax.sharding import PartitionSpec as P

C = 256
TEMB = 512
SIDE = 16
POS = 256
SHARDS = 32
ROWS = C // SHARDS
HALF = 128
WBLOCKS = 22
WROWS = WBLOCKS * ROWS
NORM_EPS = 1e-06
GROUP_SIZE = ROWS * POS
F32 = jnp.float32
BF16 = jnp.bfloat16

OFFSETS, GAINS, BIASES, CONV_BIAS, QV_BIAS, OUT_BIAS, TEMB_BIAS = 0, 1, 4, 7, 9, 11, 12
D_GAINS, D_BIASES, D_CONV_BIAS, D_QV_BIAS, D_OUT_BIAS = 0, 3, 6, 8, 10
PART = 16


def dot_nn(a, b):
    return lax.dot_general(a, b, (((1,), (0,)), ((), ())), preferred_element_type=F32)


def dot_nt(a, b):
    return lax.dot_general(a, b, (((1,), (1,)), ((), ())), preferred_element_type=F32)


def dot_tn(a, b):
    return lax.dot_general(a, b, (((0,), (0,)), ((), ())), preferred_element_type=F32)


def group_sum(values):
    column = jnp.sum(values, axis=1, keepdims=True)
    return group_column(column)


def group_column(column):
    grouped = column.reshape(SHARDS, ROWS, 1)
    total = jnp.sum(grouped, axis=1, keepdims=True)
    return jnp.broadcast_to(total, grouped.shape).reshape(C, 1)


def norm_hat(values):
    average = group_sum(values) * (1.0 / GROUP_SIZE)
    centered = values - average
    spread = group_sum(centered * centered) * (1.0 / GROUP_SIZE)
    inverse = lax.rsqrt(spread + NORM_EPS)
    return centered * inverse, inverse


def norm_back(hat, inverse, grad_out, gain):
    gain_grad = jnp.sum(grad_out * hat, axis=1, keepdims=True)
    bias_grad = jnp.sum(grad_out, axis=1, keepdims=True)
    first_mean = group_column(bias_grad * gain) * (1.0 / GROUP_SIZE)
    second_mean = group_column(gain_grad * gain) * (1.0 / GROUP_SIZE)
    grad_in = inverse * (grad_out * gain - first_mean - hat * second_mean)
    return grad_in, gain_grad, bias_grad


def sigmoid(values):
    return 1.0 / (1.0 + jnp.exp(-values))


def tap_steps(tap):
    return tap // 3 - 1, tap % 3 - 1


def shifted(values, row_step, col_step, axis):
    if row_step == 0 and col_step == 0:
        return values
    moved = pltpu.roll(values, (-(row_step * SIDE + col_step)) % POS, axis)
    shape = (1, POS) if axis == 1 else (POS, POS)
    cell = lax.broadcasted_iota(jnp.int32, shape, axis)
    valid = None
    if col_step:
        column = (cell & (SIDE - 1)) + col_step
        valid = (column >= 0) & (column < SIDE)
    if row_step:
        row = cell + row_step * SIDE
        inside = (row >= 0) & (row < POS)
        valid = inside if valid is None else valid & inside
    return moved * valid.astype(F32)


def load_weights(mine_ref, theirs_ref, first_row, blocks, first_core, weights):
    for pair in range(blocks // 2):
        rows = slice(first_row + 16 * pair, first_row + 16 * pair + 16)
        mine = mine_ref[:, rows, :].astype(F32)
        theirs = theirs_ref[:, 16 * pair : 16 * pair + 16, :].astype(F32)
        for part in range(2):
            rows = slice(ROWS * part, ROWS * part + ROWS)
            a = mine[:, rows, :].reshape(C, HALF)
            b = theirs[:, rows, :].reshape(C, HALF)
            weights[2 * pair + part, :, 0:HALF] = jnp.where(first_core, a, b).astype(BF16)
            weights[2 * pair + part, :, HALF:C] = jnp.where(first_core, b, a).astype(BF16)


def load_image(ref, at):
    block = ref[:, at : at + 16, :].astype(F32)
    left = block[:, 0:ROWS, :].reshape(C, HALF)
    right = block[:, ROWS : 2 * ROWS, :].reshape(C, HALF)
    return jnp.concatenate([left, right], axis=1)


def image_rows(values):
    left = values[:, 0:HALF].reshape(SHARDS, ROWS, HALF)
    right = values[:, HALF:C].reshape(SHARDS, ROWS, HALF)
    return jnp.concatenate([left, right], axis=1).astype(BF16)


def store_taps(target, values):
    for tap in range(9):
        row_step, col_step = tap_steps(tap)
        target[tap, :, :] = shifted(values, row_step, col_step, 1).astype(BF16)


def convolve(weights, taps):
    total = None
    for tap in range(9):
        product = dot_nn(weights[tap], taps[tap])
        total = product if total is None else total + product
    return total


def convolve_back(weights, low):
    turned = low.astype(F32).T
    total = None
    for tap in range(9):
        row_step, col_step = tap_steps(tap)
        moved = shifted(turned, -row_step, -col_step, 0).astype(BF16)
        product = dot_nn(moved, weights[tap])
        total = product if total is None else total + product
    return total.T


def store_weight_grads(own_ref, swap_ref, pair, first_core, grads):
    low = [v[:, 0:HALF].reshape(SHARDS, ROWS, HALF) for v in grads]
    high = [v[:, HALF:C].reshape(SHARDS, ROWS, HALF) for v in grads]
    low, high = jnp.concatenate(low, axis=1), jnp.concatenate(high, axis=1)
    rows = slice(16 * pair, 16 * pair + 16)
    own_ref[:, rows, :] = jnp.where(first_core, low, high).astype(BF16)
    swap_ref[:, rows, :] = jnp.where(first_core, high, low).astype(BF16)


def columns_of(listed):
    lane = lax.broadcasted_iota(jnp.int32, (C, HALF), 1)
    table = jnp.zeros((C, HALF), F32)
    for k, column in enumerate(listed):
        table = jnp.where(lane == k, column, table)
    return table


def column(ref, lane):
    return ref[:, lane : lane + 1]


def row_sum(values):
    return jnp.sum(values, axis=1, keepdims=True)


def slope(values):
    sigma = sigmoid(values)
    return sigma * (1.0 + values * (1.0 - sigma))


def first_kernel(recv_ref, taps_ref, hat_ref, params_ref, stats_ref):
    columns = recv_ref[:, AT_PARAMS : AT_PARAMS + ROWS, :].astype(F32).reshape(C, HALF)
    columns = (
        columns
        + pltpu.roll(columns, HALF - PART, 1)
        + pltpu.roll(columns, HALF - 2 * PART, 1)
    )
    params_ref[...] = columns
    hat, inverse = norm_hat(load_image(recv_ref, AT_SOURCE))
    hat_ref[...] = hat
    stats_ref[...] = jnp.broadcast_to(inverse, (C, HALF))
    pre = hat * columns[:, GAINS : GAINS + 1] + columns[:, BIASES : BIASES + 1]
    store_taps(taps_ref, (pre * sigmoid(pre)).astype(BF16).astype(F32))


def middle_kernel(
    core_ref, recv_ref, other_ref, taps_one, params, weights, taps_ref, hat_ref, stats_ref
):
    load_weights(recv_ref, other_ref, 0, FIRST_BLOCKS, core_ref[0] == 0, weights)
    middle = convolve(weights, taps_one) + (column(params, CONV_BIAS) + column(params, OFFSETS))
    hat, inverse = norm_hat(middle)
    hat_ref[...] = hat
    stats_ref[...] = jnp.broadcast_to(inverse, (C, HALF))
    pre = hat * column(params, GAINS + 1) + column(params, BIASES + 1)
    keep = load_image(recv_ref, AT_KEEP) * (1.0 / 0.9)
    store_taps(taps_ref, (pre * sigmoid(pre) * keep).astype(BF16).astype(F32))


def attention_kernel(
    core_ref, recv_ref, other_ref, taps_two, params, out_weight,
    own_ref, swap_ref, weights, outputs_ref, attended_ref, grad_ref, sums_ref,
):
    first_core = core_ref[0] == 0
    load_weights(recv_ref, other_ref, FIRST_ROWS, SECOND_BLOCKS, first_core, weights)
    source = load_image(recv_ref, AT_SOURCE)
    residual = source + convolve(weights, taps_two) + column(params, CONV_BIAS + 1)
    hat, inverse = norm_hat(residual)
    normed = (hat * column(params, GAINS + 2) + column(params, BIASES + 2)).astype(BF16)
    queries = (dot_nn(weights[9], normed) + column(params, QV_BIAS)).astype(BF16)
    keys = dot_nn(weights[10], normed).astype(BF16)
    vals = (dot_nn(weights[11], normed) + column(params, QV_BIAS + 1)).astype(BF16)
    scale = C ** (-0.5)
    scores = dot_tn(queries, keys) * scale
    exps = jnp.exp(scores - jnp.max(scores, axis=1, keepdims=True))
    probs = exps / row_sum(exps)
    probs_low = probs.astype(BF16)
    attended = dot_nt(vals, probs_low).astype(BF16)
    attended_ref[...] = attended
    outputs = residual + dot_nn(out_weight[FIRST_BLOCKS - 1], attended) + column(params, OUT_BIAS)
    outputs_ref[...] = image_rows(outputs)

    cotangent = load_image(recv_ref, AT_COTANGENT)
    cot_low = cotangent.astype(BF16)
    attended_grad = dot_tn(out_weight[FIRST_BLOCKS - 1], cot_low).astype(BF16)
    dprobs = dot_tn(attended_grad, vals)
    dscores = (probs * (dprobs - row_sum(probs * dprobs))).astype(BF16)
    query_grad = (dot_nt(keys, dscores) * scale).astype(BF16)
    key_grad = (dot_nn(queries, dscores) * scale).astype(BF16)
    value_grad = dot_nn(attended_grad, probs_low).astype(BF16)
    normed_grad = None
    for k, gradient in enumerate((query_grad, key_grad, value_grad)):
        product = dot_tn(weights[9 + k], gradient)
        normed_grad = product if normed_grad is None else normed_grad + product
    branch, gain_grad, bias_grad = norm_back(hat, inverse, normed_grad, column(params, GAINS + 2))
    residual_grad = cotangent + branch
    grad_ref[...] = residual_grad
    low = residual_grad.astype(BF16)
    grads = [dot_nt(low, taps_two[tap]) for tap in range(9)]
    grads += [dot_nt(gradient, normed) for gradient in (query_grad, key_grad, value_grad)]
    for pair in range(SECOND_BLOCKS // 2):
        store_weight_grads(own_ref, swap_ref, pair, first_core, grads[2 * pair : 2 * pair + 2])
    listed = {
        D_GAINS + 2: gain_grad,
        D_BIASES + 2: bias_grad,
        D_CONV_BIAS + 1: row_sum(residual_grad),
        D_QV_BIAS: row_sum(query_grad.astype(F32)),
        D_QV_BIAS + 1: row_sum(value_grad.astype(F32)),
        D_OUT_BIAS: row_sum(cotangent),
    }
    zero = jnp.zeros((C, 1), F32)
    sums_ref[...] = columns_of([listed.get(k, zero) for k in range(PART)])


def middle_back_kernel(
    core_ref, recv_ref, weights, taps_one, hat_ref, stats, params, attended, grad_ref, sums,
    own_ref, swap_ref, low_ref, sums_ref,
):
    second_grad = convolve_back(weights, grad_ref[...].astype(BF16))
    hat = hat_ref[...]
    gain = column(params, GAINS + 1)
    pre = hat * gain + column(params, BIASES + 1)
    keep = load_image(recv_ref, AT_KEEP) * (1.0 / 0.9)
    pre_grad = second_grad * keep * slope(pre)
    middle_grad, gain_grad, bias_grad = norm_back(hat, column(stats, 0), pre_grad, gain)
    low = middle_grad.astype(BF16)
    low_ref[...] = low
    grads = [dot_nt(low, taps_one[tap]) for tap in range(9)]
    grads += [dot_nt(load_image(recv_ref, AT_COTANGENT).astype(BF16), attended[...])]
    for pair in range(FIRST_BLOCKS // 2):
        store_weight_grads(
            own_ref, swap_ref, pair, core_ref[0] == 0, grads[2 * pair : 2 * pair + 2]
        )
    listed = {D_GAINS + 1: gain_grad, D_BIASES + 1: bias_grad, D_CONV_BIAS: row_sum(middle_grad)}
    zero = jnp.zeros((C, 1), F32)
    sums_ref[...] = sums[...] + columns_of([listed.get(k, zero) for k in range(PART)])


def first_back_kernel(
    weights, hat_ref, stats, params, low_ref, grad_ref, sums, outputs, own, swapped, send_ref
):
    first_grad = convolve_back(weights, low_ref[...])
    hat = hat_ref[...]
    gain = column(params, GAINS)
    pre = hat * gain + column(params, BIASES)
    branch, gain_grad, bias_grad = norm_back(hat, column(stats, 0), first_grad * slope(pre), gain)
    for pair in range(SECOND_BLOCKS // 2):
        rows = slice(16 * pair, 16 * pair + 16)
        both = own[:, rows, :].astype(F32) + swapped[:, rows, :].astype(F32)
        to = FIRST_ROWS + 16 * pair
        send_ref[:, to : to + 16, :] = both.astype(BF16)
    send_ref[:, WROWS : WROWS + 16, :] = outputs[...]
    send_ref[:, WROWS + 16 : WROWS + 32, :] = image_rows(grad_ref[...] + branch)

    zero = jnp.zeros((C, 1), F32)
    listed = {D_GAINS: gain_grad, D_BIASES: bias_grad}
    table = sums[...] + columns_of([listed.get(k, zero) for k in range(PART)])
    high = table.astype(BF16).astype(F32)
    low = pltpu.roll(table - high, PART, 1)
    lane = lax.broadcasted_iota(jnp.int32, (C, HALF), 1)
    table = jnp.where(lane < PART, high, low)
    send_ref[:, WROWS + 32 : WROWS + 40, :] = table.reshape(SHARDS, ROWS, HALF).astype(BF16)


AT_SOURCE, AT_KEEP, AT_COTANGENT, AT_PARAMS = WROWS, WROWS + 16, WROWS + 32, WROWS + 48
IN_ROWS = WROWS + 56
OUT_ROWS = WROWS + 40
FIRST_BLOCKS, SECOND_BLOCKS = 10, 12
FIRST_ROWS, SECOND_ROWS = FIRST_BLOCKS * ROWS, SECOND_BLOCKS * ROWS


def local_call(kernel, core, *operands, out):
    in_specs = [pl.BlockSpec(memory_space=pltpu.VMEM) for _ in operands]
    if core is not None:
        in_specs = [pl.BlockSpec(memory_space=pltpu.SMEM)] + in_specs
        operands = (core, *operands)
    shapes = tuple(jax.ShapeDtypeStruct(shape, dtype) for shape, dtype in out)
    return pl.pallas_call(
        kernel,
        out_shape=shapes,
        in_specs=in_specs,
        out_specs=tuple(pl.BlockSpec(memory_space=pltpu.VMEM) for _ in out),
        compiler_params=pltpu.CompilerParams(vmem_limit_bytes=VMEM_LIMIT),
    )(*operands)


VMEM_LIMIT = 24 * 1024 * 1024


def run_block(core, received, swap):
    other_one = swap(received[:, :FIRST_ROWS])
    other_two = swap(received[:, FIRST_ROWS:WROWS])
    image, table = ((C, POS), F32), ((C, HALF), F32)
    taps, low = ((9, C, POS), BF16), ((C, POS), BF16)

    taps_one, hat_one, params, stats_one = local_call(
        first_kernel, None, received, out=(taps, image, table, table)
    )
    weights_one, taps_two, hat_two, stats_two = local_call(
        middle_kernel, core, received, other_one, taps_one, params,
        out=(((FIRST_BLOCKS, C, C), BF16), taps, image, table),
    )
    second = ((SHARDS, SECOND_ROWS, HALF), BF16)
    rows = ((SHARDS, 16, HALF), BF16)
    own_two, swap_two, weights_two, outputs, attended, residual_grad, sums = local_call(
        attention_kernel, core, received, other_two, taps_two, params, weights_one,
        out=(second, second, ((SECOND_BLOCKS, C, C), BF16), rows, low, image, table),
    )
    swapped_two = swap(swap_two)
    first = ((SHARDS, FIRST_ROWS, HALF), BF16)
    own_one, swap_one, middle_low, sums = local_call(
        middle_back_kernel, core, received, weights_two, taps_one, hat_two, stats_two, params,
        attended, residual_grad, sums, out=(first, first, low, table),
    )
    swapped_one = swap(swap_one)
    (send,) = local_call(
        first_back_kernel, None, weights_one, hat_one, stats_one, params, middle_low,
        residual_grad, sums, outputs, own_two, swapped_two,
        out=(((SHARDS, OUT_ROWS, HALF), BF16),),
    )
    both = (own_one.astype(F32) + swapped_one.astype(F32)).astype(BF16)
    return lax.dynamic_update_slice(send, both, (0, 0, 0))


def collect_kernel(back_ref, swished_ref, sums_ref):
    for pair in range(WROWS // 16):
        rows = slice(16 * pair, 16 * pair + 16)
        total = back_ref[0, rows, :].astype(F32)
        for image in range(1, SHARDS):
            total = total + back_ref[image, rows, :].astype(F32)
        sums_ref[rows, :] = total.astype(BF16)
    small = back_ref[:, WROWS + 32 : WROWS + 40, :].astype(F32)
    table = jnp.zeros((ROWS, HALF), F32)
    temb = jnp.zeros((ROWS, TEMB), F32)
    for image in range(SHARDS):
        values = small[image] + pltpu.roll(small[image], HALF - PART, 1)
        table = table + values
        offsets_grad = values[:, D_CONV_BIAS : D_CONV_BIAS + 1]
        temb = temb + offsets_grad * swished_ref[image : image + 1, :]
    lane = lax.broadcasted_iota(jnp.int32, (ROWS, HALF), 1)
    high = table.astype(BF16).astype(F32)
    low = pltpu.roll(table - high, PART, 1)
    parts = jnp.where(lane < PART, high, jnp.where(lane < 2 * PART, low, 0.0))
    blocks = [parts] + [temb[:, HALF * k : HALF * k + HALF] for k in range(TEMB // HALF)]
    blocks = blocks + [jnp.zeros((ROWS, HALF), F32)]
    for pair in range(len(blocks) // 2):
        rows = slice(WROWS + 16 * pair, WROWS + 16 * pair + 16)
        both = jnp.concatenate(blocks[2 * pair : 2 * pair + 2], axis=0)
        sums_ref[rows, :] = both.astype(BF16)


SUM_ROWS = WROWS + ROWS + TEMB * ROWS // HALF + ROWS


def collect(back, swished):
    return pl.pallas_call(
        collect_kernel,
        out_shape=jax.ShapeDtypeStruct((SUM_ROWS, HALF), BF16),
        in_specs=[pl.BlockSpec(memory_space=pltpu.VMEM)] * 2,
        out_specs=pl.BlockSpec(memory_space=pltpu.VMEM),
        compiler_params=pltpu.CompilerParams(vmem_limit_bytes=8 * 1024 * 1024),
    )(back, swished)


def images_kernel(back_ref, outputs_ref, grad_ref):
    for at, target in ((WROWS, outputs_ref), (WROWS + 16, grad_ref)):
        block = back_ref[:, at : at + 16, :].astype(F32)
        cut = jnp.concatenate([block[:, :ROWS, :], block[:, ROWS:, :]], axis=2)
        target[...] = jnp.swapaxes(cut, 0, 1).astype(BF16)


def images(back):
    shape = jax.ShapeDtypeStruct((ROWS, SHARDS, POS), BF16)
    return pl.pallas_call(
        images_kernel,
        out_shape=(shape, shape),
        in_specs=[pl.BlockSpec(memory_space=pltpu.VMEM)],
        out_specs=(pl.BlockSpec(memory_space=pltpu.VMEM), pl.BlockSpec(memory_space=pltpu.VMEM)),
        compiler_params=pltpu.CompilerParams(vmem_limit_bytes=8 * 1024 * 1024),
    )(back)


def finish_kernel(core_ref, mine_ref, theirs_ref, *refs):
    results, scratch, sems = refs[:10], refs[10:20], refs[20]
    first_core = core_ref[0] == 0
    (gain, bias, conv_w, conv_b, temb_w, temb_b, qkv_w, qv_b, out_w, out_b) = scratch

    def weight_grad(block):
        rows = slice(ROWS * block, ROWS * block + ROWS)
        mine, theirs = mine_ref[rows, :], theirs_ref[rows, :]
        return jnp.concatenate(
            [jnp.where(first_core, mine, theirs), jnp.where(first_core, theirs, mine)], axis=1
        )

    copies = [pltpu.make_async_copy(scratch[k], results[k], sems.at[k]) for k in range(10)]
    for conv in range(2):
        for tap in range(9):
            conv_w[conv, tap, :, :] = weight_grad(FIRST_BLOCKS * conv + tap)
    copies[2].start()
    for k in range(3):
        qkv_w[k, :, :] = weight_grad(FIRST_BLOCKS + 9 + k)
    copies[6].start()
    out_w[...] = weight_grad(FIRST_BLOCKS - 1)
    copies[8].start()
    shared = mine_ref[WROWS:, :] + theirs_ref[WROWS:, :]
    small = shared[:ROWS, :] + pltpu.roll(shared[:ROWS, :], HALF - PART, 1)
    for part in range(TEMB // HALF):
        rows = slice(ROWS + ROWS * part, 2 * ROWS + ROWS * part)
        temb_w[:, HALF * part : HALF * part + HALF] = shared[rows, :]
    copies[4].start()
    padded = jnp.concatenate([small, jnp.zeros((HALF - ROWS, HALF), F32)], axis=0)
    table = padded.T[:PART, :ROWS]
    gain[...] = table[D_GAINS : D_GAINS + 3]
    bias[...] = table[D_BIASES : D_BIASES + 3]
    conv_b[...] = table[D_CONV_BIAS : D_CONV_BIAS + 2]
    temb_b[...] = table[D_CONV_BIAS : D_CONV_BIAS + 1]
    qv_b[...] = table[D_QV_BIAS : D_QV_BIAS + 2]
    out_b[...] = table[D_OUT_BIAS : D_OUT_BIAS + 1]
    for k in (0, 1, 3, 5, 7, 9):
        copies[k].start()
    for copy in copies:
        copy.wait()


def finish(core, mine, theirs):
    shapes = [
        (3, ROWS), (3, ROWS), (2, 9, ROWS, C), (2, ROWS), (ROWS, TEMB), (1, ROWS),
        (3, ROWS, C), (2, ROWS), (ROWS, C), (1, ROWS),
    ]
    return pl.pallas_call(
        finish_kernel,
        out_shape=[jax.ShapeDtypeStruct(shape, F32) for shape in shapes],
        in_specs=[
            pl.BlockSpec(memory_space=pltpu.SMEM),
            pl.BlockSpec(memory_space=pltpu.VMEM),
            pl.BlockSpec(memory_space=pltpu.VMEM),
        ],
        out_specs=[pl.BlockSpec(memory_space=pltpu.HBM) for _ in shapes],
        scratch_shapes=[pltpu.VMEM(shape, F32) for shape in shapes]
        + [pltpu.SemaphoreType.DMA((10,))],
        compiler_params=pltpu.CompilerParams(vmem_limit_bytes=8 * 1024 * 1024),
    )(core, mine, theirs)


def prepare_kernel(core_ref, *refs):
    count = PREPARE_ARRAYS
    arrays, (send_ref, swished_ref) = refs[:count], refs[count : count + 2]
    held, (angles, sems) = refs[count + 2 : 2 * count + 2], refs[2 * count + 2 :]
    (
        steps_ref, gain_ref, bias_ref, conv_bias_ref, qv_ref, out_bias_ref, temb_bias_ref,
        temb_ref, conv_ref, qkv_ref, out_ref, inputs_ref, mask_ref, cotangent_ref,
    ) = held
    copies = [pltpu.make_async_copy(arrays[k], held[k], sems.at[k]) for k in range(count)]
    for copy in copies:
        copy.start()
    first_core = core_ref[0] == 0
    for copy in copies[:8]:
        copy.wait()

    half_dim = TEMB // 2
    index = lax.broadcasted_iota(jnp.int32, (1, half_dim), 1).astype(F32)
    rates = jnp.exp(-math.log(10000.0) * index / (half_dim - 1))
    for image in range(SHARDS):
        angles[image : image + 1, :] = rates * steps_ref[image].astype(F32)
    features = jnp.concatenate([jnp.sin(angles[...]), jnp.cos(angles[...])], axis=1)
    swished = features * sigmoid(features)
    swished_ref[...] = swished
    offsets = None
    rest = swished
    for _ in range(3):
        part = rest.astype(BF16)
        rest = rest - part.astype(F32)
        product = dot_nt(temb_ref[...], part)
        offsets = product if offsets is None else offsets + product

    rows = jnp.concatenate(
        [
            jnp.zeros((1, ROWS), F32), gain_ref[...], bias_ref[...], conv_bias_ref[...],
            qv_ref[...], out_bias_ref[...], temb_bias_ref[...], jnp.zeros((3, ROWS), F32),
        ],
        axis=0,
    )
    square = jnp.concatenate([rows] * (HALF // PART), axis=0)
    square = jnp.concatenate([square, jnp.zeros((HALF, HALF - ROWS), F32)], axis=1)
    columns = square.T[:ROWS, :]
    lane = lax.broadcasted_iota(jnp.int32, (ROWS, HALF), 1)
    offset_lane = (lane & (PART - 1)) == OFFSETS
    offsets = offsets + columns[:, TEMB_BIAS : TEMB_BIAS + 1]
    for image in range(SHARDS):
        values = jnp.where(offset_lane, offsets[:, image : image + 1], columns)
        high = values.astype(BF16).astype(F32)
        mid = (values - high).astype(BF16).astype(F32)
        low = values - high - mid
        parts = jnp.where(
            lane < PART,
            high,
            jnp.where(lane < 2 * PART, mid, jnp.where(lane < 3 * PART, low, 0.0)),
        )
        send_ref[image, WROWS + 48 : WROWS + 56, :] = parts.astype(BF16)

    for copy in copies[8:]:
        copy.wait()

    def half(values):
        values = values.astype(F32)
        return jnp.where(first_core, values[:, :HALF], values[:, HALF:])

    shard = jnp.concatenate(
        [
            half(conv_ref[0].reshape(9 * ROWS, C)),
            half(out_ref[...]),
            half(conv_ref[1].reshape(9 * ROWS, C)),
            half(qkv_ref[...].reshape(3 * ROWS, C)),
        ],
        axis=0,
    ).astype(BF16)
    send_ref[:, :WROWS, :] = jnp.broadcast_to(shard[None], (SHARDS, WROWS, HALF))

    def put(at, values):
        turned = jnp.swapaxes(values.astype(F32), 0, 1)
        cut = jnp.concatenate([turned[:, :, :HALF], turned[:, :, HALF:]], axis=1)
        send_ref[:, at : at + 16, :] = cut.astype(BF16)

    put(WROWS, inputs_ref[...])
    put(WROWS + 16, mask_ref[...])
    put(WROWS + 32, cotangent_ref[...])


PREPARE_ARRAYS = 14


def prepare(core, timesteps, *arrays):
    held = [pltpu.SMEM((SHARDS,), jnp.int32)]
    held += [pltpu.VMEM(array.shape, array.dtype) for array in arrays]
    return pl.pallas_call(
        prepare_kernel,
        out_shape=(
            jax.ShapeDtypeStruct((SHARDS, IN_ROWS, HALF), BF16),
            jax.ShapeDtypeStruct((SHARDS, TEMB), F32),
        ),
        in_specs=[pl.BlockSpec(memory_space=pltpu.SMEM)]
        + [pl.BlockSpec(memory_space=pltpu.HBM)] * PREPARE_ARRAYS,
        out_specs=(pl.BlockSpec(memory_space=pltpu.VMEM), pl.BlockSpec(memory_space=pltpu.VMEM)),
        scratch_shapes=held
        + [pltpu.VMEM((SHARDS, TEMB // 2), F32), pltpu.SemaphoreType.DMA((PREPARE_ARRAYS,))],
        compiler_params=pltpu.CompilerParams(vmem_limit_bytes=16 * 1024 * 1024),
    )(core, *[pltpu.with_memory_space_constraint(a, pltpu.HBM) for a in (timesteps, *arrays)])


def on_device(
    inputs,
    timesteps,
    keep_mask,
    norm_gain,
    norm_bias,
    conv_weight,
    conv_bias,
    temb_weight,
    temb_bias,
    qkv_weight,
    qv_bias,
    out_weight,
    out_bias,
    cotangent,
):
    member = lax.axis_index("img")
    core = member % 2
    core_pairs = [(m, m ^ 1) for m in range(4)]
    plane_pairs = [(m, m ^ 2) for m in range(4)]
    sent, swished = prepare(
        core.reshape(1),
        timesteps,
        norm_gain,
        norm_bias,
        conv_bias,
        qv_bias,
        out_bias.reshape(1, ROWS),
        temb_bias.reshape(1, ROWS),
        temb_weight.T,
        conv_weight,
        qkv_weight,
        out_weight,
        inputs,
        keep_mask,
        cotangent,
    )
    received = lax.all_to_all(sent, "ch", split_axis=0, concat_axis=0, tiled=True)
    send = run_block(
        core.reshape(1), received, lambda values: lax.ppermute(values, "img", core_pairs)
    )
    back = lax.all_to_all(send, "ch", split_axis=0, concat_axis=0, tiled=True)

    sums = collect(back, swished)
    plane = lax.ppermute(sums, "img", plane_pairs)
    outputs, input_grad = images(back)
    plane, outputs, input_grad = lax.optimization_barrier((plane, outputs, input_grad))
    sums = sums.astype(F32) + plane.astype(F32)
    theirs = lax.ppermute(sums, "img", core_pairs)
    (gain, bias, conv_w, conv_b, temb_w, temb_b, qkv_w, qv_b, out_w, out_b) = finish(
        core.reshape(1), sums, theirs
    )
    return (
        outputs,
        input_grad,
        gain,
        bias,
        conv_w,
        conv_b,
        temb_w.T,
        temb_b[0],
        qkv_w,
        qv_b,
        out_w,
        out_b[0],
    )


def solution(mesh):
    placed = (
        P("ch", "img", None),
        P("img"),
        P("ch", "img", None),
        P(None, "ch"),
        P(None, "ch"),
        P(None, None, "ch", None),
        P(None, "ch"),
        P(None, "ch"),
        P("ch"),
        P(None, "ch", None),
        P(None, "ch"),
        P("ch", None),
        P("ch"),
        P("ch", "img", None),
    )
    return jax.shard_map(
        on_device,
        mesh=mesh,
        in_specs=placed,
        out_specs=(
            P("ch", "img", None),
            P("ch", "img", None),
            P(None, "ch"),
            P(None, "ch"),
            P(None, None, "ch", None),
            P(None, "ch"),
            P(None, "ch"),
            P("ch"),
            P(None, "ch", None),
            P(None, "ch"),
            P("ch", None),
            P("ch"),
        ),
        check_vma=False,
    )
```

```python
import functools
import math

import jax
import jax.numpy as jnp
from jax import lax
from jax.experimental import pallas as pl
from jax.experimental.pallas import tpu as pltpu
from jax.sharding import PartitionSpec as P

C = 256
TEMB = 512
SIDE = 16
POS = 256
SHARDS = 32
ROWS = C // SHARDS
HALF = 128
WBLOCKS = 22
WROWS = WBLOCKS * ROWS
NORM_EPS = 1e-06
GROUP_SIZE = ROWS * POS
F32 = jnp.float32
BF16 = jnp.bfloat16

OFFSETS, GAINS, BIASES, CONV_BIAS, QV_BIAS, OUT_BIAS, TEMB_BIAS = 0, 1, 4, 7, 9, 11, 12
D_GAINS, D_BIASES, D_CONV_BIAS, D_QV_BIAS, D_OUT_BIAS = 0, 3, 6, 8, 10
PART = 16


def dot_nn(a, b):
    return lax.dot_general(a, b, (((1,), (0,)), ((), ())), preferred_element_type=F32)


def dot_nt(a, b):
    return lax.dot_general(a, b, (((1,), (1,)), ((), ())), preferred_element_type=F32)


def dot_tn(a, b):
    return lax.dot_general(a, b, (((0,), (0,)), ((), ())), preferred_element_type=F32)


def group_sum(values):
    column = jnp.sum(values, axis=1, keepdims=True)
    return group_column(column)


def group_column(column):
    grouped = column.reshape(SHARDS, ROWS, 1)
    total = jnp.sum(grouped, axis=1, keepdims=True)
    return jnp.broadcast_to(total, grouped.shape).reshape(C, 1)


def norm_hat(values):
    average = group_sum(values) * (1.0 / GROUP_SIZE)
    centered = values - average
    spread = group_sum(centered * centered) * (1.0 / GROUP_SIZE)
    inverse = lax.rsqrt(spread + NORM_EPS)
    return centered * inverse, inverse


def norm_back(hat, inverse, grad_out, gain):
    gain_grad = jnp.sum(grad_out * hat, axis=1, keepdims=True)
    bias_grad = jnp.sum(grad_out, axis=1, keepdims=True)
    first_mean = group_column(bias_grad * gain) * (1.0 / GROUP_SIZE)
    second_mean = group_column(gain_grad * gain) * (1.0 / GROUP_SIZE)
    grad_in = inverse * (grad_out * gain - first_mean - hat * second_mean)
    return grad_in, gain_grad, bias_grad


def sigmoid(values):
    return 1.0 / (1.0 + jnp.exp(-values))


def rolled(values, steps, axis):
    return pltpu.roll(values, steps % POS, axis)


def column_shifted(values, step, axis):
    shape = (1, POS) if axis == 1 else (POS, POS)
    cell = (lax.broadcasted_iota(jnp.int32, shape, axis) & (SIDE - 1)) + step
    valid = (cell >= 0) & (cell < SIDE)
    return rolled(values, -step, axis) * valid.astype(F32)


def row_shifted(values, step):
    cell = lax.broadcasted_iota(jnp.int32, (1, POS), 1) + step * SIDE
    valid = (cell >= 0) & (cell < POS)
    return rolled(values, -step * SIDE, 1) * valid.astype(F32)


def load_weights(mine_ref, theirs_ref, first_row, blocks, first_core, weights):
    for pair in range(blocks // 2):
        rows = slice(first_row + 16 * pair, first_row + 16 * pair + 16)
        mine = mine_ref[:, rows, :].astype(F32)
        theirs = theirs_ref[:, 16 * pair : 16 * pair + 16, :].astype(F32)
        for part in range(2):
            rows = slice(ROWS * part, ROWS * part + ROWS)
            a = mine[:, rows, :].reshape(C, HALF)
            b = theirs[:, rows, :].reshape(C, HALF)
            weights[2 * pair + part, :, 0:HALF] = jnp.where(first_core, a, b).astype(BF16)
            weights[2 * pair + part, :, HALF:C] = jnp.where(first_core, b, a).astype(BF16)


def load_image(ref, at):
    block = ref[:, at : at + 16, :].astype(F32)
    left = block[:, 0:ROWS, :].reshape(C, HALF)
    right = block[:, ROWS : 2 * ROWS, :].reshape(C, HALF)
    return jnp.concatenate([left, right], axis=1)


def image_rows(values):
    left = values[:, 0:HALF].reshape(SHARDS, ROWS, HALF)
    right = values[:, HALF:C].reshape(SHARDS, ROWS, HALF)
    return jnp.concatenate([left, right], axis=1).astype(BF16)


def store_shifts(target, values):
    for step in (-1, 0, 1):
        moved = (column_shifted(values, step, 1) if step else values).astype(BF16)
        target[0, step + 1, :, :] = moved[:HALF]
        target[1, step + 1, :, :] = moved[HALF:]


def convolve(weights, shifts):
    stacked = jnp.concatenate([shifts[k % 2, k // 2] for k in range(6)], axis=0)
    total = None
    for row in (0, -1, 1):
        matrix = jnp.concatenate([weights[3 * row + 3 + k] for k in range(3)], axis=1)
        product = dot_nn(matrix, stacked)
        total = product if row == 0 else total + row_shifted(product, row)
    return total


def convolve_back(weights, low):
    turned = low.astype(F32).T.astype(BF16)
    edge = jnp.zeros((SIDE, C), BF16)
    stacked = jnp.concatenate(
        [
            jnp.concatenate([turned[SIDE:], edge], axis=0),
            turned,
            jnp.concatenate([edge, turned[:-SIDE]], axis=0),
        ],
        axis=1,
    )
    total = None
    for step in (0, -1, 1):
        matrix = jnp.concatenate([weights[3 * k + step + 1] for k in range(3)], axis=0)
        product = dot_nn(stacked, matrix)
        total = product if step == 0 else total + column_shifted(product, -step, 0)
    return total.T


def own_first(ref, core):
    count = math.prod(ref.shape[1:-1])
    halves = [ref[core].reshape(count, POS), ref[1 - core].reshape(count, POS)]
    return jnp.concatenate(halves, axis=0)


def store_weight_grads(own_ref, swap_ref, first_block, products):
    for target, at in ((own_ref, 0), (swap_ref, 1)):
        blocks = []
        for product in products:
            lanes = product.shape[1] // 2
            for k in range(lanes // HALF):
                start = at * lanes + k * HALF
                blocks.append(product[:, start : start + HALF].reshape(SHARDS, ROWS, HALF))
        for pair in range(len(blocks) // 2):
            rows = slice((first_block + 2 * pair) * ROWS, (first_block + 2 * pair + 2) * ROWS)
            target[:, rows, :] = jnp.concatenate(
                blocks[2 * pair : 2 * pair + 2], axis=1
            ).astype(BF16)


def conv_weight_grads(low, shifts, core):
    wide = low.astype(F32)
    operand = own_first(shifts, core)
    grads = []
    for row in (-1, 0, 1):
        moved = row_shifted(wide, -row).astype(BF16) if row else low
        grads.append(dot_nt(moved, operand))
    return grads


def columns_of(listed):
    lane = lax.broadcasted_iota(jnp.int32, (C, HALF), 1)
    table = jnp.zeros((C, HALF), F32)
    for k, column in enumerate(listed):
        table = jnp.where(lane == k, column, table)
    return table


def column(ref, lane):
    return ref[:, lane : lane + 1]


def row_sum(values):
    return jnp.sum(values, axis=1, keepdims=True)


def slope(values):
    sigma = sigmoid(values)
    return sigma * (1.0 + values * (1.0 - sigma))


def first_kernel(recv_ref, taps_ref, hat_ref, params_ref, stats_ref):
    columns = recv_ref[:, AT_PARAMS : AT_PARAMS + ROWS, :].astype(F32).reshape(C, HALF)
    columns = (
        columns
        + pltpu.roll(columns, HALF - PART, 1)
        + pltpu.roll(columns, HALF - 2 * PART, 1)
    )
    params_ref[...] = columns
    hat, inverse = norm_hat(load_image(recv_ref, AT_SOURCE))
    hat_ref[...] = hat
    stats_ref[...] = jnp.broadcast_to(inverse, (C, HALF))
    pre = hat * columns[:, GAINS : GAINS + 1] + columns[:, BIASES : BIASES + 1]
    store_shifts(taps_ref, (pre * sigmoid(pre)).astype(BF16).astype(F32))


def middle_kernel(
    core_ref, recv_ref, other_ref, taps_one, params, weights, taps_ref, hat_ref, stats_ref
):
    load_weights(recv_ref, other_ref, 0, IN_CUT, core_ref[0] == 0, weights)
    middle = convolve(weights, taps_one) + (column(params, CONV_BIAS) + column(params, OFFSETS))
    hat, inverse = norm_hat(middle)
    hat_ref[...] = hat
    stats_ref[...] = jnp.broadcast_to(inverse, (C, HALF))
    pre = hat * column(params, GAINS + 1) + column(params, BIASES + 1)
    keep = load_image(recv_ref, AT_KEEP) * (1.0 / 0.9)
    store_shifts(taps_ref, (pre * sigmoid(pre) * keep).astype(BF16).astype(F32))


def attention_kernel(
    core_ref, recv_ref, other_ref, taps_two, params, first_weights,
    own_ref, swap_ref, weights, outputs_ref, attended_ref, grad_ref, sums_ref, normed_ref,
):
    first_core = core_ref[0] == 0
    load_weights(recv_ref, other_ref, IN_CUT_ROWS, WBLOCKS - IN_CUT, first_core, weights)
    cotangent = load_image(recv_ref, AT_COTANGENT)
    cot_low = cotangent.astype(BF16)
    attended_grad = dot_tn(first_weights[OUT_BLOCK], cot_low).astype(BF16)
    source = load_image(recv_ref, AT_SOURCE)
    residual = source + convolve(weights, taps_two) + column(params, CONV_BIAS + 1)
    hat, inverse = norm_hat(residual)
    normed = (hat * column(params, GAINS + 2) + column(params, BIASES + 2)).astype(BF16)
    scale = C ** (-0.5)
    queries = (dot_nn(first_weights[QUERY_BLOCK], normed) + column(params, QV_BIAS)).astype(BF16)
    keys = dot_nn(first_weights[KEY_BLOCK], normed).astype(BF16)
    vals = (dot_nn(weights[VALUE_BLOCK - IN_CUT], normed) + column(params, QV_BIAS + 1)).astype(BF16)
    scores = dot_tn(queries, keys) * scale
    dprobs = dot_tn(attended_grad, vals)
    exps = jnp.exp(scores - jnp.max(scores, axis=1, keepdims=True))
    probs = exps / row_sum(exps)
    probs_low = probs.astype(BF16)
    dscores = (probs * (dprobs - row_sum(probs * dprobs))).astype(BF16)
    query_grad = (dot_nt(keys, dscores) * scale).astype(BF16)
    key_grad = (dot_nn(queries, dscores) * scale).astype(BF16)
    value_grad = dot_nn(attended_grad, probs_low).astype(BF16)
    matrices = [first_weights[QUERY_BLOCK], first_weights[KEY_BLOCK], weights[VALUE_BLOCK - IN_CUT]]
    normed_grad = dot_tn(
        jnp.concatenate(matrices, axis=0),
        jnp.concatenate([query_grad, key_grad, value_grad], axis=0),
    )
    normed_ref[0] = normed[:HALF]
    normed_ref[1] = normed[HALF:]
    operand = own_first(normed_ref, core_ref[0])
    dqkv = [dot_nt(gradient, operand) for gradient in (query_grad, key_grad, value_grad)]
    attended = dot_nt(vals, probs_low).astype(BF16)
    attended_ref[0] = attended[:HALF]
    attended_ref[1] = attended[HALF:]
    outputs = residual + dot_nn(first_weights[OUT_BLOCK], attended) + column(params, OUT_BIAS)
    outputs_ref[...] = image_rows(outputs)
    branch, gain_grad, bias_grad = norm_back(hat, inverse, normed_grad, column(params, GAINS + 2))
    residual_grad = cotangent + branch
    grad_ref[...] = residual_grad
    low = residual_grad.astype(BF16)
    store_weight_grads(own_ref, swap_ref, 0, dqkv[:2] + conv_weight_grads(low, taps_two, core_ref[0]) + dqkv[2:])
    listed = {
        D_GAINS + 2: gain_grad,
        D_BIASES + 2: bias_grad,
        D_CONV_BIAS + 1: row_sum(residual_grad),
        D_QV_BIAS: row_sum(query_grad.astype(F32)),
        D_QV_BIAS + 1: row_sum(value_grad.astype(F32)),
        D_OUT_BIAS: row_sum(cotangent),
    }
    zero = jnp.zeros((C, 1), F32)
    sums_ref[...] = columns_of([listed.get(k, zero) for k in range(PART)])


def middle_back_kernel(
    core_ref, recv_ref, weights, taps_one, hat_ref, stats, params, attended, grad_ref, sums,
    own_ref, swap_ref, low_ref, sums_ref,
):
    hat = hat_ref[...]
    gain = column(params, GAINS + 1)
    pre = hat * gain + column(params, BIASES + 1)
    keep = load_image(recv_ref, AT_KEEP) * (1.0 / 0.9)
    factor = keep * slope(pre)
    cot_low = load_image(recv_ref, AT_COTANGENT).astype(BF16)
    out_grad = dot_nt(cot_low, own_first(attended, core_ref[0]))
    second_grad = convolve_back(weights, grad_ref[...].astype(BF16))
    pre_grad = second_grad * factor
    middle_grad, gain_grad, bias_grad = norm_back(hat, column(stats, 0), pre_grad, gain)
    low = middle_grad.astype(BF16)
    low_ref[...] = low
    grads = conv_weight_grads(low, taps_one, core_ref[0]) + [out_grad]
    store_weight_grads(own_ref, swap_ref, 0, grads)
    listed = {D_GAINS + 1: gain_grad, D_BIASES + 1: bias_grad, D_CONV_BIAS: row_sum(middle_grad)}
    zero = jnp.zeros((C, 1), F32)
    sums_ref[...] = sums[...] + columns_of([listed.get(k, zero) for k in range(PART)])


def first_back_kernel(
    weights, hat_ref, stats, params, low_ref, grad_ref, sums, outputs, own, swapped, send_ref
):
    hat = hat_ref[...]
    gain = column(params, GAINS)
    pre = hat * gain + column(params, BIASES)
    factor = slope(pre)
    first_grad = convolve_back(weights, low_ref[...])
    branch, gain_grad, bias_grad = norm_back(hat, column(stats, 0), first_grad * factor, gain)
    for pair in range((WBLOCKS - OUT_CUT) // 2):
        rows = slice(16 * pair, 16 * pair + 16)
        both = own[:, rows, :].astype(F32) + swapped[:, rows, :].astype(F32)
        to = OUT_CUT_ROWS + 16 * pair
        send_ref[:, to : to + 16, :] = both.astype(BF16)
    send_ref[:, WROWS : WROWS + 16, :] = outputs[...]
    send_ref[:, WROWS + 16 : WROWS + 32, :] = image_rows(grad_ref[...] + branch)

    zero = jnp.zeros((C, 1), F32)
    listed = {D_GAINS: gain_grad, D_BIASES: bias_grad}
    table = sums[...] + columns_of([listed.get(k, zero) for k in range(PART)])
    high = table.astype(BF16).astype(F32)
    low = pltpu.roll(table - high, PART, 1)
    lane = lax.broadcasted_iota(jnp.int32, (C, HALF), 1)
    table = jnp.where(lane < PART, high, low)
    send_ref[:, WROWS + 32 : WROWS + 40, :] = table.reshape(SHARDS, ROWS, HALF).astype(BF16)


AT_SOURCE, AT_KEEP, AT_COTANGENT, AT_PARAMS = WROWS, WROWS + 16, WROWS + 32, WROWS + 48
IN_ROWS = WROWS + 56
OUT_ROWS = WROWS + 40
OUT_BLOCK, QUERY_BLOCK, KEY_BLOCK, SECOND_CONV, VALUE_BLOCK = 9, 10, 11, 12, 21
IN_CUT, OUT_CUT = 12, 10
IN_CUT_ROWS, OUT_CUT_ROWS = IN_CUT * ROWS, OUT_CUT * ROWS


def local_call(kernel, core, *operands, out):
    in_specs = [pl.BlockSpec(memory_space=pltpu.VMEM) for _ in operands]
    if core is not None:
        in_specs = [pl.BlockSpec(memory_space=pltpu.SMEM)] + in_specs
        operands = (core, *operands)
    shapes = tuple(jax.ShapeDtypeStruct(shape, dtype) for shape, dtype in out)
    return pl.pallas_call(
        kernel,
        out_shape=shapes,
        in_specs=in_specs,
        out_specs=tuple(pl.BlockSpec(memory_space=pltpu.VMEM) for _ in out),
        compiler_params=pltpu.CompilerParams(vmem_limit_bytes=VMEM_LIMIT),
    )(*operands)


VMEM_LIMIT = 24 * 1024 * 1024


def run_block(core, received, swap):
    other_one = swap(received[:, :IN_CUT_ROWS])
    other_two = swap(received[:, IN_CUT_ROWS:WROWS])
    image, table = ((C, POS), F32), ((C, HALF), F32)
    taps, low = ((2, 3, HALF, POS), BF16), ((C, POS), BF16)
    halves = ((2, HALF, POS), BF16)

    taps_one, hat_one, params, stats_one = local_call(
        first_kernel, None, received, out=(taps, image, table, table)
    )
    weights_one, taps_two, hat_two, stats_two = local_call(
        middle_kernel, core, received, other_one, taps_one, params,
        out=(((IN_CUT, C, C), BF16), taps, image, table),
    )
    second = ((SHARDS, WROWS - OUT_CUT_ROWS, HALF), BF16)
    rows = ((SHARDS, 16, HALF), BF16)
    own_two, swap_two, weights_two, outputs, attended, residual_grad, sums, _ = local_call(
        attention_kernel, core, received, other_two, taps_two, params, weights_one,
        out=(second, second, ((WBLOCKS - IN_CUT, C, C), BF16), rows, halves, image, table, halves),
    )
    swapped_two = swap(swap_two)
    first = ((SHARDS, OUT_CUT_ROWS, HALF), BF16)
    own_one, swap_one, middle_low, sums = local_call(
        middle_back_kernel, core, received, weights_two, taps_one, hat_two, stats_two, params,
        attended, residual_grad, sums, out=(first, first, low, table),
    )
    swapped_one = swap(swap_one)
    (send,) = local_call(
        first_back_kernel, None, weights_one, hat_one, stats_one, params, middle_low,
        residual_grad, sums, outputs, own_two, swapped_two,
        out=(((SHARDS, OUT_ROWS, HALF), BF16),),
    )
    both = (own_one.astype(F32) + swapped_one.astype(F32)).astype(BF16)
    return lax.dynamic_update_slice(send, both, (0, 0, 0))


def collect_kernel(back_ref, swished_ref, sums_ref):
    for pair in range(WROWS // 16):
        rows = slice(16 * pair, 16 * pair + 16)
        total = back_ref[0, rows, :].astype(F32)
        for image in range(1, SHARDS):
            total = total + back_ref[image, rows, :].astype(F32)
        sums_ref[rows, :] = total.astype(BF16)
    small = back_ref[:, WROWS + 32 : WROWS + 40, :].astype(F32)
    table = jnp.zeros((ROWS, HALF), F32)
    temb = jnp.zeros((ROWS, TEMB), F32)
    for image in range(SHARDS):
        values = small[image] + pltpu.roll(small[image], HALF - PART, 1)
        table = table + values
        offsets_grad = values[:, D_CONV_BIAS : D_CONV_BIAS + 1]
        temb = temb + offsets_grad * swished_ref[image : image + 1, :]
    lane = lax.broadcasted_iota(jnp.int32, (ROWS, HALF), 1)
    high = table.astype(BF16).astype(F32)
    low = pltpu.roll(table - high, PART, 1)
    parts = jnp.where(lane < PART, high, jnp.where(lane < 2 * PART, low, 0.0))
    blocks = [parts] + [temb[:, HALF * k : HALF * k + HALF] for k in range(TEMB // HALF)]
    blocks = blocks + [jnp.zeros((ROWS, HALF), F32)]
    for pair in range(len(blocks) // 2):
        rows = slice(WROWS + 16 * pair, WROWS + 16 * pair + 16)
        both = jnp.concatenate(blocks[2 * pair : 2 * pair + 2], axis=0)
        sums_ref[rows, :] = both.astype(BF16)


SUM_ROWS = WROWS + ROWS + TEMB * ROWS // HALF + ROWS


def collect(back, swished):
    return pl.pallas_call(
        collect_kernel,
        out_shape=jax.ShapeDtypeStruct((SUM_ROWS, HALF), BF16),
        in_specs=[pl.BlockSpec(memory_space=pltpu.VMEM)] * 2,
        out_specs=pl.BlockSpec(memory_space=pltpu.VMEM),
        compiler_params=pltpu.CompilerParams(vmem_limit_bytes=8 * 1024 * 1024),
    )(back, swished)


def images_kernel(back_ref, outputs_ref, grad_ref):
    for at, target in ((WROWS, outputs_ref), (WROWS + 16, grad_ref)):
        block = back_ref[:, at : at + 16, :].astype(F32)
        cut = jnp.concatenate([block[:, :ROWS, :], block[:, ROWS:, :]], axis=2)
        target[...] = jnp.swapaxes(cut, 0, 1).astype(BF16)


def images(back):
    shape = jax.ShapeDtypeStruct((ROWS, SHARDS, POS), BF16)
    return pl.pallas_call(
        images_kernel,
        out_shape=(shape, shape),
        in_specs=[pl.BlockSpec(memory_space=pltpu.VMEM)],
        out_specs=(pl.BlockSpec(memory_space=pltpu.VMEM), pl.BlockSpec(memory_space=pltpu.VMEM)),
        compiler_params=pltpu.CompilerParams(vmem_limit_bytes=8 * 1024 * 1024),
    )(back)


def finish_kernel(core_ref, mine_ref, theirs_ref, *refs):
    results, scratch, sems = refs[:10], refs[10:20], refs[20]
    first_core = core_ref[0] == 0
    (gain, bias, conv_w, conv_b, temb_w, temb_b, qkv_w, qv_b, out_w, out_b) = scratch

    def weight_grad(block):
        rows = slice(ROWS * block, ROWS * block + ROWS)
        mine, theirs = mine_ref[rows, :], theirs_ref[rows, :]
        return jnp.concatenate(
            [jnp.where(first_core, mine, theirs), jnp.where(first_core, theirs, mine)], axis=1
        )

    copies = [pltpu.make_async_copy(scratch[k], results[k], sems.at[k]) for k in range(10)]
    for conv in range(2):
        for tap in range(9):
            conv_w[conv, tap, :, :] = weight_grad(SECOND_CONV * conv + tap)
    copies[2].start()
    for k in range(3):
        qkv_w[k, :, :] = weight_grad((QUERY_BLOCK, KEY_BLOCK, VALUE_BLOCK)[k])
    copies[6].start()
    out_w[...] = weight_grad(OUT_BLOCK)
    copies[8].start()
    shared = mine_ref[WROWS:, :] + theirs_ref[WROWS:, :]
    small = shared[:ROWS, :] + pltpu.roll(shared[:ROWS, :], HALF - PART, 1)
    for part in range(TEMB // HALF):
        rows = slice(ROWS + ROWS * part, 2 * ROWS + ROWS * part)
        temb_w[:, HALF * part : HALF * part + HALF] = shared[rows, :]
    copies[4].start()
    padded = jnp.concatenate([small, jnp.zeros((HALF - ROWS, HALF), F32)], axis=0)
    table = padded.T[:PART, :ROWS]
    gain[...] = table[D_GAINS : D_GAINS + 3]
    bias[...] = table[D_BIASES : D_BIASES + 3]
    conv_b[...] = table[D_CONV_BIAS : D_CONV_BIAS + 2]
    temb_b[...] = table[D_CONV_BIAS : D_CONV_BIAS + 1]
    qv_b[...] = table[D_QV_BIAS : D_QV_BIAS + 2]
    out_b[...] = table[D_OUT_BIAS : D_OUT_BIAS + 1]
    for k in (0, 1, 3, 5, 7, 9):
        copies[k].start()
    for copy in copies:
        copy.wait()


def finish(core, mine, theirs):
    shapes = [
        (3, ROWS), (3, ROWS), (2, 9, ROWS, C), (2, ROWS), (ROWS, TEMB), (1, ROWS),
        (3, ROWS, C), (2, ROWS), (ROWS, C), (1, ROWS),
    ]
    return pl.pallas_call(
        finish_kernel,
        out_shape=[jax.ShapeDtypeStruct(shape, F32) for shape in shapes],
        in_specs=[
            pl.BlockSpec(memory_space=pltpu.SMEM),
            pl.BlockSpec(memory_space=pltpu.VMEM),
            pl.BlockSpec(memory_space=pltpu.VMEM),
        ],
        out_specs=[pl.BlockSpec(memory_space=pltpu.HBM) for _ in shapes],
        scratch_shapes=[pltpu.VMEM(shape, F32) for shape in shapes]
        + [pltpu.SemaphoreType.DMA((10,))],
        compiler_params=pltpu.CompilerParams(vmem_limit_bytes=8 * 1024 * 1024),
    )(core, mine, theirs)


def prepare_kernel(core_ref, *refs):
    count = PREPARE_ARRAYS
    arrays, (send_ref, swished_ref) = refs[:count], refs[count : count + 2]
    held, (angles, sems) = refs[count + 2 : 2 * count + 2], refs[2 * count + 2 :]
    (
        steps_ref, gain_ref, bias_ref, conv_bias_ref, qv_ref, out_bias_ref, temb_bias_ref,
        temb_ref, conv_ref, qkv_ref, out_ref, inputs_ref, mask_ref, cotangent_ref,
    ) = held
    copies = [pltpu.make_async_copy(arrays[k], held[k], sems.at[k]) for k in range(count)]
    for copy in copies:
        copy.start()
    first_core = core_ref[0] == 0
    for copy in copies[:8]:
        copy.wait()

    half_dim = TEMB // 2
    index = lax.broadcasted_iota(jnp.int32, (1, half_dim), 1).astype(F32)
    rates = jnp.exp(-math.log(10000.0) * index / (half_dim - 1))
    for image in range(SHARDS):
        angles[image : image + 1, :] = rates * steps_ref[image].astype(F32)
    features = jnp.concatenate([jnp.sin(angles[...]), jnp.cos(angles[...])], axis=1)
    swished = features * sigmoid(features)
    swished_ref[...] = swished
    offsets = None
    rest = swished
    for _ in range(3):
        part = rest.astype(BF16)
        rest = rest - part.astype(F32)
        product = dot_nt(temb_ref[...], part)
        offsets = product if offsets is None else offsets + product

    rows = jnp.concatenate(
        [
            jnp.zeros((1, ROWS), F32), gain_ref[...], bias_ref[...], conv_bias_ref[...],
            qv_ref[...], out_bias_ref[...], temb_bias_ref[...], jnp.zeros((3, ROWS), F32),
        ],
        axis=0,
    )
    square = jnp.concatenate([rows] * (HALF // PART), axis=0)
    square = jnp.concatenate([square, jnp.zeros((HALF, HALF - ROWS), F32)], axis=1)
    columns = square.T[:ROWS, :]
    lane = lax.broadcasted_iota(jnp.int32, (ROWS, HALF), 1)
    offset_lane = (lane & (PART - 1)) == OFFSETS
    offsets = offsets + columns[:, TEMB_BIAS : TEMB_BIAS + 1]
    for image in range(SHARDS):
        values = jnp.where(offset_lane, offsets[:, image : image + 1], columns)
        high = values.astype(BF16).astype(F32)
        mid = (values - high).astype(BF16).astype(F32)
        low = values - high - mid
        parts = jnp.where(
            lane < PART,
            high,
            jnp.where(lane < 2 * PART, mid, jnp.where(lane < 3 * PART, low, 0.0)),
        )
        send_ref[image, WROWS + 48 : WROWS + 56, :] = parts.astype(BF16)

    for copy in copies[8:]:
        copy.wait()

    def half(values):
        values = values.astype(F32)
        return jnp.where(first_core, values[:, :HALF], values[:, HALF:])

    shard = jnp.concatenate(
        [
            half(conv_ref[0].reshape(9 * ROWS, C)),
            half(out_ref[...]),
            half(qkv_ref[0]),
            half(qkv_ref[1]),
            half(conv_ref[1].reshape(9 * ROWS, C)),
            half(qkv_ref[2]),
        ],
        axis=0,
    ).astype(BF16)
    send_ref[:, :WROWS, :] = jnp.broadcast_to(shard[None], (SHARDS, WROWS, HALF))

    def put(at, values):
        turned = jnp.swapaxes(values.astype(F32), 0, 1)
        cut = jnp.concatenate([turned[:, :, :HALF], turned[:, :, HALF:]], axis=1)
        send_ref[:, at : at + 16, :] = cut.astype(BF16)

    put(WROWS, inputs_ref[...])
    put(WROWS + 16, mask_ref[...])
    put(WROWS + 32, cotangent_ref[...])


PREPARE_ARRAYS = 14


def prepare(core, timesteps, *arrays):
    held = [pltpu.SMEM((SHARDS,), jnp.int32)]
    held += [pltpu.VMEM(array.shape, array.dtype) for array in arrays]
    return pl.pallas_call(
        prepare_kernel,
        out_shape=(
            jax.ShapeDtypeStruct((SHARDS, IN_ROWS, HALF), BF16),
            jax.ShapeDtypeStruct((SHARDS, TEMB), F32),
        ),
        in_specs=[pl.BlockSpec(memory_space=pltpu.SMEM)]
        + [pl.BlockSpec(memory_space=pltpu.HBM)] * PREPARE_ARRAYS,
        out_specs=(pl.BlockSpec(memory_space=pltpu.VMEM), pl.BlockSpec(memory_space=pltpu.VMEM)),
        scratch_shapes=held
        + [pltpu.VMEM((SHARDS, TEMB // 2), F32), pltpu.SemaphoreType.DMA((PREPARE_ARRAYS,))],
        compiler_params=pltpu.CompilerParams(vmem_limit_bytes=16 * 1024 * 1024),
    )(core, *[pltpu.with_memory_space_constraint(a, pltpu.HBM) for a in (timesteps, *arrays)])


def on_device(
    inputs,
    timesteps,
    keep_mask,
    norm_gain,
    norm_bias,
    conv_weight,
    conv_bias,
    temb_weight,
    temb_bias,
    qkv_weight,
    qv_bias,
    out_weight,
    out_bias,
    cotangent,
):
    member = lax.axis_index("img")
    core = member % 2
    core_pairs = [(m, m ^ 1) for m in range(4)]
    plane_pairs = [(m, m ^ 2) for m in range(4)]
    sent, swished = prepare(
        core.reshape(1),
        timesteps,
        norm_gain,
        norm_bias,
        conv_bias,
        qv_bias,
        out_bias.reshape(1, ROWS),
        temb_bias.reshape(1, ROWS),
        temb_weight.T,
        conv_weight,
        qkv_weight,
        out_weight,
        inputs,
        keep_mask,
        cotangent,
    )
    received = lax.all_to_all(sent, "ch", split_axis=0, concat_axis=0, tiled=True)
    send = run_block(
        core.reshape(1), received, lambda values: lax.ppermute(values, "img", core_pairs)
    )
    back = lax.all_to_all(send, "ch", split_axis=0, concat_axis=0, tiled=True)

    sums = collect(back, swished)
    plane = lax.ppermute(sums, "img", plane_pairs)
    outputs, input_grad = images(back)
    plane, outputs, input_grad = lax.optimization_barrier((plane, outputs, input_grad))
    sums = sums.astype(F32) + plane.astype(F32)
    theirs = lax.ppermute(sums, "img", core_pairs)
    (gain, bias, conv_w, conv_b, temb_w, temb_b, qkv_w, qv_b, out_w, out_b) = finish(
        core.reshape(1), sums, theirs
    )
    return (
        outputs,
        input_grad,
        gain,
        bias,
        conv_w,
        conv_b,
        temb_w.T,
        temb_b[0],
        qkv_w,
        qv_b,
        out_w,
        out_b[0],
    )


def solution(mesh):
    placed = (
        P("ch", "img", None),
        P("img"),
        P("ch", "img", None),
        P(None, "ch"),
        P(None, "ch"),
        P(None, None, "ch", None),
        P(None, "ch"),
        P(None, "ch"),
        P("ch"),
        P(None, "ch", None),
        P(None, "ch"),
        P("ch", None),
        P("ch"),
        P("ch", "img", None),
    )
    return jax.shard_map(
        on_device,
        mesh=mesh,
        in_specs=placed,
        out_specs=(
            P("ch", "img", None),
            P("ch", "img", None),
            P(None, "ch"),
            P(None, "ch"),
            P(None, None, "ch", None),
            P(None, "ch"),
            P(None, "ch"),
            P("ch"),
            P(None, "ch", None),
            P(None, "ch"),
            P("ch", None),
            P("ch"),
        ),
        check_vma=False,
    )
```

```python
import functools
import math

import jax
import jax.numpy as jnp
from jax import lax
from jax.experimental import pallas as pl
from jax.experimental.pallas import tpu as pltpu
from jax.sharding import PartitionSpec as P

C = 256
TEMB = 512
SIDE = 16
POS = 256
SHARDS = 32
ROWS = C // SHARDS
HALF = 128
WBLOCKS = 22
WROWS = WBLOCKS * ROWS
NORM_EPS = 1e-06
GROUP_SIZE = ROWS * POS
F32 = jnp.float32
BF16 = jnp.bfloat16

OFFSETS, GAINS, BIASES, CONV_BIAS, QV_BIAS, OUT_BIAS, TEMB_BIAS = 0, 1, 4, 7, 9, 11, 12
D_GAINS, D_BIASES, D_CONV_BIAS, D_QV_BIAS, D_OUT_BIAS = 0, 3, 6, 8, 10
PART = 16


def dot_nn(a, b):
    return lax.dot_general(a, b, (((1,), (0,)), ((), ())), preferred_element_type=F32)


def dot_nt(a, b):
    return lax.dot_general(a, b, (((1,), (1,)), ((), ())), preferred_element_type=F32)


def dot_tn(a, b):
    return lax.dot_general(a, b, (((0,), (0,)), ((), ())), preferred_element_type=F32)


def group_sum(values):
    column = jnp.sum(values, axis=1, keepdims=True)
    return group_column(column)


def group_column(column):
    grouped = column.reshape(SHARDS, ROWS, 1)
    total = jnp.sum(grouped, axis=1, keepdims=True)
    return jnp.broadcast_to(total, grouped.shape).reshape(C, 1)


def norm_hat(values):
    average = group_sum(values) * (1.0 / GROUP_SIZE)
    centered = values - average
    spread = group_sum(centered * centered) * (1.0 / GROUP_SIZE)
    inverse = lax.rsqrt(spread + NORM_EPS)
    return centered * inverse, inverse


def norm_back(hat, inverse, grad_out, gain):
    gain_grad = jnp.sum(grad_out * hat, axis=1, keepdims=True)
    bias_grad = jnp.sum(grad_out, axis=1, keepdims=True)
    first_mean = group_column(bias_grad * gain) * (1.0 / GROUP_SIZE)
    second_mean = group_column(gain_grad * gain) * (1.0 / GROUP_SIZE)
    grad_in = inverse * (grad_out * gain - first_mean - hat * second_mean)
    return grad_in, gain_grad, bias_grad


def sigmoid(values):
    return 0.5 + 0.5 * jnp.tanh(0.5 * values)


def rolled(values, steps, axis):
    return pltpu.roll(values, steps % POS, axis)


def column_shifted(values, step, axis):
    shape = (1, POS) if axis == 1 else (POS, POS)
    cell = (lax.broadcasted_iota(jnp.int32, shape, axis) & (SIDE - 1)) + step
    valid = (cell >= 0) & (cell < SIDE)
    return rolled(values, -step, axis) * valid.astype(F32)


def row_shifted(values, step):
    moved = rolled(values, -step * SIDE, 1)
    lane = lax.broadcasted_iota(jnp.int32, (1, HALF), 1)
    if step > 0:
        edge = jnp.where(lane < HALF - SIDE, moved[:, HALF:], 0.0)
        return jnp.concatenate([moved[:, :HALF], edge], axis=1)
    edge = jnp.where(lane >= SIDE, moved[:, :HALF], 0.0)
    return jnp.concatenate([edge, moved[:, HALF:]], axis=1)


def load_weights(mine_ref, theirs_ref, first_row, blocks, first_core, weights):
    for pair in range(blocks // 2):
        rows = slice(first_row + 16 * pair, first_row + 16 * pair + 16)
        mine = mine_ref[:, rows, :].astype(F32)
        theirs = theirs_ref[:, 16 * pair : 16 * pair + 16, :].astype(F32)
        for part in range(2):
            rows = slice(ROWS * part, ROWS * part + ROWS)
            a = mine[:, rows, :].reshape(C, HALF)
            b = theirs[:, rows, :].reshape(C, HALF)
            weights[2 * pair + part, :, 0:HALF] = jnp.where(first_core, a, b).astype(BF16)
            weights[2 * pair + part, :, HALF:C] = jnp.where(first_core, b, a).astype(BF16)


def load_image(ref, at):
    block = ref[:, at : at + 16, :].astype(F32)
    left = block[:, 0:ROWS, :].reshape(C, HALF)
    right = block[:, ROWS : 2 * ROWS, :].reshape(C, HALF)
    return jnp.concatenate([left, right], axis=1)


def image_rows(values):
    left = values[:, 0:HALF].reshape(SHARDS, ROWS, HALF)
    right = values[:, HALF:C].reshape(SHARDS, ROWS, HALF)
    return jnp.concatenate([left, right], axis=1).astype(BF16)


def store_shifts(target, values):
    for step in (-1, 0, 1):
        moved = (column_shifted(values, step, 1) if step else values).astype(BF16)
        target[0, step + 1, :, :] = moved[:HALF]
        target[1, step + 1, :, :] = moved[HALF:]


def convolve(weights, shifts):
    stacked = jnp.concatenate([shifts[k % 2, k // 2] for k in range(6)], axis=0)
    total = None
    for row in (0, -1, 1):
        matrix = jnp.concatenate([weights[3 * row + 3 + k] for k in range(3)], axis=1)
        product = dot_nn(matrix, stacked)
        total = product if row == 0 else total + row_shifted(product, row)
    return total


def convolve_back(weights, low):
    turned = low.astype(F32).T.astype(BF16)
    edge = jnp.zeros((SIDE, C), BF16)
    stacked = jnp.concatenate(
        [
            jnp.concatenate([turned[SIDE:], edge], axis=0),
            turned,
            jnp.concatenate([edge, turned[:-SIDE]], axis=0),
        ],
        axis=1,
    )
    total = None
    for step in (0, -1, 1):
        matrix = jnp.concatenate([weights[3 * k + step + 1] for k in range(3)], axis=0)
        product = dot_nn(stacked, matrix)
        total = product if step == 0 else total + column_shifted(product, -step, 0)
    return total.T


def own_first(ref, core):
    count = math.prod(ref.shape[1:-1])
    halves = [ref[core].reshape(count, POS), ref[1 - core].reshape(count, POS)]
    return jnp.concatenate(halves, axis=0)


def lane_blocks(product):
    count = product.shape[1] // HALF
    cut = [product[:, HALF * k : HALF * k + HALF] for k in range(count)]
    return [values.reshape(SHARDS, ROWS, HALF) for values in cut]


def store_weight_grads(own_ref, swap_ref, products):
    blocks = [lane_blocks(product) for product in products]
    for target, at in ((own_ref, 0), (swap_ref, 1)):
        listed = []
        for cut in blocks:
            listed += cut[: len(cut) // 2] if at == 0 else cut[len(cut) // 2 :]
        if len(listed) % 2:
            listed.append(jnp.zeros_like(listed[0]))
        for pair in range(len(listed) // 2):
            both = jnp.concatenate(listed[2 * pair : 2 * pair + 2], axis=1)
            rows = slice(PAIR_ROWS * pair, PAIR_ROWS * pair + PAIR_ROWS)
            target[rows, :] = both.reshape(PAIR_ROWS, HALF).astype(BF16)


def conv_weight_grads(low, shifts, core):
    wide = low.astype(F32)
    operand = own_first(shifts, core)
    grads = []
    for row in (-1, 0, 1):
        moved = row_shifted(wide, -row).astype(BF16) if row else low
        grads.append(dot_nt(moved, operand))
    return grads


def columns_of(listed, table):
    lane = lax.broadcasted_iota(jnp.int32, (C, HALF), 1)
    for k, column in listed.items():
        table = jnp.where(lane == k, column, table)
    return table


def column(ref, lane):
    return ref[:, lane : lane + 1]


def row_sum(values):
    return jnp.sum(values, axis=1, keepdims=True)


def slope(values):
    sigma = sigmoid(values)
    return sigma * (1.0 + values * (1.0 - sigma))


def first_kernel(recv_ref, taps_ref, hat_ref, params_ref, stats_ref):
    columns = recv_ref[:, AT_PARAMS : AT_PARAMS + ROWS, :].astype(F32).reshape(C, HALF)
    columns = (
        columns
        + pltpu.roll(columns, HALF - PART, 1)
        + pltpu.roll(columns, HALF - 2 * PART, 1)
    )
    params_ref[...] = columns
    hat, inverse = norm_hat(load_image(recv_ref, AT_SOURCE))
    hat_ref[...] = hat
    stats_ref[...] = jnp.broadcast_to(inverse, (C, HALF))
    pre = hat * columns[:, GAINS : GAINS + 1] + columns[:, BIASES : BIASES + 1]
    store_shifts(taps_ref, (pre * sigmoid(pre)).astype(BF16).astype(F32))


def middle_kernel(
    core_ref, recv_ref, other_ref, taps_one, params, weights, taps_ref, hat_ref, stats_ref
):
    load_weights(recv_ref, other_ref, 0, IN_CUT, core_ref[0] == 0, weights)
    middle = convolve(weights, taps_one) + (column(params, CONV_BIAS) + column(params, OFFSETS))
    hat, inverse = norm_hat(middle)
    hat_ref[...] = hat
    stats_ref[...] = jnp.broadcast_to(inverse, (C, HALF))
    pre = hat * column(params, GAINS + 1) + column(params, BIASES + 1)
    keep = load_image(recv_ref, AT_KEEP) * (1.0 / 0.9)
    store_shifts(taps_ref, (pre * sigmoid(pre) * keep).astype(BF16).astype(F32))


def attention_kernel(
    core_ref, recv_ref, other_ref, taps_two, params, first_weights,
    weights, outputs_ref, grad_ref, sums_ref, normed_ref, halves_ref, grads_ref,
):
    first_core = core_ref[0] == 0
    load_weights(recv_ref, other_ref, IN_CUT_ROWS, WBLOCKS - IN_CUT, first_core, weights)
    cotangent = load_image(recv_ref, AT_COTANGENT)
    cot_low = cotangent.astype(BF16)
    attended_grad = dot_tn(first_weights[OUT_BLOCK], cot_low).astype(BF16)
    source = load_image(recv_ref, AT_SOURCE)
    residual = source + convolve(weights, taps_two) + column(params, CONV_BIAS + 1)
    hat, inverse = norm_hat(residual)
    normed = (hat * column(params, GAINS + 2) + column(params, BIASES + 2)).astype(BF16)
    scale = C ** (-0.5)
    queries = (dot_nn(first_weights[QUERY_BLOCK], normed) + column(params, QV_BIAS)).astype(BF16)
    keys = dot_nn(first_weights[KEY_BLOCK], normed).astype(BF16)
    vals = (dot_nn(weights[VALUE_BLOCK - IN_CUT], normed) + column(params, QV_BIAS + 1)).astype(BF16)
    scores = dot_tn(queries, keys) * scale
    dprobs = dot_tn(attended_grad, vals)
    exps = jnp.exp(scores - jnp.max(scores, axis=1, keepdims=True))
    probs = exps / row_sum(exps)
    probs_low = probs.astype(BF16)
    dscores = (probs * (dprobs - row_sum(probs * dprobs))).astype(BF16)
    query_grad = (dot_nt(keys, dscores) * scale).astype(BF16)
    key_grad = (dot_nn(queries, dscores) * scale).astype(BF16)
    value_grad = dot_nn(attended_grad, probs_low).astype(BF16)
    matrices = [first_weights[QUERY_BLOCK], first_weights[KEY_BLOCK], weights[VALUE_BLOCK - IN_CUT]]
    normed_grad = dot_tn(
        jnp.concatenate(matrices, axis=0),
        jnp.concatenate([query_grad, key_grad, value_grad], axis=0),
    )
    normed_ref[0] = normed[:HALF]
    normed_ref[1] = normed[HALF:]
    for k, gradient in enumerate((query_grad, key_grad, value_grad)):
        grads_ref[k, :, :] = gradient
    attended = dot_nt(vals, probs_low).astype(BF16)
    halves_ref[0] = attended[:HALF]
    halves_ref[1] = attended[HALF:]
    outputs = residual + dot_nn(first_weights[OUT_BLOCK], attended) + column(params, OUT_BIAS)
    outputs_ref[...] = image_rows(outputs)
    branch, gain_grad, bias_grad = norm_back(hat, inverse, normed_grad, column(params, GAINS + 2))
    residual_grad = cotangent + branch
    grad_ref[...] = residual_grad
    listed = {
        D_GAINS + 2: gain_grad,
        D_BIASES + 2: bias_grad,
        D_CONV_BIAS + 1: row_sum(residual_grad),
        D_QV_BIAS: row_sum(query_grad.astype(F32)),
        D_QV_BIAS + 1: row_sum(value_grad.astype(F32)),
        D_OUT_BIAS: row_sum(cotangent),
    }
    sums_ref[...] = columns_of(listed, jnp.zeros((C, HALF), F32))


def early_grads_kernel(
    core_ref, recv_ref, taps_one, taps_two, grad_ref, normed_ref, halves_ref, grads_ref,
    own_ref, swap_ref,
):
    core = core_ref[0]
    other_half = taps_one[1 - core].reshape(3 * HALF, POS)
    swap_ref[EARLY_ROWS : EARLY_ROWS + 3 * HALF, :] = other_half[:, :HALF]
    swap_ref[EARLY_ROWS + 3 * HALF :, :] = other_half[:, HALF:]
    operand = own_first(normed_ref, core)
    dqkv = [dot_nt(grads_ref[k], operand) for k in range(3)]
    cot_low = load_image(recv_ref, AT_COTANGENT).astype(BF16)
    out_grad = dot_nt(cot_low, own_first(halves_ref, core))
    low = grad_ref[...].astype(BF16)
    grads = dqkv[:2] + conv_weight_grads(low, taps_two, core) + [dqkv[2], out_grad]
    store_weight_grads(own_ref, swap_ref, grads)


def middle_back_kernel(
    recv_ref, weights, hat_ref, stats, params, grad_ref, sums, low_ref, sums_ref
):
    hat = hat_ref[...]
    gain = column(params, GAINS + 1)
    pre = hat * gain + column(params, BIASES + 1)
    keep = load_image(recv_ref, AT_KEEP) * (1.0 / 0.9)
    factor = keep * slope(pre)
    second_grad = convolve_back(weights, grad_ref[...].astype(BF16))
    pre_grad = second_grad * factor
    middle_grad, gain_grad, bias_grad = norm_back(hat, column(stats, 0), pre_grad, gain)
    low_ref[...] = middle_grad.astype(BF16)
    listed = {D_GAINS + 1: gain_grad, D_BIASES + 1: bias_grad, D_CONV_BIAS: row_sum(middle_grad)}
    sums_ref[...] = columns_of(listed, sums[...])


def first_back_kernel(weights, hat_ref, stats, params, low_ref, grad_ref, sums, tail_ref):
    hat = hat_ref[...]
    gain = column(params, GAINS)
    pre = hat * gain + column(params, BIASES)
    factor = slope(pre)
    first_grad = convolve_back(weights, low_ref[...])
    branch, gain_grad, bias_grad = norm_back(hat, column(stats, 0), first_grad * factor, gain)
    tail_ref[:, :16, :] = image_rows(grad_ref[...] + branch)

    table = columns_of({D_GAINS: gain_grad, D_BIASES: bias_grad}, sums[...])
    high = table.astype(BF16).astype(F32)
    low = pltpu.roll(table - high, PART, 1)
    lane = lax.broadcasted_iota(jnp.int32, (C, HALF), 1)
    table = jnp.where(lane < PART, high, low).reshape(SHARDS, ROWS, HALF)
    tail_ref[:, 16:, :] = jnp.concatenate([table, jnp.zeros_like(table)], axis=1).astype(BF16)


def gather_kernel(core_ref, shifts, low_ref, their_low, own, swapped, outputs, tail, send_ref):
    mine = shifts[core_ref[0]].reshape(3 * HALF, POS)
    left = swapped[EARLY_ROWS : EARLY_ROWS + 3 * HALF, :]
    right = swapped[EARLY_ROWS + 3 * HALF :, :]
    operand = jnp.concatenate([mine, left, right], axis=1)
    wide = [low_ref[...].astype(F32), their_low[...].astype(F32)]
    blocks = []
    for row in (-1, 0, 1):
        moved = [row_shifted(values, -row) if row else values for values in wide]
        blocks += lane_blocks(dot_nt(jnp.concatenate(moved, axis=1).astype(BF16), operand))

    def early(pair):
        rows = slice(PAIR_ROWS * pair, PAIR_ROWS * pair + PAIR_ROWS)
        both = own[rows, :].astype(F32) + swapped[rows, :].astype(F32)
        return both.reshape(SHARDS, 16, HALF)

    blocks.append(early(EARLY_PAIRS - 1)[:, :ROWS, :])
    for pair in range(len(blocks) // 2):
        rows = jnp.concatenate(blocks[2 * pair : 2 * pair + 2], axis=1)
        send_ref[:, 16 * pair : 16 * pair + 16, :] = rows.astype(BF16)
    for pair in range(EARLY_PAIRS - 1):
        to = OUT_CUT_ROWS + 16 * pair
        send_ref[:, to : to + 16, :] = early(pair).astype(BF16)
    send_ref[:, WROWS : WROWS + 16, :] = outputs[...]
    send_ref[:, WROWS + 16 : WROWS + 40, :] = tail[:, :24, :]


AT_SOURCE, AT_KEEP, AT_COTANGENT, AT_PARAMS = WROWS, WROWS + 16, WROWS + 32, WROWS + 48
IN_ROWS = WROWS + 56
OUT_ROWS = WROWS + 40
OUT_BLOCK, QUERY_BLOCK, KEY_BLOCK, SECOND_CONV, VALUE_BLOCK = 9, 10, 11, 12, 21
IN_CUT, OUT_CUT = 12, 10
IN_CUT_ROWS, OUT_CUT_ROWS = IN_CUT * ROWS, OUT_CUT * ROWS
EARLY_PAIRS, PAIR_ROWS = (WBLOCKS - OUT_CUT) // 2 + 1, 16 * SHARDS
EARLY_ROWS = EARLY_PAIRS * PAIR_ROWS


def local_call(kernel, core, *operands, out):
    in_specs = [pl.BlockSpec(memory_space=pltpu.VMEM) for _ in operands]
    if core is not None:
        in_specs = [pl.BlockSpec(memory_space=pltpu.SMEM)] + in_specs
        operands = (core, *operands)
    shapes = tuple(jax.ShapeDtypeStruct(shape, dtype) for shape, dtype in out)
    return pl.pallas_call(
        kernel,
        out_shape=shapes,
        in_specs=in_specs,
        out_specs=tuple(pl.BlockSpec(memory_space=pltpu.VMEM) for _ in out),
        compiler_params=pltpu.CompilerParams(vmem_limit_bytes=VMEM_LIMIT),
    )(*operands)


VMEM_LIMIT = 24 * 1024 * 1024


def run_block(core, received, swap):
    other_one = swap(received[:, :IN_CUT_ROWS])
    other_two = swap(received[:, IN_CUT_ROWS:WROWS])
    image, table = ((C, POS), F32), ((C, HALF), F32)
    taps, low = ((2, 3, HALF, POS), BF16), ((C, POS), BF16)
    halves = ((2, HALF, POS), BF16)

    taps_one, hat_one, params, stats_one = local_call(
        first_kernel, None, received, out=(taps, image, table, table)
    )
    weights_one, taps_two, hat_two, stats_two = local_call(
        middle_kernel, core, received, other_one, taps_one, params,
        out=(((IN_CUT, C, C), BF16), taps, image, table),
    )
    rows = ((SHARDS, 16, HALF), BF16)
    weights_two, outputs, residual_grad, sums, normed, attended, gradients = local_call(
        attention_kernel, core, received, other_two, taps_two, params, weights_one,
        out=(((WBLOCKS - IN_CUT, C, C), BF16), rows, image, table, halves, halves, ((3, C, POS), BF16)),
    )
    own, swap_early = local_call(
        early_grads_kernel, core, received, taps_one, taps_two, residual_grad, normed, attended,
        gradients,
        out=(((EARLY_ROWS, HALF), BF16), ((EARLY_ROWS + 6 * HALF, HALF), BF16)),
    )
    swapped = swap(swap_early)
    low_one, sums = local_call(
        middle_back_kernel, None, received, weights_two, hat_two, stats_two, params,
        residual_grad, sums, out=(low, table),
    )
    their_low = swap(low_one)
    (tail,) = local_call(
        first_back_kernel, None, weights_one, hat_one, stats_one, params, low_one,
        residual_grad, sums, out=(((SHARDS, 32, HALF), BF16),),
    )
    (send,) = local_call(
        gather_kernel, core, taps_one, low_one, their_low, own, swapped, outputs, tail,
        out=(((SHARDS, OUT_ROWS, HALF), BF16),),
    )
    return send


def collect_kernel(back_ref, swished_ref, sums_ref):
    for pair in range(WROWS // 16):
        rows = slice(16 * pair, 16 * pair + 16)
        total = back_ref[0, rows, :].astype(F32)
        for image in range(1, SHARDS):
            total = total + back_ref[image, rows, :].astype(F32)
        sums_ref[rows, :] = total.astype(BF16)
    small = back_ref[:, WROWS + 32 : WROWS + 40, :].astype(F32)
    table = jnp.zeros((ROWS, HALF), F32)
    temb = jnp.zeros((ROWS, TEMB), F32)
    for image in range(SHARDS):
        values = small[image] + pltpu.roll(small[image], HALF - PART, 1)
        table = table + values
        offsets_grad = values[:, D_CONV_BIAS : D_CONV_BIAS + 1]
        temb = temb + offsets_grad * swished_ref[image : image + 1, :]
    lane = lax.broadcasted_iota(jnp.int32, (ROWS, HALF), 1)
    high = table.astype(BF16).astype(F32)
    low = pltpu.roll(table - high, PART, 1)
    parts = jnp.where(lane < PART, high, jnp.where(lane < 2 * PART, low, 0.0))
    blocks = [parts] + [temb[:, HALF * k : HALF * k + HALF] for k in range(TEMB // HALF)]
    blocks = blocks + [jnp.zeros((ROWS, HALF), F32)]
    for pair in range(len(blocks) // 2):
        rows = slice(WROWS + 16 * pair, WROWS + 16 * pair + 16)
        both = jnp.concatenate(blocks[2 * pair : 2 * pair + 2], axis=0)
        sums_ref[rows, :] = both.astype(BF16)


SUM_ROWS = WROWS + ROWS + TEMB * ROWS // HALF + ROWS


def collect(back, swished):
    return pl.pallas_call(
        collect_kernel,
        out_shape=jax.ShapeDtypeStruct((SUM_ROWS, HALF), BF16),
        in_specs=[pl.BlockSpec(memory_space=pltpu.VMEM)] * 2,
        out_specs=pl.BlockSpec(memory_space=pltpu.VMEM),
        compiler_params=pltpu.CompilerParams(vmem_limit_bytes=8 * 1024 * 1024),
    )(back, swished)


def images_kernel(back_ref, outputs_ref, grad_ref):
    for at, target in ((WROWS, outputs_ref), (WROWS + 16, grad_ref)):
        block = back_ref[:, at : at + 16, :].astype(F32)
        cut = jnp.concatenate([block[:, :ROWS, :], block[:, ROWS:, :]], axis=2)
        target[...] = jnp.swapaxes(cut, 0, 1).astype(BF16)


def images(back):
    shape = jax.ShapeDtypeStruct((ROWS, SHARDS, POS), BF16)
    return pl.pallas_call(
        images_kernel,
        out_shape=(shape, shape),
        in_specs=[pl.BlockSpec(memory_space=pltpu.VMEM)],
        out_specs=(pl.BlockSpec(memory_space=pltpu.VMEM), pl.BlockSpec(memory_space=pltpu.VMEM)),
        compiler_params=pltpu.CompilerParams(vmem_limit_bytes=8 * 1024 * 1024),
    )(back)


def finish_kernel(core_ref, mine_ref, theirs_ref, *refs):
    results, scratch, sems = refs[:10], refs[10:20], refs[20]
    first_core = core_ref[0] == 0
    (gain, bias, conv_w, conv_b, temb_w, temb_b, qkv_w, qv_b, out_w, out_b) = scratch

    def weight_grad(block):
        rows = slice(ROWS * block, ROWS * block + ROWS)
        mine, theirs = mine_ref[rows, :], theirs_ref[rows, :]
        return jnp.concatenate(
            [jnp.where(first_core, mine, theirs), jnp.where(first_core, theirs, mine)], axis=1
        )

    copies = [pltpu.make_async_copy(scratch[k], results[k], sems.at[k]) for k in range(10)]
    for conv in range(2):
        for tap in range(9):
            conv_w[conv, tap, :, :] = weight_grad(SECOND_CONV * conv + tap)
    copies[2].start()
    for k in range(3):
        qkv_w[k, :, :] = weight_grad((QUERY_BLOCK, KEY_BLOCK, VALUE_BLOCK)[k])
    copies[6].start()
    out_w[...] = weight_grad(OUT_BLOCK)
    copies[8].start()
    shared = mine_ref[WROWS:, :] + theirs_ref[WROWS:, :]
    small = shared[:ROWS, :] + pltpu.roll(shared[:ROWS, :], HALF - PART, 1)
    for part in range(TEMB // HALF):
        rows = slice(ROWS + ROWS * part, 2 * ROWS + ROWS * part)
        temb_w[:, HALF * part : HALF * part + HALF] = shared[rows, :]
    copies[4].start()
    padded = jnp.concatenate([small, jnp.zeros((HALF - ROWS, HALF), F32)], axis=0)
    table = padded.T[:PART, :ROWS]
    gain[...] = table[D_GAINS : D_GAINS + 3]
    bias[...] = table[D_BIASES : D_BIASES + 3]
    conv_b[...] = table[D_CONV_BIAS : D_CONV_BIAS + 2]
    temb_b[...] = table[D_CONV_BIAS : D_CONV_BIAS + 1]
    qv_b[...] = table[D_QV_BIAS : D_QV_BIAS + 2]
    out_b[...] = table[D_OUT_BIAS : D_OUT_BIAS + 1]
    for k in (0, 1, 3, 5, 7, 9):
        copies[k].start()
    for copy in copies:
        copy.wait()


def finish(core, mine, theirs):
    shapes = [
        (3, ROWS), (3, ROWS), (2, 9, ROWS, C), (2, ROWS), (ROWS, TEMB), (1, ROWS),
        (3, ROWS, C), (2, ROWS), (ROWS, C), (1, ROWS),
    ]
    return pl.pallas_call(
        finish_kernel,
        out_shape=[jax.ShapeDtypeStruct(shape, F32) for shape in shapes],
        in_specs=[
            pl.BlockSpec(memory_space=pltpu.SMEM),
            pl.BlockSpec(memory_space=pltpu.VMEM),
            pl.BlockSpec(memory_space=pltpu.VMEM),
        ],
        out_specs=[pl.BlockSpec(memory_space=pltpu.HBM) for _ in shapes],
        scratch_shapes=[pltpu.VMEM(shape, F32) for shape in shapes]
        + [pltpu.SemaphoreType.DMA((10,))],
        compiler_params=pltpu.CompilerParams(vmem_limit_bytes=8 * 1024 * 1024),
    )(core, mine, theirs)


def prepare_kernel(core_ref, *refs):
    count = PREPARE_ARRAYS
    arrays, (send_ref, swished_ref) = refs[:count], refs[count : count + 2]
    held, (angles, sems) = refs[count + 2 : 2 * count + 2], refs[2 * count + 2 :]
    (
        steps_ref, gain_ref, bias_ref, conv_bias_ref, qv_ref, out_bias_ref, temb_bias_ref,
        temb_ref, conv_ref, qkv_ref, out_ref, inputs_ref, mask_ref, cotangent_ref,
    ) = held
    copies = [pltpu.make_async_copy(arrays[k], held[k], sems.at[k]) for k in range(count)]
    for copy in copies:
        copy.start()
    first_core = core_ref[0] == 0
    for copy in copies[:8]:
        copy.wait()

    half_dim = TEMB // 2
    index = lax.broadcasted_iota(jnp.int32, (1, half_dim), 1).astype(F32)
    rates = jnp.exp(-math.log(10000.0) * index / (half_dim - 1))
    for image in range(SHARDS):
        angles[image : image + 1, :] = rates * steps_ref[image].astype(F32)
    features = jnp.concatenate([jnp.sin(angles[...]), jnp.cos(angles[...])], axis=1)
    swished = features * sigmoid(features)
    swished_ref[...] = swished
    offsets = None
    rest = swished
    for _ in range(3):
        part = rest.astype(BF16)
        rest = rest - part.astype(F32)
        product = dot_nt(temb_ref[...], part)
        offsets = product if offsets is None else offsets + product

    rows = jnp.concatenate(
        [
            jnp.zeros((1, ROWS), F32), gain_ref[...], bias_ref[...], conv_bias_ref[...],
            qv_ref[...], out_bias_ref[...], temb_bias_ref[...], jnp.zeros((3, ROWS), F32),
        ],
        axis=0,
    )
    square = jnp.concatenate([rows] * (HALF // PART), axis=0)
    square = jnp.concatenate([square, jnp.zeros((HALF, HALF - ROWS), F32)], axis=1)
    columns = square.T[:ROWS, :]
    lane = lax.broadcasted_iota(jnp.int32, (ROWS, HALF), 1)
    offset_lane = (lane & (PART - 1)) == OFFSETS
    offsets = offsets + columns[:, TEMB_BIAS : TEMB_BIAS + 1]
    for image in range(SHARDS):
        values = jnp.where(offset_lane, offsets[:, image : image + 1], columns)
        high = values.astype(BF16).astype(F32)
        mid = (values - high).astype(BF16).astype(F32)
        low = values - high - mid
        parts = jnp.where(
            lane < PART,
            high,
            jnp.where(lane < 2 * PART, mid, jnp.where(lane < 3 * PART, low, 0.0)),
        )
        send_ref[image, WROWS + 48 : WROWS + 56, :] = parts.astype(BF16)

    for copy in copies[8:]:
        copy.wait()

    def half(values):
        values = values.astype(F32)
        return jnp.where(first_core, values[:, :HALF], values[:, HALF:])

    shard = jnp.concatenate(
        [
            half(conv_ref[0].reshape(9 * ROWS, C)),
            half(out_ref[...]),
            half(qkv_ref[0]),
            half(qkv_ref[1]),
            half(conv_ref[1].reshape(9 * ROWS, C)),
            half(qkv_ref[2]),
        ],
        axis=0,
    ).astype(BF16)
    send_ref[:, :WROWS, :] = jnp.broadcast_to(shard[None], (SHARDS, WROWS, HALF))

    def put(at, values):
        turned = jnp.swapaxes(values.astype(F32), 0, 1)
        cut = jnp.concatenate([turned[:, :, :HALF], turned[:, :, HALF:]], axis=1)
        send_ref[:, at : at + 16, :] = cut.astype(BF16)

    put(WROWS, inputs_ref[...])
    put(WROWS + 16, mask_ref[...])
    put(WROWS + 32, cotangent_ref[...])


PREPARE_ARRAYS = 14


def prepare(core, timesteps, *arrays):
    held = [pltpu.SMEM((SHARDS,), jnp.int32)]
    held += [pltpu.VMEM(array.shape, array.dtype) for array in arrays]
    return pl.pallas_call(
        prepare_kernel,
        out_shape=(
            jax.ShapeDtypeStruct((SHARDS, IN_ROWS, HALF), BF16),
            jax.ShapeDtypeStruct((SHARDS, TEMB), F32),
        ),
        in_specs=[pl.BlockSpec(memory_space=pltpu.SMEM)]
        + [pl.BlockSpec(memory_space=pltpu.HBM)] * PREPARE_ARRAYS,
        out_specs=(pl.BlockSpec(memory_space=pltpu.VMEM), pl.BlockSpec(memory_space=pltpu.VMEM)),
        scratch_shapes=held
        + [pltpu.VMEM((SHARDS, TEMB // 2), F32), pltpu.SemaphoreType.DMA((PREPARE_ARRAYS,))],
        compiler_params=pltpu.CompilerParams(vmem_limit_bytes=16 * 1024 * 1024),
    )(core, *[pltpu.with_memory_space_constraint(a, pltpu.HBM) for a in (timesteps, *arrays)])


def on_device(
    inputs,
    timesteps,
    keep_mask,
    norm_gain,
    norm_bias,
    conv_weight,
    conv_bias,
    temb_weight,
    temb_bias,
    qkv_weight,
    qv_bias,
    out_weight,
    out_bias,
    cotangent,
):
    member = lax.axis_index("img")
    core = member % 2
    core_pairs = [(m, m ^ 1) for m in range(4)]
    plane_pairs = [(m, m ^ 2) for m in range(4)]
    sent, swished = prepare(
        core.reshape(1),
        timesteps,
        norm_gain,
        norm_bias,
        conv_bias,
        qv_bias,
        out_bias.reshape(1, ROWS),
        temb_bias.reshape(1, ROWS),
        temb_weight.T,
        conv_weight,
        qkv_weight,
        out_weight,
        inputs,
        keep_mask,
        cotangent,
    )
    received = lax.all_to_all(sent, "ch", split_axis=0, concat_axis=0, tiled=True)
    send = run_block(
        core.reshape(1), received, lambda values: lax.ppermute(values, "img", core_pairs)
    )
    back = lax.all_to_all(send, "ch", split_axis=0, concat_axis=0, tiled=True)

    sums = collect(back, swished)
    plane = lax.ppermute(sums, "img", plane_pairs)
    outputs, input_grad = images(back)
    plane, outputs, input_grad = lax.optimization_barrier((plane, outputs, input_grad))
    sums = sums.astype(F32) + plane.astype(F32)
    theirs = lax.ppermute(sums, "img", core_pairs)
    (gain, bias, conv_w, conv_b, temb_w, temb_b, qkv_w, qv_b, out_w, out_b) = finish(
        core.reshape(1), sums, theirs
    )
    return (
        outputs,
        input_grad,
        gain,
        bias,
        conv_w,
        conv_b,
        temb_w.T,
        temb_b[0],
        qkv_w,
        qv_b,
        out_w,
        out_b[0],
    )


def solution(mesh):
    placed = (
        P("ch", "img", None),
        P("img"),
        P("ch", "img", None),
        P(None, "ch"),
        P(None, "ch"),
        P(None, None, "ch", None),
        P(None, "ch"),
        P(None, "ch"),
        P("ch"),
        P(None, "ch", None),
        P(None, "ch"),
        P("ch", None),
        P("ch"),
        P("ch", "img", None),
    )
    return jax.shard_map(
        on_device,
        mesh=mesh,
        in_specs=placed,
        out_specs=(
            P("ch", "img", None),
            P("ch", "img", None),
            P(None, "ch"),
            P(None, "ch"),
            P(None, None, "ch", None),
            P(None, "ch"),
            P(None, "ch"),
            P("ch"),
            P(None, "ch", None),
            P(None, "ch"),
            P("ch", None),
            P("ch"),
        ),
        check_vma=False,
    )
```

```python
import functools
import math

import jax
import jax.numpy as jnp
from jax import lax
from jax.experimental import pallas as pl
from jax.experimental.pallas import tpu as pltpu
from jax.sharding import PartitionSpec as P

C = 256
TEMB = 512
SIDE = 16
POS = 256
SHARDS = 32
ROWS = C // SHARDS
HALF = 128
WBLOCKS = 22
WROWS = WBLOCKS * ROWS
NORM_EPS = 1e-06
GROUP_SIZE = ROWS * POS
F32 = jnp.float32
BF16 = jnp.bfloat16

OFFSETS, GAINS, BIASES, CONV_BIAS, QV_BIAS, OUT_BIAS, TEMB_BIAS = 0, 1, 4, 7, 9, 11, 12
D_GAINS, D_BIASES, D_CONV_BIAS, D_QV_BIAS, D_OUT_BIAS = 0, 3, 6, 8, 10
PART = 16


def dot_nn(a, b):
    return lax.dot_general(a, b, (((1,), (0,)), ((), ())), preferred_element_type=F32)


def dot_nt(a, b):
    return lax.dot_general(a, b, (((1,), (1,)), ((), ())), preferred_element_type=F32)


def dot_tn(a, b):
    return lax.dot_general(a, b, (((0,), (0,)), ((), ())), preferred_element_type=F32)


def group_sum(values):
    column = jnp.sum(values, axis=1, keepdims=True)
    return group_column(column)


def group_column(column):
    grouped = column.reshape(SHARDS, ROWS, 1)
    total = jnp.sum(grouped, axis=1, keepdims=True)
    return jnp.broadcast_to(total, grouped.shape).reshape(C, 1)


def norm_hat(values):
    average = group_sum(values) * (1.0 / GROUP_SIZE)
    centered = values - average
    spread = group_sum(centered * centered) * (1.0 / GROUP_SIZE)
    inverse = lax.rsqrt(spread + NORM_EPS)
    return centered * inverse, inverse


def norm_back(hat, inverse, grad_out, gain):
    gain_grad = jnp.sum(grad_out * hat, axis=1, keepdims=True)
    bias_grad = jnp.sum(grad_out, axis=1, keepdims=True)
    first_mean = group_column(bias_grad * gain) * (1.0 / GROUP_SIZE)
    second_mean = group_column(gain_grad * gain) * (1.0 / GROUP_SIZE)
    grad_in = inverse * (grad_out * gain - first_mean - hat * second_mean)
    return grad_in, gain_grad, bias_grad


def sigmoid(values):
    return 0.5 + 0.5 * jnp.tanh(0.5 * values)


def rolled(values, steps, axis):
    return pltpu.roll(values, steps % POS, axis)


def column_shifted(values, step, axis):
    shape = (1, POS) if axis == 1 else (POS, POS)
    cell = (lax.broadcasted_iota(jnp.int32, shape, axis) & (SIDE - 1)) + step
    valid = (cell >= 0) & (cell < SIDE)
    return rolled(values, -step, axis) * valid.astype(F32)


def row_shifted(values, step):
    moved = rolled(values, -step * SIDE, 1)
    lane = lax.broadcasted_iota(jnp.int32, (1, HALF), 1)
    if step > 0:
        edge = jnp.where(lane < HALF - SIDE, moved[:, HALF:], 0.0)
        return jnp.concatenate([moved[:, :HALF], edge], axis=1)
    edge = jnp.where(lane >= SIDE, moved[:, :HALF], 0.0)
    return jnp.concatenate([edge, moved[:, HALF:]], axis=1)


def store_matrices(ref, first_row, target):
    for pair in range(target.shape[0] // 2):
        rows = ref[:, first_row + 16 * pair : first_row + 16 * pair + 16, :].astype(F32)
        for part in range(2):
            cut = rows[:, ROWS * part : ROWS * part + ROWS, :]
            target[2 * pair + part, :, :] = cut.reshape(C, HALF).astype(BF16)


def matrix(own, other, block, first_other):
    return jnp.concatenate([own[block], other[block - first_other]], axis=1)


def own_first(ref, core):
    halves = [ref[core], ref[1 - core]]
    return jnp.concatenate([half.reshape(-1, POS) for half in halves], axis=0)


def in_order(values, core):
    top, bottom = values[:HALF], values[HALF:]
    first = core == 0
    return jnp.concatenate(
        [jnp.where(first, top, bottom), jnp.where(first, bottom, top)], axis=0
    )


def load_image(ref, at):
    block = ref[:, at : at + 16, :].astype(F32)
    left = block[:, 0:ROWS, :].reshape(C, HALF)
    right = block[:, ROWS : 2 * ROWS, :].reshape(C, HALF)
    return jnp.concatenate([left, right], axis=1)


def image_rows(values):
    left = values[:, 0:HALF].reshape(SHARDS, ROWS, HALF)
    right = values[:, HALF:C].reshape(SHARDS, ROWS, HALF)
    return jnp.concatenate([left, right], axis=1).astype(BF16)


def store_shifts(target, values):
    for step in (-1, 0, 1):
        moved = (column_shifted(values, step, 1) if step else values).astype(BF16)
        target[0, step + 1, :, :] = moved[:HALF]
        target[1, step + 1, :, :] = moved[HALF:]


def half_convolve(matrices, shifts):
    operand = shifts.reshape(3 * HALF, POS)
    total = None
    for row in (0, -1, 1):
        product = dot_nn(jnp.concatenate(matrices[3 * row + 3 : 3 * row + 6], axis=1), operand)
        total = product if row == 0 else total + row_shifted(product, row)
    return total


def convolve(matrices, shifts, core):
    operand = [shifts[half, step] for step in range(3) for half in (core, 1 - core)]
    operand = jnp.concatenate(operand, axis=0)
    total = None
    for row in (0, -1, 1):
        product = dot_nn(jnp.concatenate(matrices[3 * row + 3 : 3 * row + 6], axis=1), operand)
        total = product if row == 0 else total + row_shifted(product, row)
    return total


def convolve_back(matrices, low, core):
    turned = low.astype(F32).T.astype(BF16)
    edge = jnp.zeros((SIDE, C), BF16)
    stacked = jnp.concatenate(
        [
            jnp.concatenate([turned[SIDE:], edge], axis=0),
            turned,
            jnp.concatenate([edge, turned[:-SIDE]], axis=0),
        ],
        axis=1,
    )
    total = None
    for step in (0, -1, 1):
        product = dot_nn(stacked, jnp.concatenate(matrices[step + 1 :: 3], axis=0))
        total = product if step == 0 else total + column_shifted(product, -step, 0)
    return in_order(total.T, core)


def lane_blocks(product):
    count = product.shape[1] // HALF
    cut = [product[:, HALF * k : HALF * k + HALF] for k in range(count)]
    return [values.reshape(SHARDS, ROWS, HALF) for values in cut]


def conv_weight_grads(lows, shifts):
    operand = jnp.concatenate([part.reshape(3 * HALF, POS) for part in shifts], axis=1)
    wide = [low.astype(F32) for low in lows]
    blocks = []
    for row in (-1, 0, 1):
        moved = [row_shifted(values, -row) if row else values for values in wide]
        blocks += lane_blocks(dot_nt(jnp.concatenate(moved, axis=1).astype(BF16), operand))
    return blocks


def store_blocks(target, blocks):
    for pair in range(len(blocks) // 2):
        rows = jnp.concatenate(blocks[2 * pair : 2 * pair + 2], axis=1)
        target[:, 16 * pair : 16 * pair + 16, :] = rows.astype(BF16)


def columns_of(listed, table):
    lane = lax.broadcasted_iota(jnp.int32, (C, HALF), 1)
    for k, column in listed.items():
        table = jnp.where(lane == k, column, table)
    return table


def column(ref, lane):
    return ref[:, lane : lane + 1]


def row_sum(values):
    return jnp.sum(values, axis=1, keepdims=True)


def slope(values):
    sigma = sigmoid(values)
    return sigma * (1.0 + values * (1.0 - sigma))


def first_kernel(core_ref, recv_ref, taps_ref, hat_ref, params_ref, stats_ref, own_ref, partial_ref):
    columns = recv_ref[:, AT_PARAMS : AT_PARAMS + ROWS, :].astype(F32).reshape(C, HALF)
    columns = (
        columns
        + pltpu.roll(columns, HALF - PART, 1)
        + pltpu.roll(columns, HALF - 2 * PART, 1)
    )
    params_ref[...] = columns
    hat, inverse = norm_hat(load_image(recv_ref, AT_SOURCE))
    hat_ref[...] = hat
    stats_ref[...] = jnp.broadcast_to(inverse, (C, HALF))
    pre = hat * columns[:, GAINS : GAINS + 1] + columns[:, BIASES : BIASES + 1]
    store_shifts(taps_ref, (pre * sigmoid(pre)).astype(BF16).astype(F32))
    store_matrices(recv_ref, 0, own_ref)
    partial_ref[...] = half_convolve([own_ref[tap] for tap in range(9)], taps_ref[core_ref[0]])


def middle_kernel(
    core_ref, recv_ref, swapped, taps_one, params, partial,
    other, taps_ref, hat_ref, stats_ref, halves_ref,
):
    store_matrices(swapped, 0, other)
    rest = half_convolve([other[tap] for tap in range(9)], taps_one[1 - core_ref[0]])
    middle = partial[...] + rest
    middle = middle + (column(params, CONV_BIAS) + column(params, OFFSETS))
    hat, inverse = norm_hat(middle)
    hat_ref[...] = hat
    stats_ref[...] = jnp.broadcast_to(inverse, (C, HALF))
    pre = hat * column(params, GAINS + 1) + column(params, BIASES + 1)
    keep = load_image(recv_ref, AT_KEEP) * (1.0 / 0.9)
    store_shifts(taps_ref, (pre * sigmoid(pre) * keep).astype(BF16).astype(F32))
    away = 1 - core_ref[0]
    halves_ref[0 : 3 * HALF, :] = taps_one[away].reshape(3 * HALF, POS)
    halves_ref[3 * HALF : 6 * HALF, :] = taps_ref[away].reshape(3 * HALF, POS)
    halves_ref[6 * HALF :, :] = load_image(recv_ref, AT_COTANGENT).astype(BF16)


def attention_kernel(
    core_ref, recv_ref, swapped, taps_two, params, own, other_one,
    other, outputs_ref, grad_ref, sums_ref, normed_ref, halves_ref, grads_ref, swap_ref,
):
    core = core_ref[0]
    store_matrices(swapped, 0, other)
    out_matrix = matrix(own, other_one, OUT_BLOCK, 0)
    qkv = [
        matrix(own, other_one, QUERY_BLOCK, 0),
        matrix(own, other_one, KEY_BLOCK, 0),
        matrix(own, other, VALUE_BLOCK, IN_CUT),
    ]
    cotangent = load_image(recv_ref, AT_COTANGENT)
    cot_low = cotangent.astype(BF16)
    attended_grad = in_order(dot_tn(out_matrix, cot_low), core).astype(BF16)
    source = load_image(recv_ref, AT_SOURCE)
    matrices = [matrix(own, other, SECOND_CONV + tap, IN_CUT) for tap in range(9)]
    residual = source + convolve(matrices, taps_two, core) + column(params, CONV_BIAS + 1)
    hat, inverse = norm_hat(residual)
    normed = (hat * column(params, GAINS + 2) + column(params, BIASES + 2)).astype(BF16)
    scale = C ** (-0.5)
    normed_ref[0] = normed[:HALF]
    normed_ref[1] = normed[HALF:]
    operand = own_first(normed_ref, core)
    queries = (dot_nn(qkv[0], operand) + column(params, QV_BIAS)).astype(BF16)
    keys = dot_nn(qkv[1], operand).astype(BF16)
    vals = (dot_nn(qkv[2], operand) + column(params, QV_BIAS + 1)).astype(BF16)
    scores = dot_tn(queries, keys) * scale
    dprobs = dot_tn(attended_grad, vals)
    exps = jnp.exp(scores - jnp.max(scores, axis=1, keepdims=True))
    probs = exps / row_sum(exps)
    probs_low = probs.astype(BF16)
    dscores = (probs * (dprobs - row_sum(probs * dprobs))).astype(BF16)
    query_grad = (dot_nt(keys, dscores) * scale).astype(BF16)
    key_grad = (dot_nn(queries, dscores) * scale).astype(BF16)
    value_grad = dot_nn(attended_grad, probs_low).astype(BF16)
    normed_grad = dot_tn(
        jnp.concatenate(qkv, axis=0),
        jnp.concatenate([query_grad, key_grad, value_grad], axis=0),
    )
    normed_grad = in_order(normed_grad, core)
    for k, gradient in enumerate((query_grad, key_grad, value_grad)):
        grads_ref[k, :, :] = gradient
    attended = dot_nt(vals, probs_low).astype(BF16)
    halves_ref[0] = attended[:HALF]
    halves_ref[1] = attended[HALF:]
    product = dot_nn(out_matrix, own_first(halves_ref, core))
    outputs = residual + product + column(params, OUT_BIAS)
    outputs_ref[...] = image_rows(outputs)
    branch, gain_grad, bias_grad = norm_back(hat, inverse, normed_grad, column(params, GAINS + 2))
    residual_grad = cotangent + branch
    grad_ref[...] = residual_grad
    swap_ref[0:HALF, :] = normed_ref[1 - core]
    swap_ref[HALF:C, :] = halves_ref[1 - core]
    swap_ref[C : 2 * C, :] = residual_grad.astype(BF16)
    for k, gradient in enumerate((query_grad, key_grad, value_grad)):
        swap_ref[C * k + 2 * C : C * k + 3 * C, :] = gradient
    listed = {
        D_GAINS + 2: gain_grad,
        D_BIASES + 2: bias_grad,
        D_CONV_BIAS + 1: row_sum(residual_grad),
        D_QV_BIAS: row_sum(query_grad.astype(F32)),
        D_QV_BIAS + 1: row_sum(value_grad.astype(F32)),
        D_OUT_BIAS: row_sum(cotangent),
    }
    sums_ref[...] = columns_of(listed, jnp.zeros((C, HALF), F32))


def middle_back_kernel(
    core_ref, recv_ref, own, other, hat_ref, stats, params, grad_ref, sums, low_ref, sums_ref
):
    hat = hat_ref[...]
    gain = column(params, GAINS + 1)
    pre = hat * gain + column(params, BIASES + 1)
    keep = load_image(recv_ref, AT_KEEP) * (1.0 / 0.9)
    factor = keep * slope(pre)
    matrices = [matrix(own, other, SECOND_CONV + tap, IN_CUT) for tap in range(9)]
    second_grad = convolve_back(matrices, grad_ref[...].astype(BF16), core_ref[0])
    pre_grad = second_grad * factor
    middle_grad, gain_grad, bias_grad = norm_back(hat, column(stats, 0), pre_grad, gain)
    low_ref[...] = middle_grad.astype(BF16)
    listed = {D_GAINS + 1: gain_grad, D_BIASES + 1: bias_grad, D_CONV_BIAS: row_sum(middle_grad)}
    sums_ref[...] = columns_of(listed, sums[...])


def first_back_kernel(
    core_ref, own, other, hat_ref, stats, params, low_ref, grad_ref, sums, tail_ref
):
    hat = hat_ref[...]
    gain = column(params, GAINS)
    pre = hat * gain + column(params, BIASES)
    factor = slope(pre)
    matrices = [matrix(own, other, tap, 0) for tap in range(9)]
    first_grad = convolve_back(matrices, low_ref[...], core_ref[0])
    branch, gain_grad, bias_grad = norm_back(hat, column(stats, 0), first_grad * factor, gain)
    tail_ref[:, :16, :] = image_rows(grad_ref[...] + branch)

    table = columns_of({D_GAINS: gain_grad, D_BIASES: bias_grad}, sums[...])
    high = table.astype(BF16).astype(F32)
    low = pltpu.roll(table - high, PART, 1)
    lane = lax.broadcasted_iota(jnp.int32, (C, HALF), 1)
    table = jnp.where(lane < PART, high, low).reshape(SHARDS, ROWS, HALF)
    tail_ref[:, 16:, :] = jnp.concatenate([table, jnp.zeros_like(table)], axis=1).astype(BF16)


def second_grads_kernel(
    core_ref, recv_ref, taps_two, normed, attended, gradients, grad_ref, their_shifts, theirs,
    late_ref,
):
    core = core_ref[0]
    low = grad_ref[...].astype(BF16)
    second = conv_weight_grads(
        [low, theirs[C : 2 * C, :]], [taps_two[core], their_shifts[3 * HALF : 6 * HALF, :]]
    )
    operand = jnp.concatenate([normed[core], theirs[0:HALF, :]], axis=1)
    grads = jnp.concatenate([gradients[...].reshape(3 * C, POS), theirs[2 * C :, :]], axis=1)
    qkv = dot_nt(grads, operand)
    query, key, value = [lane_blocks(qkv[C * k : C * k + C])[0] for k in range(3)]
    operand = jnp.concatenate([attended[core], theirs[HALF:C, :]], axis=1)
    cotangent = load_image(recv_ref, AT_COTANGENT).astype(BF16)
    cotangents = jnp.concatenate([cotangent, their_shifts[6 * HALF :, :]], axis=1)
    out = lane_blocks(dot_nt(cotangents, operand))[0]
    store_blocks(late_ref, [query, key, *second, value, out, jnp.zeros_like(out)])


def gather_kernel(
    core_ref, taps_one, low_ref, their_shifts, their_low, late, outputs, tail, send_ref
):
    first = conv_weight_grads(
        [low_ref[...], their_low[...]], [taps_one[core_ref[0]], their_shifts[0 : 3 * HALF, :]]
    )
    cut = WROWS - IN_CUT_ROWS + 16
    out = late[:, cut : cut + 16, :].astype(F32)[:, :ROWS, :]
    store_blocks(send_ref, first + [out])
    send_ref[:, IN_CUT_ROWS - 16 : WROWS, :] = late[:, :cut, :]
    send_ref[:, WROWS : WROWS + 16, :] = outputs[...]
    send_ref[:, WROWS + 16 : WROWS + 40, :] = tail[:, :24, :]


AT_SOURCE, AT_KEEP, AT_COTANGENT, AT_PARAMS = WROWS, WROWS + 16, WROWS + 32, WROWS + 48
IN_ROWS = WROWS + 56
OUT_ROWS = WROWS + 40
OUT_BLOCK, QUERY_BLOCK, KEY_BLOCK, SECOND_CONV, VALUE_BLOCK = 9, 10, 11, 12, 21
IN_CUT = 12
IN_CUT_ROWS = IN_CUT * ROWS


def local_call(kernel, core, *operands, out):
    in_specs = [pl.BlockSpec(memory_space=pltpu.VMEM) for _ in operands]
    if core is not None:
        in_specs = [pl.BlockSpec(memory_space=pltpu.SMEM)] + in_specs
        operands = (core, *operands)
    shapes = tuple(jax.ShapeDtypeStruct(shape, dtype) for shape, dtype in out)
    return pl.pallas_call(
        kernel,
        out_shape=shapes,
        in_specs=in_specs,
        out_specs=tuple(pl.BlockSpec(memory_space=pltpu.VMEM) for _ in out),
        compiler_params=pltpu.CompilerParams(vmem_limit_bytes=VMEM_LIMIT),
    )(*operands)


VMEM_LIMIT = 24 * 1024 * 1024


def run_block(core, received, swap):
    swapped_one = swap(received[:, :IN_CUT_ROWS])
    swapped_two = swap(received[:, IN_CUT_ROWS:WROWS])
    image, table = ((C, POS), F32), ((C, HALF), F32)
    taps, low = ((2, 3, HALF, POS), BF16), ((C, POS), BF16)
    halves = ((2, HALF, POS), BF16)

    def matrices(count):
        return ((count, C, HALF), BF16)


    taps_one, hat_one, params, stats_one, own_weights, partial = local_call(
        first_kernel, core, received, out=(taps, image, table, table, matrices(WBLOCKS), image)
    )
    other_weights, taps_two, hat_two, stats_two, halves_out = local_call(
        middle_kernel, core, received, swapped_one, taps_one, params, partial,
        out=(matrices(IN_CUT), taps, image, table, ((6 * HALF + C, POS), BF16)),
    )
    rows = ((SHARDS, 16, HALF), BF16)
    their_shifts = swap(halves_out)
    other_two, outputs, residual_grad, sums, normed, attended, gradients, swapping = local_call(
        attention_kernel, core, received, swapped_two, taps_two, params, own_weights, other_weights,
        out=(
            matrices(WBLOCKS - IN_CUT), rows, image, table, halves, halves, ((3, C, POS), BF16),
            ((5 * C, POS), BF16),
        ),
    )
    theirs = swap(swapping)
    residual_grad, their_shifts = lax.optimization_barrier((residual_grad, their_shifts))
    low_one, sums = local_call(
        middle_back_kernel, core, received, own_weights, other_two, hat_two, stats_two, params,
        residual_grad, sums, out=(low, table),
    )
    their_low = swap(low_one)
    (tail,) = local_call(
        first_back_kernel, core, own_weights, other_weights, hat_one, stats_one, params, low_one,
        residual_grad, sums, out=(((SHARDS, 32, HALF), BF16),),
    )
    (late,) = local_call(
        second_grads_kernel, core, received, taps_two, normed, attended, gradients, residual_grad,
        their_shifts, theirs, out=(((SHARDS, WROWS - IN_CUT_ROWS + 32, HALF), BF16),),
    )
    (send,) = local_call(
        gather_kernel, core, taps_one, low_one, their_shifts, their_low, late, outputs, tail,
        out=(((SHARDS, OUT_ROWS, HALF), BF16),),
    )
    return send


def collect_kernel(back_ref, swished_ref, sums_ref):
    for pair in range(WROWS // 16):
        rows = slice(16 * pair, 16 * pair + 16)
        total = back_ref[0, rows, :].astype(F32)
        for image in range(1, SHARDS):
            total = total + back_ref[image, rows, :].astype(F32)
        sums_ref[rows, :] = total.astype(BF16)
    small = back_ref[:, WROWS + 32 : WROWS + 40, :].astype(F32)
    table = jnp.zeros((ROWS, HALF), F32)
    temb = jnp.zeros((ROWS, TEMB), F32)
    for image in range(SHARDS):
        values = small[image] + pltpu.roll(small[image], HALF - PART, 1)
        table = table + values
        offsets_grad = values[:, D_CONV_BIAS : D_CONV_BIAS + 1]
        temb = temb + offsets_grad * swished_ref[image : image + 1, :]
    lane = lax.broadcasted_iota(jnp.int32, (ROWS, HALF), 1)
    high = table.astype(BF16).astype(F32)
    low = pltpu.roll(table - high, PART, 1)
    parts = jnp.where(lane < PART, high, jnp.where(lane < 2 * PART, low, 0.0))
    blocks = [parts] + [temb[:, HALF * k : HALF * k + HALF] for k in range(TEMB // HALF)]
    blocks = blocks + [jnp.zeros((ROWS, HALF), F32)]
    for pair in range(len(blocks) // 2):
        rows = slice(WROWS + 16 * pair, WROWS + 16 * pair + 16)
        both = jnp.concatenate(blocks[2 * pair : 2 * pair + 2], axis=0)
        sums_ref[rows, :] = both.astype(BF16)


SUM_ROWS = WROWS + ROWS + TEMB * ROWS // HALF + ROWS


def collect(back, swished):
    return pl.pallas_call(
        collect_kernel,
        out_shape=jax.ShapeDtypeStruct((SUM_ROWS, HALF), BF16),
        in_specs=[pl.BlockSpec(memory_space=pltpu.VMEM)] * 2,
        out_specs=pl.BlockSpec(memory_space=pltpu.VMEM),
        compiler_params=pltpu.CompilerParams(vmem_limit_bytes=8 * 1024 * 1024),
    )(back, swished)


def images_kernel(back_ref, outputs_ref, grad_ref):
    for at, target in ((WROWS, outputs_ref), (WROWS + 16, grad_ref)):
        block = back_ref[:, at : at + 16, :].astype(F32)
        cut = jnp.concatenate([block[:, :ROWS, :], block[:, ROWS:, :]], axis=2)
        target[...] = jnp.swapaxes(cut, 0, 1).astype(BF16)


def images(back):
    shape = jax.ShapeDtypeStruct((ROWS, SHARDS, POS), BF16)
    return pl.pallas_call(
        images_kernel,
        out_shape=(shape, shape),
        in_specs=[pl.BlockSpec(memory_space=pltpu.VMEM)],
        out_specs=(pl.BlockSpec(memory_space=pltpu.VMEM), pl.BlockSpec(memory_space=pltpu.VMEM)),
        compiler_params=pltpu.CompilerParams(vmem_limit_bytes=8 * 1024 * 1024),
    )(back)


def finish_kernel(core_ref, mine_ref, theirs_ref, *refs):
    results, scratch, sems = refs[:10], refs[10:20], refs[20]
    first_core = core_ref[0] == 0
    (gain, bias, conv_w, conv_b, temb_w, temb_b, qkv_w, qv_b, out_w, out_b) = scratch

    def weight_grad(block):
        rows = slice(ROWS * block, ROWS * block + ROWS)
        mine, theirs = mine_ref[rows, :], theirs_ref[rows, :]
        return jnp.concatenate(
            [jnp.where(first_core, mine, theirs), jnp.where(first_core, theirs, mine)], axis=1
        )

    copies = [pltpu.make_async_copy(scratch[k], results[k], sems.at[k]) for k in range(10)]
    for conv in range(2):
        for tap in range(9):
            conv_w[conv, tap, :, :] = weight_grad(SECOND_CONV * conv + tap)
    copies[2].start()
    for k in range(3):
        qkv_w[k, :, :] = weight_grad((QUERY_BLOCK, KEY_BLOCK, VALUE_BLOCK)[k])
    copies[6].start()
    out_w[...] = weight_grad(OUT_BLOCK)
    copies[8].start()
    shared = mine_ref[WROWS:, :] + theirs_ref[WROWS:, :]
    small = shared[:ROWS, :] + pltpu.roll(shared[:ROWS, :], HALF - PART, 1)
    for part in range(TEMB // HALF):
        rows = slice(ROWS + ROWS * part, 2 * ROWS + ROWS * part)
        temb_w[:, HALF * part : HALF * part + HALF] = shared[rows, :]
    copies[4].start()
    padded = jnp.concatenate([small, jnp.zeros((HALF - ROWS, HALF), F32)], axis=0)
    table = padded.T[:PART, :ROWS]
    gain[...] = table[D_GAINS : D_GAINS + 3]
    bias[...] = table[D_BIASES : D_BIASES + 3]
    conv_b[...] = table[D_CONV_BIAS : D_CONV_BIAS + 2]
    temb_b[...] = table[D_CONV_BIAS : D_CONV_BIAS + 1]
    qv_b[...] = table[D_QV_BIAS : D_QV_BIAS + 2]
    out_b[...] = table[D_OUT_BIAS : D_OUT_BIAS + 1]
    for k in (0, 1, 3, 5, 7, 9):
        copies[k].start()
    for copy in copies:
        copy.wait()


def finish(core, mine, theirs):
    shapes = [
        (3, ROWS), (3, ROWS), (2, 9, ROWS, C), (2, ROWS), (ROWS, TEMB), (1, ROWS),
        (3, ROWS, C), (2, ROWS), (ROWS, C), (1, ROWS),
    ]
    return pl.pallas_call(
        finish_kernel,
        out_shape=[jax.ShapeDtypeStruct(shape, F32) for shape in shapes],
        in_specs=[
            pl.BlockSpec(memory_space=pltpu.SMEM),
            pl.BlockSpec(memory_space=pltpu.VMEM),
            pl.BlockSpec(memory_space=pltpu.VMEM),
        ],
        out_specs=[pl.BlockSpec(memory_space=pltpu.HBM) for _ in shapes],
        scratch_shapes=[pltpu.VMEM(shape, F32) for shape in shapes]
        + [pltpu.SemaphoreType.DMA((10,))],
        compiler_params=pltpu.CompilerParams(vmem_limit_bytes=8 * 1024 * 1024),
    )(core, mine, theirs)


def prepare_kernel(core_ref, *refs):
    count = PREPARE_ARRAYS
    arrays, (send_ref, swished_ref) = refs[:count], refs[count : count + 2]
    held, (angles, sems) = refs[count + 2 : 2 * count + 2], refs[2 * count + 2 :]
    (
        steps_ref, gain_ref, bias_ref, conv_bias_ref, qv_ref, out_bias_ref, temb_bias_ref,
        temb_ref, conv_ref, qkv_ref, out_ref, inputs_ref, mask_ref, cotangent_ref,
    ) = held
    copies = [pltpu.make_async_copy(arrays[k], held[k], sems.at[k]) for k in range(count)]
    for copy in copies:
        copy.start()
    first_core = core_ref[0] == 0
    for copy in copies[:8]:
        copy.wait()

    half_dim = TEMB // 2
    index = lax.broadcasted_iota(jnp.int32, (1, half_dim), 1).astype(F32)
    rates = jnp.exp(-math.log(10000.0) * index / (half_dim - 1))
    for image in range(SHARDS):
        angles[image : image + 1, :] = rates * steps_ref[image].astype(F32)
    features = jnp.concatenate([jnp.sin(angles[...]), jnp.cos(angles[...])], axis=1)
    swished = features * sigmoid(features)
    swished_ref[...] = swished
    offsets = None
    rest = swished
    for _ in range(3):
        part = rest.astype(BF16)
        rest = rest - part.astype(F32)
        product = dot_nt(temb_ref[...], part)
        offsets = product if offsets is None else offsets + product

    rows = jnp.concatenate(
        [
            jnp.zeros((1, ROWS), F32), gain_ref[...], bias_ref[...], conv_bias_ref[...],
            qv_ref[...], out_bias_ref[...], temb_bias_ref[...], jnp.zeros((3, ROWS), F32),
        ],
        axis=0,
    )
    square = jnp.concatenate([rows] * (HALF // PART), axis=0)
    square = jnp.concatenate([square, jnp.zeros((HALF, HALF - ROWS), F32)], axis=1)
    columns = square.T[:ROWS, :]
    lane = lax.broadcasted_iota(jnp.int32, (ROWS, HALF), 1)
    offset_lane = (lane & (PART - 1)) == OFFSETS
    offsets = offsets + columns[:, TEMB_BIAS : TEMB_BIAS + 1]
    for image in range(SHARDS):
        values = jnp.where(offset_lane, offsets[:, image : image + 1], columns)
        high = values.astype(BF16).astype(F32)
        mid = (values - high).astype(BF16).astype(F32)
        low = values - high - mid
        parts = jnp.where(
            lane < PART,
            high,
            jnp.where(lane < 2 * PART, mid, jnp.where(lane < 3 * PART, low, 0.0)),
        )
        send_ref[image, WROWS + 48 : WROWS + 56, :] = parts.astype(BF16)

    for copy in copies[8:]:
        copy.wait()

    def half(values):
        values = values.astype(F32)
        return jnp.where(first_core, values[:, :HALF], values[:, HALF:])

    shard = jnp.concatenate(
        [
            half(conv_ref[0].reshape(9 * ROWS, C)),
            half(out_ref[...]),
            half(qkv_ref[0]),
            half(qkv_ref[1]),
            half(conv_ref[1].reshape(9 * ROWS, C)),
            half(qkv_ref[2]),
        ],
        axis=0,
    ).astype(BF16)
    send_ref[:, :WROWS, :] = jnp.broadcast_to(shard[None], (SHARDS, WROWS, HALF))

    def put(at, values):
        turned = jnp.swapaxes(values.astype(F32), 0, 1)
        cut = jnp.concatenate([turned[:, :, :HALF], turned[:, :, HALF:]], axis=1)
        send_ref[:, at : at + 16, :] = cut.astype(BF16)

    put(WROWS, inputs_ref[...])
    put(WROWS + 16, mask_ref[...])
    put(WROWS + 32, cotangent_ref[...])


PREPARE_ARRAYS = 14


def prepare(core, timesteps, *arrays):
    held = [pltpu.SMEM((SHARDS,), jnp.int32)]
    held += [pltpu.VMEM(array.shape, array.dtype) for array in arrays]
    return pl.pallas_call(
        prepare_kernel,
        out_shape=(
            jax.ShapeDtypeStruct((SHARDS, IN_ROWS, HALF), BF16),
            jax.ShapeDtypeStruct((SHARDS, TEMB), F32),
        ),
        in_specs=[pl.BlockSpec(memory_space=pltpu.SMEM)]
        + [pl.BlockSpec(memory_space=pltpu.HBM)] * PREPARE_ARRAYS,
        out_specs=(pl.BlockSpec(memory_space=pltpu.VMEM), pl.BlockSpec(memory_space=pltpu.VMEM)),
        scratch_shapes=held
        + [pltpu.VMEM((SHARDS, TEMB // 2), F32), pltpu.SemaphoreType.DMA((PREPARE_ARRAYS,))],
        compiler_params=pltpu.CompilerParams(vmem_limit_bytes=16 * 1024 * 1024),
    )(core, *[pltpu.with_memory_space_constraint(a, pltpu.HBM) for a in (timesteps, *arrays)])


def on_device(
    inputs,
    timesteps,
    keep_mask,
    norm_gain,
    norm_bias,
    conv_weight,
    conv_bias,
    temb_weight,
    temb_bias,
    qkv_weight,
    qv_bias,
    out_weight,
    out_bias,
    cotangent,
):
    member = lax.axis_index("img")
    core = member % 2
    core_pairs = [(m, m ^ 1) for m in range(4)]
    plane_pairs = [(m, m ^ 2) for m in range(4)]
    sent, swished = prepare(
        core.reshape(1),
        timesteps,
        norm_gain,
        norm_bias,
        conv_bias,
        qv_bias,
        out_bias.reshape(1, ROWS),
        temb_bias.reshape(1, ROWS),
        temb_weight.T,
        conv_weight,
        qkv_weight,
        out_weight,
        inputs,
        keep_mask,
        cotangent,
    )
    received = lax.all_to_all(sent, "ch", split_axis=0, concat_axis=0, tiled=True)
    send = run_block(
        core.reshape(1), received, lambda values: lax.ppermute(values, "img", core_pairs)
    )
    back = lax.all_to_all(send, "ch", split_axis=0, concat_axis=0, tiled=True)

    sums = collect(back, swished)
    plane = lax.ppermute(sums, "img", plane_pairs)
    outputs, input_grad = images(back)
    plane, outputs, input_grad = lax.optimization_barrier((plane, outputs, input_grad))
    sums = sums.astype(F32) + plane.astype(F32)
    theirs = lax.ppermute(sums, "img", core_pairs)
    (gain, bias, conv_w, conv_b, temb_w, temb_b, qkv_w, qv_b, out_w, out_b) = finish(
        core.reshape(1), sums, theirs
    )
    return (
        outputs,
        input_grad,
        gain,
        bias,
        conv_w,
        conv_b,
        temb_w.T,
        temb_b[0],
        qkv_w,
        qv_b,
        out_w,
        out_b[0],
    )


def solution(mesh):
    placed = (
        P("ch", "img", None),
        P("img"),
        P("ch", "img", None),
        P(None, "ch"),
        P(None, "ch"),
        P(None, None, "ch", None),
        P(None, "ch"),
        P(None, "ch"),
        P("ch"),
        P(None, "ch", None),
        P(None, "ch"),
        P("ch", None),
        P("ch"),
        P("ch", "img", None),
    )
    return jax.shard_map(
        on_device,
        mesh=mesh,
        in_specs=placed,
        out_specs=(
            P("ch", "img", None),
            P("ch", "img", None),
            P(None, "ch"),
            P(None, "ch"),
            P(None, None, "ch", None),
            P(None, "ch"),
            P(None, "ch"),
            P("ch"),
            P(None, "ch", None),
            P(None, "ch"),
            P("ch", None),
            P("ch"),
        ),
        check_vma=False,
    )
```

```python
import functools
import math

import jax
import jax.numpy as jnp
from jax import lax
from jax.experimental import pallas as pl
from jax.experimental.pallas import tpu as pltpu
from jax.sharding import PartitionSpec as P

C = 256
TEMB = 512
SIDE = 16
POS = 256
SHARDS = 32
ROWS = C // SHARDS
HALF = 128
WBLOCKS = 22
WROWS = WBLOCKS * ROWS
NORM_EPS = 1e-06
GROUP_SIZE = ROWS * POS
F32 = jnp.float32
BF16 = jnp.bfloat16

OFFSETS, GAINS, BIASES, CONV_BIAS, QV_BIAS, OUT_BIAS, TEMB_BIAS = 0, 1, 4, 7, 9, 11, 12
D_GAINS, D_BIASES, D_CONV_BIAS, D_QV_BIAS, D_OUT_BIAS = 0, 3, 6, 8, 10
PART = 16


def dot_nn(a, b):
    return lax.dot_general(a, b, (((1,), (0,)), ((), ())), preferred_element_type=F32)


def dot_nt(a, b):
    return lax.dot_general(a, b, (((1,), (1,)), ((), ())), preferred_element_type=F32)


def dot_tn(a, b):
    return lax.dot_general(a, b, (((0,), (0,)), ((), ())), preferred_element_type=F32)


def group_sum(values):
    column = jnp.sum(values, axis=1, keepdims=True)
    return group_column(column)


def group_column(column):
    grouped = column.reshape(SHARDS, ROWS, 1)
    total = jnp.sum(grouped, axis=1, keepdims=True)
    return jnp.broadcast_to(total, grouped.shape).reshape(C, 1)


def norm_hat(values):
    average = group_sum(values) * (1.0 / GROUP_SIZE)
    centered = values - average
    spread = group_sum(centered * centered) * (1.0 / GROUP_SIZE)
    inverse = lax.rsqrt(spread + NORM_EPS)
    return centered * inverse, inverse


def norm_back(hat, inverse, grad_out, gain):
    gain_grad = jnp.sum(grad_out * hat, axis=1, keepdims=True)
    bias_grad = jnp.sum(grad_out, axis=1, keepdims=True)
    first_mean = group_column(bias_grad * gain) * (1.0 / GROUP_SIZE)
    second_mean = group_column(gain_grad * gain) * (1.0 / GROUP_SIZE)
    grad_in = inverse * (grad_out * gain - first_mean - hat * second_mean)
    return grad_in, gain_grad, bias_grad


def sigmoid(values):
    return 0.5 + 0.5 * jnp.tanh(0.5 * values)


def rolled(values, steps, axis):
    return pltpu.roll(values, steps % POS, axis)


def column_shifted(values, step, axis):
    shape = (1, POS) if axis == 1 else (POS, POS)
    cell = (lax.broadcasted_iota(jnp.int32, shape, axis) & (SIDE - 1)) + step
    valid = (cell >= 0) & (cell < SIDE)
    return rolled(values, -step, axis) * valid.astype(F32)


def row_shifted(values, step):
    moved = rolled(values, -step * SIDE, 1)
    lane = lax.broadcasted_iota(jnp.int32, (1, HALF), 1)
    if step > 0:
        edge = jnp.where(lane < HALF - SIDE, moved[:, HALF:], 0.0)
        return jnp.concatenate([moved[:, :HALF], edge], axis=1)
    edge = jnp.where(lane >= SIDE, moved[:, :HALF], 0.0)
    return jnp.concatenate([edge, moved[:, HALF:]], axis=1)


def store_matrices(ref, first_row, target):
    for pair in range(target.shape[0] // 2):
        rows = ref[:, first_row + 16 * pair : first_row + 16 * pair + 16, :].astype(F32)
        for part in range(2):
            cut = rows[:, ROWS * part : ROWS * part + ROWS, :]
            target[2 * pair + part, :, :] = cut.reshape(C, HALF).astype(BF16)


def matrix(own, other, block, first_other):
    return jnp.concatenate([own[block], other[block - first_other]], axis=1)


def own_first(ref, core):
    halves = [ref[core], ref[1 - core]]
    return jnp.concatenate([half.reshape(-1, POS) for half in halves], axis=0)


def in_order(values, core):
    top, bottom = values[:HALF], values[HALF:]
    first = core == 0
    return jnp.concatenate(
        [jnp.where(first, top, bottom), jnp.where(first, bottom, top)], axis=0
    )


def load_image(ref, at):
    block = ref[:, at : at + 16, :].astype(F32)
    left = block[:, 0:ROWS, :].reshape(C, HALF)
    right = block[:, ROWS : 2 * ROWS, :].reshape(C, HALF)
    return jnp.concatenate([left, right], axis=1)


def image_rows(values):
    left = values[:, 0:HALF].reshape(SHARDS, ROWS, HALF)
    right = values[:, HALF:C].reshape(SHARDS, ROWS, HALF)
    return jnp.concatenate([left, right], axis=1).astype(BF16)


def store_shifts(target, values):
    for step in (-1, 0, 1):
        moved = (column_shifted(values, step, 1) if step else values).astype(BF16)
        target[0, step + 1, :, :] = moved[:HALF]
        target[1, step + 1, :, :] = moved[HALF:]


def half_convolve(matrices, shifts):
    operand = shifts.reshape(3 * HALF, POS)
    total = None
    for row in (0, -1, 1):
        product = dot_nn(jnp.concatenate(matrices[3 * row + 3 : 3 * row + 6], axis=1), operand)
        total = product if row == 0 else total + row_shifted(product, row)
    return total


def convolve(matrices, shifts, core):
    operand = [shifts[half, step] for step in range(3) for half in (core, 1 - core)]
    operand = jnp.concatenate(operand, axis=0)
    total = None
    for row in (0, -1, 1):
        product = dot_nn(jnp.concatenate(matrices[3 * row + 3 : 3 * row + 6], axis=1), operand)
        total = product if row == 0 else total + row_shifted(product, row)
    return total


def convolve_back(matrices, low, core):
    turned = low.astype(F32).T.astype(BF16)
    edge = jnp.zeros((SIDE, C), BF16)
    stacked = jnp.concatenate(
        [
            jnp.concatenate([turned[SIDE:], edge], axis=0),
            turned,
            jnp.concatenate([edge, turned[:-SIDE]], axis=0),
        ],
        axis=1,
    )
    total = None
    for step in (0, -1, 1):
        product = dot_nn(stacked, jnp.concatenate(matrices[step + 1 :: 3], axis=0))
        total = product if step == 0 else total + column_shifted(product, -step, 0)
    return in_order(total.T, core)


def lane_blocks(product):
    count = product.shape[1] // HALF
    cut = [product[:, HALF * k : HALF * k + HALF] for k in range(count)]
    return [values.reshape(SHARDS, ROWS, HALF) for values in cut]


def conv_weight_grads(lows, shifts):
    wide = [part.reshape(3 * HALF, POS) for part in shifts]
    rows = []
    for row in (-1, 0, 1):
        moved = [row_shifted(part.astype(F32), row).astype(BF16) if row else part for part in wide]
        rows.append(jnp.concatenate(moved, axis=1))
    return lane_blocks(dot_nt(jnp.concatenate(lows, axis=1), jnp.concatenate(rows, axis=0)))


def store_blocks(target, blocks):
    for pair in range(len(blocks) // 2):
        rows = jnp.concatenate(blocks[2 * pair : 2 * pair + 2], axis=1)
        target[:, 16 * pair : 16 * pair + 16, :] = rows.astype(BF16)


def columns_of(listed, table):
    lane = lax.broadcasted_iota(jnp.int32, (C, HALF), 1)
    for k, column in listed.items():
        table = jnp.where(lane == k, column, table)
    return table


def column(ref, lane):
    return ref[:, lane : lane + 1]


def by_rows(dot, left, right):
    return jnp.concatenate([dot(left[:HALF], right), dot(left[HALF:], right)], axis=0)


def row_sum(values):
    return jnp.sum(values, axis=1, keepdims=True)


def slope(values):
    sigma = sigmoid(values)
    return sigma * (1.0 + values * (1.0 - sigma))


def first_kernel(core_ref, recv_ref, taps_ref, hat_ref, params_ref, stats_ref, own_ref, partial_ref):
    columns = recv_ref[:, AT_PARAMS : AT_PARAMS + ROWS, :].astype(F32).reshape(C, HALF)
    columns = (
        columns
        + pltpu.roll(columns, HALF - PART, 1)
        + pltpu.roll(columns, HALF - 2 * PART, 1)
    )
    params_ref[...] = columns
    hat, inverse = norm_hat(load_image(recv_ref, AT_SOURCE))
    hat_ref[...] = hat
    stats_ref[...] = jnp.broadcast_to(inverse, (C, HALF))
    pre = hat * columns[:, GAINS : GAINS + 1] + columns[:, BIASES : BIASES + 1]
    store_shifts(taps_ref, (pre * sigmoid(pre)).astype(BF16).astype(F32))
    store_matrices(recv_ref, 0, own_ref)
    partial_ref[...] = half_convolve([own_ref[tap] for tap in range(9)], taps_ref[core_ref[0]])


def middle_kernel(
    core_ref, recv_ref, swapped, taps_one, params, partial,
    other, taps_ref, hat_ref, stats_ref, halves_ref,
):
    store_matrices(swapped, 0, other)
    rest = half_convolve([other[tap] for tap in range(9)], taps_one[1 - core_ref[0]])
    middle = partial[...] + rest
    middle = middle + (column(params, CONV_BIAS) + column(params, OFFSETS))
    hat, inverse = norm_hat(middle)
    hat_ref[...] = hat
    stats_ref[...] = jnp.broadcast_to(inverse, (C, HALF))
    pre = hat * column(params, GAINS + 1) + column(params, BIASES + 1)
    keep = load_image(recv_ref, AT_KEEP) * (1.0 / 0.9)
    store_shifts(taps_ref, (pre * sigmoid(pre) * keep).astype(BF16).astype(F32))
    away = 1 - core_ref[0]
    halves_ref[0 : 3 * HALF, :] = taps_one[away].reshape(3 * HALF, POS)
    halves_ref[3 * HALF : 6 * HALF, :] = taps_ref[away].reshape(3 * HALF, POS)
    halves_ref[6 * HALF :, :] = load_image(recv_ref, AT_COTANGENT).astype(BF16)


def attention_kernel(
    core_ref, recv_ref, swapped, taps_two, params, own, other_one,
    other, outputs_ref, grad_ref, sums_ref, normed_ref, halves_ref, grads_ref, swap_ref, turned,
):
    core = core_ref[0]
    store_matrices(swapped, 0, other)
    out_matrix = matrix(own, other_one, OUT_BLOCK, 0)
    qkv = [
        matrix(own, other_one, QUERY_BLOCK, 0),
        matrix(own, other_one, KEY_BLOCK, 0),
        matrix(own, other, VALUE_BLOCK, IN_CUT),
    ]
    for k in range(3):
        turned[:, C * k : C * k + C] = qkv[k].T
    cotangent = load_image(recv_ref, AT_COTANGENT)
    cot_low = cotangent.astype(BF16)
    attended_grad = in_order(dot_tn(out_matrix, cot_low), core).astype(BF16)
    source = load_image(recv_ref, AT_SOURCE)
    matrices = [matrix(own, other, SECOND_CONV + tap, IN_CUT) for tap in range(9)]
    residual = source + convolve(matrices, taps_two, core) + column(params, CONV_BIAS + 1)
    hat, inverse = norm_hat(residual)
    normed = (hat * column(params, GAINS + 2) + column(params, BIASES + 2)).astype(BF16)
    scale = C ** (-0.5)
    normed_ref[0] = normed[:HALF]
    normed_ref[1] = normed[HALF:]
    operand = own_first(normed_ref, core)
    queries = (by_rows(dot_nn, qkv[0], operand) + column(params, QV_BIAS)).astype(BF16)
    keys = by_rows(dot_nn, qkv[1], operand).astype(BF16)
    vals = (by_rows(dot_nn, qkv[2], operand) + column(params, QV_BIAS + 1)).astype(BF16)
    scores = dot_tn(queries, keys) * scale
    dprobs = dot_tn(attended_grad, vals)
    exps = jnp.exp(scores - jnp.max(scores, axis=1, keepdims=True))
    probs = exps / row_sum(exps)
    probs_low = probs.astype(BF16)
    dscores = (probs * (dprobs - row_sum(probs * dprobs))).astype(BF16)
    query_grad = (by_rows(dot_nt, keys, dscores) * scale).astype(BF16)
    key_grad = (by_rows(dot_nn, queries, dscores) * scale).astype(BF16)
    value_grad = by_rows(dot_nn, attended_grad, probs_low).astype(BF16)
    grads = jnp.concatenate([query_grad, key_grad, value_grad], axis=0)
    normed_grad = by_rows(dot_nn, turned, grads)
    normed_grad = in_order(normed_grad, core)
    for k, gradient in enumerate((query_grad, key_grad, value_grad)):
        grads_ref[k, :, :] = gradient
    attended = by_rows(dot_nt, vals, probs_low).astype(BF16)
    halves_ref[0] = attended[:HALF]
    halves_ref[1] = attended[HALF:]
    product = by_rows(dot_nn, out_matrix, own_first(halves_ref, core))
    outputs = residual + product + column(params, OUT_BIAS)
    outputs_ref[...] = image_rows(outputs)
    branch, gain_grad, bias_grad = norm_back(hat, inverse, normed_grad, column(params, GAINS + 2))
    residual_grad = cotangent + branch
    grad_ref[...] = residual_grad
    swap_ref[0:HALF, :] = normed_ref[1 - core]
    swap_ref[HALF:C, :] = halves_ref[1 - core]
    swap_ref[C : 2 * C, :] = residual_grad.astype(BF16)
    for k, gradient in enumerate((query_grad, key_grad, value_grad)):
        swap_ref[C * k + 2 * C : C * k + 3 * C, :] = gradient
    listed = {
        D_GAINS + 2: gain_grad,
        D_BIASES + 2: bias_grad,
        D_CONV_BIAS + 1: row_sum(residual_grad),
        D_QV_BIAS: row_sum(query_grad.astype(F32)),
        D_QV_BIAS + 1: row_sum(value_grad.astype(F32)),
        D_OUT_BIAS: row_sum(cotangent),
    }
    sums_ref[...] = columns_of(listed, jnp.zeros((C, HALF), F32))


def middle_back_kernel(
    core_ref, recv_ref, own, other, hat_ref, stats, params, grad_ref, sums, low_ref, sums_ref
):
    hat = hat_ref[...]
    gain = column(params, GAINS + 1)
    pre = hat * gain + column(params, BIASES + 1)
    keep = load_image(recv_ref, AT_KEEP) * (1.0 / 0.9)
    factor = keep * slope(pre)
    matrices = [matrix(own, other, SECOND_CONV + tap, IN_CUT) for tap in range(9)]
    second_grad = convolve_back(matrices, grad_ref[...].astype(BF16), core_ref[0])
    pre_grad = second_grad * factor
    middle_grad, gain_grad, bias_grad = norm_back(hat, column(stats, 0), pre_grad, gain)
    low_ref[...] = middle_grad.astype(BF16)
    listed = {D_GAINS + 1: gain_grad, D_BIASES + 1: bias_grad, D_CONV_BIAS: row_sum(middle_grad)}
    sums_ref[...] = columns_of(listed, sums[...])


def first_back_kernel(
    core_ref, own, other, hat_ref, stats, params, low_ref, grad_ref, sums, tail_ref
):
    hat = hat_ref[...]
    gain = column(params, GAINS)
    pre = hat * gain + column(params, BIASES)
    factor = slope(pre)
    matrices = [matrix(own, other, tap, 0) for tap in range(9)]
    first_grad = convolve_back(matrices, low_ref[...], core_ref[0])
    branch, gain_grad, bias_grad = norm_back(hat, column(stats, 0), first_grad * factor, gain)
    tail_ref[:, :16, :] = image_rows(grad_ref[...] + branch)

    table = columns_of({D_GAINS: gain_grad, D_BIASES: bias_grad}, sums[...])
    high = table.astype(BF16).astype(F32)
    low = pltpu.roll(table - high, PART, 1)
    lane = lax.broadcasted_iota(jnp.int32, (C, HALF), 1)
    table = jnp.where(lane < PART, high, low).reshape(SHARDS, ROWS, HALF)
    tail_ref[:, 16:, :] = jnp.concatenate([table, jnp.zeros_like(table)], axis=1).astype(BF16)


def second_grads_kernel(
    core_ref, recv_ref, taps_two, normed, attended, gradients, grad_ref, their_shifts, theirs,
    late_ref,
):
    core = core_ref[0]
    low = grad_ref[...].astype(BF16)
    second = conv_weight_grads(
        [low, theirs[C : 2 * C, :]], [taps_two[core], their_shifts[3 * HALF : 6 * HALF, :]]
    )
    operand = jnp.concatenate([normed[core], theirs[0:HALF, :]], axis=1)
    grads = jnp.concatenate([gradients[...].reshape(3 * C, POS), theirs[2 * C :, :]], axis=1)
    qkv = dot_nt(grads, operand)
    query, key, value = [lane_blocks(qkv[C * k : C * k + C])[0] for k in range(3)]
    operand = jnp.concatenate([attended[core], theirs[HALF:C, :]], axis=1)
    cotangent = load_image(recv_ref, AT_COTANGENT).astype(BF16)
    cotangents = jnp.concatenate([cotangent, their_shifts[6 * HALF :, :]], axis=1)
    out = lane_blocks(dot_nt(cotangents, operand))[0]
    store_blocks(late_ref, [query, key, *second, value, out, jnp.zeros_like(out)])


def gather_kernel(
    core_ref, taps_one, low_ref, their_shifts, their_low, late, outputs, tail, send_ref
):
    first = conv_weight_grads(
        [low_ref[...], their_low[...]], [taps_one[core_ref[0]], their_shifts[0 : 3 * HALF, :]]
    )
    cut = WROWS - IN_CUT_ROWS + 16
    out = late[:, cut : cut + 16, :].astype(F32)[:, :ROWS, :]
    store_blocks(send_ref, first + [out])
    send_ref[:, IN_CUT_ROWS - 16 : WROWS, :] = late[:, :cut, :]
    send_ref[:, WROWS : WROWS + 16, :] = outputs[...]
    send_ref[:, WROWS + 16 : WROWS + 40, :] = tail[:, :24, :]


AT_SOURCE, AT_KEEP, AT_COTANGENT, AT_PARAMS = WROWS, WROWS + 16, WROWS + 32, WROWS + 48
IN_ROWS = WROWS + 56
OUT_ROWS = WROWS + 40
OUT_BLOCK, QUERY_BLOCK, KEY_BLOCK, SECOND_CONV, VALUE_BLOCK = 9, 10, 11, 12, 21
IN_CUT = 12
IN_CUT_ROWS = IN_CUT * ROWS


def local_call(kernel, core, *operands, out, scratch=()):
    in_specs = [pl.BlockSpec(memory_space=pltpu.VMEM) for _ in operands]
    if core is not None:
        in_specs = [pl.BlockSpec(memory_space=pltpu.SMEM)] + in_specs
        operands = (core, *operands)
    shapes = tuple(jax.ShapeDtypeStruct(shape, dtype) for shape, dtype in out)
    return pl.pallas_call(
        kernel,
        out_shape=shapes,
        in_specs=in_specs,
        out_specs=tuple(pl.BlockSpec(memory_space=pltpu.VMEM) for _ in out),
        scratch_shapes=[pltpu.VMEM(shape, dtype) for shape, dtype in scratch],
        compiler_params=pltpu.CompilerParams(vmem_limit_bytes=VMEM_LIMIT),
    )(*operands)


VMEM_LIMIT = 24 * 1024 * 1024


def run_block(core, received, swap):
    swapped_one = swap(received[:, :IN_CUT_ROWS])
    swapped_two = swap(received[:, IN_CUT_ROWS:WROWS])
    image, table = ((C, POS), F32), ((C, HALF), F32)
    taps, low = ((2, 3, HALF, POS), BF16), ((C, POS), BF16)
    halves = ((2, HALF, POS), BF16)

    def matrices(count):
        return ((count, C, HALF), BF16)


    taps_one, hat_one, params, stats_one, own_weights, partial = local_call(
        first_kernel, core, received, out=(taps, image, table, table, matrices(WBLOCKS), image)
    )
    other_weights, taps_two, hat_two, stats_two, halves_out = local_call(
        middle_kernel, core, received, swapped_one, taps_one, params, partial,
        out=(matrices(IN_CUT), taps, image, table, ((6 * HALF + C, POS), BF16)),
    )
    rows = ((SHARDS, 16, HALF), BF16)
    their_shifts = swap(halves_out)
    other_two, outputs, residual_grad, sums, normed, attended, gradients, swapping = local_call(
        attention_kernel, core, received, swapped_two, taps_two, params, own_weights, other_weights,
        out=(
            matrices(WBLOCKS - IN_CUT), rows, image, table, halves, halves, ((3, C, POS), BF16),
            ((5 * C, POS), BF16),
        ),
        scratch=(((C, 3 * C), BF16),),
    )
    theirs = swap(swapping)
    residual_grad, their_shifts = lax.optimization_barrier((residual_grad, their_shifts))
    low_one, sums = local_call(
        middle_back_kernel, core, received, own_weights, other_two, hat_two, stats_two, params,
        residual_grad, sums, out=(low, table),
    )
    their_low = swap(low_one)
    (tail,) = local_call(
        first_back_kernel, core, own_weights, other_weights, hat_one, stats_one, params, low_one,
        residual_grad, sums, out=(((SHARDS, 32, HALF), BF16),),
    )
    (late,) = local_call(
        second_grads_kernel, core, received, taps_two, normed, attended, gradients, residual_grad,
        their_shifts, theirs, out=(((SHARDS, WROWS - IN_CUT_ROWS + 32, HALF), BF16),),
    )
    (send,) = local_call(
        gather_kernel, core, taps_one, low_one, their_shifts, their_low, late, outputs, tail,
        out=(((SHARDS, OUT_ROWS, HALF), BF16),),
    )
    return send


def collect_kernel(back_ref, swished_ref, sums_ref):
    for pair in range(WROWS // 16):
        rows = slice(16 * pair, 16 * pair + 16)
        total = back_ref[0, rows, :].astype(F32)
        for image in range(1, SHARDS):
            total = total + back_ref[image, rows, :].astype(F32)
        sums_ref[rows, :] = total.astype(BF16)
    small = back_ref[:, WROWS + 32 : WROWS + 40, :].astype(F32)
    table = jnp.zeros((ROWS, HALF), F32)
    temb = jnp.zeros((ROWS, TEMB), F32)
    for image in range(SHARDS):
        values = small[image] + pltpu.roll(small[image], HALF - PART, 1)
        table = table + values
        offsets_grad = values[:, D_CONV_BIAS : D_CONV_BIAS + 1]
        temb = temb + offsets_grad * swished_ref[image : image + 1, :]
    lane = lax.broadcasted_iota(jnp.int32, (ROWS, HALF), 1)
    high = table.astype(BF16).astype(F32)
    low = pltpu.roll(table - high, PART, 1)
    parts = jnp.where(lane < PART, high, jnp.where(lane < 2 * PART, low, 0.0))
    blocks = [parts] + [temb[:, HALF * k : HALF * k + HALF] for k in range(TEMB // HALF)]
    blocks = blocks + [jnp.zeros((ROWS, HALF), F32)]
    for pair in range(len(blocks) // 2):
        rows = slice(WROWS + 16 * pair, WROWS + 16 * pair + 16)
        both = jnp.concatenate(blocks[2 * pair : 2 * pair + 2], axis=0)
        sums_ref[rows, :] = both.astype(BF16)


SUM_ROWS = WROWS + ROWS + TEMB * ROWS // HALF + ROWS


def collect(back, swished):
    return pl.pallas_call(
        collect_kernel,
        out_shape=jax.ShapeDtypeStruct((SUM_ROWS, HALF), BF16),
        in_specs=[pl.BlockSpec(memory_space=pltpu.VMEM)] * 2,
        out_specs=pl.BlockSpec(memory_space=pltpu.VMEM),
        compiler_params=pltpu.CompilerParams(vmem_limit_bytes=8 * 1024 * 1024),
    )(back, swished)


def images_kernel(back_ref, outputs_ref, grad_ref):
    for at, target in ((WROWS, outputs_ref), (WROWS + 16, grad_ref)):
        block = back_ref[:, at : at + 16, :].astype(F32)
        cut = jnp.concatenate([block[:, :ROWS, :], block[:, ROWS:, :]], axis=2)
        target[...] = jnp.swapaxes(cut, 0, 1).astype(BF16)


def images(back):
    shape = jax.ShapeDtypeStruct((ROWS, SHARDS, POS), BF16)
    return pl.pallas_call(
        images_kernel,
        out_shape=(shape, shape),
        in_specs=[pl.BlockSpec(memory_space=pltpu.VMEM)],
        out_specs=(pl.BlockSpec(memory_space=pltpu.VMEM), pl.BlockSpec(memory_space=pltpu.VMEM)),
        compiler_params=pltpu.CompilerParams(vmem_limit_bytes=8 * 1024 * 1024),
    )(back)


def finish_kernel(core_ref, mine_ref, theirs_ref, *refs):
    results, scratch, sems = refs[:10], refs[10:20], refs[20]
    first_core = core_ref[0] == 0
    (gain, bias, conv_w, conv_b, temb_w, temb_b, qkv_w, qv_b, out_w, out_b) = scratch

    def weight_grad(block):
        rows = slice(ROWS * block, ROWS * block + ROWS)
        mine, theirs = mine_ref[rows, :], theirs_ref[rows, :]
        return jnp.concatenate(
            [jnp.where(first_core, mine, theirs), jnp.where(first_core, theirs, mine)], axis=1
        )

    copies = [pltpu.make_async_copy(scratch[k], results[k], sems.at[k]) for k in range(10)]
    for conv in range(2):
        for tap in range(9):
            conv_w[conv, tap, :, :] = weight_grad(SECOND_CONV * conv + tap)
    copies[2].start()
    for k in range(3):
        qkv_w[k, :, :] = weight_grad((QUERY_BLOCK, KEY_BLOCK, VALUE_BLOCK)[k])
    copies[6].start()
    out_w[...] = weight_grad(OUT_BLOCK)
    copies[8].start()
    shared = mine_ref[WROWS:, :] + theirs_ref[WROWS:, :]
    small = shared[:ROWS, :] + pltpu.roll(shared[:ROWS, :], HALF - PART, 1)
    for part in range(TEMB // HALF):
        rows = slice(ROWS + ROWS * part, 2 * ROWS + ROWS * part)
        temb_w[:, HALF * part : HALF * part + HALF] = shared[rows, :]
    copies[4].start()
    padded = jnp.concatenate([small, jnp.zeros((HALF - ROWS, HALF), F32)], axis=0)
    table = padded.T[:PART, :ROWS]
    gain[...] = table[D_GAINS : D_GAINS + 3]
    bias[...] = table[D_BIASES : D_BIASES + 3]
    conv_b[...] = table[D_CONV_BIAS : D_CONV_BIAS + 2]
    temb_b[...] = table[D_CONV_BIAS : D_CONV_BIAS + 1]
    qv_b[...] = table[D_QV_BIAS : D_QV_BIAS + 2]
    out_b[...] = table[D_OUT_BIAS : D_OUT_BIAS + 1]
    for k in (0, 1, 3, 5, 7, 9):
        copies[k].start()
    for copy in copies:
        copy.wait()


def finish(core, mine, theirs):
    shapes = [
        (3, ROWS), (3, ROWS), (2, 9, ROWS, C), (2, ROWS), (ROWS, TEMB), (1, ROWS),
        (3, ROWS, C), (2, ROWS), (ROWS, C), (1, ROWS),
    ]
    return pl.pallas_call(
        finish_kernel,
        out_shape=[jax.ShapeDtypeStruct(shape, F32) for shape in shapes],
        in_specs=[
            pl.BlockSpec(memory_space=pltpu.SMEM),
            pl.BlockSpec(memory_space=pltpu.VMEM),
            pl.BlockSpec(memory_space=pltpu.VMEM),
        ],
        out_specs=[pl.BlockSpec(memory_space=pltpu.HBM) for _ in shapes],
        scratch_shapes=[pltpu.VMEM(shape, F32) for shape in shapes]
        + [pltpu.SemaphoreType.DMA((10,))],
        compiler_params=pltpu.CompilerParams(vmem_limit_bytes=8 * 1024 * 1024),
    )(core, mine, theirs)


def prepare_kernel(core_ref, *refs):
    count = PREPARE_ARRAYS
    arrays, (send_ref, swished_ref) = refs[:count], refs[count : count + 2]
    held, (angles, sems) = refs[count + 2 : 2 * count + 2], refs[2 * count + 2 :]
    (
        steps_ref, gain_ref, bias_ref, conv_bias_ref, qv_ref, out_bias_ref, temb_bias_ref,
        temb_ref, conv_ref, qkv_ref, out_ref, inputs_ref, mask_ref, cotangent_ref,
    ) = held
    copies = [pltpu.make_async_copy(arrays[k], held[k], sems.at[k]) for k in range(count)]
    for copy in copies:
        copy.start()
    first_core = core_ref[0] == 0
    for copy in copies[:8]:
        copy.wait()

    half_dim = TEMB // 2
    index = lax.broadcasted_iota(jnp.int32, (1, half_dim), 1).astype(F32)
    rates = jnp.exp(-math.log(10000.0) * index / (half_dim - 1))
    for image in range(SHARDS):
        angles[image : image + 1, :] = rates * steps_ref[image].astype(F32)
    angle = angles[...]
    turns = jnp.floor(angle * (2.0 / math.pi) + 0.5)
    rest = angle - turns * 1.5703125
    rest = rest - turns * 4.837512969970703125e-4
    rest = rest - turns * 7.549789954891882e-8
    square = rest * rest
    sine = rest + rest * square * (
        -1.6666654611e-1 + square * (8.3321608736e-3 + square * -1.9515295891e-4)
    )
    cosine = 1.0 - 0.5 * square + square * square * (
        4.166664568298827e-2 + square * (-1.388731625493765e-3 + square * 2.443315711809948e-5)
    )
    quarter = turns.astype(jnp.int32) & 3
    odd = (quarter & 1) == 1
    sines = jnp.where(odd, cosine, sine)
    cosines = jnp.where(odd, sine, cosine)
    sines = jnp.where(quarter >= 2, -sines, sines)
    cosines = jnp.where((quarter == 1) | (quarter == 2), -cosines, cosines)
    features = jnp.concatenate([sines, cosines], axis=1)
    swished = features * sigmoid(features)
    swished_ref[...] = swished
    offsets = None
    rest = swished
    for _ in range(3):
        part = rest.astype(BF16)
        rest = rest - part.astype(F32)
        product = dot_nt(temb_ref[...], part)
        offsets = product if offsets is None else offsets + product

    rows = jnp.concatenate(
        [
            jnp.zeros((1, ROWS), F32), gain_ref[...], bias_ref[...], conv_bias_ref[...],
            qv_ref[...], out_bias_ref[...], temb_bias_ref[...], jnp.zeros((3, ROWS), F32),
        ],
        axis=0,
    )
    square = jnp.concatenate([rows] * (HALF // PART), axis=0)
    square = jnp.concatenate([square, jnp.zeros((HALF, HALF - ROWS), F32)], axis=1)
    columns = square.T[:ROWS, :]
    lane = lax.broadcasted_iota(jnp.int32, (ROWS, HALF), 1)
    offset_lane = (lane & (PART - 1)) == OFFSETS
    offsets = offsets + columns[:, TEMB_BIAS : TEMB_BIAS + 1]
    for image in range(SHARDS):
        values = jnp.where(offset_lane, offsets[:, image : image + 1], columns)
        high = values.astype(BF16).astype(F32)
        mid = (values - high).astype(BF16).astype(F32)
        low = values - high - mid
        parts = jnp.where(
            lane < PART,
            high,
            jnp.where(lane < 2 * PART, mid, jnp.where(lane < 3 * PART, low, 0.0)),
        )
        send_ref[image, WROWS + 48 : WROWS + 56, :] = parts.astype(BF16)

    for copy in copies[8:]:
        copy.wait()

    def half(values):
        values = values.astype(F32)
        return jnp.where(first_core, values[:, :HALF], values[:, HALF:])

    shard = jnp.concatenate(
        [
            half(conv_ref[0].reshape(9 * ROWS, C)),
            half(out_ref[...]),
            half(qkv_ref[0]),
            half(qkv_ref[1]),
            half(conv_ref[1].reshape(9 * ROWS, C)),
            half(qkv_ref[2]),
        ],
        axis=0,
    ).astype(BF16)
    send_ref[:, :WROWS, :] = jnp.broadcast_to(shard[None], (SHARDS, WROWS, HALF))

    def put(at, values):
        turned = jnp.swapaxes(values.astype(F32), 0, 1)
        cut = jnp.concatenate([turned[:, :, :HALF], turned[:, :, HALF:]], axis=1)
        send_ref[:, at : at + 16, :] = cut.astype(BF16)

    put(WROWS, inputs_ref[...])
    put(WROWS + 16, mask_ref[...])
    put(WROWS + 32, cotangent_ref[...])


PREPARE_ARRAYS = 14


def prepare(core, timesteps, *arrays):
    held = [pltpu.SMEM((SHARDS,), jnp.int32)]
    held += [pltpu.VMEM(array.shape, array.dtype) for array in arrays]
    return pl.pallas_call(
        prepare_kernel,
        out_shape=(
            jax.ShapeDtypeStruct((SHARDS, IN_ROWS, HALF), BF16),
            jax.ShapeDtypeStruct((SHARDS, TEMB), F32),
        ),
        in_specs=[pl.BlockSpec(memory_space=pltpu.SMEM)]
        + [pl.BlockSpec(memory_space=pltpu.HBM)] * PREPARE_ARRAYS,
        out_specs=(pl.BlockSpec(memory_space=pltpu.VMEM), pl.BlockSpec(memory_space=pltpu.VMEM)),
        scratch_shapes=held
        + [pltpu.VMEM((SHARDS, TEMB // 2), F32), pltpu.SemaphoreType.DMA((PREPARE_ARRAYS,))],
        compiler_params=pltpu.CompilerParams(vmem_limit_bytes=16 * 1024 * 1024),
    )(core, *[pltpu.with_memory_space_constraint(a, pltpu.HBM) for a in (timesteps, *arrays)])


def on_device(
    inputs,
    timesteps,
    keep_mask,
    norm_gain,
    norm_bias,
    conv_weight,
    conv_bias,
    temb_weight,
    temb_bias,
    qkv_weight,
    qv_bias,
    out_weight,
    out_bias,
    cotangent,
):
    member = lax.axis_index("img")
    core = member % 2
    core_pairs = [(m, m ^ 1) for m in range(4)]
    plane_pairs = [(m, m ^ 2) for m in range(4)]
    sent, swished = prepare(
        core.reshape(1),
        timesteps,
        norm_gain,
        norm_bias,
        conv_bias,
        qv_bias,
        out_bias.reshape(1, ROWS),
        temb_bias.reshape(1, ROWS),
        temb_weight.T,
        conv_weight,
        qkv_weight,
        out_weight,
        inputs,
        keep_mask,
        cotangent,
    )
    received = lax.all_to_all(sent, "ch", split_axis=0, concat_axis=0, tiled=True)
    send = run_block(
        core.reshape(1), received, lambda values: lax.ppermute(values, "img", core_pairs)
    )
    back = lax.all_to_all(send, "ch", split_axis=0, concat_axis=0, tiled=True)

    sums = collect(back, swished)
    plane = lax.ppermute(sums, "img", plane_pairs)
    outputs, input_grad = images(back)
    plane, outputs, input_grad = lax.optimization_barrier((plane, outputs, input_grad))
    sums = sums.astype(F32) + plane.astype(F32)
    theirs = lax.ppermute(sums, "img", core_pairs)
    (gain, bias, conv_w, conv_b, temb_w, temb_b, qkv_w, qv_b, out_w, out_b) = finish(
        core.reshape(1), sums, theirs
    )
    return (
        outputs,
        input_grad,
        gain,
        bias,
        conv_w,
        conv_b,
        temb_w.T,
        temb_b[0],
        qkv_w,
        qv_b,
        out_w,
        out_b[0],
    )


def solution(mesh):
    placed = (
        P("ch", "img", None),
        P("img"),
        P("ch", "img", None),
        P(None, "ch"),
        P(None, "ch"),
        P(None, None, "ch", None),
        P(None, "ch"),
        P(None, "ch"),
        P("ch"),
        P(None, "ch", None),
        P(None, "ch"),
        P("ch", None),
        P("ch"),
        P("ch", "img", None),
    )
    return jax.shard_map(
        on_device,
        mesh=mesh,
        in_specs=placed,
        out_specs=(
            P("ch", "img", None),
            P("ch", "img", None),
            P(None, "ch"),
            P(None, "ch"),
            P(None, None, "ch", None),
            P(None, "ch"),
            P(None, "ch"),
            P("ch"),
            P(None, "ch", None),
            P(None, "ch"),
            P("ch", None),
            P("ch"),
        ),
        check_vma=False,
    )
```

```python
import functools
import math

import jax
import jax.numpy as jnp
from jax import lax
from jax.experimental import pallas as pl
from jax.experimental.pallas import tpu as pltpu
from jax.sharding import PartitionSpec as P

C = 256
TEMB = 512
SIDE = 16
POS = 256
SHARDS = 32
ROWS = C // SHARDS
HALF = 128
WBLOCKS = 22
WROWS = WBLOCKS * ROWS
NORM_EPS = 1e-06
GROUP_SIZE = ROWS * POS
F32 = jnp.float32
BF16 = jnp.bfloat16

OFFSETS, GAINS, BIASES, CONV_BIAS, QV_BIAS, OUT_BIAS, TEMB_BIAS = 0, 1, 4, 7, 9, 11, 12
D_GAINS, D_BIASES, D_CONV_BIAS, D_QV_BIAS, D_OUT_BIAS = 0, 3, 6, 8, 10
PART = 16


def dot_nn(a, b):
    return lax.dot_general(a, b, (((1,), (0,)), ((), ())), preferred_element_type=F32)


def dot_nt(a, b):
    return lax.dot_general(a, b, (((1,), (1,)), ((), ())), preferred_element_type=F32)


def dot_tn(a, b):
    return lax.dot_general(a, b, (((0,), (0,)), ((), ())), preferred_element_type=F32)


def group_sum(values):
    column = jnp.sum(values, axis=1, keepdims=True)
    return group_column(column)


def group_column(column):
    grouped = column.reshape(SHARDS, ROWS, 1)
    total = jnp.sum(grouped, axis=1, keepdims=True)
    return jnp.broadcast_to(total, grouped.shape).reshape(C, 1)


def norm_hat(values):
    average = group_sum(values) * (1.0 / GROUP_SIZE)
    centered = values - average
    spread = group_sum(centered * centered) * (1.0 / GROUP_SIZE)
    inverse = lax.rsqrt(spread + NORM_EPS)
    return centered * inverse, inverse


def norm_back(hat, inverse, grad_out, gain):
    gain_grad = jnp.sum(grad_out * hat, axis=1, keepdims=True)
    bias_grad = jnp.sum(grad_out, axis=1, keepdims=True)
    first_mean = group_column(bias_grad * gain) * (1.0 / GROUP_SIZE)
    second_mean = group_column(gain_grad * gain) * (1.0 / GROUP_SIZE)
    grad_in = inverse * (grad_out * gain - first_mean - hat * second_mean)
    return grad_in, gain_grad, bias_grad


def sigmoid(values):
    return 0.5 + 0.5 * jnp.tanh(0.5 * values)


def rolled(values, steps, axis):
    return pltpu.roll(values, steps % POS, axis)


def column_shifted(values, step, axis):
    shape = (1, POS) if axis == 1 else (POS, POS)
    cell = (lax.broadcasted_iota(jnp.int32, shape, axis) & (SIDE - 1)) + step
    valid = (cell >= 0) & (cell < SIDE)
    return rolled(values, -step, axis) * valid.astype(F32)


def row_shifted(values, step):
    moved = rolled(values, -step * SIDE, 1)
    lane = lax.broadcasted_iota(jnp.int32, (1, HALF), 1)
    if step > 0:
        edge = jnp.where(lane < HALF - SIDE, moved[:, HALF:], 0.0)
        return jnp.concatenate([moved[:, :HALF], edge], axis=1)
    edge = jnp.where(lane >= SIDE, moved[:, :HALF], 0.0)
    return jnp.concatenate([edge, moved[:, HALF:]], axis=1)


def store_matrices(ref, target, first, count):
    for pair in range(count // 2):
        rows = ref[:, 16 * pair : 16 * pair + 16, :].astype(F32)
        for part in range(2):
            cut = rows[:, ROWS * part : ROWS * part + ROWS, :]
            target[first + 2 * pair + part, :, :] = cut.reshape(C, HALF).astype(BF16)


def matrix(own, other, block, first_other):
    return jnp.concatenate([own[block], other[block - first_other]], axis=1)


def own_first(ref, core):
    halves = [ref[core], ref[1 - core]]
    return jnp.concatenate([half.reshape(-1, POS) for half in halves], axis=0)


def in_order(values, core):
    top, bottom = values[:HALF], values[HALF:]
    first = core == 0
    return jnp.concatenate(
        [jnp.where(first, top, bottom), jnp.where(first, bottom, top)], axis=0
    )


def load_image(ref, at):
    block = ref[:, at : at + 16, :].astype(F32)
    left = block[:, 0:ROWS, :].reshape(C, HALF)
    right = block[:, ROWS : 2 * ROWS, :].reshape(C, HALF)
    return jnp.concatenate([left, right], axis=1)


def image_rows(values):
    left = values[:, 0:HALF].reshape(SHARDS, ROWS, HALF)
    right = values[:, HALF:C].reshape(SHARDS, ROWS, HALF)
    return jnp.concatenate([left, right], axis=1).astype(BF16)


def store_shifts(target, values):
    for step in (-1, 0, 1):
        moved = (column_shifted(values, step, 1) if step else values).astype(BF16)
        target[0, step + 1, :, :] = moved[:HALF]
        target[1, step + 1, :, :] = moved[HALF:]


def half_convolve(matrices, shifts):
    operand = shifts.reshape(3 * HALF, POS)
    total = None
    for row in (0, -1, 1):
        product = dot_nn(jnp.concatenate(matrices[3 * row + 3 : 3 * row + 6], axis=1), operand)
        total = product if row == 0 else total + row_shifted(product, row)
    return total


def convolve(matrices, shifts, core):
    operand = [shifts[half, step] for step in range(3) for half in (core, 1 - core)]
    operand = jnp.concatenate(operand, axis=0)
    total = None
    for row in (0, -1, 1):
        product = dot_nn(jnp.concatenate(matrices[3 * row + 3 : 3 * row + 6], axis=1), operand)
        total = product if row == 0 else total + row_shifted(product, row)
    return total


def convolve_back(matrices, low, core):
    turned = low.T
    edge = jnp.zeros((SIDE, C), BF16)
    stacked = jnp.concatenate(
        [
            jnp.concatenate([turned[SIDE:], edge], axis=0),
            turned,
            jnp.concatenate([edge, turned[:-SIDE]], axis=0),
        ],
        axis=1,
    )
    total = None
    for step in (0, -1, 1):
        product = dot_nn(stacked, jnp.concatenate(matrices[step + 1 :: 3], axis=0))
        total = product if step == 0 else total + column_shifted(product, -step, 0)
    return in_order(total.T, core)


def lane_blocks(product):
    count = product.shape[1] // HALF
    cut = [product[:, HALF * k : HALF * k + HALF] for k in range(count)]
    return [values.reshape(SHARDS, ROWS, HALF) for values in cut]


def conv_weight_grads(lows, shifts):
    wide = [part.reshape(3 * HALF, POS) for part in shifts]
    rows = []
    for row in (-1, 0, 1):
        moved = [row_shifted(part.astype(F32), row).astype(BF16) if row else part for part in wide]
        rows.append(jnp.concatenate(moved, axis=1))
    return lane_blocks(dot_nt(jnp.concatenate(lows, axis=1), jnp.concatenate(rows, axis=0)))


def store_blocks(target, blocks):
    for pair in range(len(blocks) // 2):
        rows = jnp.concatenate(blocks[2 * pair : 2 * pair + 2], axis=1)
        target[:, 16 * pair : 16 * pair + 16, :] = rows.astype(BF16)


def columns_of(listed, table):
    lane = lax.broadcasted_iota(jnp.int32, (C, HALF), 1)
    for k, column in listed.items():
        table = jnp.where(lane == k, column, table)
    return table


def column(ref, lane):
    return ref[:, lane : lane + 1]


def by_rows(dot, left, right):
    return jnp.concatenate([dot(left[:HALF], right), dot(left[HALF:], right)], axis=0)


def row_sum(values):
    return jnp.sum(values, axis=1, keepdims=True)


def slope(values):
    sigma = sigmoid(values)
    return sigma * (1.0 + values * (1.0 - sigma))


def first_kernel(core_ref, recv_ref, taps_ref, hat_ref, params_ref, stats_ref, own_ref, partial_ref):
    columns = recv_ref[:, AT_PARAMS : AT_PARAMS + ROWS, :].astype(F32).reshape(C, HALF)
    columns = (
        columns
        + pltpu.roll(columns, HALF - PART, 1)
        + pltpu.roll(columns, HALF - 2 * PART, 1)
    )
    params_ref[...] = columns
    hat, inverse = norm_hat(load_image(recv_ref, AT_SOURCE))
    hat_ref[...] = hat
    stats_ref[...] = jnp.broadcast_to(inverse, (C, HALF))
    pre = hat * columns[:, GAINS : GAINS + 1] + columns[:, BIASES : BIASES + 1]
    store_shifts(taps_ref, (pre * sigmoid(pre)).astype(BF16).astype(F32))
    store_matrices(recv_ref, own_ref, 0, WBLOCKS)
    partial_ref[...] = half_convolve([own_ref[tap] for tap in range(9)], taps_ref[core_ref[0]])


def middle_kernel(
    core_ref, recv_ref, swapped, taps_one, params, partial,
    other, taps_ref, hat_ref, stats_ref, halves_ref,
):
    store_matrices(swapped, other, 0, IN_CUT)
    rest = half_convolve([other[tap] for tap in range(9)], taps_one[1 - core_ref[0]])
    middle = partial[...] + rest
    middle = middle + (column(params, CONV_BIAS) + column(params, OFFSETS))
    hat, inverse = norm_hat(middle)
    hat_ref[...] = hat
    stats_ref[...] = jnp.broadcast_to(inverse, (C, HALF))
    pre = hat * column(params, GAINS + 1) + column(params, BIASES + 1)
    keep = load_image(recv_ref, AT_KEEP) * (1.0 / 0.9)
    store_shifts(taps_ref, (pre * sigmoid(pre) * keep).astype(BF16).astype(F32))
    away = 1 - core_ref[0]
    halves_ref[0 : 3 * HALF, :] = taps_one[away].reshape(3 * HALF, POS)
    halves_ref[3 * HALF : 6 * HALF, :] = taps_ref[away].reshape(3 * HALF, POS)
    halves_ref[6 * HALF :, :] = load_image(recv_ref, AT_COTANGENT).astype(BF16)


def attention_kernel(
    core_ref, recv_ref, swapped_two, swapped_three, taps_two, params, own, other_one,
    other, outputs_ref, grad_ref, sums_ref, normed_ref, halves_ref, grads_ref, swap_ref, turned,
):
    core = core_ref[0]
    half = (WBLOCKS - IN_CUT) // 2
    store_matrices(swapped_two, other, 0, half)
    store_matrices(swapped_three, other, half, half)
    out_matrix = matrix(own, other_one, OUT_BLOCK, 0)
    qkv = [
        matrix(own, other, QUERY_BLOCK, IN_CUT),
        matrix(own, other, KEY_BLOCK, IN_CUT),
        matrix(own, other, VALUE_BLOCK, IN_CUT),
    ]
    for k in range(3):
        turned[:, C * k : C * k + C] = qkv[k].T
    cotangent = load_image(recv_ref, AT_COTANGENT)
    cot_low = cotangent.astype(BF16)
    attended_grad = in_order(dot_tn(out_matrix, cot_low), core).astype(BF16)
    source = load_image(recv_ref, AT_SOURCE)
    matrices = [matrix(own, other, SECOND_CONV + tap, IN_CUT) for tap in range(9)]
    residual = source + convolve(matrices, taps_two, core) + column(params, CONV_BIAS + 1)
    hat, inverse = norm_hat(residual)
    normed = (hat * column(params, GAINS + 2) + column(params, BIASES + 2)).astype(BF16)
    scale = C ** (-0.5)
    normed_ref[0] = normed[:HALF]
    normed_ref[1] = normed[HALF:]
    operand = own_first(normed_ref, core)
    queries = (by_rows(dot_nn, qkv[0], operand) + column(params, QV_BIAS)).astype(BF16)
    keys = by_rows(dot_nn, qkv[1], operand).astype(BF16)
    vals = (by_rows(dot_nn, qkv[2], operand) + column(params, QV_BIAS + 1)).astype(BF16)
    scores = dot_tn(queries, keys) * scale
    dprobs = dot_tn(attended_grad, vals)
    exps = jnp.exp(scores - jnp.max(scores, axis=1, keepdims=True))
    probs = exps / row_sum(exps)
    probs_low = probs.astype(BF16)
    dscores = (probs * (dprobs - row_sum(probs * dprobs))).astype(BF16)
    query_grad = (by_rows(dot_nt, keys, dscores) * scale).astype(BF16)
    key_grad = (by_rows(dot_nn, queries, dscores) * scale).astype(BF16)
    value_grad = by_rows(dot_nn, attended_grad, probs_low).astype(BF16)
    grads = jnp.concatenate([query_grad, key_grad, value_grad], axis=0)
    normed_grad = by_rows(dot_nn, turned, grads)
    normed_grad = in_order(normed_grad, core)
    for k, gradient in enumerate((query_grad, key_grad, value_grad)):
        grads_ref[k, :, :] = gradient
    attended = by_rows(dot_nt, vals, probs_low).astype(BF16)
    halves_ref[0] = attended[:HALF]
    halves_ref[1] = attended[HALF:]
    product = by_rows(dot_nn, out_matrix, own_first(halves_ref, core))
    outputs = residual + product + column(params, OUT_BIAS)
    outputs_ref[...] = image_rows(outputs)
    branch, gain_grad, bias_grad = norm_back(hat, inverse, normed_grad, column(params, GAINS + 2))
    residual_grad = cotangent + branch
    grad_ref[...] = residual_grad
    swap_ref[0:HALF, :] = normed_ref[1 - core]
    swap_ref[HALF:C, :] = halves_ref[1 - core]
    swap_ref[C : 2 * C, :] = residual_grad.astype(BF16)
    for k, gradient in enumerate((query_grad, key_grad, value_grad)):
        swap_ref[C * k + 2 * C : C * k + 3 * C, :] = gradient
    listed = {
        D_GAINS + 2: gain_grad,
        D_BIASES + 2: bias_grad,
        D_CONV_BIAS + 1: row_sum(residual_grad),
        D_QV_BIAS: row_sum(query_grad.astype(F32)),
        D_QV_BIAS + 1: row_sum(value_grad.astype(F32)),
        D_OUT_BIAS: row_sum(cotangent),
    }
    sums_ref[...] = columns_of(listed, jnp.zeros((C, HALF), F32))


def middle_back_kernel(
    core_ref, recv_ref, own, other, hat_ref, stats, params, grad_ref, sums, low_ref, sums_ref
):
    hat = hat_ref[...]
    gain = column(params, GAINS + 1)
    pre = hat * gain + column(params, BIASES + 1)
    keep = load_image(recv_ref, AT_KEEP) * (1.0 / 0.9)
    factor = keep * slope(pre)
    matrices = [matrix(own, other, SECOND_CONV + tap, IN_CUT) for tap in range(9)]
    second_grad = convolve_back(matrices, grad_ref[...].astype(BF16), core_ref[0])
    pre_grad = second_grad * factor
    middle_grad, gain_grad, bias_grad = norm_back(hat, column(stats, 0), pre_grad, gain)
    low_ref[...] = middle_grad.astype(BF16)
    listed = {D_GAINS + 1: gain_grad, D_BIASES + 1: bias_grad, D_CONV_BIAS: row_sum(middle_grad)}
    sums_ref[...] = columns_of(listed, sums[...])


def first_back_kernel(
    core_ref, own, other, hat_ref, stats, params, low_ref, grad_ref, sums, tail_ref
):
    hat = hat_ref[...]
    gain = column(params, GAINS)
    pre = hat * gain + column(params, BIASES)
    factor = slope(pre)
    matrices = [matrix(own, other, tap, 0) for tap in range(9)]
    first_grad = convolve_back(matrices, low_ref[...], core_ref[0])
    branch, gain_grad, bias_grad = norm_back(hat, column(stats, 0), first_grad * factor, gain)
    tail_ref[:, :16, :] = image_rows(grad_ref[...] + branch)

    table = columns_of({D_GAINS: gain_grad, D_BIASES: bias_grad}, sums[...])
    high = table.astype(BF16).astype(F32)
    low = pltpu.roll(table - high, PART, 1)
    lane = lax.broadcasted_iota(jnp.int32, (C, HALF), 1)
    table = jnp.where(lane < PART, high, low).reshape(SHARDS, ROWS, HALF)
    tail_ref[:, 16:, :] = jnp.concatenate([table, jnp.zeros_like(table)], axis=1).astype(BF16)


def second_grads_kernel(
    core_ref, recv_ref, taps_two, normed, attended, gradients, grad_ref, their_shifts, theirs,
    late_ref,
):
    core = core_ref[0]
    low = grad_ref[...].astype(BF16)
    second = conv_weight_grads(
        [low, theirs[C : 2 * C, :]], [taps_two[core], their_shifts[3 * HALF : 6 * HALF, :]]
    )
    operand = jnp.concatenate([normed[core], theirs[0:HALF, :]], axis=1)
    grads = jnp.concatenate([gradients[...].reshape(3 * C, POS), theirs[2 * C :, :]], axis=1)
    qkv = dot_nt(grads, operand)
    query, key, value = [lane_blocks(qkv[C * k : C * k + C])[0] for k in range(3)]
    operand = jnp.concatenate([attended[core], theirs[HALF:C, :]], axis=1)
    cotangent = load_image(recv_ref, AT_COTANGENT).astype(BF16)
    cotangents = jnp.concatenate([cotangent, their_shifts[6 * HALF :, :]], axis=1)
    out = lane_blocks(dot_nt(cotangents, operand))[0]
    store_blocks(late_ref, [query, key, *second, value, out, jnp.zeros_like(out)])


def gather_kernel(
    core_ref, taps_one, low_ref, their_shifts, their_low, late, outputs, tail, send_ref
):
    first = conv_weight_grads(
        [low_ref[...], their_low[...]], [taps_one[core_ref[0]], their_shifts[0 : 3 * HALF, :]]
    )
    cut = WROWS - IN_CUT_ROWS
    out = late[:, cut : cut + 16, :].astype(F32)[:, :ROWS, :]
    store_blocks(send_ref, first + [out])
    send_ref[:, IN_CUT_ROWS:WROWS, :] = late[:, :cut, :]
    send_ref[:, WROWS : WROWS + 16, :] = outputs[...]
    send_ref[:, WROWS + 16 : WROWS + 40, :] = tail[:, :24, :]


AT_SOURCE, AT_KEEP, AT_COTANGENT, AT_PARAMS = WROWS, WROWS + 16, WROWS + 32, WROWS + 48
IN_ROWS = WROWS + 56
OUT_ROWS = WROWS + 40
OUT_BLOCK, QUERY_BLOCK, KEY_BLOCK, SECOND_CONV, VALUE_BLOCK = 9, 10, 11, 12, 21
IN_CUT = 10
IN_CUT_ROWS = IN_CUT * ROWS


def local_call(kernel, core, *operands, out, scratch=()):
    in_specs = [pl.BlockSpec(memory_space=pltpu.VMEM) for _ in operands]
    if core is not None:
        in_specs = [pl.BlockSpec(memory_space=pltpu.SMEM)] + in_specs
        operands = (core, *operands)
    shapes = tuple(jax.ShapeDtypeStruct(shape, dtype) for shape, dtype in out)
    return pl.pallas_call(
        kernel,
        out_shape=shapes,
        in_specs=in_specs,
        out_specs=tuple(pl.BlockSpec(memory_space=pltpu.VMEM) for _ in out),
        scratch_shapes=[pltpu.VMEM(shape, dtype) for shape, dtype in scratch],
        compiler_params=pltpu.CompilerParams(vmem_limit_bytes=VMEM_LIMIT),
    )(*operands)


VMEM_LIMIT = 24 * 1024 * 1024


def run_block(core, received, swap):
    swapped_one = swap(received[:, :IN_CUT_ROWS])
    middle_row = (IN_CUT_ROWS + WROWS) // 2
    swapped_two = swap(received[:, IN_CUT_ROWS:middle_row])
    swapped_three = swap(received[:, middle_row:WROWS])
    image, table = ((C, POS), F32), ((C, HALF), F32)
    taps, low = ((2, 3, HALF, POS), BF16), ((C, POS), BF16)
    halves = ((2, HALF, POS), BF16)

    def matrices(count):
        return ((count, C, HALF), BF16)


    taps_one, hat_one, params, stats_one, own_weights, partial = local_call(
        first_kernel, core, received, out=(taps, image, table, table, matrices(WBLOCKS), image)
    )
    other_weights, taps_two, hat_two, stats_two, halves_out = local_call(
        middle_kernel, core, received, swapped_one, taps_one, params, partial,
        out=(matrices(IN_CUT), taps, image, table, ((6 * HALF + C, POS), BF16)),
    )
    rows = ((SHARDS, 16, HALF), BF16)
    their_shifts = swap(halves_out)
    other_two, outputs, residual_grad, sums, normed, attended, gradients, swapping = local_call(
        attention_kernel, core, received, swapped_two, swapped_three, taps_two, params, own_weights,
        other_weights,
        out=(
            matrices(WBLOCKS - IN_CUT), rows, image, table, halves, halves, ((3, C, POS), BF16),
            ((5 * C, POS), BF16),
        ),
        scratch=(((C, 3 * C), BF16),),
    )
    theirs = swap(swapping)
    residual_grad, their_shifts = lax.optimization_barrier((residual_grad, their_shifts))
    low_one, sums = local_call(
        middle_back_kernel, core, received, own_weights, other_two, hat_two, stats_two, params,
        residual_grad, sums, out=(low, table),
    )
    their_low = swap(low_one)
    (tail,) = local_call(
        first_back_kernel, core, own_weights, other_weights, hat_one, stats_one, params, low_one,
        residual_grad, sums, out=(((SHARDS, 32, HALF), BF16),),
    )
    (late,) = local_call(
        second_grads_kernel, core, received, taps_two, normed, attended, gradients, residual_grad,
        their_shifts, theirs, out=(((SHARDS, WROWS - IN_CUT_ROWS + 16, HALF), BF16),),
    )
    (send,) = local_call(
        gather_kernel, core, taps_one, low_one, their_shifts, their_low, late, outputs, tail,
        out=(((SHARDS, OUT_ROWS, HALF), BF16),),
    )
    return send


def collect_kernel(back_ref, swished_ref, sums_ref):
    for pair in range(WROWS // 16):
        rows = slice(16 * pair, 16 * pair + 16)
        total = back_ref[0, rows, :].astype(F32)
        for image in range(1, SHARDS):
            total = total + back_ref[image, rows, :].astype(F32)
        sums_ref[rows, :] = total.astype(BF16)
    small = back_ref[:, WROWS + 32 : WROWS + 40, :].astype(F32)
    table = jnp.zeros((ROWS, HALF), F32)
    temb = jnp.zeros((ROWS, TEMB), F32)
    for image in range(SHARDS):
        values = small[image] + pltpu.roll(small[image], HALF - PART, 1)
        table = table + values
        offsets_grad = values[:, D_CONV_BIAS : D_CONV_BIAS + 1]
        temb = temb + offsets_grad * swished_ref[image : image + 1, :]
    lane = lax.broadcasted_iota(jnp.int32, (ROWS, HALF), 1)
    high = table.astype(BF16).astype(F32)
    low = pltpu.roll(table - high, PART, 1)
    parts = jnp.where(lane < PART, high, jnp.where(lane < 2 * PART, low, 0.0))
    blocks = [parts] + [temb[:, HALF * k : HALF * k + HALF] for k in range(TEMB // HALF)]
    blocks = blocks + [jnp.zeros((ROWS, HALF), F32)]
    for pair in range(len(blocks) // 2):
        rows = slice(WROWS + 16 * pair, WROWS + 16 * pair + 16)
        both = jnp.concatenate(blocks[2 * pair : 2 * pair + 2], axis=0)
        sums_ref[rows, :] = both.astype(BF16)


SUM_ROWS = WROWS + ROWS + TEMB * ROWS // HALF + ROWS


def collect(back, swished):
    return pl.pallas_call(
        collect_kernel,
        out_shape=jax.ShapeDtypeStruct((SUM_ROWS, HALF), BF16),
        in_specs=[pl.BlockSpec(memory_space=pltpu.VMEM)] * 2,
        out_specs=pl.BlockSpec(memory_space=pltpu.VMEM),
        compiler_params=pltpu.CompilerParams(vmem_limit_bytes=8 * 1024 * 1024),
    )(back, swished)


def images_kernel(back_ref, outputs_ref, grad_ref):
    for at, target in ((WROWS, outputs_ref), (WROWS + 16, grad_ref)):
        block = back_ref[:, at : at + 16, :].astype(F32)
        cut = jnp.concatenate([block[:, :ROWS, :], block[:, ROWS:, :]], axis=2)
        target[...] = jnp.swapaxes(cut, 0, 1).astype(BF16)


def images(back):
    shape = jax.ShapeDtypeStruct((ROWS, SHARDS, POS), BF16)
    return pl.pallas_call(
        images_kernel,
        out_shape=(shape, shape),
        in_specs=[pl.BlockSpec(memory_space=pltpu.VMEM)],
        out_specs=(pl.BlockSpec(memory_space=pltpu.VMEM), pl.BlockSpec(memory_space=pltpu.VMEM)),
        compiler_params=pltpu.CompilerParams(vmem_limit_bytes=8 * 1024 * 1024),
    )(back)


def finish_kernel(core_ref, mine_ref, theirs_ref, *refs):
    results, scratch, sems = refs[:10], refs[10:20], refs[20]
    first_core = core_ref[0] == 0
    (gain, bias, conv_w, conv_b, temb_w, temb_b, qkv_w, qv_b, out_w, out_b) = scratch

    def weight_grad(block):
        rows = slice(ROWS * block, ROWS * block + ROWS)
        mine, theirs = mine_ref[rows, :], theirs_ref[rows, :]
        return jnp.concatenate(
            [jnp.where(first_core, mine, theirs), jnp.where(first_core, theirs, mine)], axis=1
        )

    copies = [pltpu.make_async_copy(scratch[k], results[k], sems.at[k]) for k in range(10)]
    for conv in range(2):
        for tap in range(9):
            conv_w[conv, tap, :, :] = weight_grad(SECOND_CONV * conv + tap)
    copies[2].start()
    for k in range(3):
        qkv_w[k, :, :] = weight_grad((QUERY_BLOCK, KEY_BLOCK, VALUE_BLOCK)[k])
    copies[6].start()
    out_w[...] = weight_grad(OUT_BLOCK)
    copies[8].start()
    shared = mine_ref[WROWS:, :] + theirs_ref[WROWS:, :]
    small = shared[:ROWS, :] + pltpu.roll(shared[:ROWS, :], HALF - PART, 1)
    for part in range(TEMB // HALF):
        rows = slice(ROWS + ROWS * part, 2 * ROWS + ROWS * part)
        temb_w[:, HALF * part : HALF * part + HALF] = shared[rows, :]
    copies[4].start()
    padded = jnp.concatenate([small, jnp.zeros((HALF - ROWS, HALF), F32)], axis=0)
    table = padded.T[:PART, :ROWS]
    gain[...] = table[D_GAINS : D_GAINS + 3]
    bias[...] = table[D_BIASES : D_BIASES + 3]
    conv_b[...] = table[D_CONV_BIAS : D_CONV_BIAS + 2]
    temb_b[...] = table[D_CONV_BIAS : D_CONV_BIAS + 1]
    qv_b[...] = table[D_QV_BIAS : D_QV_BIAS + 2]
    out_b[...] = table[D_OUT_BIAS : D_OUT_BIAS + 1]
    for k in (0, 1, 3, 5, 7, 9):
        copies[k].start()
    for copy in copies:
        copy.wait()


def finish(core, mine, theirs):
    shapes = [
        (3, ROWS), (3, ROWS), (2, 9, ROWS, C), (2, ROWS), (ROWS, TEMB), (1, ROWS),
        (3, ROWS, C), (2, ROWS), (ROWS, C), (1, ROWS),
    ]
    return pl.pallas_call(
        finish_kernel,
        out_shape=[jax.ShapeDtypeStruct(shape, F32) for shape in shapes],
        in_specs=[
            pl.BlockSpec(memory_space=pltpu.SMEM),
            pl.BlockSpec(memory_space=pltpu.VMEM),
            pl.BlockSpec(memory_space=pltpu.VMEM),
        ],
        out_specs=[pl.BlockSpec(memory_space=pltpu.HBM) for _ in shapes],
        scratch_shapes=[pltpu.VMEM(shape, F32) for shape in shapes]
        + [pltpu.SemaphoreType.DMA((10,))],
        compiler_params=pltpu.CompilerParams(vmem_limit_bytes=8 * 1024 * 1024),
    )(core, mine, theirs)


def prepare_kernel(core_ref, *refs):
    count = PREPARE_ARRAYS
    arrays, (send_ref, swished_ref) = refs[:count], refs[count : count + 2]
    held, (angles, sems) = refs[count + 2 : 2 * count + 2], refs[2 * count + 2 :]
    (
        steps_ref, gain_ref, bias_ref, conv_bias_ref, qv_ref, out_bias_ref, temb_bias_ref,
        temb_ref, conv_ref, qkv_ref, out_ref, inputs_ref, mask_ref, cotangent_ref,
    ) = held
    copies = [pltpu.make_async_copy(arrays[k], held[k], sems.at[k]) for k in range(count)]
    for copy in copies:
        copy.start()
    first_core = core_ref[0] == 0
    for copy in copies[:8]:
        copy.wait()

    half_dim = TEMB // 2
    index = lax.broadcasted_iota(jnp.int32, (1, half_dim), 1).astype(F32)
    rates = jnp.exp(-math.log(10000.0) * index / (half_dim - 1))
    for image in range(SHARDS):
        angles[image : image + 1, :] = rates * steps_ref[image].astype(F32)
    angle = angles[...]
    turns = jnp.floor(angle * (2.0 / math.pi) + 0.5)
    rest = angle - turns * 1.5703125
    rest = rest - turns * 4.837512969970703125e-4
    rest = rest - turns * 7.549789954891882e-8
    square = rest * rest
    sine = rest + rest * square * (
        -1.6666654611e-1 + square * (8.3321608736e-3 + square * -1.9515295891e-4)
    )
    cosine = 1.0 - 0.5 * square + square * square * (
        4.166664568298827e-2 + square * (-1.388731625493765e-3 + square * 2.443315711809948e-5)
    )
    quarter = turns.astype(jnp.int32) & 3
    odd = (quarter & 1) == 1
    sines = jnp.where(odd, cosine, sine)
    cosines = jnp.where(odd, sine, cosine)
    sines = jnp.where(quarter >= 2, -sines, sines)
    cosines = jnp.where((quarter == 1) | (quarter == 2), -cosines, cosines)
    features = jnp.concatenate([sines, cosines], axis=1)
    swished = features * sigmoid(features)
    swished_ref[...] = swished
    offsets = None
    rest = swished
    for _ in range(3):
        part = rest.astype(BF16)
        rest = rest - part.astype(F32)
        product = dot_nt(temb_ref[...], part)
        offsets = product if offsets is None else offsets + product

    rows = jnp.concatenate(
        [
            jnp.zeros((1, ROWS), F32), gain_ref[...], bias_ref[...], conv_bias_ref[...],
            qv_ref[...], out_bias_ref[...], temb_bias_ref[...], jnp.zeros((3, ROWS), F32),
        ],
        axis=0,
    )
    square = jnp.concatenate([rows] * (HALF // PART), axis=0)
    square = jnp.concatenate([square, jnp.zeros((HALF, HALF - ROWS), F32)], axis=1)
    columns = square.T[:ROWS, :]
    lane = lax.broadcasted_iota(jnp.int32, (ROWS, HALF), 1)
    offset_lane = (lane & (PART - 1)) == OFFSETS
    offsets = offsets + columns[:, TEMB_BIAS : TEMB_BIAS + 1]
    for image in range(SHARDS):
        values = jnp.where(offset_lane, offsets[:, image : image + 1], columns)
        high = values.astype(BF16).astype(F32)
        mid = (values - high).astype(BF16).astype(F32)
        low = values - high - mid
        parts = jnp.where(
            lane < PART,
            high,
            jnp.where(lane < 2 * PART, mid, jnp.where(lane < 3 * PART, low, 0.0)),
        )
        send_ref[image, WROWS + 48 : WROWS + 56, :] = parts.astype(BF16)

    for copy in copies[8:]:
        copy.wait()

    def half(values):
        values = values.astype(F32)
        return jnp.where(first_core, values[:, :HALF], values[:, HALF:])

    shard = jnp.concatenate(
        [
            half(conv_ref[0].reshape(9 * ROWS, C)),
            half(out_ref[...]),
            half(qkv_ref[0]),
            half(qkv_ref[1]),
            half(conv_ref[1].reshape(9 * ROWS, C)),
            half(qkv_ref[2]),
        ],
        axis=0,
    ).astype(BF16)
    send_ref[:, :WROWS, :] = jnp.broadcast_to(shard[None], (SHARDS, WROWS, HALF))

    def put(at, values):
        turned = jnp.swapaxes(values.astype(F32), 0, 1)
        cut = jnp.concatenate([turned[:, :, :HALF], turned[:, :, HALF:]], axis=1)
        send_ref[:, at : at + 16, :] = cut.astype(BF16)

    put(WROWS, inputs_ref[...])
    put(WROWS + 16, mask_ref[...])
    put(WROWS + 32, cotangent_ref[...])


PREPARE_ARRAYS = 14


def prepare(core, timesteps, *arrays):
    held = [pltpu.SMEM((SHARDS,), jnp.int32)]
    held += [pltpu.VMEM(array.shape, array.dtype) for array in arrays]
    return pl.pallas_call(
        prepare_kernel,
        out_shape=(
            jax.ShapeDtypeStruct((SHARDS, IN_ROWS, HALF), BF16),
            jax.ShapeDtypeStruct((SHARDS, TEMB), F32),
        ),
        in_specs=[pl.BlockSpec(memory_space=pltpu.SMEM)]
        + [pl.BlockSpec(memory_space=pltpu.HBM)] * PREPARE_ARRAYS,
        out_specs=(pl.BlockSpec(memory_space=pltpu.VMEM), pl.BlockSpec(memory_space=pltpu.VMEM)),
        scratch_shapes=held
        + [pltpu.VMEM((SHARDS, TEMB // 2), F32), pltpu.SemaphoreType.DMA((PREPARE_ARRAYS,))],
        compiler_params=pltpu.CompilerParams(vmem_limit_bytes=16 * 1024 * 1024),
    )(core, *[pltpu.with_memory_space_constraint(a, pltpu.HBM) for a in (timesteps, *arrays)])


def on_device(
    inputs,
    timesteps,
    keep_mask,
    norm_gain,
    norm_bias,
    conv_weight,
    conv_bias,
    temb_weight,
    temb_bias,
    qkv_weight,
    qv_bias,
    out_weight,
    out_bias,
    cotangent,
):
    member = lax.axis_index("img")
    core = member % 2
    core_pairs = [(m, m ^ 1) for m in range(4)]
    plane_pairs = [(m, m ^ 2) for m in range(4)]
    sent, swished = prepare(
        core.reshape(1),
        timesteps,
        norm_gain,
        norm_bias,
        conv_bias,
        qv_bias,
        out_bias.reshape(1, ROWS),
        temb_bias.reshape(1, ROWS),
        temb_weight.T,
        conv_weight,
        qkv_weight,
        out_weight,
        inputs,
        keep_mask,
        cotangent,
    )
    received = lax.all_to_all(sent, "ch", split_axis=0, concat_axis=0, tiled=True)
    send = run_block(
        core.reshape(1), received, lambda values: lax.ppermute(values, "img", core_pairs)
    )
    back = lax.all_to_all(send, "ch", split_axis=0, concat_axis=0, tiled=True)

    sums = collect(back, swished)
    plane = lax.ppermute(sums, "img", plane_pairs)
    outputs, input_grad = images(back)
    plane, outputs, input_grad = lax.optimization_barrier((plane, outputs, input_grad))
    sums = sums.astype(F32) + plane.astype(F32)
    theirs = lax.ppermute(sums, "img", core_pairs)
    (gain, bias, conv_w, conv_b, temb_w, temb_b, qkv_w, qv_b, out_w, out_b) = finish(
        core.reshape(1), sums, theirs
    )
    return (
        outputs,
        input_grad,
        gain,
        bias,
        conv_w,
        conv_b,
        temb_w.T,
        temb_b[0],
        qkv_w,
        qv_b,
        out_w,
        out_b[0],
    )


def solution(mesh):
    placed = (
        P("ch", "img", None),
        P("img"),
        P("ch", "img", None),
        P(None, "ch"),
        P(None, "ch"),
        P(None, None, "ch", None),
        P(None, "ch"),
        P(None, "ch"),
        P("ch"),
        P(None, "ch", None),
        P(None, "ch"),
        P("ch", None),
        P("ch"),
        P("ch", "img", None),
    )
    return jax.shard_map(
        on_device,
        mesh=mesh,
        in_specs=placed,
        out_specs=(
            P("ch", "img", None),
            P("ch", "img", None),
            P(None, "ch"),
            P(None, "ch"),
            P(None, None, "ch", None),
            P(None, "ch"),
            P(None, "ch"),
            P("ch"),
            P(None, "ch", None),
            P(None, "ch"),
            P("ch", None),
            P("ch"),
        ),
        check_vma=False,
    )
```

```python
import functools
import math

import jax
import jax.numpy as jnp
from jax import lax
from jax.experimental import pallas as pl
from jax.experimental.pallas import tpu as pltpu
from jax.sharding import PartitionSpec as P

C = 256
TEMB = 512
SIDE = 16
POS = 256
SHARDS = 32
ROWS = C // SHARDS
HALF = 128
WBLOCKS = 22
WROWS = WBLOCKS * ROWS
ORDER = (
    22, 13, 6, 20, 19, 23, 5, 14, 1, 24, 26, 10, 7, 21, 9, 28, 18, 2, 11, 3, 12, 4, 15,
    25, 16, 31, 29, 30, 0, 17, 8, 27,
)
PLACE = tuple(ORDER.index(k) for k in range(SHARDS))
NORM_EPS = 1e-06
GROUP_SIZE = ROWS * POS
F32 = jnp.float32
BF16 = jnp.bfloat16

OFFSETS, GAINS, BIASES, CONV_BIAS, QV_BIAS, OUT_BIAS, TEMB_BIAS = 0, 1, 4, 7, 9, 11, 12
D_GAINS, D_BIASES, D_CONV_BIAS, D_QV_BIAS, D_OUT_BIAS = 0, 3, 6, 8, 10
PART = 16


def arranged(values, order):
    return jnp.concatenate([values[k : k + 1] for k in order], axis=0)


def dot_nn(a, b):
    return lax.dot_general(a, b, (((1,), (0,)), ((), ())), preferred_element_type=F32)


def dot_nt(a, b):
    return lax.dot_general(a, b, (((1,), (1,)), ((), ())), preferred_element_type=F32)


def dot_tn(a, b):
    return lax.dot_general(a, b, (((0,), (0,)), ((), ())), preferred_element_type=F32)


def group_sum(values):
    column = jnp.sum(values, axis=1, keepdims=True)
    return group_column(column)


def group_column(column):
    grouped = column.reshape(SHARDS, ROWS, 1)
    total = jnp.sum(grouped, axis=1, keepdims=True)
    return jnp.broadcast_to(total, grouped.shape).reshape(C, 1)


def norm_hat(values):
    average = group_sum(values) * (1.0 / GROUP_SIZE)
    centered = values - average
    spread = group_sum(centered * centered) * (1.0 / GROUP_SIZE)
    inverse = lax.rsqrt(spread + NORM_EPS)
    return centered * inverse, inverse


def norm_back(hat, inverse, grad_out, gain):
    gain_grad = jnp.sum(grad_out * hat, axis=1, keepdims=True)
    bias_grad = jnp.sum(grad_out, axis=1, keepdims=True)
    first_mean = group_column(bias_grad * gain) * (1.0 / GROUP_SIZE)
    second_mean = group_column(gain_grad * gain) * (1.0 / GROUP_SIZE)
    grad_in = inverse * (grad_out * gain - first_mean - hat * second_mean)
    return grad_in, gain_grad, bias_grad


def sigmoid(values):
    return 0.5 + 0.5 * jnp.tanh(0.5 * values)


def rolled(values, steps, axis):
    return pltpu.roll(values, steps % POS, axis)


def column_shifted(values, step, axis):
    shape = (1, POS) if axis == 1 else (POS, POS)
    cell = (lax.broadcasted_iota(jnp.int32, shape, axis) & (SIDE - 1)) + step
    valid = (cell >= 0) & (cell < SIDE)
    return rolled(values, -step, axis) * valid.astype(F32)


def row_shifted(values, step):
    moved = rolled(values, -step * SIDE, 1)
    lane = lax.broadcasted_iota(jnp.int32, (1, HALF), 1)
    if step > 0:
        edge = jnp.where(lane < HALF - SIDE, moved[:, HALF:], 0.0)
        return jnp.concatenate([moved[:, :HALF], edge], axis=1)
    edge = jnp.where(lane >= SIDE, moved[:, :HALF], 0.0)
    return jnp.concatenate([edge, moved[:, HALF:]], axis=1)


def store_matrices(ref, target, first, count):
    for pair in range(count // 2):
        rows = arranged(ref[:, 16 * pair : 16 * pair + 16, :].astype(F32), PLACE)
        for part in range(2):
            cut = rows[:, ROWS * part : ROWS * part + ROWS, :]
            target[first + 2 * pair + part, :, :] = cut.reshape(C, HALF).astype(BF16)


def matrix(own, other, block, first_other):
    return jnp.concatenate([own[block], other[block - first_other]], axis=1)


def own_first(ref, core):
    halves = [ref[core], ref[1 - core]]
    return jnp.concatenate([half.reshape(-1, POS) for half in halves], axis=0)


def in_order(values, core):
    top, bottom = values[:HALF], values[HALF:]
    first = core == 0
    return jnp.concatenate(
        [jnp.where(first, top, bottom), jnp.where(first, bottom, top)], axis=0
    )


def load_image(ref, at):
    block = arranged(ref[:, at : at + 16, :].astype(F32), PLACE)
    left = block[:, 0:ROWS, :].reshape(C, HALF)
    right = block[:, ROWS : 2 * ROWS, :].reshape(C, HALF)
    return jnp.concatenate([left, right], axis=1)


def image_rows(values):
    left = values[:, 0:HALF].reshape(SHARDS, ROWS, HALF)
    right = values[:, HALF:C].reshape(SHARDS, ROWS, HALF)
    return jnp.concatenate([left, right], axis=1).astype(BF16)


def store_shifts(target, values):
    for step in (-1, 0, 1):
        moved = (column_shifted(values, step, 1) if step else values).astype(BF16)
        target[0, step + 1, :, :] = moved[:HALF]
        target[1, step + 1, :, :] = moved[HALF:]


def half_convolve(matrices, shifts):
    operand = shifts.reshape(3 * HALF, POS)
    total = None
    for row in (0, -1, 1):
        product = dot_nn(jnp.concatenate(matrices[3 * row + 3 : 3 * row + 6], axis=1), operand)
        total = product if row == 0 else total + row_shifted(product, row)
    return total


def convolve(matrices, shifts, core):
    operand = [shifts[half, step] for step in range(3) for half in (core, 1 - core)]
    operand = jnp.concatenate(operand, axis=0)
    total = None
    for row in (0, -1, 1):
        product = dot_nn(jnp.concatenate(matrices[3 * row + 3 : 3 * row + 6], axis=1), operand)
        total = product if row == 0 else total + row_shifted(product, row)
    return total


def convolve_back(matrices, low, core):
    turned = low.T
    edge = jnp.zeros((SIDE, C), BF16)
    stacked = jnp.concatenate(
        [
            jnp.concatenate([turned[SIDE:], edge], axis=0),
            turned,
            jnp.concatenate([edge, turned[:-SIDE]], axis=0),
        ],
        axis=1,
    )
    total = None
    for step in (0, -1, 1):
        product = dot_nn(stacked, jnp.concatenate(matrices[step + 1 :: 3], axis=0))
        total = product if step == 0 else total + column_shifted(product, -step, 0)
    return in_order(total.T, core)


def lane_blocks(product):
    count = product.shape[1] // HALF
    cut = [product[:, HALF * k : HALF * k + HALF] for k in range(count)]
    return [values.reshape(SHARDS, ROWS, HALF) for values in cut]


def conv_weight_grads(lows, shifts):
    wide = [part.reshape(3 * HALF, POS) for part in shifts]
    rows = []
    for row in (-1, 0, 1):
        moved = [row_shifted(part.astype(F32), row).astype(BF16) if row else part for part in wide]
        rows.append(jnp.concatenate(moved, axis=1))
    return lane_blocks(dot_nt(jnp.concatenate(lows, axis=1), jnp.concatenate(rows, axis=0)))


def store_blocks(target, blocks, order=range(SHARDS)):
    for pair in range(len(blocks) // 2):
        rows = jnp.concatenate(blocks[2 * pair : 2 * pair + 2], axis=1)
        target[:, 16 * pair : 16 * pair + 16, :] = arranged(rows, order).astype(BF16)


def columns_of(listed, table):
    lane = lax.broadcasted_iota(jnp.int32, (C, HALF), 1)
    for k, column in listed.items():
        table = jnp.where(lane == k, column, table)
    return table


def column(ref, lane):
    return ref[:, lane : lane + 1]


def by_rows(dot, left, right):
    return jnp.concatenate([dot(left[:HALF], right), dot(left[HALF:], right)], axis=0)


def row_sum(values):
    return jnp.sum(values, axis=1, keepdims=True)


def slope(values):
    sigma = sigmoid(values)
    return sigma * (1.0 + values * (1.0 - sigma))


def first_kernel(core_ref, recv_ref, taps_ref, hat_ref, params_ref, stats_ref, own_ref, partial_ref):
    columns = recv_ref[:, AT_PARAMS : AT_PARAMS + ROWS, :].astype(F32)
    columns = arranged(columns, PLACE).reshape(C, HALF)
    columns = (
        columns
        + pltpu.roll(columns, HALF - PART, 1)
        + pltpu.roll(columns, HALF - 2 * PART, 1)
    )
    params_ref[...] = columns
    hat, inverse = norm_hat(load_image(recv_ref, AT_SOURCE))
    hat_ref[...] = hat
    stats_ref[...] = jnp.broadcast_to(inverse, (C, HALF))
    pre = hat * columns[:, GAINS : GAINS + 1] + columns[:, BIASES : BIASES + 1]
    store_shifts(taps_ref, (pre * sigmoid(pre)).astype(BF16).astype(F32))
    store_matrices(recv_ref, own_ref, 0, WBLOCKS)
    partial_ref[...] = half_convolve([own_ref[tap] for tap in range(9)], taps_ref[core_ref[0]])


def middle_kernel(
    core_ref, recv_ref, swapped, taps_one, params, partial,
    other, taps_ref, hat_ref, stats_ref, halves_ref,
):
    store_matrices(swapped, other, 0, IN_CUT)
    rest = half_convolve([other[tap] for tap in range(9)], taps_one[1 - core_ref[0]])
    middle = partial[...] + rest
    middle = middle + (column(params, CONV_BIAS) + column(params, OFFSETS))
    hat, inverse = norm_hat(middle)
    hat_ref[...] = hat
    stats_ref[...] = jnp.broadcast_to(inverse, (C, HALF))
    pre = hat * column(params, GAINS + 1) + column(params, BIASES + 1)
    keep = load_image(recv_ref, AT_KEEP) * (1.0 / 0.9)
    store_shifts(taps_ref, (pre * sigmoid(pre) * keep).astype(BF16).astype(F32))
    away = 1 - core_ref[0]
    halves_ref[0 : 3 * HALF, :] = taps_one[away].reshape(3 * HALF, POS)
    halves_ref[3 * HALF : 6 * HALF, :] = taps_ref[away].reshape(3 * HALF, POS)
    halves_ref[6 * HALF :, :] = load_image(recv_ref, AT_COTANGENT).astype(BF16)


def attention_kernel(
    core_ref, recv_ref, swapped_two, swapped_three, taps_two, params, own, other_one,
    other, outputs_ref, grad_ref, sums_ref, normed_ref, halves_ref, grads_ref, swap_ref, turned,
):
    core = core_ref[0]
    half = (WBLOCKS - IN_CUT) // 2
    store_matrices(swapped_two, other, 0, half)
    store_matrices(swapped_three, other, half, half)
    out_matrix = matrix(own, other_one, OUT_BLOCK, 0)
    qkv = [
        matrix(own, other, QUERY_BLOCK, IN_CUT),
        matrix(own, other, KEY_BLOCK, IN_CUT),
        matrix(own, other, VALUE_BLOCK, IN_CUT),
    ]
    for k in range(3):
        turned[:, C * k : C * k + C] = qkv[k].T
    cotangent = load_image(recv_ref, AT_COTANGENT)
    cot_low = cotangent.astype(BF16)
    attended_grad = in_order(dot_tn(out_matrix, cot_low), core).astype(BF16)
    source = load_image(recv_ref, AT_SOURCE)
    matrices = [matrix(own, other, SECOND_CONV + tap, IN_CUT) for tap in range(9)]
    residual = source + convolve(matrices, taps_two, core) + column(params, CONV_BIAS + 1)
    hat, inverse = norm_hat(residual)
    normed = (hat * column(params, GAINS + 2) + column(params, BIASES + 2)).astype(BF16)
    scale = C ** (-0.5)
    normed_ref[0] = normed[:HALF]
    normed_ref[1] = normed[HALF:]
    operand = own_first(normed_ref, core)
    queries = (by_rows(dot_nn, qkv[0], operand) + column(params, QV_BIAS)).astype(BF16)
    keys = by_rows(dot_nn, qkv[1], operand).astype(BF16)
    vals = (by_rows(dot_nn, qkv[2], operand) + column(params, QV_BIAS + 1)).astype(BF16)
    scores = dot_tn(queries, keys) * scale
    dprobs = dot_tn(attended_grad, vals)
    exps = jnp.exp(scores - jnp.max(scores, axis=1, keepdims=True))
    probs = exps / row_sum(exps)
    probs_low = probs.astype(BF16)
    dscores = (probs * (dprobs - row_sum(probs * dprobs))).astype(BF16)
    query_grad = (by_rows(dot_nt, keys, dscores) * scale).astype(BF16)
    key_grad = (by_rows(dot_nn, queries, dscores) * scale).astype(BF16)
    value_grad = by_rows(dot_nn, attended_grad, probs_low).astype(BF16)
    grads = jnp.concatenate([query_grad, key_grad, value_grad], axis=0)
    normed_grad = by_rows(dot_nn, turned, grads)
    normed_grad = in_order(normed_grad, core)
    for k, gradient in enumerate((query_grad, key_grad, value_grad)):
        grads_ref[k, :, :] = gradient
    attended = by_rows(dot_nt, vals, probs_low).astype(BF16)
    halves_ref[0] = attended[:HALF]
    halves_ref[1] = attended[HALF:]
    product = by_rows(dot_nn, out_matrix, own_first(halves_ref, core))
    outputs = residual + product + column(params, OUT_BIAS)
    outputs_ref[...] = image_rows(outputs)
    branch, gain_grad, bias_grad = norm_back(hat, inverse, normed_grad, column(params, GAINS + 2))
    residual_grad = cotangent + branch
    grad_ref[...] = residual_grad
    swap_ref[0:HALF, :] = normed_ref[1 - core]
    swap_ref[HALF:C, :] = halves_ref[1 - core]
    swap_ref[C : 2 * C, :] = residual_grad.astype(BF16)
    for k, gradient in enumerate((query_grad, key_grad, value_grad)):
        swap_ref[C * k + 2 * C : C * k + 3 * C, :] = gradient
    listed = {
        D_GAINS + 2: gain_grad,
        D_BIASES + 2: bias_grad,
        D_CONV_BIAS + 1: row_sum(residual_grad),
        D_QV_BIAS: row_sum(query_grad.astype(F32)),
        D_QV_BIAS + 1: row_sum(value_grad.astype(F32)),
        D_OUT_BIAS: row_sum(cotangent),
    }
    sums_ref[...] = columns_of(listed, jnp.zeros((C, HALF), F32))


def middle_back_kernel(
    core_ref, recv_ref, own, other, hat_ref, stats, params, grad_ref, sums, low_ref, sums_ref
):
    hat = hat_ref[...]
    gain = column(params, GAINS + 1)
    pre = hat * gain + column(params, BIASES + 1)
    keep = load_image(recv_ref, AT_KEEP) * (1.0 / 0.9)
    factor = keep * slope(pre)
    matrices = [matrix(own, other, SECOND_CONV + tap, IN_CUT) for tap in range(9)]
    second_grad = convolve_back(matrices, grad_ref[...].astype(BF16), core_ref[0])
    pre_grad = second_grad * factor
    middle_grad, gain_grad, bias_grad = norm_back(hat, column(stats, 0), pre_grad, gain)
    low_ref[...] = middle_grad.astype(BF16)
    listed = {D_GAINS + 1: gain_grad, D_BIASES + 1: bias_grad, D_CONV_BIAS: row_sum(middle_grad)}
    sums_ref[...] = columns_of(listed, sums[...])


def first_back_kernel(
    core_ref, own, other, hat_ref, stats, params, low_ref, grad_ref, sums, tail_ref
):
    hat = hat_ref[...]
    gain = column(params, GAINS)
    pre = hat * gain + column(params, BIASES)
    factor = slope(pre)
    matrices = [matrix(own, other, tap, 0) for tap in range(9)]
    first_grad = convolve_back(matrices, low_ref[...], core_ref[0])
    branch, gain_grad, bias_grad = norm_back(hat, column(stats, 0), first_grad * factor, gain)
    tail_ref[:, :16, :] = image_rows(grad_ref[...] + branch)

    table = columns_of({D_GAINS: gain_grad, D_BIASES: bias_grad}, sums[...])
    high = table.astype(BF16).astype(F32)
    low = pltpu.roll(table - high, PART, 1)
    lane = lax.broadcasted_iota(jnp.int32, (C, HALF), 1)
    table = jnp.where(lane < PART, high, low).reshape(SHARDS, ROWS, HALF)
    tail_ref[:, 16:, :] = jnp.concatenate([table, jnp.zeros_like(table)], axis=1).astype(BF16)


def second_grads_kernel(
    core_ref, recv_ref, taps_two, normed, attended, gradients, grad_ref, their_shifts, theirs,
    late_ref,
):
    core = core_ref[0]
    low = grad_ref[...].astype(BF16)
    second = conv_weight_grads(
        [low, theirs[C : 2 * C, :]], [taps_two[core], their_shifts[3 * HALF : 6 * HALF, :]]
    )
    operand = jnp.concatenate([normed[core], theirs[0:HALF, :]], axis=1)
    grads = jnp.concatenate([gradients[...].reshape(3 * C, POS), theirs[2 * C :, :]], axis=1)
    qkv = dot_nt(grads, operand)
    query, key, value = [lane_blocks(qkv[C * k : C * k + C])[0] for k in range(3)]
    operand = jnp.concatenate([attended[core], theirs[HALF:C, :]], axis=1)
    cotangent = load_image(recv_ref, AT_COTANGENT).astype(BF16)
    cotangents = jnp.concatenate([cotangent, their_shifts[6 * HALF :, :]], axis=1)
    out = lane_blocks(dot_nt(cotangents, operand))[0]
    store_blocks(late_ref, [query, key, *second, value, out, jnp.zeros_like(out)])


def gather_kernel(
    core_ref, taps_one, low_ref, their_shifts, their_low, late, outputs, tail, send_ref
):
    first = conv_weight_grads(
        [low_ref[...], their_low[...]], [taps_one[core_ref[0]], their_shifts[0 : 3 * HALF, :]]
    )
    cut = WROWS - IN_CUT_ROWS
    out = late[:, cut : cut + 16, :].astype(F32)[:, :ROWS, :]
    store_blocks(send_ref, first + [out], ORDER)
    send_ref[:, IN_CUT_ROWS:WROWS, :] = arranged(late[:, :cut, :], ORDER)
    send_ref[:, WROWS : WROWS + 16, :] = arranged(outputs[...], ORDER)
    send_ref[:, WROWS + 16 : WROWS + 40, :] = arranged(tail[:, :24, :], ORDER)


AT_SOURCE, AT_KEEP, AT_COTANGENT, AT_PARAMS = WROWS, WROWS + 16, WROWS + 32, WROWS + 48
IN_ROWS = WROWS + 56
OUT_ROWS = WROWS + 40
OUT_BLOCK, QUERY_BLOCK, KEY_BLOCK, SECOND_CONV, VALUE_BLOCK = 9, 10, 11, 12, 21
IN_CUT = 10
IN_CUT_ROWS = IN_CUT * ROWS


def local_call(kernel, core, *operands, out, scratch=()):
    in_specs = [pl.BlockSpec(memory_space=pltpu.VMEM) for _ in operands]
    if core is not None:
        in_specs = [pl.BlockSpec(memory_space=pltpu.SMEM)] + in_specs
        operands = (core, *operands)
    shapes = tuple(jax.ShapeDtypeStruct(shape, dtype) for shape, dtype in out)
    return pl.pallas_call(
        kernel,
        out_shape=shapes,
        in_specs=in_specs,
        out_specs=tuple(pl.BlockSpec(memory_space=pltpu.VMEM) for _ in out),
        scratch_shapes=[pltpu.VMEM(shape, dtype) for shape, dtype in scratch],
        compiler_params=pltpu.CompilerParams(vmem_limit_bytes=VMEM_LIMIT),
    )(*operands)


VMEM_LIMIT = 24 * 1024 * 1024


def run_block(core, received, swap):
    swapped_one = swap(received[:, :IN_CUT_ROWS])
    middle_row = (IN_CUT_ROWS + WROWS) // 2
    swapped_two = swap(received[:, IN_CUT_ROWS:middle_row])
    swapped_three = swap(received[:, middle_row:WROWS])
    image, table = ((C, POS), F32), ((C, HALF), F32)
    taps, low = ((2, 3, HALF, POS), BF16), ((C, POS), BF16)
    halves = ((2, HALF, POS), BF16)

    def matrices(count):
        return ((count, C, HALF), BF16)


    taps_one, hat_one, params, stats_one, own_weights, partial = local_call(
        first_kernel, core, received, out=(taps, image, table, table, matrices(WBLOCKS), image)
    )
    other_weights, taps_two, hat_two, stats_two, halves_out = local_call(
        middle_kernel, core, received, swapped_one, taps_one, params, partial,
        out=(matrices(IN_CUT), taps, image, table, ((6 * HALF + C, POS), BF16)),
    )
    rows = ((SHARDS, 16, HALF), BF16)
    their_shifts = swap(halves_out)
    other_two, outputs, residual_grad, sums, normed, attended, gradients, swapping = local_call(
        attention_kernel, core, received, swapped_two, swapped_three, taps_two, params, own_weights,
        other_weights,
        out=(
            matrices(WBLOCKS - IN_CUT), rows, image, table, halves, halves, ((3, C, POS), BF16),
            ((5 * C, POS), BF16),
        ),
        scratch=(((C, 3 * C), BF16),),
    )
    theirs = swap(swapping)
    residual_grad, their_shifts = lax.optimization_barrier((residual_grad, their_shifts))
    low_one, sums = local_call(
        middle_back_kernel, core, received, own_weights, other_two, hat_two, stats_two, params,
        residual_grad, sums, out=(low, table),
    )
    their_low = swap(low_one)
    (tail,) = local_call(
        first_back_kernel, core, own_weights, other_weights, hat_one, stats_one, params, low_one,
        residual_grad, sums, out=(((SHARDS, 32, HALF), BF16),),
    )
    (late,) = local_call(
        second_grads_kernel, core, received, taps_two, normed, attended, gradients, residual_grad,
        their_shifts, theirs, out=(((SHARDS, WROWS - IN_CUT_ROWS + 16, HALF), BF16),),
    )
    (send,) = local_call(
        gather_kernel, core, taps_one, low_one, their_shifts, their_low, late, outputs, tail,
        out=(((SHARDS, OUT_ROWS, HALF), BF16),),
    )
    return send


def collect_kernel(back_ref, swished_ref, sums_ref):
    for pair in range(WROWS // 16):
        rows = slice(16 * pair, 16 * pair + 16)
        total = back_ref[0, rows, :].astype(F32)
        for image in range(1, SHARDS):
            total = total + back_ref[image, rows, :].astype(F32)
        sums_ref[rows, :] = total.astype(BF16)
    small = back_ref[:, WROWS + 32 : WROWS + 40, :].astype(F32)
    table = jnp.zeros((ROWS, HALF), F32)
    temb = jnp.zeros((ROWS, TEMB), F32)
    for image in range(SHARDS):
        values = small[image] + pltpu.roll(small[image], HALF - PART, 1)
        table = table + values
        offsets_grad = values[:, D_CONV_BIAS : D_CONV_BIAS + 1]
        owner = ORDER[image]
        temb = temb + offsets_grad * swished_ref[owner : owner + 1, :]
    lane = lax.broadcasted_iota(jnp.int32, (ROWS, HALF), 1)
    high = table.astype(BF16).astype(F32)
    low = pltpu.roll(table - high, PART, 1)
    parts = jnp.where(lane < PART, high, jnp.where(lane < 2 * PART, low, 0.0))
    blocks = [parts] + [temb[:, HALF * k : HALF * k + HALF] for k in range(TEMB // HALF)]
    blocks = blocks + [jnp.zeros((ROWS, HALF), F32)]
    for pair in range(len(blocks) // 2):
        rows = slice(WROWS + 16 * pair, WROWS + 16 * pair + 16)
        both = jnp.concatenate(blocks[2 * pair : 2 * pair + 2], axis=0)
        sums_ref[rows, :] = both.astype(BF16)


SUM_ROWS = WROWS + ROWS + TEMB * ROWS // HALF + ROWS


def collect(back, swished):
    return pl.pallas_call(
        collect_kernel,
        out_shape=jax.ShapeDtypeStruct((SUM_ROWS, HALF), BF16),
        in_specs=[pl.BlockSpec(memory_space=pltpu.VMEM)] * 2,
        out_specs=pl.BlockSpec(memory_space=pltpu.VMEM),
        compiler_params=pltpu.CompilerParams(vmem_limit_bytes=8 * 1024 * 1024),
    )(back, swished)


def images_kernel(back_ref, outputs_ref, grad_ref):
    for at, target in ((WROWS, outputs_ref), (WROWS + 16, grad_ref)):
        block = arranged(back_ref[:, at : at + 16, :].astype(F32), PLACE)
        cut = jnp.concatenate([block[:, :ROWS, :], block[:, ROWS:, :]], axis=2)
        target[...] = jnp.swapaxes(cut, 0, 1).astype(BF16)


def images(back):
    shape = jax.ShapeDtypeStruct((ROWS, SHARDS, POS), BF16)
    return pl.pallas_call(
        images_kernel,
        out_shape=(shape, shape),
        in_specs=[pl.BlockSpec(memory_space=pltpu.VMEM)],
        out_specs=(pl.BlockSpec(memory_space=pltpu.VMEM), pl.BlockSpec(memory_space=pltpu.VMEM)),
        compiler_params=pltpu.CompilerParams(vmem_limit_bytes=8 * 1024 * 1024),
    )(back)


def finish_kernel(core_ref, mine_ref, theirs_ref, *refs):
    results, scratch, sems = refs[:10], refs[10:20], refs[20]
    first_core = core_ref[0] == 0
    (gain, bias, conv_w, conv_b, temb_w, temb_b, qkv_w, qv_b, out_w, out_b) = scratch

    def weight_grad(block):
        rows = slice(ROWS * block, ROWS * block + ROWS)
        mine, theirs = mine_ref[rows, :], theirs_ref[rows, :]
        return jnp.concatenate(
            [jnp.where(first_core, mine, theirs), jnp.where(first_core, theirs, mine)], axis=1
        )

    copies = [pltpu.make_async_copy(scratch[k], results[k], sems.at[k]) for k in range(10)]
    for conv in range(2):
        for tap in range(9):
            conv_w[conv, tap, :, :] = weight_grad(SECOND_CONV * conv + tap)
    copies[2].start()
    for k in range(3):
        qkv_w[k, :, :] = weight_grad((QUERY_BLOCK, KEY_BLOCK, VALUE_BLOCK)[k])
    copies[6].start()
    out_w[...] = weight_grad(OUT_BLOCK)
    copies[8].start()
    shared = mine_ref[WROWS:, :] + theirs_ref[WROWS:, :]
    small = shared[:ROWS, :] + pltpu.roll(shared[:ROWS, :], HALF - PART, 1)
    for part in range(TEMB // HALF):
        rows = slice(ROWS + ROWS * part, 2 * ROWS + ROWS * part)
        temb_w[:, HALF * part : HALF * part + HALF] = shared[rows, :]
    copies[4].start()
    padded = jnp.concatenate([small, jnp.zeros((HALF - ROWS, HALF), F32)], axis=0)
    table = padded.T[:PART, :ROWS]
    gain[...] = table[D_GAINS : D_GAINS + 3]
    bias[...] = table[D_BIASES : D_BIASES + 3]
    conv_b[...] = table[D_CONV_BIAS : D_CONV_BIAS + 2]
    temb_b[...] = table[D_CONV_BIAS : D_CONV_BIAS + 1]
    qv_b[...] = table[D_QV_BIAS : D_QV_BIAS + 2]
    out_b[...] = table[D_OUT_BIAS : D_OUT_BIAS + 1]
    for k in (0, 1, 3, 5, 7, 9):
        copies[k].start()
    for copy in copies:
        copy.wait()


def finish(core, mine, theirs):
    shapes = [
        (3, ROWS), (3, ROWS), (2, 9, ROWS, C), (2, ROWS), (ROWS, TEMB), (1, ROWS),
        (3, ROWS, C), (2, ROWS), (ROWS, C), (1, ROWS),
    ]
    return pl.pallas_call(
        finish_kernel,
        out_shape=[jax.ShapeDtypeStruct(shape, F32) for shape in shapes],
        in_specs=[
            pl.BlockSpec(memory_space=pltpu.SMEM),
            pl.BlockSpec(memory_space=pltpu.VMEM),
            pl.BlockSpec(memory_space=pltpu.VMEM),
        ],
        out_specs=[pl.BlockSpec(memory_space=pltpu.HBM) for _ in shapes],
        scratch_shapes=[pltpu.VMEM(shape, F32) for shape in shapes]
        + [pltpu.SemaphoreType.DMA((10,))],
        compiler_params=pltpu.CompilerParams(vmem_limit_bytes=8 * 1024 * 1024),
    )(core, mine, theirs)


def prepare_kernel(core_ref, *refs):
    count = PREPARE_ARRAYS
    arrays, (send_ref, swished_ref) = refs[:count], refs[count : count + 2]
    held, (angles, sems) = refs[count + 2 : 2 * count + 2], refs[2 * count + 2 :]
    (
        steps_ref, gain_ref, bias_ref, conv_bias_ref, qv_ref, out_bias_ref, temb_bias_ref,
        temb_ref, conv_ref, qkv_ref, out_ref, inputs_ref, mask_ref, cotangent_ref,
    ) = held
    copies = [pltpu.make_async_copy(arrays[k], held[k], sems.at[k]) for k in range(count)]
    for copy in copies:
        copy.start()
    first_core = core_ref[0] == 0
    for copy in copies[:8]:
        copy.wait()

    half_dim = TEMB // 2
    index = lax.broadcasted_iota(jnp.int32, (1, half_dim), 1).astype(F32)
    rates = jnp.exp(-math.log(10000.0) * index / (half_dim - 1))
    for image in range(SHARDS):
        angles[image : image + 1, :] = rates * steps_ref[image].astype(F32)
    angle = angles[...]
    turns = jnp.floor(angle * (2.0 / math.pi) + 0.5)
    rest = angle - turns * 1.5703125
    rest = rest - turns * 4.837512969970703125e-4
    rest = rest - turns * 7.549789954891882e-8
    square = rest * rest
    sine = rest + rest * square * (
        -1.6666654611e-1 + square * (8.3321608736e-3 + square * -1.9515295891e-4)
    )
    cosine = 1.0 - 0.5 * square + square * square * (
        4.166664568298827e-2 + square * (-1.388731625493765e-3 + square * 2.443315711809948e-5)
    )
    quarter = turns.astype(jnp.int32) & 3
    odd = (quarter & 1) == 1
    sines = jnp.where(odd, cosine, sine)
    cosines = jnp.where(odd, sine, cosine)
    sines = jnp.where(quarter >= 2, -sines, sines)
    cosines = jnp.where((quarter == 1) | (quarter == 2), -cosines, cosines)
    features = jnp.concatenate([sines, cosines], axis=1)
    swished = features * sigmoid(features)
    swished_ref[...] = swished
    offsets = None
    rest = swished
    for _ in range(3):
        part = rest.astype(BF16)
        rest = rest - part.astype(F32)
        product = dot_nt(temb_ref[...], part)
        offsets = product if offsets is None else offsets + product

    rows = jnp.concatenate(
        [
            jnp.zeros((1, ROWS), F32), gain_ref[...], bias_ref[...], conv_bias_ref[...],
            qv_ref[...], out_bias_ref[...], temb_bias_ref[...], jnp.zeros((3, ROWS), F32),
        ],
        axis=0,
    )
    square = jnp.concatenate([rows] * (HALF // PART), axis=0)
    square = jnp.concatenate([square, jnp.zeros((HALF, HALF - ROWS), F32)], axis=1)
    columns = square.T[:ROWS, :]
    lane = lax.broadcasted_iota(jnp.int32, (ROWS, HALF), 1)
    offset_lane = (lane & (PART - 1)) == OFFSETS
    offsets = offsets + columns[:, TEMB_BIAS : TEMB_BIAS + 1]
    for image in range(SHARDS):
        values = jnp.where(offset_lane, offsets[:, image : image + 1], columns)
        high = values.astype(BF16).astype(F32)
        mid = (values - high).astype(BF16).astype(F32)
        low = values - high - mid
        parts = jnp.where(
            lane < PART,
            high,
            jnp.where(lane < 2 * PART, mid, jnp.where(lane < 3 * PART, low, 0.0)),
        )
        send_ref[PLACE[image], WROWS + 48 : WROWS + 56, :] = parts.astype(BF16)

    for copy in copies[8:]:
        copy.wait()

    def half(values):
        values = values.astype(F32)
        return jnp.where(first_core, values[:, :HALF], values[:, HALF:])

    shard = jnp.concatenate(
        [
            half(conv_ref[0].reshape(9 * ROWS, C)),
            half(out_ref[...]),
            half(qkv_ref[0]),
            half(qkv_ref[1]),
            half(conv_ref[1].reshape(9 * ROWS, C)),
            half(qkv_ref[2]),
        ],
        axis=0,
    ).astype(BF16)
    send_ref[:, :WROWS, :] = jnp.broadcast_to(shard[None], (SHARDS, WROWS, HALF))

    def put(at, values):
        turned = jnp.swapaxes(values.astype(F32), 0, 1)
        cut = jnp.concatenate([turned[:, :, :HALF], turned[:, :, HALF:]], axis=1)
        send_ref[:, at : at + 16, :] = arranged(cut, ORDER).astype(BF16)

    put(WROWS, inputs_ref[...])
    put(WROWS + 16, mask_ref[...])
    put(WROWS + 32, cotangent_ref[...])


PREPARE_ARRAYS = 14


def prepare(core, timesteps, *arrays):
    held = [pltpu.SMEM((SHARDS,), jnp.int32)]
    held += [pltpu.VMEM(array.shape, array.dtype) for array in arrays]
    return pl.pallas_call(
        prepare_kernel,
        out_shape=(
            jax.ShapeDtypeStruct((SHARDS, IN_ROWS, HALF), BF16),
            jax.ShapeDtypeStruct((SHARDS, TEMB), F32),
        ),
        in_specs=[pl.BlockSpec(memory_space=pltpu.SMEM)]
        + [pl.BlockSpec(memory_space=pltpu.HBM)] * PREPARE_ARRAYS,
        out_specs=(pl.BlockSpec(memory_space=pltpu.VMEM), pl.BlockSpec(memory_space=pltpu.VMEM)),
        scratch_shapes=held
        + [pltpu.VMEM((SHARDS, TEMB // 2), F32), pltpu.SemaphoreType.DMA((PREPARE_ARRAYS,))],
        compiler_params=pltpu.CompilerParams(vmem_limit_bytes=16 * 1024 * 1024),
    )(core, *[pltpu.with_memory_space_constraint(a, pltpu.HBM) for a in (timesteps, *arrays)])


def exchange(values):
    return lax.all_to_all(
        values, "ch", split_axis=0, concat_axis=0, tiled=True, axis_index_groups=[list(ORDER)]
    )


def on_device(
    inputs,
    timesteps,
    keep_mask,
    norm_gain,
    norm_bias,
    conv_weight,
    conv_bias,
    temb_weight,
    temb_bias,
    qkv_weight,
    qv_bias,
    out_weight,
    out_bias,
    cotangent,
):
    member = lax.axis_index("img")
    core = member % 2
    core_pairs = [(m, m ^ 1) for m in range(4)]
    plane_pairs = [(m, m ^ 2) for m in range(4)]
    sent, swished = prepare(
        core.reshape(1),
        timesteps,
        norm_gain,
        norm_bias,
        conv_bias,
        qv_bias,
        out_bias.reshape(1, ROWS),
        temb_bias.reshape(1, ROWS),
        temb_weight.T,
        conv_weight,
        qkv_weight,
        out_weight,
        inputs,
        keep_mask,
        cotangent,
    )
    received = exchange(sent)
    send = run_block(
        core.reshape(1), received, lambda values: lax.ppermute(values, "img", core_pairs)
    )
    back = exchange(send)

    sums = collect(back, swished)
    plane = lax.ppermute(sums, "img", plane_pairs)
    outputs, input_grad = images(back)
    plane, outputs, input_grad = lax.optimization_barrier((plane, outputs, input_grad))
    sums = sums.astype(F32) + plane.astype(F32)
    theirs = lax.ppermute(sums, "img", core_pairs)
    (gain, bias, conv_w, conv_b, temb_w, temb_b, qkv_w, qv_b, out_w, out_b) = finish(
        core.reshape(1), sums, theirs
    )
    return (
        outputs,
        input_grad,
        gain,
        bias,
        conv_w,
        conv_b,
        temb_w.T,
        temb_b[0],
        qkv_w,
        qv_b,
        out_w,
        out_b[0],
    )


def solution(mesh):
    placed = (
        P("ch", "img", None),
        P("img"),
        P("ch", "img", None),
        P(None, "ch"),
        P(None, "ch"),
        P(None, None, "ch", None),
        P(None, "ch"),
        P(None, "ch"),
        P("ch"),
        P(None, "ch", None),
        P(None, "ch"),
        P("ch", None),
        P("ch"),
        P("ch", "img", None),
    )
    return jax.shard_map(
        on_device,
        mesh=mesh,
        in_specs=placed,
        out_specs=(
            P("ch", "img", None),
            P("ch", "img", None),
            P(None, "ch"),
            P(None, "ch"),
            P(None, None, "ch", None),
            P(None, "ch"),
            P(None, "ch"),
            P("ch"),
            P(None, "ch", None),
            P(None, "ch"),
            P("ch", None),
            P("ch"),
        ),
        check_vma=False,
    )
```

```python
import functools
import math

import jax
import jax.numpy as jnp
from jax import lax
from jax.experimental import pallas as pl
from jax.experimental.pallas import tpu as pltpu
from jax.sharding import PartitionSpec as P

C = 256
TEMB = 512
SIDE = 16
POS = 256
SHARDS = 32
ROWS = C // SHARDS
HALF = 128
WBLOCKS = 22
WROWS = WBLOCKS * ROWS
FARTHEST = 22
ORDER = tuple((FARTHEST + k) % SHARDS for k in range(SHARDS))
PLACE = tuple(ORDER.index(k) for k in range(SHARDS))
NORM_EPS = 1e-06
GROUP_SIZE = ROWS * POS
F32 = jnp.float32
BF16 = jnp.bfloat16

OFFSETS, GAINS, BIASES, CONV_BIAS, QV_BIAS, OUT_BIAS, TEMB_BIAS = 0, 1, 4, 7, 9, 11, 12
D_GAINS, D_BIASES, D_CONV_BIAS, D_QV_BIAS, D_OUT_BIAS = 0, 3, 6, 8, 10
PART = 16


def arranged(values, order):
    return jnp.concatenate([values[k : k + 1] for k in order], axis=0)


def dot_nn(a, b):
    return lax.dot_general(a, b, (((1,), (0,)), ((), ())), preferred_element_type=F32)


def dot_nt(a, b):
    return lax.dot_general(a, b, (((1,), (1,)), ((), ())), preferred_element_type=F32)


def dot_tn(a, b):
    return lax.dot_general(a, b, (((0,), (0,)), ((), ())), preferred_element_type=F32)


def group_sum(values):
    column = jnp.sum(values, axis=1, keepdims=True)
    return group_column(column)


def group_column(column):
    grouped = column.reshape(SHARDS, ROWS, 1)
    total = jnp.sum(grouped, axis=1, keepdims=True)
    return jnp.broadcast_to(total, grouped.shape).reshape(C, 1)


def norm_hat(values):
    average = group_sum(values) * (1.0 / GROUP_SIZE)
    centered = values - average
    spread = group_sum(centered * centered) * (1.0 / GROUP_SIZE)
    inverse = lax.rsqrt(spread + NORM_EPS)
    return centered * inverse, inverse


def norm_back(hat, inverse, grad_out, gain):
    gain_grad = jnp.sum(grad_out * hat, axis=1, keepdims=True)
    bias_grad = jnp.sum(grad_out, axis=1, keepdims=True)
    first_mean = group_column(bias_grad * gain) * (1.0 / GROUP_SIZE)
    second_mean = group_column(gain_grad * gain) * (1.0 / GROUP_SIZE)
    grad_in = inverse * (grad_out * gain - first_mean - hat * second_mean)
    return grad_in, gain_grad, bias_grad


def sigmoid(values):
    return 0.5 + 0.5 * jnp.tanh(0.5 * values)


def rolled(values, steps, axis):
    return pltpu.roll(values, steps % POS, axis)


def column_shifted(values, step, axis):
    shape = (1, POS) if axis == 1 else (POS, POS)
    cell = (lax.broadcasted_iota(jnp.int32, shape, axis) & (SIDE - 1)) + step
    valid = (cell >= 0) & (cell < SIDE)
    return rolled(values, -step, axis) * valid.astype(F32)


def row_shifted(values, step):
    moved = rolled(values, -step * SIDE, 1)
    lane = lax.broadcasted_iota(jnp.int32, (1, HALF), 1)
    if step > 0:
        edge = jnp.where(lane < HALF - SIDE, moved[:, HALF:], 0.0)
        return jnp.concatenate([moved[:, :HALF], edge], axis=1)
    edge = jnp.where(lane >= SIDE, moved[:, :HALF], 0.0)
    return jnp.concatenate([edge, moved[:, HALF:]], axis=1)


def store_matrices(ref, target, first, count):
    for pair in range(count // 2):
        rows = arranged(ref[:, 16 * pair : 16 * pair + 16, :].astype(F32), PLACE)
        for part in range(2):
            cut = rows[:, ROWS * part : ROWS * part + ROWS, :]
            target[first + 2 * pair + part, :, :] = cut.reshape(C, HALF).astype(BF16)


def matrix(own, other, block, first_other):
    return jnp.concatenate([own[block], other[block - first_other]], axis=1)


def own_first(ref, core):
    halves = [ref[core], ref[1 - core]]
    return jnp.concatenate([half.reshape(-1, POS) for half in halves], axis=0)


def in_order(values, core):
    top, bottom = values[:HALF], values[HALF:]
    first = core == 0
    return jnp.concatenate(
        [jnp.where(first, top, bottom), jnp.where(first, bottom, top)], axis=0
    )


def load_image(ref, at):
    block = arranged(ref[:, at : at + 16, :].astype(F32), PLACE)
    left = block[:, 0:ROWS, :].reshape(C, HALF)
    right = block[:, ROWS : 2 * ROWS, :].reshape(C, HALF)
    return jnp.concatenate([left, right], axis=1)


def image_rows(values):
    left = values[:, 0:HALF].reshape(SHARDS, ROWS, HALF)
    right = values[:, HALF:C].reshape(SHARDS, ROWS, HALF)
    return jnp.concatenate([left, right], axis=1).astype(BF16)


def store_shifts(target, values):
    for step in (-1, 0, 1):
        moved = (column_shifted(values, step, 1) if step else values).astype(BF16)
        target[0, step + 1, :, :] = moved[:HALF]
        target[1, step + 1, :, :] = moved[HALF:]


def half_convolve(matrices, shifts):
    operand = shifts.reshape(3 * HALF, POS)
    total = None
    for row in (0, -1, 1):
        product = dot_nn(jnp.concatenate(matrices[3 * row + 3 : 3 * row + 6], axis=1), operand)
        total = product if row == 0 else total + row_shifted(product, row)
    return total


def convolve(matrices, shifts, core):
    operand = [shifts[half, step] for step in range(3) for half in (core, 1 - core)]
    operand = jnp.concatenate(operand, axis=0)
    total = None
    for row in (0, -1, 1):
        product = dot_nn(jnp.concatenate(matrices[3 * row + 3 : 3 * row + 6], axis=1), operand)
        total = product if row == 0 else total + row_shifted(product, row)
    return total


def convolve_back(matrices, low, core):
    turned = low.T
    edge = jnp.zeros((SIDE, C), BF16)
    stacked = jnp.concatenate(
        [
            jnp.concatenate([turned[SIDE:], edge], axis=0),
            turned,
            jnp.concatenate([edge, turned[:-SIDE]], axis=0),
        ],
        axis=1,
    )
    total = None
    for step in (0, -1, 1):
        product = dot_nn(stacked, jnp.concatenate(matrices[step + 1 :: 3], axis=0))
        total = product if step == 0 else total + column_shifted(product, -step, 0)
    return in_order(total.T, core)


def lane_blocks(product):
    count = product.shape[1] // HALF
    cut = [product[:, HALF * k : HALF * k + HALF] for k in range(count)]
    return [values.reshape(SHARDS, ROWS, HALF) for values in cut]


def conv_weight_grads(lows, shifts):
    wide = [part.reshape(3 * HALF, POS) for part in shifts]
    rows = []
    for row in (-1, 0, 1):
        moved = [row_shifted(part.astype(F32), row).astype(BF16) if row else part for part in wide]
        rows.append(jnp.concatenate(moved, axis=1))
    return lane_blocks(dot_nt(jnp.concatenate(lows, axis=1), jnp.concatenate(rows, axis=0)))


def store_blocks(target, blocks, order=range(SHARDS)):
    for pair in range(len(blocks) // 2):
        rows = jnp.concatenate(blocks[2 * pair : 2 * pair + 2], axis=1)
        target[:, 16 * pair : 16 * pair + 16, :] = arranged(rows, order).astype(BF16)


def columns_of(listed, table):
    lane = lax.broadcasted_iota(jnp.int32, (C, HALF), 1)
    for k, column in listed.items():
        table = jnp.where(lane == k, column, table)
    return table


def column(ref, lane):
    return ref[:, lane : lane + 1]


def by_rows(dot, left, right):
    return jnp.concatenate([dot(left[:HALF], right), dot(left[HALF:], right)], axis=0)


def row_sum(values):
    return jnp.sum(values, axis=1, keepdims=True)


def slope(values):
    sigma = sigmoid(values)
    return sigma * (1.0 + values * (1.0 - sigma))


def first_kernel(core_ref, recv_ref, taps_ref, hat_ref, params_ref, stats_ref, own_ref, partial_ref):
    columns = recv_ref[:, AT_PARAMS : AT_PARAMS + ROWS, :].astype(F32)
    columns = arranged(columns, PLACE).reshape(C, HALF)
    columns = (
        columns
        + pltpu.roll(columns, HALF - PART, 1)
        + pltpu.roll(columns, HALF - 2 * PART, 1)
    )
    params_ref[...] = columns
    hat, inverse = norm_hat(load_image(recv_ref, AT_SOURCE))
    hat_ref[...] = hat
    stats_ref[...] = jnp.broadcast_to(inverse, (C, HALF))
    pre = hat * columns[:, GAINS : GAINS + 1] + columns[:, BIASES : BIASES + 1]
    store_shifts(taps_ref, (pre * sigmoid(pre)).astype(BF16).astype(F32))
    store_matrices(recv_ref, own_ref, 0, WBLOCKS)
    partial_ref[...] = half_convolve([own_ref[tap] for tap in range(9)], taps_ref[core_ref[0]])


def middle_kernel(
    core_ref, recv_ref, swapped, taps_one, params, partial,
    other, taps_ref, hat_ref, stats_ref, halves_ref,
):
    store_matrices(swapped, other, 0, IN_CUT)
    rest = half_convolve([other[tap] for tap in range(9)], taps_one[1 - core_ref[0]])
    middle = partial[...] + rest
    middle = middle + (column(params, CONV_BIAS) + column(params, OFFSETS))
    hat, inverse = norm_hat(middle)
    hat_ref[...] = hat
    stats_ref[...] = jnp.broadcast_to(inverse, (C, HALF))
    pre = hat * column(params, GAINS + 1) + column(params, BIASES + 1)
    keep = load_image(recv_ref, AT_KEEP) * (1.0 / 0.9)
    store_shifts(taps_ref, (pre * sigmoid(pre) * keep).astype(BF16).astype(F32))
    away = 1 - core_ref[0]
    halves_ref[0 : 3 * HALF, :] = taps_one[away].reshape(3 * HALF, POS)
    halves_ref[3 * HALF : 6 * HALF, :] = taps_ref[away].reshape(3 * HALF, POS)
    halves_ref[6 * HALF :, :] = load_image(recv_ref, AT_COTANGENT).astype(BF16)


def attention_kernel(
    core_ref, recv_ref, swapped_two, swapped_three, taps_two, params, own, other_one,
    other, outputs_ref, grad_ref, sums_ref, normed_ref, halves_ref, grads_ref, swap_ref, turned,
):
    core = core_ref[0]
    half = (WBLOCKS - IN_CUT) // 2
    store_matrices(swapped_two, other, 0, half)
    store_matrices(swapped_three, other, half, half)
    out_matrix = matrix(own, other_one, OUT_BLOCK, 0)
    qkv = [
        matrix(own, other, QUERY_BLOCK, IN_CUT),
        matrix(own, other, KEY_BLOCK, IN_CUT),
        matrix(own, other, VALUE_BLOCK, IN_CUT),
    ]
    for k in range(3):
        turned[:, C * k : C * k + C] = qkv[k].T
    cotangent = load_image(recv_ref, AT_COTANGENT)
    cot_low = cotangent.astype(BF16)
    attended_grad = in_order(dot_tn(out_matrix, cot_low), core).astype(BF16)
    source = load_image(recv_ref, AT_SOURCE)
    matrices = [matrix(own, other, SECOND_CONV + tap, IN_CUT) for tap in range(9)]
    residual = source + convolve(matrices, taps_two, core) + column(params, CONV_BIAS + 1)
    hat, inverse = norm_hat(residual)
    normed = (hat * column(params, GAINS + 2) + column(params, BIASES + 2)).astype(BF16)
    scale = C ** (-0.5)
    normed_ref[0] = normed[:HALF]
    normed_ref[1] = normed[HALF:]
    operand = own_first(normed_ref, core)
    queries = (by_rows(dot_nn, qkv[0], operand) + column(params, QV_BIAS)).astype(BF16)
    keys = by_rows(dot_nn, qkv[1], operand).astype(BF16)
    vals = (by_rows(dot_nn, qkv[2], operand) + column(params, QV_BIAS + 1)).astype(BF16)
    scores = dot_tn(queries, keys) * scale
    dprobs = dot_tn(attended_grad, vals)
    exps = jnp.exp(scores - jnp.max(scores, axis=1, keepdims=True))
    probs = exps / row_sum(exps)
    probs_low = probs.astype(BF16)
    dscores = (probs * (dprobs - row_sum(probs * dprobs))).astype(BF16)
    query_grad = (by_rows(dot_nt, keys, dscores) * scale).astype(BF16)
    key_grad = (by_rows(dot_nn, queries, dscores) * scale).astype(BF16)
    value_grad = by_rows(dot_nn, attended_grad, probs_low).astype(BF16)
    grads = jnp.concatenate([query_grad, key_grad, value_grad], axis=0)
    normed_grad = by_rows(dot_nn, turned, grads)
    normed_grad = in_order(normed_grad, core)
    for k, gradient in enumerate((query_grad, key_grad, value_grad)):
        grads_ref[k, :, :] = gradient
    attended = by_rows(dot_nt, vals, probs_low).astype(BF16)
    halves_ref[0] = attended[:HALF]
    halves_ref[1] = attended[HALF:]
    product = by_rows(dot_nn, out_matrix, own_first(halves_ref, core))
    outputs = residual + product + column(params, OUT_BIAS)
    outputs_ref[...] = image_rows(outputs)
    branch, gain_grad, bias_grad = norm_back(hat, inverse, normed_grad, column(params, GAINS + 2))
    residual_grad = cotangent + branch
    grad_ref[...] = residual_grad
    swap_ref[0:HALF, :] = normed_ref[1 - core]
    swap_ref[HALF:C, :] = halves_ref[1 - core]
    swap_ref[C : 2 * C, :] = residual_grad.astype(BF16)
    for k, gradient in enumerate((query_grad, key_grad, value_grad)):
        swap_ref[C * k + 2 * C : C * k + 3 * C, :] = gradient
    listed = {
        D_GAINS + 2: gain_grad,
        D_BIASES + 2: bias_grad,
        D_CONV_BIAS + 1: row_sum(residual_grad),
        D_QV_BIAS: row_sum(query_grad.astype(F32)),
        D_QV_BIAS + 1: row_sum(value_grad.astype(F32)),
        D_OUT_BIAS: row_sum(cotangent),
    }
    sums_ref[...] = columns_of(listed, jnp.zeros((C, HALF), F32))


def middle_back_kernel(
    core_ref, recv_ref, own, other, hat_ref, stats, params, grad_ref, sums, low_ref, sums_ref
):
    hat = hat_ref[...]
    gain = column(params, GAINS + 1)
    pre = hat * gain + column(params, BIASES + 1)
    keep = load_image(recv_ref, AT_KEEP) * (1.0 / 0.9)
    factor = keep * slope(pre)
    matrices = [matrix(own, other, SECOND_CONV + tap, IN_CUT) for tap in range(9)]
    second_grad = convolve_back(matrices, grad_ref[...].astype(BF16), core_ref[0])
    pre_grad = second_grad * factor
    middle_grad, gain_grad, bias_grad = norm_back(hat, column(stats, 0), pre_grad, gain)
    low_ref[...] = middle_grad.astype(BF16)
    listed = {D_GAINS + 1: gain_grad, D_BIASES + 1: bias_grad, D_CONV_BIAS: row_sum(middle_grad)}
    sums_ref[...] = columns_of(listed, sums[...])


def first_back_kernel(
    core_ref, own, other, hat_ref, stats, params, low_ref, grad_ref, sums, tail_ref
):
    hat = hat_ref[...]
    gain = column(params, GAINS)
    pre = hat * gain + column(params, BIASES)
    factor = slope(pre)
    matrices = [matrix(own, other, tap, 0) for tap in range(9)]
    first_grad = convolve_back(matrices, low_ref[...], core_ref[0])
    branch, gain_grad, bias_grad = norm_back(hat, column(stats, 0), first_grad * factor, gain)
    tail_ref[:, :16, :] = image_rows(grad_ref[...] + branch)

    table = columns_of({D_GAINS: gain_grad, D_BIASES: bias_grad}, sums[...])
    high = table.astype(BF16).astype(F32)
    low = pltpu.roll(table - high, PART, 1)
    lane = lax.broadcasted_iota(jnp.int32, (C, HALF), 1)
    table = jnp.where(lane < PART, high, low).reshape(SHARDS, ROWS, HALF)
    tail_ref[:, 16:, :] = jnp.concatenate([table, jnp.zeros_like(table)], axis=1).astype(BF16)


def second_grads_kernel(
    core_ref, recv_ref, taps_two, normed, attended, gradients, grad_ref, their_shifts, theirs,
    late_ref,
):
    core = core_ref[0]
    low = grad_ref[...].astype(BF16)
    second = conv_weight_grads(
        [low, theirs[C : 2 * C, :]], [taps_two[core], their_shifts[3 * HALF : 6 * HALF, :]]
    )
    operand = jnp.concatenate([normed[core], theirs[0:HALF, :]], axis=1)
    grads = jnp.concatenate([gradients[...].reshape(3 * C, POS), theirs[2 * C :, :]], axis=1)
    qkv = dot_nt(grads, operand)
    query, key, value = [lane_blocks(qkv[C * k : C * k + C])[0] for k in range(3)]
    operand = jnp.concatenate([attended[core], theirs[HALF:C, :]], axis=1)
    cotangent = load_image(recv_ref, AT_COTANGENT).astype(BF16)
    cotangents = jnp.concatenate([cotangent, their_shifts[6 * HALF :, :]], axis=1)
    out = lane_blocks(dot_nt(cotangents, operand))[0]
    store_blocks(late_ref, [query, key, *second, value, out, jnp.zeros_like(out)])


def gather_kernel(
    core_ref, taps_one, low_ref, their_shifts, their_low, late, outputs, tail, send_ref
):
    first = conv_weight_grads(
        [low_ref[...], their_low[...]], [taps_one[core_ref[0]], their_shifts[0 : 3 * HALF, :]]
    )
    cut = WROWS - IN_CUT_ROWS
    out = late[:, cut : cut + 16, :].astype(F32)[:, :ROWS, :]
    store_blocks(send_ref, first + [out], ORDER)
    send_ref[:, IN_CUT_ROWS:WROWS, :] = arranged(late[:, :cut, :], ORDER)
    send_ref[:, WROWS : WROWS + 16, :] = arranged(outputs[...], ORDER)
    send_ref[:, WROWS + 16 : WROWS + 40, :] = arranged(tail[:, :24, :], ORDER)


AT_SOURCE, AT_KEEP, AT_COTANGENT, AT_PARAMS = WROWS, WROWS + 16, WROWS + 32, WROWS + 48
IN_ROWS = WROWS + 56
OUT_ROWS = WROWS + 40
OUT_BLOCK, QUERY_BLOCK, KEY_BLOCK, SECOND_CONV, VALUE_BLOCK = 9, 10, 11, 12, 21
IN_CUT = 10
IN_CUT_ROWS = IN_CUT * ROWS


def local_call(kernel, core, *operands, out, scratch=()):
    in_specs = [pl.BlockSpec(memory_space=pltpu.VMEM) for _ in operands]
    if core is not None:
        in_specs = [pl.BlockSpec(memory_space=pltpu.SMEM)] + in_specs
        operands = (core, *operands)
    shapes = tuple(jax.ShapeDtypeStruct(shape, dtype) for shape, dtype in out)
    return pl.pallas_call(
        kernel,
        out_shape=shapes,
        in_specs=in_specs,
        out_specs=tuple(pl.BlockSpec(memory_space=pltpu.VMEM) for _ in out),
        scratch_shapes=[pltpu.VMEM(shape, dtype) for shape, dtype in scratch],
        compiler_params=pltpu.CompilerParams(vmem_limit_bytes=VMEM_LIMIT),
    )(*operands)


VMEM_LIMIT = 24 * 1024 * 1024


def run_block(core, received, swap):
    swapped_one = swap(received[:, :IN_CUT_ROWS])
    middle_row = (IN_CUT_ROWS + WROWS) // 2
    swapped_two = swap(received[:, IN_CUT_ROWS:middle_row])
    swapped_three = swap(received[:, middle_row:WROWS])
    image, table = ((C, POS), F32), ((C, HALF), F32)
    taps, low = ((2, 3, HALF, POS), BF16), ((C, POS), BF16)
    halves = ((2, HALF, POS), BF16)

    def matrices(count):
        return ((count, C, HALF), BF16)


    taps_one, hat_one, params, stats_one, own_weights, partial = local_call(
        first_kernel, core, received, out=(taps, image, table, table, matrices(WBLOCKS), image)
    )
    other_weights, taps_two, hat_two, stats_two, halves_out = local_call(
        middle_kernel, core, received, swapped_one, taps_one, params, partial,
        out=(matrices(IN_CUT), taps, image, table, ((6 * HALF + C, POS), BF16)),
    )
    rows = ((SHARDS, 16, HALF), BF16)
    their_shifts = swap(halves_out)
    other_two, outputs, residual_grad, sums, normed, attended, gradients, swapping = local_call(
        attention_kernel, core, received, swapped_two, swapped_three, taps_two, params, own_weights,
        other_weights,
        out=(
            matrices(WBLOCKS - IN_CUT), rows, image, table, halves, halves, ((3, C, POS), BF16),
            ((5 * C, POS), BF16),
        ),
        scratch=(((C, 3 * C), BF16),),
    )
    theirs = swap(swapping)
    residual_grad, their_shifts = lax.optimization_barrier((residual_grad, their_shifts))
    low_one, sums = local_call(
        middle_back_kernel, core, received, own_weights, other_two, hat_two, stats_two, params,
        residual_grad, sums, out=(low, table),
    )
    their_low = swap(low_one)
    (tail,) = local_call(
        first_back_kernel, core, own_weights, other_weights, hat_one, stats_one, params, low_one,
        residual_grad, sums, out=(((SHARDS, 32, HALF), BF16),),
    )
    (late,) = local_call(
        second_grads_kernel, core, received, taps_two, normed, attended, gradients, residual_grad,
        their_shifts, theirs, out=(((SHARDS, WROWS - IN_CUT_ROWS + 16, HALF), BF16),),
    )
    (send,) = local_call(
        gather_kernel, core, taps_one, low_one, their_shifts, their_low, late, outputs, tail,
        out=(((SHARDS, OUT_ROWS, HALF), BF16),),
    )
    return send


def collect_kernel(back_ref, swished_ref, sums_ref):
    for pair in range(WROWS // 16):
        rows = slice(16 * pair, 16 * pair + 16)
        total = back_ref[0, rows, :].astype(F32)
        for image in range(1, SHARDS):
            total = total + back_ref[image, rows, :].astype(F32)
        sums_ref[rows, :] = total.astype(BF16)
    small = back_ref[:, WROWS + 32 : WROWS + 40, :].astype(F32)
    table = jnp.zeros((ROWS, HALF), F32)
    temb = jnp.zeros((ROWS, TEMB), F32)
    for image in range(SHARDS):
        values = small[image] + pltpu.roll(small[image], HALF - PART, 1)
        table = table + values
        offsets_grad = values[:, D_CONV_BIAS : D_CONV_BIAS + 1]
        owner = ORDER[image]
        temb = temb + offsets_grad * swished_ref[owner : owner + 1, :]
    lane = lax.broadcasted_iota(jnp.int32, (ROWS, HALF), 1)
    high = table.astype(BF16).astype(F32)
    low = pltpu.roll(table - high, PART, 1)
    parts = jnp.where(lane < PART, high, jnp.where(lane < 2 * PART, low, 0.0))
    blocks = [parts] + [temb[:, HALF * k : HALF * k + HALF] for k in range(TEMB // HALF)]
    blocks = blocks + [jnp.zeros((ROWS, HALF), F32)]
    for pair in range(len(blocks) // 2):
        rows = slice(WROWS + 16 * pair, WROWS + 16 * pair + 16)
        both = jnp.concatenate(blocks[2 * pair : 2 * pair + 2], axis=0)
        sums_ref[rows, :] = both.astype(BF16)


SUM_ROWS = WROWS + ROWS + TEMB * ROWS // HALF + ROWS


def collect(back, swished):
    return pl.pallas_call(
        collect_kernel,
        out_shape=jax.ShapeDtypeStruct((SUM_ROWS, HALF), BF16),
        in_specs=[pl.BlockSpec(memory_space=pltpu.VMEM)] * 2,
        out_specs=pl.BlockSpec(memory_space=pltpu.VMEM),
        compiler_params=pltpu.CompilerParams(vmem_limit_bytes=8 * 1024 * 1024),
    )(back, swished)


def images_kernel(back_ref, outputs_ref, grad_ref):
    for at, target in ((WROWS, outputs_ref), (WROWS + 16, grad_ref)):
        block = arranged(back_ref[:, at : at + 16, :].astype(F32), PLACE)
        cut = jnp.concatenate([block[:, :ROWS, :], block[:, ROWS:, :]], axis=2)
        target[...] = jnp.swapaxes(cut, 0, 1).astype(BF16)


def images(back):
    shape = jax.ShapeDtypeStruct((ROWS, SHARDS, POS), BF16)
    return pl.pallas_call(
        images_kernel,
        out_shape=(shape, shape),
        in_specs=[pl.BlockSpec(memory_space=pltpu.VMEM)],
        out_specs=(pl.BlockSpec(memory_space=pltpu.VMEM), pl.BlockSpec(memory_space=pltpu.VMEM)),
        compiler_params=pltpu.CompilerParams(vmem_limit_bytes=8 * 1024 * 1024),
    )(back)


def finish_kernel(core_ref, mine_ref, theirs_ref, *refs):
    results, scratch, sems = refs[:10], refs[10:20], refs[20]
    first_core = core_ref[0] == 0
    (gain, bias, conv_w, conv_b, temb_w, temb_b, qkv_w, qv_b, out_w, out_b) = scratch

    def weight_grad(block):
        rows = slice(ROWS * block, ROWS * block + ROWS)
        mine, theirs = mine_ref[rows, :], theirs_ref[rows, :]
        return jnp.concatenate(
            [jnp.where(first_core, mine, theirs), jnp.where(first_core, theirs, mine)], axis=1
        )

    copies = [pltpu.make_async_copy(scratch[k], results[k], sems.at[k]) for k in range(10)]
    for conv in range(2):
        for tap in range(9):
            conv_w[conv, tap, :, :] = weight_grad(SECOND_CONV * conv + tap)
    copies[2].start()
    for k in range(3):
        qkv_w[k, :, :] = weight_grad((QUERY_BLOCK, KEY_BLOCK, VALUE_BLOCK)[k])
    copies[6].start()
    out_w[...] = weight_grad(OUT_BLOCK)
    copies[8].start()
    shared = mine_ref[WROWS:, :] + theirs_ref[WROWS:, :]
    small = shared[:ROWS, :] + pltpu.roll(shared[:ROWS, :], HALF - PART, 1)
    for part in range(TEMB // HALF):
        rows = slice(ROWS + ROWS * part, 2 * ROWS + ROWS * part)
        temb_w[:, HALF * part : HALF * part + HALF] = shared[rows, :]
    copies[4].start()
    padded = jnp.concatenate([small, jnp.zeros((HALF - ROWS, HALF), F32)], axis=0)
    table = padded.T[:PART, :ROWS]
    gain[...] = table[D_GAINS : D_GAINS + 3]
    bias[...] = table[D_BIASES : D_BIASES + 3]
    conv_b[...] = table[D_CONV_BIAS : D_CONV_BIAS + 2]
    temb_b[...] = table[D_CONV_BIAS : D_CONV_BIAS + 1]
    qv_b[...] = table[D_QV_BIAS : D_QV_BIAS + 2]
    out_b[...] = table[D_OUT_BIAS : D_OUT_BIAS + 1]
    for k in (0, 1, 3, 5, 7, 9):
        copies[k].start()
    for copy in copies:
        copy.wait()


def finish(core, mine, theirs):
    shapes = [
        (3, ROWS), (3, ROWS), (2, 9, ROWS, C), (2, ROWS), (ROWS, TEMB), (1, ROWS),
        (3, ROWS, C), (2, ROWS), (ROWS, C), (1, ROWS),
    ]
    return pl.pallas_call(
        finish_kernel,
        out_shape=[jax.ShapeDtypeStruct(shape, F32) for shape in shapes],
        in_specs=[
            pl.BlockSpec(memory_space=pltpu.SMEM),
            pl.BlockSpec(memory_space=pltpu.VMEM),
            pl.BlockSpec(memory_space=pltpu.VMEM),
        ],
        out_specs=[pl.BlockSpec(memory_space=pltpu.HBM) for _ in shapes],
        scratch_shapes=[pltpu.VMEM(shape, F32) for shape in shapes]
        + [pltpu.SemaphoreType.DMA((10,))],
        compiler_params=pltpu.CompilerParams(vmem_limit_bytes=8 * 1024 * 1024),
    )(core, mine, theirs)


def prepare_kernel(core_ref, *refs):
    count = PREPARE_ARRAYS
    arrays, (send_ref, swished_ref) = refs[:count], refs[count : count + 2]
    held, (angles, sems) = refs[count + 2 : 2 * count + 2], refs[2 * count + 2 :]
    (
        steps_ref, gain_ref, bias_ref, conv_bias_ref, qv_ref, out_bias_ref, temb_bias_ref,
        temb_ref, conv_ref, qkv_ref, out_ref, inputs_ref, mask_ref, cotangent_ref,
    ) = held
    copies = [pltpu.make_async_copy(arrays[k], held[k], sems.at[k]) for k in range(count)]
    for copy in copies:
        copy.start()
    first_core = core_ref[0] == 0
    for copy in copies[:8]:
        copy.wait()

    half_dim = TEMB // 2
    index = lax.broadcasted_iota(jnp.int32, (1, half_dim), 1).astype(F32)
    rates = jnp.exp(-math.log(10000.0) * index / (half_dim - 1))
    for image in range(SHARDS):
        angles[image : image + 1, :] = rates * steps_ref[image].astype(F32)
    angle = angles[...]
    turns = jnp.floor(angle * (2.0 / math.pi) + 0.5)
    rest = angle - turns * 1.5703125
    rest = rest - turns * 4.837512969970703125e-4
    rest = rest - turns * 7.549789954891882e-8
    square = rest * rest
    sine = rest + rest * square * (
        -1.6666654611e-1 + square * (8.3321608736e-3 + square * -1.9515295891e-4)
    )
    cosine = 1.0 - 0.5 * square + square * square * (
        4.166664568298827e-2 + square * (-1.388731625493765e-3 + square * 2.443315711809948e-5)
    )
    quarter = turns.astype(jnp.int32) & 3
    odd = (quarter & 1) == 1
    sines = jnp.where(odd, cosine, sine)
    cosines = jnp.where(odd, sine, cosine)
    sines = jnp.where(quarter >= 2, -sines, sines)
    cosines = jnp.where((quarter == 1) | (quarter == 2), -cosines, cosines)
    features = jnp.concatenate([sines, cosines], axis=1)
    swished = features * sigmoid(features)
    swished_ref[...] = swished
    offsets = None
    rest = swished
    for _ in range(3):
        part = rest.astype(BF16)
        rest = rest - part.astype(F32)
        product = dot_nt(temb_ref[...], part)
        offsets = product if offsets is None else offsets + product

    rows = jnp.concatenate(
        [
            jnp.zeros((1, ROWS), F32), gain_ref[...], bias_ref[...], conv_bias_ref[...],
            qv_ref[...], out_bias_ref[...], temb_bias_ref[...], jnp.zeros((3, ROWS), F32),
        ],
        axis=0,
    )
    square = jnp.concatenate([rows] * (HALF // PART), axis=0)
    square = jnp.concatenate([square, jnp.zeros((HALF, HALF - ROWS), F32)], axis=1)
    columns = square.T[:ROWS, :]
    lane = lax.broadcasted_iota(jnp.int32, (ROWS, HALF), 1)
    offset_lane = (lane & (PART - 1)) == OFFSETS
    offsets = offsets + columns[:, TEMB_BIAS : TEMB_BIAS + 1]
    for image in range(SHARDS):
        values = jnp.where(offset_lane, offsets[:, image : image + 1], columns)
        high = values.astype(BF16).astype(F32)
        mid = (values - high).astype(BF16).astype(F32)
        low = values - high - mid
        parts = jnp.where(
            lane < PART,
            high,
            jnp.where(lane < 2 * PART, mid, jnp.where(lane < 3 * PART, low, 0.0)),
        )
        send_ref[PLACE[image], WROWS + 48 : WROWS + 56, :] = parts.astype(BF16)

    for copy in copies[8:]:
        copy.wait()

    def half(values):
        values = values.astype(F32)
        return jnp.where(first_core, values[:, :HALF], values[:, HALF:])

    shard = jnp.concatenate(
        [
            half(conv_ref[0].reshape(9 * ROWS, C)),
            half(out_ref[...]),
            half(qkv_ref[0]),
            half(qkv_ref[1]),
            half(conv_ref[1].reshape(9 * ROWS, C)),
            half(qkv_ref[2]),
        ],
        axis=0,
    ).astype(BF16)
    send_ref[:, :WROWS, :] = jnp.broadcast_to(shard[None], (SHARDS, WROWS, HALF))

    def put(at, values):
        turned = jnp.swapaxes(values.astype(F32), 0, 1)
        cut = jnp.concatenate([turned[:, :, :HALF], turned[:, :, HALF:]], axis=1)
        send_ref[:, at : at + 16, :] = arranged(cut, ORDER).astype(BF16)

    put(WROWS, inputs_ref[...])
    put(WROWS + 16, mask_ref[...])
    put(WROWS + 32, cotangent_ref[...])


PREPARE_ARRAYS = 14


def prepare(core, timesteps, *arrays):
    held = [pltpu.SMEM((SHARDS,), jnp.int32)]
    held += [pltpu.VMEM(array.shape, array.dtype) for array in arrays]
    return pl.pallas_call(
        prepare_kernel,
        out_shape=(
            jax.ShapeDtypeStruct((SHARDS, IN_ROWS, HALF), BF16),
            jax.ShapeDtypeStruct((SHARDS, TEMB), F32),
        ),
        in_specs=[pl.BlockSpec(memory_space=pltpu.SMEM)]
        + [pl.BlockSpec(memory_space=pltpu.HBM)] * PREPARE_ARRAYS,
        out_specs=(pl.BlockSpec(memory_space=pltpu.VMEM), pl.BlockSpec(memory_space=pltpu.VMEM)),
        scratch_shapes=held
        + [pltpu.VMEM((SHARDS, TEMB // 2), F32), pltpu.SemaphoreType.DMA((PREPARE_ARRAYS,))],
        compiler_params=pltpu.CompilerParams(vmem_limit_bytes=16 * 1024 * 1024),
    )(core, *[pltpu.with_memory_space_constraint(a, pltpu.HBM) for a in (timesteps, *arrays)])


def exchange(values):
    return lax.all_to_all(
        values, "ch", split_axis=0, concat_axis=0, tiled=True, axis_index_groups=[list(ORDER)]
    )


def on_device(
    inputs,
    timesteps,
    keep_mask,
    norm_gain,
    norm_bias,
    conv_weight,
    conv_bias,
    temb_weight,
    temb_bias,
    qkv_weight,
    qv_bias,
    out_weight,
    out_bias,
    cotangent,
):
    member = lax.axis_index("img")
    core = member % 2
    core_pairs = [(m, m ^ 1) for m in range(4)]
    plane_pairs = [(m, m ^ 2) for m in range(4)]
    sent, swished = prepare(
        core.reshape(1),
        timesteps,
        norm_gain,
        norm_bias,
        conv_bias,
        qv_bias,
        out_bias.reshape(1, ROWS),
        temb_bias.reshape(1, ROWS),
        temb_weight.T,
        conv_weight,
        qkv_weight,
        out_weight,
        inputs,
        keep_mask,
        cotangent,
    )
    received = exchange(sent)
    send = run_block(
        core.reshape(1), received, lambda values: lax.ppermute(values, "img", core_pairs)
    )
    back = exchange(send)

    sums = collect(back, swished)
    plane = lax.ppermute(sums, "img", plane_pairs)
    outputs, input_grad = images(back)
    plane, outputs, input_grad = lax.optimization_barrier((plane, outputs, input_grad))
    sums = sums.astype(F32) + plane.astype(F32)
    theirs = lax.ppermute(sums, "img", core_pairs)
    (gain, bias, conv_w, conv_b, temb_w, temb_b, qkv_w, qv_b, out_w, out_b) = finish(
        core.reshape(1), sums, theirs
    )
    return (
        outputs,
        input_grad,
        gain,
        bias,
        conv_w,
        conv_b,
        temb_w.T,
        temb_b[0],
        qkv_w,
        qv_b,
        out_w,
        out_b[0],
    )


def solution(mesh):
    placed = (
        P("ch", "img", None),
        P("img"),
        P("ch", "img", None),
        P(None, "ch"),
        P(None, "ch"),
        P(None, None, "ch", None),
        P(None, "ch"),
        P(None, "ch"),
        P("ch"),
        P(None, "ch", None),
        P(None, "ch"),
        P("ch", None),
        P("ch"),
        P("ch", "img", None),
    )
    return jax.shard_map(
        on_device,
        mesh=mesh,
        in_specs=placed,
        out_specs=(
            P("ch", "img", None),
            P("ch", "img", None),
            P(None, "ch"),
            P(None, "ch"),
            P(None, None, "ch", None),
            P(None, "ch"),
            P(None, "ch"),
            P("ch"),
            P(None, "ch", None),
            P(None, "ch"),
            P("ch", None),
            P("ch"),
        ),
        check_vma=False,
    )
```

```python
import functools
import math

import jax
import jax.numpy as jnp
from jax import lax
from jax.experimental import pallas as pl
from jax.experimental.pallas import tpu as pltpu
from jax.sharding import PartitionSpec as P

C = 256
TEMB = 512
SIDE = 16
POS = 256
SHARDS = 32
ROWS = C // SHARDS
HALF = 128
WBLOCKS = 22
WROWS = WBLOCKS * ROWS
FARTHEST = 22
ORDER = tuple((FARTHEST + k) % SHARDS for k in range(SHARDS))
PLACE = tuple(ORDER.index(k) for k in range(SHARDS))
NORM_EPS = 1e-06
GROUP_SIZE = ROWS * POS
F32 = jnp.float32
BF16 = jnp.bfloat16

OFFSETS, GAINS, BIASES, CONV_BIAS, QV_BIAS, OUT_BIAS, TEMB_BIAS = 0, 1, 4, 7, 9, 11, 12
D_GAINS, D_BIASES, D_CONV_BIAS, D_QV_BIAS, D_OUT_BIAS = 0, 3, 6, 8, 10
PART = 16


def arranged(values, order):
    return jnp.concatenate([values[k : k + 1] for k in order], axis=0)


def dot_nn(a, b):
    return lax.dot_general(a, b, (((1,), (0,)), ((), ())), preferred_element_type=F32)


def dot_nt(a, b):
    return lax.dot_general(a, b, (((1,), (1,)), ((), ())), preferred_element_type=F32)


def dot_tn(a, b):
    return lax.dot_general(a, b, (((0,), (0,)), ((), ())), preferred_element_type=F32)


def group_sum(values):
    column = jnp.sum(values, axis=1, keepdims=True)
    return group_column(column)


def group_column(column):
    grouped = column.reshape(SHARDS, ROWS, 1)
    total = jnp.sum(grouped, axis=1, keepdims=True)
    return jnp.broadcast_to(total, grouped.shape).reshape(C, 1)


def norm_hat(values):
    average = group_sum(values) * (1.0 / GROUP_SIZE)
    centered = values - average
    spread = group_sum(centered * centered) * (1.0 / GROUP_SIZE)
    inverse = lax.rsqrt(spread + NORM_EPS)
    return centered * inverse, inverse


def norm_back(hat, inverse, grad_out, gain):
    gain_grad = jnp.sum(grad_out * hat, axis=1, keepdims=True)
    bias_grad = jnp.sum(grad_out, axis=1, keepdims=True)
    first_mean = group_column(bias_grad * gain) * (1.0 / GROUP_SIZE)
    second_mean = group_column(gain_grad * gain) * (1.0 / GROUP_SIZE)
    grad_in = inverse * (grad_out * gain - first_mean - hat * second_mean)
    return grad_in, gain_grad, bias_grad


def sigmoid(values):
    return 0.5 + 0.5 * jnp.tanh(0.5 * values)


def rolled(values, steps, axis):
    return pltpu.roll(values, steps % POS, axis)


def column_shifted(values, step, axis):
    shape = (1, POS) if axis == 1 else (POS, POS)
    cell = (lax.broadcasted_iota(jnp.int32, shape, axis) & (SIDE - 1)) + step
    valid = (cell >= 0) & (cell < SIDE)
    return rolled(values, -step, axis) * valid.astype(F32)


def row_shifted(values, step):
    moved = rolled(values, -step * SIDE, 1)
    lane = lax.broadcasted_iota(jnp.int32, (1, HALF), 1)
    if step > 0:
        edge = jnp.where(lane < HALF - SIDE, moved[:, HALF:], 0.0)
        return jnp.concatenate([moved[:, :HALF], edge], axis=1)
    edge = jnp.where(lane >= SIDE, moved[:, :HALF], 0.0)
    return jnp.concatenate([edge, moved[:, HALF:]], axis=1)


def store_matrices(ref, target, first, count):
    for pair in range(count // 2):
        rows = arranged(ref[:, 16 * pair : 16 * pair + 16, :].astype(F32), PLACE)
        for part in range(2):
            cut = rows[:, ROWS * part : ROWS * part + ROWS, :]
            target[first + 2 * pair + part, :, :] = cut.reshape(C, HALF).astype(BF16)


def matrix(own, other, block, first_other):
    return jnp.concatenate([own[block], other[block - first_other]], axis=1)


def own_first(ref, core):
    halves = [ref[core], ref[1 - core]]
    return jnp.concatenate([half.reshape(-1, POS) for half in halves], axis=0)


def in_order(values, core):
    top, bottom = values[:HALF], values[HALF:]
    first = core == 0
    return jnp.concatenate(
        [jnp.where(first, top, bottom), jnp.where(first, bottom, top)], axis=0
    )


def load_image(ref, at):
    block = arranged(ref[:, at : at + 16, :].astype(F32), PLACE)
    left = block[:, 0:ROWS, :].reshape(C, HALF)
    right = block[:, ROWS : 2 * ROWS, :].reshape(C, HALF)
    return jnp.concatenate([left, right], axis=1)


def image_rows(values):
    left = values[:, 0:HALF].reshape(SHARDS, ROWS, HALF)
    right = values[:, HALF:C].reshape(SHARDS, ROWS, HALF)
    return jnp.concatenate([left, right], axis=1).astype(BF16)


def store_shifts(target, values):
    for step in (-1, 0, 1):
        moved = (column_shifted(values, step, 1) if step else values).astype(BF16)
        target[0, step + 1, :, :] = moved[:HALF]
        target[1, step + 1, :, :] = moved[HALF:]


def half_convolve(matrices, shifts):
    operand = shifts.reshape(3 * HALF, POS)
    total = None
    for row in (0, -1, 1):
        product = dot_nn(jnp.concatenate(matrices[3 * row + 3 : 3 * row + 6], axis=1), operand)
        total = product if row == 0 else total + row_shifted(product, row)
    return total


def convolve(matrices, shifts, core):
    operand = [shifts[half, step] for step in range(3) for half in (core, 1 - core)]
    operand = jnp.concatenate(operand, axis=0)
    total = None
    for row in (0, -1, 1):
        product = dot_nn(jnp.concatenate(matrices[3 * row + 3 : 3 * row + 6], axis=1), operand)
        total = product if row == 0 else total + row_shifted(product, row)
    return total


def convolve_back(matrices, low, core):
    turned = low.T
    edge = jnp.zeros((SIDE, C), BF16)
    stacked = jnp.concatenate(
        [
            jnp.concatenate([turned[SIDE:], edge], axis=0),
            turned,
            jnp.concatenate([edge, turned[:-SIDE]], axis=0),
        ],
        axis=1,
    )
    total = None
    for step in (0, -1, 1):
        product = dot_nn(stacked, jnp.concatenate(matrices[step + 1 :: 3], axis=0))
        total = product if step == 0 else total + column_shifted(product, -step, 0)
    return in_order(total.T, core)


def lane_blocks(product):
    count = product.shape[1] // HALF
    cut = [product[:, HALF * k : HALF * k + HALF] for k in range(count)]
    return [values.reshape(SHARDS, ROWS, HALF) for values in cut]


def conv_weight_grads(lows, shifts):
    wide = [part.reshape(3 * HALF, POS) for part in shifts]
    rows = []
    for row in (-1, 0, 1):
        moved = [row_shifted(part.astype(F32), row).astype(BF16) if row else part for part in wide]
        rows.append(jnp.concatenate(moved, axis=1))
    return lane_blocks(dot_nt(jnp.concatenate(lows, axis=1), jnp.concatenate(rows, axis=0)))


def image_weight_grads(low, shifts):
    part = shifts.reshape(3 * HALF, POS)
    rows = [row_shifted(part.astype(F32), row).astype(BF16) if row else part for row in (-1, 0, 1)]
    return dot_nt(low, jnp.concatenate(rows, axis=0))


def store_blocks(target, blocks, order=range(SHARDS)):
    for pair in range(len(blocks) // 2):
        rows = jnp.concatenate(blocks[2 * pair : 2 * pair + 2], axis=1)
        target[:, 16 * pair : 16 * pair + 16, :] = arranged(rows, order).astype(BF16)


def columns_of(listed, table):
    lane = lax.broadcasted_iota(jnp.int32, (C, HALF), 1)
    for k, column in listed.items():
        table = jnp.where(lane == k, column, table)
    return table


def column(ref, lane):
    return ref[:, lane : lane + 1]


def by_rows(dot, left, right):
    return jnp.concatenate([dot(left[:HALF], right), dot(left[HALF:], right)], axis=0)


def row_sum(values):
    return jnp.sum(values, axis=1, keepdims=True)


def slope(values):
    sigma = sigmoid(values)
    return sigma * (1.0 + values * (1.0 - sigma))


def first_kernel(core_ref, recv_ref, taps_ref, hat_ref, params_ref, stats_ref, own_ref, partial_ref):
    columns = recv_ref[:, AT_PARAMS : AT_PARAMS + ROWS, :].astype(F32)
    columns = arranged(columns, PLACE).reshape(C, HALF)
    columns = (
        columns
        + pltpu.roll(columns, HALF - PART, 1)
        + pltpu.roll(columns, HALF - 2 * PART, 1)
    )
    params_ref[...] = columns
    hat, inverse = norm_hat(load_image(recv_ref, AT_SOURCE))
    hat_ref[...] = hat
    stats_ref[...] = jnp.broadcast_to(inverse, (C, HALF))
    pre = hat * columns[:, GAINS : GAINS + 1] + columns[:, BIASES : BIASES + 1]
    store_shifts(taps_ref, (pre * sigmoid(pre)).astype(BF16).astype(F32))
    store_matrices(recv_ref, own_ref, 0, WBLOCKS)
    partial_ref[...] = half_convolve([own_ref[tap] for tap in range(9)], taps_ref[core_ref[0]])


def middle_kernel(
    core_ref, recv_ref, swapped, taps_one, params, partial,
    other, taps_ref, hat_ref, stats_ref, halves_ref,
):
    store_matrices(swapped, other, 0, IN_CUT)
    rest = half_convolve([other[tap] for tap in range(9)], taps_one[1 - core_ref[0]])
    middle = partial[...] + rest
    middle = middle + (column(params, CONV_BIAS) + column(params, OFFSETS))
    hat, inverse = norm_hat(middle)
    hat_ref[...] = hat
    stats_ref[...] = jnp.broadcast_to(inverse, (C, HALF))
    pre = hat * column(params, GAINS + 1) + column(params, BIASES + 1)
    keep = load_image(recv_ref, AT_KEEP) * (1.0 / 0.9)
    store_shifts(taps_ref, (pre * sigmoid(pre) * keep).astype(BF16).astype(F32))
    away = 1 - core_ref[0]
    halves_ref[0 : 3 * HALF, :] = taps_one[away].reshape(3 * HALF, POS)
    halves_ref[3 * HALF : 6 * HALF, :] = taps_ref[away].reshape(3 * HALF, POS)
    halves_ref[6 * HALF :, :] = load_image(recv_ref, AT_COTANGENT).astype(BF16)


def attention_kernel(
    core_ref, recv_ref, swapped_two, swapped_three, taps_two, params, own, other_one,
    other, outputs_ref, grad_ref, sums_ref, normed_ref, halves_ref, grads_ref, swap_ref, turned,
):
    core = core_ref[0]
    half = (WBLOCKS - IN_CUT) // 2
    store_matrices(swapped_two, other, 0, half)
    store_matrices(swapped_three, other, half, half)
    out_matrix = matrix(own, other_one, OUT_BLOCK, 0)
    qkv = [
        matrix(own, other, QUERY_BLOCK, IN_CUT),
        matrix(own, other, KEY_BLOCK, IN_CUT),
        matrix(own, other, VALUE_BLOCK, IN_CUT),
    ]
    for k in range(3):
        turned[:, C * k : C * k + C] = qkv[k].T
    cotangent = load_image(recv_ref, AT_COTANGENT)
    cot_low = cotangent.astype(BF16)
    attended_grad = in_order(dot_tn(out_matrix, cot_low), core).astype(BF16)
    source = load_image(recv_ref, AT_SOURCE)
    matrices = [matrix(own, other, SECOND_CONV + tap, IN_CUT) for tap in range(9)]
    residual = source + convolve(matrices, taps_two, core) + column(params, CONV_BIAS + 1)
    hat, inverse = norm_hat(residual)
    normed = (hat * column(params, GAINS + 2) + column(params, BIASES + 2)).astype(BF16)
    scale = C ** (-0.5)
    normed_ref[0] = normed[:HALF]
    normed_ref[1] = normed[HALF:]
    operand = own_first(normed_ref, core)
    queries = (by_rows(dot_nn, qkv[0], operand) + column(params, QV_BIAS)).astype(BF16)
    keys = by_rows(dot_nn, qkv[1], operand).astype(BF16)
    vals = (by_rows(dot_nn, qkv[2], operand) + column(params, QV_BIAS + 1)).astype(BF16)
    scores = dot_tn(queries, keys) * scale
    dprobs = dot_tn(attended_grad, vals)
    exps = jnp.exp(scores - jnp.max(scores, axis=1, keepdims=True))
    probs = exps / row_sum(exps)
    probs_low = probs.astype(BF16)
    dscores = (probs * (dprobs - row_sum(probs * dprobs))).astype(BF16)
    query_grad = (by_rows(dot_nt, keys, dscores) * scale).astype(BF16)
    key_grad = (by_rows(dot_nn, queries, dscores) * scale).astype(BF16)
    value_grad = by_rows(dot_nn, attended_grad, probs_low).astype(BF16)
    grads = jnp.concatenate([query_grad, key_grad, value_grad], axis=0)
    normed_grad = by_rows(dot_nn, turned, grads)
    normed_grad = in_order(normed_grad, core)
    for k, gradient in enumerate((query_grad, key_grad, value_grad)):
        grads_ref[k, :, :] = gradient
    attended = by_rows(dot_nt, vals, probs_low).astype(BF16)
    halves_ref[0] = attended[:HALF]
    halves_ref[1] = attended[HALF:]
    product = by_rows(dot_nn, out_matrix, own_first(halves_ref, core))
    outputs = residual + product + column(params, OUT_BIAS)
    outputs_ref[...] = image_rows(outputs)
    branch, gain_grad, bias_grad = norm_back(hat, inverse, normed_grad, column(params, GAINS + 2))
    residual_grad = cotangent + branch
    grad_ref[...] = residual_grad
    swap_ref[0:HALF, :] = normed_ref[1 - core]
    swap_ref[HALF:C, :] = halves_ref[1 - core]
    swap_ref[C : 2 * C, :] = residual_grad.astype(BF16)
    for k, gradient in enumerate((query_grad, key_grad, value_grad)):
        swap_ref[C * k + 2 * C : C * k + 3 * C, :] = gradient
    listed = {
        D_GAINS + 2: gain_grad,
        D_BIASES + 2: bias_grad,
        D_CONV_BIAS + 1: row_sum(residual_grad),
        D_QV_BIAS: row_sum(query_grad.astype(F32)),
        D_QV_BIAS + 1: row_sum(value_grad.astype(F32)),
        D_OUT_BIAS: row_sum(cotangent),
    }
    sums_ref[...] = columns_of(listed, jnp.zeros((C, HALF), F32))


def middle_back_kernel(
    core_ref, recv_ref, own, other, hat_ref, stats, params, grad_ref, sums, low_ref, sums_ref
):
    hat = hat_ref[...]
    gain = column(params, GAINS + 1)
    pre = hat * gain + column(params, BIASES + 1)
    keep = load_image(recv_ref, AT_KEEP) * (1.0 / 0.9)
    factor = keep * slope(pre)
    matrices = [matrix(own, other, SECOND_CONV + tap, IN_CUT) for tap in range(9)]
    second_grad = convolve_back(matrices, grad_ref[...].astype(BF16), core_ref[0])
    pre_grad = second_grad * factor
    middle_grad, gain_grad, bias_grad = norm_back(hat, column(stats, 0), pre_grad, gain)
    low_ref[...] = middle_grad.astype(BF16)
    listed = {D_GAINS + 1: gain_grad, D_BIASES + 1: bias_grad, D_CONV_BIAS: row_sum(middle_grad)}
    sums_ref[...] = columns_of(listed, sums[...])


def first_back_kernel(
    core_ref, own, other, hat_ref, stats, params, low_ref, grad_ref, sums, taps_two,
    tail_ref, partial_ref,
):
    hat = hat_ref[...]
    gain = column(params, GAINS)
    pre = hat * gain + column(params, BIASES)
    factor = slope(pre)
    matrices = [matrix(own, other, tap, 0) for tap in range(9)]
    first_grad = convolve_back(matrices, low_ref[...], core_ref[0])
    branch, gain_grad, bias_grad = norm_back(hat, column(stats, 0), first_grad * factor, gain)
    tail_ref[:, :16, :] = image_rows(grad_ref[...] + branch)
    partial_ref[...] = image_weight_grads(grad_ref[...].astype(BF16), taps_two[core_ref[0]])

    table = columns_of({D_GAINS: gain_grad, D_BIASES: bias_grad}, sums[...])
    high = table.astype(BF16).astype(F32)
    low = pltpu.roll(table - high, PART, 1)
    lane = lax.broadcasted_iota(jnp.int32, (C, HALF), 1)
    table = jnp.where(lane < PART, high, low).reshape(SHARDS, ROWS, HALF)
    tail_ref[:, 16:, :] = jnp.concatenate([table, jnp.zeros_like(table)], axis=1).astype(BF16)


def second_grads_kernel(
    core_ref, recv_ref, partial, normed, attended, gradients, their_shifts, theirs, late_ref
):
    core = core_ref[0]
    product = image_weight_grads(theirs[C : 2 * C, :], their_shifts[3 * HALF : 6 * HALF, :])
    second = lane_blocks(partial[...] + product)
    operand = jnp.concatenate([normed[core], theirs[0:HALF, :]], axis=1)
    grads = jnp.concatenate([gradients[...].reshape(3 * C, POS), theirs[2 * C :, :]], axis=1)
    qkv = dot_nt(grads, operand)
    query, key, value = [lane_blocks(qkv[C * k : C * k + C])[0] for k in range(3)]
    operand = jnp.concatenate([attended[core], theirs[HALF:C, :]], axis=1)
    cotangent = load_image(recv_ref, AT_COTANGENT).astype(BF16)
    cotangents = jnp.concatenate([cotangent, their_shifts[6 * HALF :, :]], axis=1)
    out = lane_blocks(dot_nt(cotangents, operand))[0]
    store_blocks(late_ref, [query, key, *second, value, out, jnp.zeros_like(out)])


def gather_kernel(
    core_ref, taps_one, low_ref, their_shifts, their_low, late, outputs, tail, send_ref
):
    first = conv_weight_grads(
        [low_ref[...], their_low[...]], [taps_one[core_ref[0]], their_shifts[0 : 3 * HALF, :]]
    )
    cut = WROWS - IN_CUT_ROWS
    out = late[:, cut : cut + 16, :].astype(F32)[:, :ROWS, :]
    store_blocks(send_ref, first + [out], ORDER)
    send_ref[:, IN_CUT_ROWS:WROWS, :] = arranged(late[:, :cut, :], ORDER)
    send_ref[:, WROWS : WROWS + 16, :] = arranged(outputs[...], ORDER)
    send_ref[:, WROWS + 16 : WROWS + 40, :] = arranged(tail[:, :24, :], ORDER)


AT_SOURCE, AT_KEEP, AT_COTANGENT, AT_PARAMS = WROWS, WROWS + 16, WROWS + 32, WROWS + 48
IN_ROWS = WROWS + 56
OUT_ROWS = WROWS + 40
OUT_BLOCK, QUERY_BLOCK, KEY_BLOCK, SECOND_CONV, VALUE_BLOCK = 9, 10, 11, 12, 21
IN_CUT = 10
IN_CUT_ROWS = IN_CUT * ROWS


def local_call(kernel, core, *operands, out, scratch=()):
    in_specs = [pl.BlockSpec(memory_space=pltpu.VMEM) for _ in operands]
    if core is not None:
        in_specs = [pl.BlockSpec(memory_space=pltpu.SMEM)] + in_specs
        operands = (core, *operands)
    shapes = tuple(jax.ShapeDtypeStruct(shape, dtype) for shape, dtype in out)
    return pl.pallas_call(
        kernel,
        out_shape=shapes,
        in_specs=in_specs,
        out_specs=tuple(pl.BlockSpec(memory_space=pltpu.VMEM) for _ in out),
        scratch_shapes=[pltpu.VMEM(shape, dtype) for shape, dtype in scratch],
        compiler_params=pltpu.CompilerParams(vmem_limit_bytes=VMEM_LIMIT),
    )(*operands)


VMEM_LIMIT = 24 * 1024 * 1024


def run_block(core, received, swap):
    swapped_one = swap(received[:, :IN_CUT_ROWS])
    middle_row = (IN_CUT_ROWS + WROWS) // 2
    swapped_two = swap(received[:, IN_CUT_ROWS:middle_row])
    swapped_three = swap(received[:, middle_row:WROWS])
    image, table = ((C, POS), F32), ((C, HALF), F32)
    taps, low = ((2, 3, HALF, POS), BF16), ((C, POS), BF16)
    halves = ((2, HALF, POS), BF16)

    def matrices(count):
        return ((count, C, HALF), BF16)


    taps_one, hat_one, params, stats_one, own_weights, partial = local_call(
        first_kernel, core, received, out=(taps, image, table, table, matrices(WBLOCKS), image)
    )
    other_weights, taps_two, hat_two, stats_two, halves_out = local_call(
        middle_kernel, core, received, swapped_one, taps_one, params, partial,
        out=(matrices(IN_CUT), taps, image, table, ((6 * HALF + C, POS), BF16)),
    )
    rows = ((SHARDS, 16, HALF), BF16)
    their_shifts = swap(halves_out)
    other_two, outputs, residual_grad, sums, normed, attended, gradients, swapping = local_call(
        attention_kernel, core, received, swapped_two, swapped_three, taps_two, params, own_weights,
        other_weights,
        out=(
            matrices(WBLOCKS - IN_CUT), rows, image, table, halves, halves, ((3, C, POS), BF16),
            ((5 * C, POS), BF16),
        ),
        scratch=(((C, 3 * C), BF16),),
    )
    theirs = swap(swapping)
    residual_grad, their_shifts = lax.optimization_barrier((residual_grad, their_shifts))
    low_one, sums = local_call(
        middle_back_kernel, core, received, own_weights, other_two, hat_two, stats_two, params,
        residual_grad, sums, out=(low, table),
    )
    their_low = swap(low_one)
    tail, partial = local_call(
        first_back_kernel, core, own_weights, other_weights, hat_one, stats_one, params, low_one,
        residual_grad, sums, taps_two, out=(((SHARDS, 32, HALF), BF16), ((C, 9 * HALF), F32)),
    )
    (late,) = local_call(
        second_grads_kernel, core, received, partial, normed, attended, gradients,
        their_shifts, theirs, out=(((SHARDS, WROWS - IN_CUT_ROWS + 16, HALF), BF16),),
    )
    (send,) = local_call(
        gather_kernel, core, taps_one, low_one, their_shifts, their_low, late, outputs, tail,
        out=(((SHARDS, OUT_ROWS, HALF), BF16),),
    )
    return send


def collect_kernel(back_ref, swished_ref, sums_ref):
    for pair in range(WROWS // 16):
        rows = slice(16 * pair, 16 * pair + 16)
        total = back_ref[0, rows, :].astype(F32)
        for image in range(1, SHARDS):
            total = total + back_ref[image, rows, :].astype(F32)
        sums_ref[rows, :] = total.astype(BF16)
    small = back_ref[:, WROWS + 32 : WROWS + 40, :].astype(F32)
    table = jnp.zeros((ROWS, HALF), F32)
    temb = jnp.zeros((ROWS, TEMB), F32)
    for image in range(SHARDS):
        values = small[image] + pltpu.roll(small[image], HALF - PART, 1)
        table = table + values
        offsets_grad = values[:, D_CONV_BIAS : D_CONV_BIAS + 1]
        owner = ORDER[image]
        temb = temb + offsets_grad * swished_ref[owner : owner + 1, :]
    lane = lax.broadcasted_iota(jnp.int32, (ROWS, HALF), 1)
    high = table.astype(BF16).astype(F32)
    low = pltpu.roll(table - high, PART, 1)
    parts = jnp.where(lane < PART, high, jnp.where(lane < 2 * PART, low, 0.0))
    blocks = [parts] + [temb[:, HALF * k : HALF * k + HALF] for k in range(TEMB // HALF)]
    blocks = blocks + [jnp.zeros((ROWS, HALF), F32)]
    for pair in range(len(blocks) // 2):
        rows = slice(WROWS + 16 * pair, WROWS + 16 * pair + 16)
        both = jnp.concatenate(blocks[2 * pair : 2 * pair + 2], axis=0)
        sums_ref[rows, :] = both.astype(BF16)


SUM_ROWS = WROWS + ROWS + TEMB * ROWS // HALF + ROWS


def collect(back, swished):
    return pl.pallas_call(
        collect_kernel,
        out_shape=jax.ShapeDtypeStruct((SUM_ROWS, HALF), BF16),
        in_specs=[pl.BlockSpec(memory_space=pltpu.VMEM)] * 2,
        out_specs=pl.BlockSpec(memory_space=pltpu.VMEM),
        compiler_params=pltpu.CompilerParams(vmem_limit_bytes=8 * 1024 * 1024),
    )(back, swished)


def images_kernel(back_ref, outputs_ref, grad_ref):
    for at, target in ((WROWS, outputs_ref), (WROWS + 16, grad_ref)):
        block = arranged(back_ref[:, at : at + 16, :].astype(F32), PLACE)
        cut = jnp.concatenate([block[:, :ROWS, :], block[:, ROWS:, :]], axis=2)
        target[...] = jnp.swapaxes(cut, 0, 1).astype(BF16)


def images(back):
    shape = jax.ShapeDtypeStruct((ROWS, SHARDS, POS), BF16)
    return pl.pallas_call(
        images_kernel,
        out_shape=(shape, shape),
        in_specs=[pl.BlockSpec(memory_space=pltpu.VMEM)],
        out_specs=(pl.BlockSpec(memory_space=pltpu.VMEM), pl.BlockSpec(memory_space=pltpu.VMEM)),
        compiler_params=pltpu.CompilerParams(vmem_limit_bytes=8 * 1024 * 1024),
    )(back)


def finish_kernel(core_ref, mine_ref, theirs_ref, *refs):
    results, scratch, sems = refs[:10], refs[10:20], refs[20]
    first_core = core_ref[0] == 0
    (gain, bias, conv_w, conv_b, temb_w, temb_b, qkv_w, qv_b, out_w, out_b) = scratch

    def weight_grad(block):
        rows = slice(ROWS * block, ROWS * block + ROWS)
        mine, theirs = mine_ref[rows, :], theirs_ref[rows, :]
        return jnp.concatenate(
            [jnp.where(first_core, mine, theirs), jnp.where(first_core, theirs, mine)], axis=1
        )

    copies = [pltpu.make_async_copy(scratch[k], results[k], sems.at[k]) for k in range(10)]
    for conv in range(2):
        for tap in range(9):
            conv_w[conv, tap, :, :] = weight_grad(SECOND_CONV * conv + tap)
    copies[2].start()
    for k in range(3):
        qkv_w[k, :, :] = weight_grad((QUERY_BLOCK, KEY_BLOCK, VALUE_BLOCK)[k])
    copies[6].start()
    out_w[...] = weight_grad(OUT_BLOCK)
    copies[8].start()
    shared = mine_ref[WROWS:, :] + theirs_ref[WROWS:, :]
    small = shared[:ROWS, :] + pltpu.roll(shared[:ROWS, :], HALF - PART, 1)
    for part in range(TEMB // HALF):
        rows = slice(ROWS + ROWS * part, 2 * ROWS + ROWS * part)
        temb_w[:, HALF * part : HALF * part + HALF] = shared[rows, :]
    copies[4].start()
    padded = jnp.concatenate([small, jnp.zeros((HALF - ROWS, HALF), F32)], axis=0)
    table = padded.T[:PART, :ROWS]
    gain[...] = table[D_GAINS : D_GAINS + 3]
    bias[...] = table[D_BIASES : D_BIASES + 3]
    conv_b[...] = table[D_CONV_BIAS : D_CONV_BIAS + 2]
    temb_b[...] = table[D_CONV_BIAS : D_CONV_BIAS + 1]
    qv_b[...] = table[D_QV_BIAS : D_QV_BIAS + 2]
    out_b[...] = table[D_OUT_BIAS : D_OUT_BIAS + 1]
    for k in (0, 1, 3, 5, 7, 9):
        copies[k].start()
    for copy in copies:
        copy.wait()


def finish(core, mine, theirs):
    shapes = [
        (3, ROWS), (3, ROWS), (2, 9, ROWS, C), (2, ROWS), (ROWS, TEMB), (1, ROWS),
        (3, ROWS, C), (2, ROWS), (ROWS, C), (1, ROWS),
    ]
    return pl.pallas_call(
        finish_kernel,
        out_shape=[jax.ShapeDtypeStruct(shape, F32) for shape in shapes],
        in_specs=[
            pl.BlockSpec(memory_space=pltpu.SMEM),
            pl.BlockSpec(memory_space=pltpu.VMEM),
            pl.BlockSpec(memory_space=pltpu.VMEM),
        ],
        out_specs=[pl.BlockSpec(memory_space=pltpu.HBM) for _ in shapes],
        scratch_shapes=[pltpu.VMEM(shape, F32) for shape in shapes]
        + [pltpu.SemaphoreType.DMA((10,))],
        compiler_params=pltpu.CompilerParams(vmem_limit_bytes=8 * 1024 * 1024),
    )(core, mine, theirs)


def prepare_kernel(core_ref, *refs):
    count = PREPARE_ARRAYS
    arrays, (send_ref, swished_ref) = refs[:count], refs[count : count + 2]
    held, (angles, sems) = refs[count + 2 : 2 * count + 2], refs[2 * count + 2 :]
    (
        steps_ref, gain_ref, bias_ref, conv_bias_ref, qv_ref, out_bias_ref, temb_bias_ref,
        temb_ref, conv_ref, qkv_ref, out_ref, inputs_ref, mask_ref, cotangent_ref,
    ) = held
    copies = [pltpu.make_async_copy(arrays[k], held[k], sems.at[k]) for k in range(count)]
    for copy in copies:
        copy.start()
    first_core = core_ref[0] == 0
    for copy in copies[:8]:
        copy.wait()

    half_dim = TEMB // 2
    index = lax.broadcasted_iota(jnp.int32, (1, half_dim), 1).astype(F32)
    rates = jnp.exp(-math.log(10000.0) * index / (half_dim - 1))
    for image in range(SHARDS):
        angles[image : image + 1, :] = rates * steps_ref[image].astype(F32)
    angle = angles[...]
    turns = jnp.floor(angle * (2.0 / math.pi) + 0.5)
    rest = angle - turns * 1.5703125
    rest = rest - turns * 4.837512969970703125e-4
    rest = rest - turns * 7.549789954891882e-8
    square = rest * rest
    sine = rest + rest * square * (
        -1.6666654611e-1 + square * (8.3321608736e-3 + square * -1.9515295891e-4)
    )
    cosine = 1.0 - 0.5 * square + square * square * (
        4.166664568298827e-2 + square * (-1.388731625493765e-3 + square * 2.443315711809948e-5)
    )
    quarter = turns.astype(jnp.int32) & 3
    odd = (quarter & 1) == 1
    sines = jnp.where(odd, cosine, sine)
    cosines = jnp.where(odd, sine, cosine)
    sines = jnp.where(quarter >= 2, -sines, sines)
    cosines = jnp.where((quarter == 1) | (quarter == 2), -cosines, cosines)
    features = jnp.concatenate([sines, cosines], axis=1)
    swished = features * sigmoid(features)
    swished_ref[...] = swished
    offsets = None
    rest = swished
    for _ in range(3):
        part = rest.astype(BF16)
        rest = rest - part.astype(F32)
        product = dot_nt(temb_ref[...], part)
        offsets = product if offsets is None else offsets + product

    rows = jnp.concatenate(
        [
            jnp.zeros((1, ROWS), F32), gain_ref[...], bias_ref[...], conv_bias_ref[...],
            qv_ref[...], out_bias_ref[...], temb_bias_ref[...], jnp.zeros((3, ROWS), F32),
        ],
        axis=0,
    )
    square = jnp.concatenate([rows] * (HALF // PART), axis=0)
    square = jnp.concatenate([square, jnp.zeros((HALF, HALF - ROWS), F32)], axis=1)
    columns = square.T[:ROWS, :]
    lane = lax.broadcasted_iota(jnp.int32, (ROWS, HALF), 1)
    offset_lane = (lane & (PART - 1)) == OFFSETS
    offsets = offsets + columns[:, TEMB_BIAS : TEMB_BIAS + 1]
    for image in range(SHARDS):
        values = jnp.where(offset_lane, offsets[:, image : image + 1], columns)
        high = values.astype(BF16).astype(F32)
        mid = (values - high).astype(BF16).astype(F32)
        low = values - high - mid
        parts = jnp.where(
            lane < PART,
            high,
            jnp.where(lane < 2 * PART, mid, jnp.where(lane < 3 * PART, low, 0.0)),
        )
        send_ref[PLACE[image], WROWS + 48 : WROWS + 56, :] = parts.astype(BF16)

    for copy in copies[8:]:
        copy.wait()

    def half(values):
        values = values.astype(F32)
        return jnp.where(first_core, values[:, :HALF], values[:, HALF:])

    shard = jnp.concatenate(
        [
            half(conv_ref[0].reshape(9 * ROWS, C)),
            half(out_ref[...]),
            half(qkv_ref[0]),
            half(qkv_ref[1]),
            half(conv_ref[1].reshape(9 * ROWS, C)),
            half(qkv_ref[2]),
        ],
        axis=0,
    ).astype(BF16)
    send_ref[:, :WROWS, :] = jnp.broadcast_to(shard[None], (SHARDS, WROWS, HALF))

    def put(at, values):
        turned = jnp.swapaxes(values.astype(F32), 0, 1)
        cut = jnp.concatenate([turned[:, :, :HALF], turned[:, :, HALF:]], axis=1)
        send_ref[:, at : at + 16, :] = arranged(cut, ORDER).astype(BF16)

    put(WROWS, inputs_ref[...])
    put(WROWS + 16, mask_ref[...])
    put(WROWS + 32, cotangent_ref[...])


PREPARE_ARRAYS = 14


def prepare(core, timesteps, *arrays):
    held = [pltpu.SMEM((SHARDS,), jnp.int32)]
    held += [pltpu.VMEM(array.shape, array.dtype) for array in arrays]
    return pl.pallas_call(
        prepare_kernel,
        out_shape=(
            jax.ShapeDtypeStruct((SHARDS, IN_ROWS, HALF), BF16),
            jax.ShapeDtypeStruct((SHARDS, TEMB), F32),
        ),
        in_specs=[pl.BlockSpec(memory_space=pltpu.SMEM)]
        + [pl.BlockSpec(memory_space=pltpu.HBM)] * PREPARE_ARRAYS,
        out_specs=(pl.BlockSpec(memory_space=pltpu.VMEM), pl.BlockSpec(memory_space=pltpu.VMEM)),
        scratch_shapes=held
        + [pltpu.VMEM((SHARDS, TEMB // 2), F32), pltpu.SemaphoreType.DMA((PREPARE_ARRAYS,))],
        compiler_params=pltpu.CompilerParams(vmem_limit_bytes=16 * 1024 * 1024),
    )(core, *[pltpu.with_memory_space_constraint(a, pltpu.HBM) for a in (timesteps, *arrays)])


def exchange(values):
    return lax.all_to_all(
        values, "ch", split_axis=0, concat_axis=0, tiled=True, axis_index_groups=[list(ORDER)]
    )


def on_device(
    inputs,
    timesteps,
    keep_mask,
    norm_gain,
    norm_bias,
    conv_weight,
    conv_bias,
    temb_weight,
    temb_bias,
    qkv_weight,
    qv_bias,
    out_weight,
    out_bias,
    cotangent,
):
    member = lax.axis_index("img")
    core = member % 2
    core_pairs = [(m, m ^ 1) for m in range(4)]
    plane_pairs = [(m, m ^ 2) for m in range(4)]
    sent, swished = prepare(
        core.reshape(1),
        timesteps,
        norm_gain,
        norm_bias,
        conv_bias,
        qv_bias,
        out_bias.reshape(1, ROWS),
        temb_bias.reshape(1, ROWS),
        temb_weight.T,
        conv_weight,
        qkv_weight,
        out_weight,
        inputs,
        keep_mask,
        cotangent,
    )
    received = exchange(sent)
    send = run_block(
        core.reshape(1), received, lambda values: lax.ppermute(values, "img", core_pairs)
    )
    back = exchange(send)

    sums = collect(back, swished)
    plane = lax.ppermute(sums, "img", plane_pairs)
    outputs, input_grad = images(back)
    plane, outputs, input_grad = lax.optimization_barrier((plane, outputs, input_grad))
    sums = sums.astype(F32) + plane.astype(F32)
    theirs = lax.ppermute(sums, "img", core_pairs)
    (gain, bias, conv_w, conv_b, temb_w, temb_b, qkv_w, qv_b, out_w, out_b) = finish(
        core.reshape(1), sums, theirs
    )
    return (
        outputs,
        input_grad,
        gain,
        bias,
        conv_w,
        conv_b,
        temb_w.T,
        temb_b[0],
        qkv_w,
        qv_b,
        out_w,
        out_b[0],
    )


def solution(mesh):
    placed = (
        P("ch", "img", None),
        P("img"),
        P("ch", "img", None),
        P(None, "ch"),
        P(None, "ch"),
        P(None, None, "ch", None),
        P(None, "ch"),
        P(None, "ch"),
        P("ch"),
        P(None, "ch", None),
        P(None, "ch"),
        P("ch", None),
        P("ch"),
        P("ch", "img", None),
    )
    return jax.shard_map(
        on_device,
        mesh=mesh,
        in_specs=placed,
        out_specs=(
            P("ch", "img", None),
            P("ch", "img", None),
            P(None, "ch"),
            P(None, "ch"),
            P(None, None, "ch", None),
            P(None, "ch"),
            P(None, "ch"),
            P("ch"),
            P(None, "ch", None),
            P(None, "ch"),
            P("ch", None),
            P("ch"),
        ),
        check_vma=False,
    )
```

```python
import functools
import math

import jax
import jax.numpy as jnp
from jax import lax
from jax.experimental import pallas as pl
from jax.experimental.pallas import tpu as pltpu
from jax.sharding import PartitionSpec as P

C = 256
TEMB = 512
SIDE = 16
POS = 256
SHARDS = 32
ROWS = C // SHARDS
HALF = 128
WBLOCKS = 22
WROWS = WBLOCKS * ROWS
FARTHEST = 22
ORDER = tuple((FARTHEST + k) % SHARDS for k in range(SHARDS))
PLACE = tuple(ORDER.index(k) for k in range(SHARDS))
NORM_EPS = 1e-06
GROUP_SIZE = ROWS * POS
F32 = jnp.float32
BF16 = jnp.bfloat16

OFFSETS, GAINS, BIASES, CONV_BIAS, QV_BIAS, OUT_BIAS, TEMB_BIAS = 0, 1, 4, 7, 9, 11, 12
D_GAINS, D_BIASES, D_CONV_BIAS, D_QV_BIAS, D_OUT_BIAS = 0, 3, 6, 8, 10
PART = 16


def arranged(values, order):
    return jnp.concatenate([values[k : k + 1] for k in order], axis=0)


def dot_nn(a, b):
    return lax.dot_general(a, b, (((1,), (0,)), ((), ())), preferred_element_type=F32)


def dot_nt(a, b):
    return lax.dot_general(a, b, (((1,), (1,)), ((), ())), preferred_element_type=F32)


def dot_tn(a, b):
    return lax.dot_general(a, b, (((0,), (0,)), ((), ())), preferred_element_type=F32)


def group_sum(values):
    column = jnp.sum(values, axis=1, keepdims=True)
    return group_column(column)


def group_column(column):
    grouped = column.reshape(SHARDS, ROWS, 1)
    total = jnp.sum(grouped, axis=1, keepdims=True)
    return jnp.broadcast_to(total, grouped.shape).reshape(C, 1)


def norm_hat(values):
    average = group_sum(values) * (1.0 / GROUP_SIZE)
    centered = values - average
    spread = group_sum(centered * centered) * (1.0 / GROUP_SIZE)
    inverse = lax.rsqrt(spread + NORM_EPS)
    return centered * inverse, inverse


def norm_back(hat, inverse, grad_out, gain):
    gain_grad = jnp.sum(grad_out * hat, axis=1, keepdims=True)
    bias_grad = jnp.sum(grad_out, axis=1, keepdims=True)
    first_mean = group_column(bias_grad * gain) * (1.0 / GROUP_SIZE)
    second_mean = group_column(gain_grad * gain) * (1.0 / GROUP_SIZE)
    grad_in = inverse * (grad_out * gain - first_mean - hat * second_mean)
    return grad_in, gain_grad, bias_grad


def sigmoid(values):
    return 0.5 + 0.5 * jnp.tanh(0.5 * values)


def rolled(values, steps, axis):
    return pltpu.roll(values, steps % POS, axis)


def column_shifted(values, step, axis):
    shape = (1, POS) if axis == 1 else (POS, POS)
    cell = (lax.broadcasted_iota(jnp.int32, shape, axis) & (SIDE - 1)) + step
    valid = (cell >= 0) & (cell < SIDE)
    return rolled(values, -step, axis) * valid.astype(F32)


def row_shifted(values, step):
    moved = rolled(values, -step * SIDE, 1)
    lane = lax.broadcasted_iota(jnp.int32, (1, HALF), 1)
    if step > 0:
        edge = jnp.where(lane < HALF - SIDE, moved[:, HALF:], 0.0)
        return jnp.concatenate([moved[:, :HALF], edge], axis=1)
    edge = jnp.where(lane >= SIDE, moved[:, :HALF], 0.0)
    return jnp.concatenate([edge, moved[:, HALF:]], axis=1)


def store_matrices(ref, target, first, count):
    for pair in range(count // 2):
        rows = arranged(ref[:, 16 * pair : 16 * pair + 16, :].astype(F32), PLACE)
        for part in range(2):
            cut = rows[:, ROWS * part : ROWS * part + ROWS, :]
            target[first + 2 * pair + part, :, :] = cut.reshape(C, HALF).astype(BF16)


def matrix(own, other, block, first_other):
    return jnp.concatenate([own[block], other[block - first_other]], axis=1)


def own_first(ref, core):
    halves = [ref[core], ref[1 - core]]
    return jnp.concatenate([half.reshape(-1, POS) for half in halves], axis=0)


def in_order(values, core):
    top, bottom = values[:HALF], values[HALF:]
    first = core == 0
    return jnp.concatenate(
        [jnp.where(first, top, bottom), jnp.where(first, bottom, top)], axis=0
    )


def load_image(ref, at):
    block = arranged(ref[:, at : at + 16, :].astype(F32), PLACE)
    left = block[:, 0:ROWS, :].reshape(C, HALF)
    right = block[:, ROWS : 2 * ROWS, :].reshape(C, HALF)
    return jnp.concatenate([left, right], axis=1)


def image_rows(values):
    left = values[:, 0:HALF].reshape(SHARDS, ROWS, HALF)
    right = values[:, HALF:C].reshape(SHARDS, ROWS, HALF)
    return jnp.concatenate([left, right], axis=1).astype(BF16)


def store_shifts(target, values):
    for step in (-1, 0, 1):
        moved = (column_shifted(values, step, 1) if step else values).astype(BF16)
        target[0, step + 1, :, :] = moved[:HALF]
        target[1, step + 1, :, :] = moved[HALF:]


def half_convolve(matrices, shifts):
    operand = shifts.reshape(3 * HALF, POS)
    total = None
    for row in (0, -1, 1):
        product = dot_nn(jnp.concatenate(matrices[3 * row + 3 : 3 * row + 6], axis=1), operand)
        total = product if row == 0 else total + row_shifted(product, row)
    return total


def convolve(matrices, shifts, core):
    operand = [shifts[half, step] for step in range(3) for half in (core, 1 - core)]
    operand = jnp.concatenate(operand, axis=0)
    total = None
    for row in (0, -1, 1):
        product = dot_nn(jnp.concatenate(matrices[3 * row + 3 : 3 * row + 6], axis=1), operand)
        total = product if row == 0 else total + row_shifted(product, row)
    return total


def convolve_back(matrices, low, core):
    turned = low.T
    edge = jnp.zeros((SIDE, C), BF16)
    stacked = jnp.concatenate(
        [
            jnp.concatenate([turned[SIDE:], edge], axis=0),
            turned,
            jnp.concatenate([edge, turned[:-SIDE]], axis=0),
        ],
        axis=1,
    )
    total = None
    for step in (0, -1, 1):
        product = dot_nn(stacked, jnp.concatenate(matrices[step + 1 :: 3], axis=0))
        total = product if step == 0 else total + column_shifted(product, -step, 0)
    return in_order(total.T, core)


def lane_blocks(product):
    count = product.shape[1] // HALF
    cut = [product[:, HALF * k : HALF * k + HALF] for k in range(count)]
    return [values.reshape(SHARDS, ROWS, HALF) for values in cut]


def conv_weight_grads(lows, shifts):
    wide = [part.reshape(3 * HALF, POS) for part in shifts]
    rows = []
    for row in (-1, 0, 1):
        moved = [row_shifted(part.astype(F32), row).astype(BF16) if row else part for part in wide]
        rows.append(jnp.concatenate(moved, axis=1))
    return lane_blocks(dot_nt(jnp.concatenate(lows, axis=1), jnp.concatenate(rows, axis=0)))


def image_weight_grads(low, shifts):
    part = shifts.reshape(3 * HALF, POS)
    rows = [row_shifted(part.astype(F32), row).astype(BF16) if row else part for row in (-1, 0, 1)]
    return dot_nt(low, jnp.concatenate(rows, axis=0))


def store_blocks(target, blocks, order=range(SHARDS)):
    for pair in range(len(blocks) // 2):
        rows = jnp.concatenate(blocks[2 * pair : 2 * pair + 2], axis=1)
        target[:, 16 * pair : 16 * pair + 16, :] = arranged(rows, order).astype(BF16)


def columns_of(listed, table):
    lane = lax.broadcasted_iota(jnp.int32, (C, HALF), 1)
    for k, column in listed.items():
        table = jnp.where(lane == k, column, table)
    return table


def column(ref, lane):
    return ref[:, lane : lane + 1]


def by_rows(dot, left, right):
    return jnp.concatenate([dot(left[:HALF], right), dot(left[HALF:], right)], axis=0)


def row_sum(values):
    return jnp.sum(values, axis=1, keepdims=True)


def slope(values):
    sigma = sigmoid(values)
    return sigma * (1.0 + values * (1.0 - sigma))


def first_kernel(core_ref, recv_ref, taps_ref, hat_ref, params_ref, stats_ref, own_ref, partial_ref):
    columns = recv_ref[:, AT_PARAMS : AT_PARAMS + ROWS, :].astype(F32)
    columns = arranged(columns, PLACE).reshape(C, HALF)
    columns = (
        columns
        + pltpu.roll(columns, HALF - PART, 1)
        + pltpu.roll(columns, HALF - 2 * PART, 1)
    )
    params_ref[...] = columns
    hat, inverse = norm_hat(load_image(recv_ref, AT_SOURCE))
    hat_ref[...] = hat
    stats_ref[...] = jnp.broadcast_to(inverse, (C, HALF))
    pre = hat * columns[:, GAINS : GAINS + 1] + columns[:, BIASES : BIASES + 1]
    store_shifts(taps_ref, (pre * sigmoid(pre)).astype(BF16).astype(F32))
    store_matrices(recv_ref, own_ref, 0, WBLOCKS)
    partial_ref[...] = half_convolve([own_ref[tap] for tap in range(9)], taps_ref[core_ref[0]])


def middle_kernel(
    core_ref, recv_ref, swapped, taps_one, params, partial,
    other, taps_ref, hat_ref, stats_ref, halves_ref,
):
    store_matrices(swapped, other, 0, IN_CUT)
    rest = half_convolve([other[tap] for tap in range(9)], taps_one[1 - core_ref[0]])
    middle = partial[...] + rest
    middle = middle + (column(params, CONV_BIAS) + column(params, OFFSETS))
    hat, inverse = norm_hat(middle)
    hat_ref[...] = hat
    stats_ref[...] = jnp.broadcast_to(inverse, (C, HALF))
    pre = hat * column(params, GAINS + 1) + column(params, BIASES + 1)
    keep = load_image(recv_ref, AT_KEEP) * (1.0 / 0.9)
    store_shifts(taps_ref, (pre * sigmoid(pre) * keep).astype(BF16).astype(F32))
    away = 1 - core_ref[0]
    halves_ref[0 : 3 * HALF, :] = taps_one[away].reshape(3 * HALF, POS)
    halves_ref[3 * HALF : 6 * HALF, :] = taps_ref[away].reshape(3 * HALF, POS)
    halves_ref[6 * HALF :, :] = load_image(recv_ref, AT_COTANGENT).astype(BF16)


def attention_kernel(
    core_ref, recv_ref, swapped_two, swapped_three, taps_two, params, own, other_one,
    other, outputs_ref, grad_ref, sums_ref, normed_ref, halves_ref, grads_ref, swap_ref, turned,
):
    core = core_ref[0]
    half = (WBLOCKS - IN_CUT) // 2
    store_matrices(swapped_two, other, 0, half)
    store_matrices(swapped_three, other, half, half)
    out_matrix = matrix(own, other_one, OUT_BLOCK, 0)
    qkv = [
        matrix(own, other, QUERY_BLOCK, IN_CUT),
        matrix(own, other, KEY_BLOCK, IN_CUT),
        matrix(own, other, VALUE_BLOCK, IN_CUT),
    ]
    for k in range(3):
        turned[:, C * k : C * k + C] = qkv[k].T
    cotangent = load_image(recv_ref, AT_COTANGENT)
    cot_low = cotangent.astype(BF16)
    attended_grad = in_order(dot_tn(out_matrix, cot_low), core).astype(BF16)
    source = load_image(recv_ref, AT_SOURCE)
    matrices = [matrix(own, other, SECOND_CONV + tap, IN_CUT) for tap in range(9)]
    residual = source + convolve(matrices, taps_two, core) + column(params, CONV_BIAS + 1)
    hat, inverse = norm_hat(residual)
    normed = (hat * column(params, GAINS + 2) + column(params, BIASES + 2)).astype(BF16)
    scale = C ** (-0.5)
    normed_ref[0] = normed[:HALF]
    normed_ref[1] = normed[HALF:]
    operand = own_first(normed_ref, core)
    queries = (by_rows(dot_nn, qkv[0], operand) + column(params, QV_BIAS)).astype(BF16)
    keys = by_rows(dot_nn, qkv[1], operand).astype(BF16)
    vals = (by_rows(dot_nn, qkv[2], operand) + column(params, QV_BIAS + 1)).astype(BF16)
    scores = dot_tn(queries, keys) * scale
    dprobs = dot_tn(attended_grad, vals)
    exps = jnp.exp(scores - jnp.max(scores, axis=1, keepdims=True))
    probs = exps / row_sum(exps)
    probs_low = probs.astype(BF16)
    dscores = (probs * (dprobs - row_sum(probs * dprobs))).astype(BF16)
    query_grad = (by_rows(dot_nt, keys, dscores) * scale).astype(BF16)
    key_grad = (by_rows(dot_nn, queries, dscores) * scale).astype(BF16)
    value_grad = by_rows(dot_nn, attended_grad, probs_low).astype(BF16)
    grads = jnp.concatenate([query_grad, key_grad, value_grad], axis=0)
    normed_grad = by_rows(dot_nn, turned, grads)
    normed_grad = in_order(normed_grad, core)
    for k, gradient in enumerate((query_grad, key_grad, value_grad)):
        grads_ref[k, :, :] = gradient
    attended = by_rows(dot_nt, vals, probs_low).astype(BF16)
    halves_ref[0] = attended[:HALF]
    halves_ref[1] = attended[HALF:]
    product = by_rows(dot_nn, out_matrix, own_first(halves_ref, core))
    outputs = residual + product + column(params, OUT_BIAS)
    outputs_ref[...] = image_rows(outputs)
    branch, gain_grad, bias_grad = norm_back(hat, inverse, normed_grad, column(params, GAINS + 2))
    residual_grad = cotangent + branch
    grad_ref[...] = residual_grad
    swap_ref[0:HALF, :] = normed_ref[1 - core]
    swap_ref[HALF:C, :] = halves_ref[1 - core]
    swap_ref[C : 2 * C, :] = residual_grad.astype(BF16)
    for k, gradient in enumerate((query_grad, key_grad, value_grad)):
        swap_ref[C * k + 2 * C : C * k + 3 * C, :] = gradient
    listed = {
        D_GAINS + 2: gain_grad,
        D_BIASES + 2: bias_grad,
        D_CONV_BIAS + 1: row_sum(residual_grad),
        D_QV_BIAS: row_sum(query_grad.astype(F32)),
        D_QV_BIAS + 1: row_sum(value_grad.astype(F32)),
        D_OUT_BIAS: row_sum(cotangent),
    }
    sums_ref[...] = columns_of(listed, jnp.zeros((C, HALF), F32))


def middle_back_kernel(
    core_ref, recv_ref, own, other, hat_ref, stats, params, grad_ref, sums, low_ref, sums_ref
):
    hat = hat_ref[...]
    gain = column(params, GAINS + 1)
    pre = hat * gain + column(params, BIASES + 1)
    keep = load_image(recv_ref, AT_KEEP) * (1.0 / 0.9)
    factor = keep * slope(pre)
    matrices = [matrix(own, other, SECOND_CONV + tap, IN_CUT) for tap in range(9)]
    second_grad = convolve_back(matrices, grad_ref[...].astype(BF16), core_ref[0])
    pre_grad = second_grad * factor
    middle_grad, gain_grad, bias_grad = norm_back(hat, column(stats, 0), pre_grad, gain)
    low_ref[...] = middle_grad.astype(BF16)
    listed = {D_GAINS + 1: gain_grad, D_BIASES + 1: bias_grad, D_CONV_BIAS: row_sum(middle_grad)}
    sums_ref[...] = columns_of(listed, sums[...])


def first_back_kernel(
    core_ref, own, other, hat_ref, stats, params, low_ref, grad_ref, sums, taps_two,
    tail_ref, partial_ref,
):
    hat = hat_ref[...]
    gain = column(params, GAINS)
    pre = hat * gain + column(params, BIASES)
    factor = slope(pre)
    matrices = [matrix(own, other, tap, 0) for tap in range(9)]
    first_grad = convolve_back(matrices, low_ref[...], core_ref[0])
    branch, gain_grad, bias_grad = norm_back(hat, column(stats, 0), first_grad * factor, gain)
    tail_ref[:, :16, :] = image_rows(grad_ref[...] + branch)
    partial_ref[...] = image_weight_grads(grad_ref[...].astype(BF16), taps_two[core_ref[0]])

    table = columns_of({D_GAINS: gain_grad, D_BIASES: bias_grad}, sums[...])
    high = table.astype(BF16).astype(F32)
    low = pltpu.roll(table - high, PART, 1)
    lane = lax.broadcasted_iota(jnp.int32, (C, HALF), 1)
    table = jnp.where(lane < PART, high, low).reshape(SHARDS, ROWS, HALF)
    tail_ref[:, 16:, :] = jnp.concatenate([table, jnp.zeros_like(table)], axis=1).astype(BF16)


def second_grads_kernel(
    core_ref, recv_ref, partial, normed, attended, gradients, their_shifts, theirs, late_ref
):
    core = core_ref[0]
    product = image_weight_grads(theirs[C : 2 * C, :], their_shifts[3 * HALF : 6 * HALF, :])
    second = lane_blocks(partial[...] + product)
    operand = jnp.concatenate([normed[core], theirs[0:HALF, :]], axis=1)
    grads = jnp.concatenate([gradients[...].reshape(3 * C, POS), theirs[2 * C :, :]], axis=1)
    qkv = dot_nt(grads, operand)
    query, key, value = [lane_blocks(qkv[C * k : C * k + C])[0] for k in range(3)]
    operand = jnp.concatenate([attended[core], theirs[HALF:C, :]], axis=1)
    cotangent = load_image(recv_ref, AT_COTANGENT).astype(BF16)
    cotangents = jnp.concatenate([cotangent, their_shifts[6 * HALF :, :]], axis=1)
    out = lane_blocks(dot_nt(cotangents, operand))[0]
    store_blocks(late_ref, [query, key, *second, value, out, jnp.zeros_like(out)])


def gather_kernel(
    core_ref, taps_one, low_ref, their_shifts, their_low, late, outputs, tail, send_ref
):
    first = conv_weight_grads(
        [low_ref[...], their_low[...]], [taps_one[core_ref[0]], their_shifts[0 : 3 * HALF, :]]
    )
    cut = WROWS - IN_CUT_ROWS
    out = late[:, cut : cut + 16, :].astype(F32)[:, :ROWS, :]
    store_blocks(send_ref, first + [out], ORDER)
    send_ref[:, IN_CUT_ROWS:WROWS, :] = arranged(late[:, :cut, :], ORDER)
    send_ref[:, WROWS : WROWS + 16, :] = arranged(outputs[...], ORDER)
    send_ref[:, WROWS + 16 : WROWS + 40, :] = arranged(tail[:, :24, :], ORDER)


AT_SOURCE, AT_KEEP, AT_COTANGENT, AT_PARAMS = WROWS, WROWS + 16, WROWS + 32, WROWS + 48
IN_ROWS = WROWS + 56
OUT_ROWS = WROWS + 40
OUT_BLOCK, QUERY_BLOCK, KEY_BLOCK, SECOND_CONV, VALUE_BLOCK = 9, 10, 11, 12, 21
IN_CUT = 10
IN_CUT_ROWS = IN_CUT * ROWS


def local_call(kernel, core, *operands, out, scratch=()):
    in_specs = [pl.BlockSpec(memory_space=pltpu.VMEM) for _ in operands]
    if core is not None:
        in_specs = [pl.BlockSpec(memory_space=pltpu.SMEM)] + in_specs
        operands = (core, *operands)
    shapes = tuple(jax.ShapeDtypeStruct(shape, dtype) for shape, dtype in out)
    return pl.pallas_call(
        kernel,
        out_shape=shapes,
        in_specs=in_specs,
        out_specs=tuple(pl.BlockSpec(memory_space=pltpu.VMEM) for _ in out),
        scratch_shapes=[pltpu.VMEM(shape, dtype) for shape, dtype in scratch],
        compiler_params=pltpu.CompilerParams(vmem_limit_bytes=VMEM_LIMIT),
    )(*operands)


VMEM_LIMIT = 24 * 1024 * 1024


def run_block(core, received, swap):
    swapped_one = swap(received[:, :IN_CUT_ROWS])
    middle_row = (IN_CUT_ROWS + WROWS) // 2
    swapped_two = swap(received[:, IN_CUT_ROWS:middle_row])
    swapped_three = swap(received[:, middle_row:WROWS])
    image, table = ((C, POS), F32), ((C, HALF), F32)
    taps, low = ((2, 3, HALF, POS), BF16), ((C, POS), BF16)
    halves = ((2, HALF, POS), BF16)

    def matrices(count):
        return ((count, C, HALF), BF16)


    taps_one, hat_one, params, stats_one, own_weights, partial = local_call(
        first_kernel, core, received, out=(taps, image, table, table, matrices(WBLOCKS), image)
    )
    other_weights, taps_two, hat_two, stats_two, halves_out = local_call(
        middle_kernel, core, received, swapped_one, taps_one, params, partial,
        out=(matrices(IN_CUT), taps, image, table, ((6 * HALF + C, POS), BF16)),
    )
    rows = ((SHARDS, 16, HALF), BF16)
    their_shifts = swap(halves_out)
    other_two, outputs, residual_grad, sums, normed, attended, gradients, swapping = local_call(
        attention_kernel, core, received, swapped_two, swapped_three, taps_two, params, own_weights,
        other_weights,
        out=(
            matrices(WBLOCKS - IN_CUT), rows, image, table, halves, halves, ((3, C, POS), BF16),
            ((5 * C, POS), BF16),
        ),
        scratch=(((C, 3 * C), BF16),),
    )
    theirs = swap(swapping)
    residual_grad, their_shifts = lax.optimization_barrier((residual_grad, their_shifts))
    low_one, sums = local_call(
        middle_back_kernel, core, received, own_weights, other_two, hat_two, stats_two, params,
        residual_grad, sums, out=(low, table),
    )
    their_low = swap(low_one)
    tail, partial = local_call(
        first_back_kernel, core, own_weights, other_weights, hat_one, stats_one, params, low_one,
        residual_grad, sums, taps_two, out=(((SHARDS, 32, HALF), BF16), ((C, 9 * HALF), F32)),
    )
    (late,) = local_call(
        second_grads_kernel, core, received, partial, normed, attended, gradients,
        their_shifts, theirs, out=(((SHARDS, WROWS - IN_CUT_ROWS + 16, HALF), BF16),),
    )
    (send,) = local_call(
        gather_kernel, core, taps_one, low_one, their_shifts, their_low, late, outputs, tail,
        out=(((SHARDS, OUT_ROWS, HALF), BF16),),
    )
    return send


def collect_kernel(back_ref, swished_ref, sums_ref):
    for pair in range(WROWS // 16):
        rows = slice(16 * pair, 16 * pair + 16)
        total = back_ref[0, rows, :].astype(F32)
        for image in range(1, SHARDS):
            total = total + back_ref[image, rows, :].astype(F32)
        sums_ref[rows, :] = total.astype(BF16)
    small = back_ref[:, WROWS + 32 : WROWS + 40, :].astype(F32)
    table = jnp.zeros((ROWS, HALF), F32)
    temb = jnp.zeros((ROWS, TEMB), F32)
    for image in range(SHARDS):
        values = small[image] + pltpu.roll(small[image], HALF - PART, 1)
        table = table + values
        offsets_grad = values[:, D_CONV_BIAS : D_CONV_BIAS + 1]
        owner = ORDER[image]
        temb = temb + offsets_grad * swished_ref[owner : owner + 1, :]
    lane = lax.broadcasted_iota(jnp.int32, (ROWS, HALF), 1)
    high = table.astype(BF16).astype(F32)
    low = pltpu.roll(table - high, PART, 1)
    parts = jnp.where(lane < PART, high, jnp.where(lane < 2 * PART, low, 0.0))
    blocks = [parts] + [temb[:, HALF * k : HALF * k + HALF] for k in range(TEMB // HALF)]
    blocks = blocks + [jnp.zeros((ROWS, HALF), F32)]
    for pair in range(len(blocks) // 2):
        rows = slice(WROWS + 16 * pair, WROWS + 16 * pair + 16)
        both = jnp.concatenate(blocks[2 * pair : 2 * pair + 2], axis=0)
        sums_ref[rows, :] = both.astype(BF16)


SUM_ROWS = WROWS + ROWS + TEMB * ROWS // HALF + ROWS


def collect(back, swished):
    return pl.pallas_call(
        collect_kernel,
        out_shape=jax.ShapeDtypeStruct((SUM_ROWS, HALF), BF16),
        in_specs=[pl.BlockSpec(memory_space=pltpu.VMEM)] * 2,
        out_specs=pl.BlockSpec(memory_space=pltpu.VMEM),
        compiler_params=pltpu.CompilerParams(vmem_limit_bytes=8 * 1024 * 1024),
    )(back, swished)


def images_kernel(back_ref, outputs_ref, grad_ref):
    for at, target in ((WROWS, outputs_ref), (WROWS + 16, grad_ref)):
        block = arranged(back_ref[:, at : at + 16, :].astype(F32), PLACE)
        cut = jnp.concatenate([block[:, :ROWS, :], block[:, ROWS:, :]], axis=2)
        target[...] = jnp.swapaxes(cut, 0, 1).astype(BF16)


def images(back):
    shape = jax.ShapeDtypeStruct((ROWS, SHARDS, POS), BF16)
    return pl.pallas_call(
        images_kernel,
        out_shape=(shape, shape),
        in_specs=[pl.BlockSpec(memory_space=pltpu.VMEM)],
        out_specs=(pl.BlockSpec(memory_space=pltpu.VMEM), pl.BlockSpec(memory_space=pltpu.VMEM)),
        compiler_params=pltpu.CompilerParams(vmem_limit_bytes=8 * 1024 * 1024),
    )(back)


def finish_kernel(core_ref, mine_ref, theirs_ref, *refs):
    results, scratch, sems = refs[:10], refs[10:20], refs[20]
    first_core = core_ref[0] == 0
    (gain, bias, conv_w, conv_b, temb_w, temb_b, qkv_w, qv_b, out_w, out_b) = scratch

    def weight_grad(block):
        rows = slice(ROWS * block, ROWS * block + ROWS)
        mine, theirs = mine_ref[rows, :], theirs_ref[rows, :]
        return jnp.concatenate(
            [jnp.where(first_core, mine, theirs), jnp.where(first_core, theirs, mine)], axis=1
        )

    copies = [pltpu.make_async_copy(scratch[k], results[k], sems.at[k]) for k in range(10)]
    for conv in range(2):
        for tap in range(9):
            conv_w[conv, tap, :, :] = weight_grad(SECOND_CONV * conv + tap)
    copies[2].start()
    for k in range(3):
        qkv_w[k, :, :] = weight_grad((QUERY_BLOCK, KEY_BLOCK, VALUE_BLOCK)[k])
    copies[6].start()
    out_w[...] = weight_grad(OUT_BLOCK)
    copies[8].start()
    shared = mine_ref[WROWS:, :] + theirs_ref[WROWS:, :]
    small = shared[:ROWS, :] + pltpu.roll(shared[:ROWS, :], HALF - PART, 1)
    for part in range(TEMB // HALF):
        rows = slice(ROWS + ROWS * part, 2 * ROWS + ROWS * part)
        temb_w[:, HALF * part : HALF * part + HALF] = shared[rows, :]
    copies[4].start()
    padded = jnp.concatenate([small, jnp.zeros((HALF - ROWS, HALF), F32)], axis=0)
    table = padded.T[:PART, :ROWS]
    gain[...] = table[D_GAINS : D_GAINS + 3]
    bias[...] = table[D_BIASES : D_BIASES + 3]
    conv_b[...] = table[D_CONV_BIAS : D_CONV_BIAS + 2]
    temb_b[...] = table[D_CONV_BIAS : D_CONV_BIAS + 1]
    qv_b[...] = table[D_QV_BIAS : D_QV_BIAS + 2]
    out_b[...] = table[D_OUT_BIAS : D_OUT_BIAS + 1]
    for k in (0, 1, 3, 5, 7, 9):
        copies[k].start()
    for copy in copies:
        copy.wait()


def finish(core, mine, theirs):
    shapes = [
        (3, ROWS), (3, ROWS), (2, 9, ROWS, C), (2, ROWS), (ROWS, TEMB), (1, ROWS),
        (3, ROWS, C), (2, ROWS), (ROWS, C), (1, ROWS),
    ]
    return pl.pallas_call(
        finish_kernel,
        out_shape=[jax.ShapeDtypeStruct(shape, F32) for shape in shapes],
        in_specs=[
            pl.BlockSpec(memory_space=pltpu.SMEM),
            pl.BlockSpec(memory_space=pltpu.VMEM),
            pl.BlockSpec(memory_space=pltpu.VMEM),
        ],
        out_specs=[pl.BlockSpec(memory_space=pltpu.HBM) for _ in shapes],
        scratch_shapes=[pltpu.VMEM(shape, F32) for shape in shapes]
        + [pltpu.SemaphoreType.DMA((10,))],
        compiler_params=pltpu.CompilerParams(vmem_limit_bytes=8 * 1024 * 1024),
    )(core, mine, theirs)


def prepare_kernel(core_ref, *refs):
    count = PREPARE_ARRAYS
    arrays, (send_ref, swished_ref) = refs[:count], refs[count : count + 2]
    held, (angles, sems) = refs[count + 2 : 2 * count + 2], refs[2 * count + 2 :]
    (
        steps_ref, gain_ref, bias_ref, conv_bias_ref, qv_ref, out_bias_ref, temb_bias_ref,
        temb_ref, conv_ref, qkv_ref, out_ref, inputs_ref, mask_ref, cotangent_ref,
    ) = held
    copies = [pltpu.make_async_copy(arrays[k], held[k], sems.at[k]) for k in range(count)]
    for copy in copies:
        copy.start()
    first_core = core_ref[0] == 0
    for copy in copies[:8]:
        copy.wait()

    half_dim = TEMB // 2
    index = lax.broadcasted_iota(jnp.int32, (1, half_dim), 1).astype(F32)
    rates = jnp.exp(-math.log(10000.0) * index / (half_dim - 1))
    for image in range(SHARDS):
        angles[image : image + 1, :] = rates * steps_ref[image].astype(F32)
    angle = angles[...]
    turns = jnp.floor(angle * (2.0 / math.pi) + 0.5)
    rest = angle - turns * 1.5703125
    rest = rest - turns * 4.837512969970703125e-4
    rest = rest - turns * 7.549789954891882e-8
    square = rest * rest
    sine = rest + rest * square * (
        -1.6666654611e-1 + square * (8.3321608736e-3 + square * -1.9515295891e-4)
    )
    cosine = 1.0 - 0.5 * square + square * square * (
        4.166664568298827e-2 + square * (-1.388731625493765e-3 + square * 2.443315711809948e-5)
    )
    quarter = turns.astype(jnp.int32) & 3
    odd = (quarter & 1) == 1
    sines = jnp.where(odd, cosine, sine)
    cosines = jnp.where(odd, sine, cosine)
    sines = jnp.where(quarter >= 2, -sines, sines)
    cosines = jnp.where((quarter == 1) | (quarter == 2), -cosines, cosines)
    features = jnp.concatenate([sines, cosines], axis=1)
    swished = features * sigmoid(features)
    swished_ref[...] = swished
    offsets = None
    rest = swished
    for _ in range(2):
        part = rest.astype(BF16)
        rest = rest - part.astype(F32)
        product = dot_nt(temb_ref[...], part)
        offsets = product if offsets is None else offsets + product

    rows = jnp.concatenate(
        [
            jnp.zeros((1, ROWS), F32), gain_ref[...], bias_ref[...], conv_bias_ref[...],
            qv_ref[...], out_bias_ref[...], temb_bias_ref[...], jnp.zeros((3, ROWS), F32),
        ],
        axis=0,
    )
    square = jnp.concatenate([rows] * (HALF // PART), axis=0)
    square = jnp.concatenate([square, jnp.zeros((HALF, HALF - ROWS), F32)], axis=1)
    columns = square.T[:ROWS, :]
    lane = lax.broadcasted_iota(jnp.int32, (ROWS, HALF), 1)
    offset_lane = (lane & (PART - 1)) == OFFSETS
    offsets = offsets + columns[:, TEMB_BIAS : TEMB_BIAS + 1]
    for image in range(SHARDS):
        values = jnp.where(offset_lane, offsets[:, image : image + 1], columns)
        high = values.astype(BF16).astype(F32)
        mid = (values - high).astype(BF16).astype(F32)
        low = values - high - mid
        parts = jnp.where(
            lane < PART,
            high,
            jnp.where(lane < 2 * PART, mid, jnp.where(lane < 3 * PART, low, 0.0)),
        )
        send_ref[PLACE[image], WROWS + 48 : WROWS + 56, :] = parts.astype(BF16)

    for copy in copies[8:]:
        copy.wait()

    def half(values):
        values = values.astype(F32)
        return jnp.where(first_core, values[:, :HALF], values[:, HALF:])

    shard = jnp.concatenate(
        [
            half(conv_ref[0].reshape(9 * ROWS, C)),
            half(out_ref[...]),
            half(qkv_ref[0]),
            half(qkv_ref[1]),
            half(conv_ref[1].reshape(9 * ROWS, C)),
            half(qkv_ref[2]),
        ],
        axis=0,
    ).astype(BF16)
    send_ref[:, :WROWS, :] = jnp.broadcast_to(shard[None], (SHARDS, WROWS, HALF))

    def put(at, values):
        turned = jnp.swapaxes(values.astype(F32), 0, 1)
        cut = jnp.concatenate([turned[:, :, :HALF], turned[:, :, HALF:]], axis=1)
        send_ref[:, at : at + 16, :] = arranged(cut, ORDER).astype(BF16)

    put(WROWS, inputs_ref[...])
    put(WROWS + 16, mask_ref[...])
    put(WROWS + 32, cotangent_ref[...])


PREPARE_ARRAYS = 14


def prepare(core, timesteps, *arrays):
    held = [pltpu.SMEM((SHARDS,), jnp.int32)]
    held += [pltpu.VMEM(array.shape, array.dtype) for array in arrays]
    return pl.pallas_call(
        prepare_kernel,
        out_shape=(
            jax.ShapeDtypeStruct((SHARDS, IN_ROWS, HALF), BF16),
            jax.ShapeDtypeStruct((SHARDS, TEMB), F32),
        ),
        in_specs=[pl.BlockSpec(memory_space=pltpu.SMEM)]
        + [pl.BlockSpec(memory_space=pltpu.HBM)] * PREPARE_ARRAYS,
        out_specs=(pl.BlockSpec(memory_space=pltpu.VMEM), pl.BlockSpec(memory_space=pltpu.VMEM)),
        scratch_shapes=held
        + [pltpu.VMEM((SHARDS, TEMB // 2), F32), pltpu.SemaphoreType.DMA((PREPARE_ARRAYS,))],
        compiler_params=pltpu.CompilerParams(vmem_limit_bytes=16 * 1024 * 1024),
    )(core, *[pltpu.with_memory_space_constraint(a, pltpu.HBM) for a in (timesteps, *arrays)])


def exchange(values):
    return lax.all_to_all(
        values, "ch", split_axis=0, concat_axis=0, tiled=True, axis_index_groups=[list(ORDER)]
    )


def on_device(
    inputs,
    timesteps,
    keep_mask,
    norm_gain,
    norm_bias,
    conv_weight,
    conv_bias,
    temb_weight,
    temb_bias,
    qkv_weight,
    qv_bias,
    out_weight,
    out_bias,
    cotangent,
):
    member = lax.axis_index("img")
    core = member % 2
    core_pairs = [(m, m ^ 1) for m in range(4)]
    plane_pairs = [(m, m ^ 2) for m in range(4)]
    sent, swished = prepare(
        core.reshape(1),
        timesteps,
        norm_gain,
        norm_bias,
        conv_bias,
        qv_bias,
        out_bias.reshape(1, ROWS),
        temb_bias.reshape(1, ROWS),
        temb_weight.T,
        conv_weight,
        qkv_weight,
        out_weight,
        inputs,
        keep_mask,
        cotangent,
    )
    received = exchange(sent)
    send = run_block(
        core.reshape(1), received, lambda values: lax.ppermute(values, "img", core_pairs)
    )
    back = exchange(send)

    sums = collect(back, swished)
    plane = lax.ppermute(sums, "img", plane_pairs)
    outputs, input_grad = images(back)
    plane, outputs, input_grad = lax.optimization_barrier((plane, outputs, input_grad))
    sums = sums.astype(F32) + plane.astype(F32)
    theirs = lax.ppermute(sums, "img", core_pairs)
    (gain, bias, conv_w, conv_b, temb_w, temb_b, qkv_w, qv_b, out_w, out_b) = finish(
        core.reshape(1), sums, theirs
    )
    return (
        outputs,
        input_grad,
        gain,
        bias,
        conv_w,
        conv_b,
        temb_w.T,
        temb_b[0],
        qkv_w,
        qv_b,
        out_w,
        out_b[0],
    )


def solution(mesh):
    placed = (
        P("ch", "img", None),
        P("img"),
        P("ch", "img", None),
        P(None, "ch"),
        P(None, "ch"),
        P(None, None, "ch", None),
        P(None, "ch"),
        P(None, "ch"),
        P("ch"),
        P(None, "ch", None),
        P(None, "ch"),
        P("ch", None),
        P("ch"),
        P("ch", "img", None),
    )
    return jax.shard_map(
        on_device,
        mesh=mesh,
        in_specs=placed,
        out_specs=(
            P("ch", "img", None),
            P("ch", "img", None),
            P(None, "ch"),
            P(None, "ch"),
            P(None, None, "ch", None),
            P(None, "ch"),
            P(None, "ch"),
            P("ch"),
            P(None, "ch", None),
            P(None, "ch"),
            P("ch", None),
            P("ch"),
        ),
        check_vma=False,
    )
```
